32 devices in a mesh: seq: 16 (over z, y, x), frame: 2 (over core).
Axes of the slice: x: 2, y: 2, z: 4, core: 2. Of those that a mesh axis runs over, the one named last changes fastest.
Arguments:
- tokens: bfloat16 [16, 3136, 768], P('seq', 'frame'), may hold values from -6 to 6
- ln_gain_first: float32 [768], replicated, may hold values from 0.1 to 1.9
- ln_bias_first: float32 [768], replicated, may hold values from -2 to 2
- w_qkv: bfloat16 [768, 2304], replicated, may hold values from -0.21875 to 0.21875
- q_bias: float32 [768], replicated, may hold values from -3 to 3
- v_bias: float32 [768], replicated, may hold values from -3 to 3
- w_out: bfloat16 [768, 768], replicated, may hold values from -6 to 6
- out_bias: float32 [768], replicated, may hold values from -2 to 2
- ln_gain_second: float32 [768], replicated, may hold values from 0.1 to 1.9
- ln_bias_second: float32 [768], replicated, may hold values from -2 to 2
- w_up: bfloat16 [768, 3072], replicated, may hold values from -0.21875 to 0.21875
- up_bias: float32 [3072], replicated, may hold values from -3 to 3
- w_down: bfloat16 [3072, 768], replicated, may hold values from -0.109375 to 0.109375
- down_bias: float32 [768], replicated, may hold values from -2 to 2
- ln_gain_third: float32 [768], replicated, may hold values from 0.1 to 1.9
- ln_bias_third: float32 [768], replicated, may hold values from -2 to 2
- w_first: bfloat16 [768, 72], replicated, may hold values from -0.078125 to 0.078125
- conv_weights: float32 [3, 8, 72], replicated, may hold values from -0.75 to 0.75
- conv_biases: float32 [4, 8], replicated, may hold values from -3 to 3
- clip_lengths: int32 [16, 2], P('seq'), may hold values from 0 to 16, as said below
- frame_mask: int32 [16, 16], P('seq'), may hold values from 0 to 1, as said below
- out_cot: bfloat16 [16, 3136, 768], P('seq', 'frame'), may hold values from -6 to 6
- pool_cot: bfloat16 [16, 128, 768], P('seq', 'frame'), may hold values from -6 to 6
- penalty_scale: float32 [], replicated, may hold values from 25088 to 50176
Outputs:
- block_output: bfloat16 [16, 3136, 768], P('seq', 'frame')
- pooled_tokens: bfloat16 [16, 128, 768], P('seq', 'frame')
- penalty: float32 [], replicated
- tokens_grad: bfloat16 [16, 3136, 768], P('seq', 'frame')
- ln_gain_first_grad: float32 [768], replicated
- ln_bias_first_grad: float32 [768], replicated
- w_qkv_grad: float32 [768, 2304], P('seq', 'frame')
- q_bias_grad: float32 [768], replicated
- v_bias_grad: float32 [768], replicated
- w_out_grad: float32 [768, 768], P('seq', 'frame')
- out_bias_grad: float32 [768], replicated
- ln_gain_second_grad: float32 [768], replicated
- ln_bias_second_grad: float32 [768], replicated
- w_up_grad: float32 [768, 3072], P('seq', 'frame')
- up_bias_grad: float32 [3072], replicated
- w_down_grad: float32 [3072, 768], P('seq', 'frame')
- down_bias_grad: float32 [768], replicated
- ln_gain_third_grad: float32 [768], replicated
- ln_bias_third_grad: float32 [768], replicated
- w_first_grad: float32 [768, 72], P('seq', 'frame')
- conv_weights_grad: float32 [3, 8, 72], replicated
- conv_biases_grad: float32 [4, 8], replicated
The draws below stay inside these ranges and needn't reach their ends.
Inputs may be any that keep to these rules, and one draw needn't show every extreme that they name: `clip_lengths`: in each row the first entry is 8, 12 or 16 and the second is 16 minus the first; in every aligned block of 4 rows one row has first entry 16. `frame_mask`: frame 0 and the first frame of the second clip are 1 in every row.
All inputs are finite; a program needn't handle non-finite values.
Results may differ from the reference program's by a relative error of at most 0.012.
Values may be sent and summed in bfloat16 or wider, within the bound.
No kernel may reach another device: no remote copies, remote signals or barrier semaphores. Data moves between devices by JAX's collectives and lax.ppermute only.
A program may use at most 512 MiB of HBM per device.

```python
import jax
import jax.numpy as jnp
from jax import lax

D = 768
HEADS = 12
HEAD_DIM = 64
FF = 3072
GRID = 14
MAPS = 8
SLOT = 16
PIX = 196
LENGTH = 3136
SEQS = 16


def clip_layout(key):
    key = jax.random.fold_in(key, 17)
    groups = SEQS // 4
    picks = jax.random.randint(jax.random.fold_in(key, 1), (SEQS,), 1, 4)
    chosen = jax.random.randint(jax.random.fold_in(key, 2), (groups,), 0, 4)
    row_place = jnp.arange(SEQS, dtype=jnp.int32) % 4
    whole_clip = row_place == jnp.repeat(chosen, 4, total_repeat_length=SEQS)
    first = jnp.where(whole_clip, SLOT, (picks + 1) * SLOT // 4)
    lengths = jnp.stack([first, SLOT - first], axis=1).astype(jnp.int32)
    row_index = jnp.arange(SEQS, dtype=jnp.int32)
    level = 4 + 56 * row_index // max(SEQS - 1, 1)
    draws = jax.random.randint(jax.random.fold_in(key, 3), (SEQS, SLOT), 0, 64)
    keeping = draws < level[:, None]
    frames = jnp.arange(SLOT, dtype=jnp.int32)[None, :]
    starts = (frames == 0) | (frames == first[:, None])
    masks = (keeping | starts).astype(jnp.int32)
    return (lengths, masks)


def draw_clip_lengths(key, part):
    shared = clip_layout(key)
    return shared[0]


def draw_frame_mask(key, part):
    shared = clip_layout(key)
    return shared[1]


def block_scale(rng, extent, split, low, top_value):
    level, own = 1.0, jax.random.fold_in(rng, 6)
    for axis_at, parts in split:
        heights = jnp.exp(jax.random.uniform(jax.random.fold_in(own, axis_at), (parts,), jnp.float32, low / len(split), top_value / len(split)))
        level = level * jnp.repeat(heights, extent[axis_at] // parts).reshape([-1 if axis == axis_at else 1 for axis in range(len(extent))])
    return level


def bell_draw(own_key, extent, width, bound, shards=(), kind=jnp.bfloat16):
    level = block_scale(own_key, extent, shards, -0.22, 0.18) if shards else 1.0
    values = jax.random.normal(own_key, extent, jnp.float32) * width * level
    return jnp.minimum(jnp.maximum(values, -bound), bound).astype(kind)


def setup_inputs(seed: int = 0) -> dict:
    streams_of = jax.random.split(jax.random.key(seed), 25)
    return {
        "tokens": bell_draw(streams_of[0], (SEQS, LENGTH, D), 1.0, 6.0, ((0, 16), (1, 2))),
        "ln_gain_first": jnp.clip(1.0 + 0.18 * jax.random.normal(streams_of[1], (D,), jnp.float32), 0.1, 1.9),
        "ln_bias_first": bell_draw(streams_of[2], (D,), 0.3, 2.0, (), jnp.float32),
        "w_qkv": bell_draw(streams_of[3], (D, 3 * D), D ** -0.5, 0.21875),
        "q_bias": bell_draw(streams_of[4], (D,), 0.5, 3.0, (), jnp.float32),
        "v_bias": bell_draw(streams_of[5], (D,), 0.5, 3.0, (), jnp.float32),
        "w_out": bell_draw(streams_of[6], (D, D), (max(1, D * 8 // LENGTH)) ** -0.5, 6.0),
        "out_bias": bell_draw(streams_of[7], (D,), 0.3, 2.0, (), jnp.float32),
        "ln_gain_second": jnp.clip(1.0 + 0.18 * jax.random.normal(streams_of[8], (D,), jnp.float32), 0.1, 1.9),
        "ln_bias_second": bell_draw(streams_of[9], (D,), 0.3, 2.0, (), jnp.float32),
        "w_up": bell_draw(streams_of[10], (D, FF), D ** -0.5, 0.21875),
        "up_bias": bell_draw(streams_of[11], (FF,), 0.5, 3.0, (), jnp.float32),
        "w_down": bell_draw(streams_of[12], (FF, D), FF ** -0.5, 0.109375),
        "down_bias": bell_draw(streams_of[13], (D,), 0.3, 2.0, (), jnp.float32),
        "ln_gain_third": jnp.clip(1.0 + 0.18 * jax.random.normal(streams_of[14], (D,), jnp.float32), 0.1, 1.9),
        "ln_bias_third": bell_draw(streams_of[15], (D,), 0.3, 2.0, (), jnp.float32),
        "w_first": bell_draw(streams_of[16], (D, 9 * MAPS), (9 * D) ** -0.5, 0.078125),
        "conv_weights": bell_draw(streams_of[17], (3, MAPS, 9 * MAPS), (9 * MAPS) ** -0.5, 0.75, (), jnp.float32),
        "conv_biases": bell_draw(streams_of[18], (4, MAPS), 0.5, 3.0, (), jnp.float32),
        "clip_lengths": draw_clip_lengths(jax.random.fold_in(streams_of[24], 71), 0),
        "frame_mask": draw_frame_mask(jax.random.fold_in(streams_of[24], 71), 0),
        "out_cot": bell_draw(streams_of[21], (SEQS, LENGTH, D), 1.0, 6.0, ((0, 16), (1, 2))),
        "pool_cot": bell_draw(streams_of[22], (SEQS, SLOT * MAPS, D), 1.0, 6.0, ((0, 16), (1, 2))),
        "penalty_scale": jnp.clip(jax.random.uniform(streams_of[23], (), jnp.float32, 25088.0, 50176.0), 25088.0, 50176.0),
    }


@jax.custom_vjp
def low(v):
    return lax.optimization_barrier(v.astype(jnp.bfloat16)).astype(jnp.float32)

@jax.custom_vjp
def low_back(v):
    return v

def low_keep(v):
    return (low(v), None)

def low_pass(kept, grad):
    return (grad,)

def back_keep(v):
    return (v, None)

def back_low(kept, grad):
    return (low(grad),)
low.defvjp(low_keep, low_pass)
low_back.defvjp(back_keep, back_low)
EPS = 1e-06
NEG = -1e+30
HIGHEST = lax.Precision.HIGHEST

def norm_rows(rows, gain, shift):
    center = rows - lax.optimization_barrier(jnp.mean(rows, axis=-1, keepdims=True))
    spread = lax.optimization_barrier(jnp.mean(center * center, axis=-1, keepdims=True))
    return center * lax.rsqrt(spread + EPS) * gain + shift

def shift_sum(taps):
    padded = jnp.pad(taps, ((0, 0), (1, 1), (1, 1), (0, 0), (0, 0)))
    total = padded[:, 0:GRID, 0:GRID, 0, :]
    for tap in range(1, 9):
        total = total + padded[:, tap // 3:tap // 3 + GRID, tap % 3:tap % 3 + GRID, tap, :]
    return total

def conv_tail(first, conv_biases, conv_weights):
    frames = first.shape[0]
    level = shift_sum(first.reshape(frames, GRID, GRID, 9, MAPS)) + conv_biases[0]
    for layer in range(3):
        hidden = jax.nn.gelu(level, approximate=False)
        taps = jnp.einsum('fijc,ck->fijk', hidden, conv_weights[layer], precision=HIGHEST)
        level = shift_sum(taps.reshape(frames, GRID, GRID, 9, MAPS)) + conv_biases[layer + 1]
    return jax.nn.sigmoid(level).reshape(frames, GRID * GRID, MAPS)

def attend(queries, keys, values, query_code, key_code):
    blocks = 4
    size = queries.shape[0] // blocks

    def one_block(items):
        block_rows, block_code = items
        scores = low_back(jnp.einsum('qhe,khe->hqk', block_rows, keys, precision=HIGHEST) * HEAD_DIM ** (-0.5))
        allowed = (block_code[:, None] == key_code[None, :])[None]
        masked = jnp.where(allowed, scores, NEG)
        top = lax.optimization_barrier(jnp.max(masked, axis=-1, keepdims=True))
        mass = lax.optimization_barrier(jnp.sum(jnp.where(allowed, jnp.exp(masked - top), 0.0), axis=-1, keepdims=True))
        probs = low(jnp.where(allowed, jnp.exp(masked - top - jnp.log(mass)), 0.0))
        return jnp.einsum('hqk,khe->qhe', probs, values, precision=HIGHEST)
    result = lax.map(jax.checkpoint(one_block), (queries.reshape(blocks, size, HEADS, HEAD_DIM), query_code.reshape(blocks, size)))
    return result.reshape(blocks * size, HEADS * HEAD_DIM)

def forward_one(weights, tokens, lengths_row, mask_row):
    gain_one, bias_one, w_qkv, q_bias, v_bias, w_out, out_bias, gain_two, bias_two, w_up, up_bias, w_down, down_bias, gain_three, bias_three, w_first, conv_weights, conv_biases = weights
    frames = jnp.arange(SLOT, dtype=jnp.int32)
    segment_frames = (frames >= lengths_row[0]).astype(jnp.int32)
    key_frames = jnp.where(mask_row > 0, segment_frames, -1)
    query_code = jnp.repeat(segment_frames, PIX)
    key_code = jnp.repeat(key_frames, PIX)
    normed_one = low(norm_rows(tokens, gain_one, bias_one))
    qkv_bias = jnp.concatenate([q_bias, jnp.zeros_like(q_bias), v_bias])
    qkv = low_back(low(jnp.dot(normed_one, w_qkv, precision=HIGHEST) + qkv_bias))
    qkv = qkv.reshape(LENGTH, 3, HEADS, HEAD_DIM)
    attended = attend(qkv[:, 0], qkv[:, 1], qkv[:, 2], query_code, key_code)
    attended = low_back(low(attended))
    middle = tokens + low_back(jnp.dot(attended, w_out, precision=HIGHEST) + out_bias)
    normed_two = low(norm_rows(middle, gain_two, bias_two))
    upper = low_back(jnp.dot(normed_two, w_up, precision=HIGHEST) + up_bias)
    hidden = low(jax.nn.gelu(upper, approximate=False))
    output = middle + low_back(jnp.dot(hidden, w_down, precision=HIGHEST) + down_bias)
    normed_three = low(norm_rows(output, gain_three, bias_three))
    first = low_back(jnp.dot(normed_three, w_first, precision=HIGHEST))
    maps = conv_tail(first.reshape(SLOT, PIX, 9 * MAPS), conv_biases, conv_weights)
    valid = (mask_row > 0).astype(jnp.float32)
    pooled = jnp.einsum('fpm,fpd->fmd', low(maps), low(output).reshape(SLOT, PIX, D), precision=HIGHEST) * valid[:, None, None]
    total_map = lax.optimization_barrier(jnp.sum(maps, axis=-1))
    intersection = 0.5 * (total_map * total_map - lax.optimization_barrier(jnp.sum(maps * maps, axis=-1)))
    return (output, pooled.reshape(SLOT * MAPS, D), jnp.sum(intersection * valid[:, None]))

def reference(tokens, ln_gain_first, ln_bias_first, w_qkv, q_bias, v_bias, w_out, out_bias, ln_gain_second, ln_bias_second, w_up, up_bias, w_down, down_bias, ln_gain_third, ln_bias_third, w_first, conv_weights, conv_biases, clip_lengths, frame_mask, out_cot, pool_cot, penalty_scale):
    weights = (ln_gain_first, ln_bias_first, w_qkv.astype(jnp.float32), q_bias, v_bias, w_out.astype(jnp.float32), out_bias, ln_gain_second, ln_bias_second, w_up.astype(jnp.float32), up_bias, w_down.astype(jnp.float32), down_bias, ln_gain_third, ln_bias_third, w_first.astype(jnp.float32), conv_weights, conv_biases)
    count = jnp.sum(frame_mask).astype(jnp.float32)
    weight_cot = penalty_scale / count

    def one_step(carry, items):
        sums, intersection_total = carry
        token_row, lengths_row, mask_row, cot_row, pool_row = items

        def forward(params, inputs):
            return forward_one(params, inputs, lengths_row, mask_row)
        (output, pooled, intersection), pullback = jax.vjp(forward, weights, token_row.astype(jnp.float32))
        grad_params, grad_tokens = pullback((cot_row.astype(jnp.float32), pool_row.astype(jnp.float32), weight_cot))
        sums = jax.tree.map(jnp.add, sums, grad_params)
        return ((sums, intersection_total + intersection), (output.astype(jnp.bfloat16), pooled.astype(jnp.bfloat16), grad_tokens.astype(jnp.bfloat16)))
    start = (jax.tree.map(jnp.zeros_like, weights), jnp.zeros((), jnp.float32))
    (sums, intersection_total), (block_output, pooled_tokens, tokens_grad) = lax.scan(one_step, start, (tokens, clip_lengths, frame_mask, out_cot, pool_cot))
    penalty = intersection_total / count
    return (block_output, pooled_tokens, penalty, tokens_grad, sums[0], sums[1], sums[2], sums[3], sums[4], sums[5], sums[6], sums[7], sums[8], sums[9], sums[10], sums[11], sums[12], sums[13], sums[14], sums[15], sums[16], sums[17])
```

```python
import functools

import jax
import jax.numpy as jnp
import numpy as np
from jax import lax
from jax.experimental import pallas as pl
from jax.experimental.pallas import tpu as pltpu
from jax.sharding import PartitionSpec as P

HEADS = 12
HEAD_DIM = 64
GRID = 14
MAPS = 8


EPS = 1e-06
NEG = -1e30
HIGHEST = lax.Precision.HIGHEST


def norm_rows(rows, gain, shift):
    center = rows - jnp.mean(rows, axis=-1, keepdims=True)
    spread = jnp.mean(center * center, axis=-1, keepdims=True)
    return center * lax.rsqrt(spread + EPS) * gain + shift


def shift_sum(taps):
    padded = jnp.pad(taps, ((0, 0), (1, 1), (1, 1), (0, 0), (0, 0)))
    total = padded[:, 0:GRID, 0:GRID, 0, :]
    for tap in range(1, 9):
        total = total + padded[:, tap // 3 : tap // 3 + GRID, tap % 3 : tap % 3 + GRID, tap, :]
    return total


def conv_tail(first, conv_biases, conv_weights):
    frames = first.shape[0]
    level = shift_sum(first.reshape(frames, GRID, GRID, 9, MAPS)) + conv_biases[0]
    for layer in range(3):
        hidden = jax.nn.gelu(level, approximate=False)
        taps = jnp.einsum("fijc,ck->fijk", hidden, conv_weights[layer], precision=HIGHEST)
        level = shift_sum(taps.reshape(frames, GRID, GRID, 9, MAPS)) + conv_biases[layer + 1]
    return jax.nn.sigmoid(level).reshape(frames, GRID * GRID, MAPS)


def exact_gelu(values):
    return jax.nn.gelu(values, approximate=False)


def pair_mask(query_code, key_code):
    return (query_code[:, :, None] == key_code[:, None, :])[:, None]


def score_rows(query_rows, key_rows):
    return jnp.einsum(
        "sqhe,skhe->shqk", query_rows, key_rows, preferred_element_type=jnp.float32
    ) * HEAD_DIM ** (-0.5)


def pair_terms(query_rows, dout_rows, lse_rows, delta_rows, key_rows, value_rows, allowed):
    scores = score_rows(query_rows, key_rows)
    probs = jnp.where(allowed, jnp.exp(scores - lse_rows[..., None]), 0.0)
    slopes = jnp.einsum(
        "sqhe,skhe->shqk", dout_rows, value_rows, preferred_element_type=jnp.float32
    )
    grads = (probs * (slopes - delta_rows[..., None])).astype(jnp.bfloat16)
    return (probs.astype(jnp.bfloat16), grads)


def column_sum(values):
    return jnp.sum(values.astype(jnp.float32), axis=0)


def plain_device(
    tokens,
    ln_gain_first,
    ln_bias_first,
    w_qkv,
    q_bias,
    v_bias,
    w_out,
    out_bias,
    ln_gain_second,
    ln_bias_second,
    w_up,
    up_bias,
    w_down,
    down_bias,
    ln_gain_third,
    ln_bias_third,
    w_first,
    conv_weights,
    conv_biases,
    clip_lengths,
    frame_mask,
    out_cot,
    pool_cot,
    penalty_scale,
):
    seq_count, local, width = tokens.shape
    pixels = GRID * GRID
    frames_here = local // pixels
    frame_total = lax.axis_size("frame")
    frame_rank = lax.axis_index("frame")
    slot_frames = frames_here * frame_total
    length = local * frame_total
    rows = seq_count * local
    image_count = seq_count * frames_here
    scale = HEAD_DIM ** (-0.5)
    positions = jnp.arange(slot_frames, dtype=jnp.int32)[None, :]
    segment_frames = (positions >= clip_lengths[:, 0:1]).astype(jnp.int32)
    key_frames = jnp.where(frame_mask > 0, segment_frames, -1)
    first_frame = frame_rank * frames_here
    query_code = jnp.repeat(
        lax.dynamic_slice_in_dim(segment_frames, first_frame, frames_here, 1), pixels, axis=1
    )
    key_code = jnp.repeat(key_frames, pixels, axis=1)
    valid_here = (
        lax.dynamic_slice_in_dim(frame_mask, first_frame, frames_here, 1)
        .reshape(image_count)
        .astype(jnp.float32)
    )
    flat = tokens.reshape(rows, width).astype(jnp.float32)
    normed_one, back_one = jax.vjp(norm_rows, flat, ln_gain_first, ln_bias_first)
    normed_one = normed_one.astype(jnp.bfloat16)
    qkv_bias = jnp.concatenate([q_bias, jnp.zeros_like(q_bias), v_bias])
    qkv = (jnp.dot(normed_one, w_qkv, preferred_element_type=jnp.float32) + qkv_bias).astype(
        jnp.bfloat16
    )
    qkv = qkv.reshape(seq_count, local, 3, HEADS, HEAD_DIM)
    queries = qkv[:, :, 0]
    keys_here = qkv[:, :, 1]
    values_here = qkv[:, :, 2]
    keys_all, values_all = (
        lax.all_gather(keys_here, "frame", axis=1, tiled=True),
        lax.all_gather(values_here, "frame", axis=1, tiled=True),
    )

    def block_of(array, index):
        return lax.dynamic_slice_in_dim(array, index * local, local, 1)

    def stats_turn(index, carry):
        allowed = pair_mask(query_code, block_of(key_code, index))

        def stats_update(state):
            top, mass = state
            masked = jnp.where(allowed, score_rows(queries, block_of(keys_all, index)), NEG)
            new_top = jnp.maximum(top, jnp.max(masked, axis=-1))
            kept = jnp.where(allowed, jnp.exp(masked - new_top[..., None]), 0.0)
            return (new_top, mass * jnp.exp(top - new_top) + jnp.sum(kept, axis=-1))

        return lax.cond(jnp.any(allowed), stats_update, lambda state: state, carry)

    start_top = jnp.full((seq_count, HEADS, local), NEG, jnp.float32)
    top, mass = lax.fori_loop(0, frame_total, stats_turn, (start_top, jnp.zeros_like(start_top)))
    lse = top + jnp.log(mass)

    def value_turn(index, total):
        allowed = pair_mask(query_code, block_of(key_code, index))

        def value_update(state):
            scores = score_rows(queries, block_of(keys_all, index))
            probs = jnp.where(allowed, jnp.exp(scores - lse[..., None]), 0.0).astype(jnp.bfloat16)
            return state + jnp.einsum(
                "shqk,skhe->sqhe",
                probs,
                block_of(values_all, index),
                preferred_element_type=jnp.float32,
            )

        return lax.cond(jnp.any(allowed), value_update, lambda state: state, total)

    attended = lax.fori_loop(0, frame_total, value_turn, jnp.zeros(queries.shape, jnp.float32))
    attended_low = attended.astype(jnp.bfloat16).reshape(rows, width)
    middle = flat + jnp.dot(attended_low, w_out, preferred_element_type=jnp.float32) + out_bias
    normed_two, back_two = jax.vjp(norm_rows, middle, ln_gain_second, ln_bias_second)
    normed_two = normed_two.astype(jnp.bfloat16)
    upper = jnp.dot(normed_two, w_up, preferred_element_type=jnp.float32) + up_bias
    hidden, gelu_back = jax.vjp(exact_gelu, upper)
    hidden = hidden.astype(jnp.bfloat16)
    output = middle + jnp.dot(hidden, w_down, preferred_element_type=jnp.float32) + down_bias
    output_low = output.astype(jnp.bfloat16)
    normed_three, back_three = jax.vjp(norm_rows, output, ln_gain_third, ln_bias_third)
    normed_three = normed_three.astype(jnp.bfloat16)
    first = jnp.dot(normed_three, w_first, preferred_element_type=jnp.float32)
    maps, tail_back = jax.vjp(
        conv_tail, first.reshape(image_count, pixels, 9 * MAPS), conv_biases, conv_weights
    )
    maps_low = maps.astype(jnp.bfloat16)
    output_frames = output_low.reshape(image_count, pixels, width)
    pooled = (
        jnp.einsum("fpm,fpd->fmd", maps_low, output_frames, preferred_element_type=jnp.float32)
        * valid_here[:, None, None]
    )
    pooled_tokens = pooled.astype(jnp.bfloat16).reshape(seq_count, frames_here * MAPS, width)
    total_map = jnp.sum(maps, axis=-1)
    intersection = 0.5 * (total_map * total_map - jnp.sum(maps * maps, axis=-1))
    intersection_local = jnp.sum(intersection * valid_here[:, None])
    count_local = jnp.sum(valid_here)
    intersection_total, count_total = lax.psum((intersection_local, count_local), ("seq", "frame"))
    penalty = intersection_total / count_total
    pool_frames = pool_cot.reshape(image_count, MAPS, width)
    weight_cot = penalty_scale / count_total
    d_maps = (
        jnp.einsum("fmd,fpd->fpm", pool_frames, output_frames, preferred_element_type=jnp.float32)
        * valid_here[:, None, None]
    )
    d_maps = d_maps + (weight_cot * valid_here)[:, None, None] * (total_map[..., None] - maps)
    d_first, d_conv_biases, d_conv_weights = tail_back(d_maps)
    d_first = d_first.reshape(rows, 9 * MAPS).astype(jnp.bfloat16)
    grad_w_first = jnp.dot(normed_three.T, d_first, preferred_element_type=jnp.float32)
    d_normed_three = jnp.dot(d_first, w_first.T, preferred_element_type=jnp.float32)
    d_from_three, d_gain_three, d_bias_three = back_three(d_normed_three)
    d_pool_rows = (
        jnp.einsum("fpm,fmd->fpd", maps_low, pool_frames, preferred_element_type=jnp.float32)
        * valid_here[:, None, None]
    )
    d_output = (
        out_cot.reshape(rows, width).astype(jnp.float32)
        + d_from_three
        + d_pool_rows.reshape(rows, width)
    )
    d_down = d_output.astype(jnp.bfloat16)
    grad_w_down = jnp.dot(hidden.T, d_down, preferred_element_type=jnp.float32)
    grad_down_bias = column_sum(d_down)
    d_hidden = jnp.dot(d_down, w_down.T, preferred_element_type=jnp.float32)
    d_upper = gelu_back(d_hidden)[0].astype(jnp.bfloat16)
    grad_w_up = jnp.dot(normed_two.T, d_upper, preferred_element_type=jnp.float32)
    grad_up_bias = column_sum(d_upper)
    d_normed_two = jnp.dot(d_upper, w_up.T, preferred_element_type=jnp.float32)
    d_from_two, d_gain_two, d_bias_two = back_two(d_normed_two)
    d_middle = d_output + d_from_two
    d_branch = d_middle.astype(jnp.bfloat16)
    grad_w_out = jnp.dot(attended_low.T, d_branch, preferred_element_type=jnp.float32)
    grad_out_bias = column_sum(d_branch)
    dout_low = jnp.dot(d_branch, w_out.T, preferred_element_type=jnp.float32).astype(jnp.bfloat16)
    dout_low = dout_low.reshape(seq_count, local, HEADS, HEAD_DIM)
    delta = jnp.sum(dout_low.astype(jnp.float32) * attended, axis=-1).transpose(0, 2, 1)
    zeros_here = jnp.zeros(queries.shape, jnp.float32)
    full_zeros = jnp.zeros((seq_count, length, HEADS, HEAD_DIM), jnp.float32)

    def both_turn(index, carry):
        allowed = pair_mask(query_code, block_of(key_code, index))

        def both_update(state):
            grad_q, grad_k, grad_v = state
            key_rows = block_of(keys_all, index)
            probs, grads = pair_terms(
                queries, dout_low, lse, delta, key_rows, block_of(values_all, index), allowed
            )
            grad_q = (
                grad_q
                + jnp.einsum("shqk,skhe->sqhe", grads, key_rows, preferred_element_type=jnp.float32)
                * scale
            )
            part_k = (
                jnp.einsum("shqk,sqhe->skhe", grads, queries, preferred_element_type=jnp.float32)
                * scale
            )
            part_v = jnp.einsum(
                "shqk,sqhe->skhe", probs, dout_low, preferred_element_type=jnp.float32
            )
            grad_k = lax.dynamic_update_slice_in_dim(grad_k, part_k, index * local, 1)
            grad_v = lax.dynamic_update_slice_in_dim(grad_v, part_v, index * local, 1)
            return (grad_q, grad_k, grad_v)

        return lax.cond(jnp.any(allowed), both_update, lambda state: state, carry)

    grad_q, grad_k_all, grad_v_all = lax.fori_loop(
        0, frame_total, both_turn, (zeros_here, full_zeros, full_zeros)
    )
    grad_k, grad_v = (
        lax.psum_scatter(
            grad_k_all.astype(jnp.bfloat16), "frame", scatter_dimension=1, tiled=True
        ).astype(jnp.float32),
        lax.psum_scatter(
            grad_v_all.astype(jnp.bfloat16), "frame", scatter_dimension=1, tiled=True
        ).astype(jnp.float32),
    )
    grad_qkv = (
        jnp.stack([grad_q, grad_k, grad_v], axis=2).astype(jnp.bfloat16).reshape(rows, 3 * width)
    )
    grad_w_qkv = jnp.dot(normed_one.T, grad_qkv, preferred_element_type=jnp.float32)
    grad_q_bias = column_sum(grad_qkv[:, :width])
    grad_v_bias = column_sum(grad_qkv[:, 2 * width :])
    d_normed_one = jnp.dot(grad_qkv, w_qkv.T, preferred_element_type=jnp.float32)
    d_from_one, d_gain_one, d_bias_one = back_one(d_normed_one)
    tokens_grad = (d_middle + d_from_one).astype(jnp.bfloat16).reshape(seq_count, local, width)
    summed = (
        lax.psum_scatter(
            grad_w_qkv.astype(jnp.bfloat16), "seq", scatter_dimension=0, tiled=True
        ).astype(jnp.float32),
        lax.psum_scatter(
            grad_w_out.astype(jnp.bfloat16), "seq", scatter_dimension=0, tiled=True
        ).astype(jnp.float32),
        lax.psum_scatter(
            grad_w_up.astype(jnp.bfloat16), "seq", scatter_dimension=0, tiled=True
        ).astype(jnp.float32),
        lax.psum_scatter(
            grad_w_down.astype(jnp.bfloat16), "seq", scatter_dimension=0, tiled=True
        ).astype(jnp.float32),
        lax.psum_scatter(
            grad_w_first.astype(jnp.bfloat16), "seq", scatter_dimension=0, tiled=True
        ).astype(jnp.float32),
    )
    grad_w_qkv, grad_w_out, grad_w_up, grad_w_down, grad_w_first = (
        lax.psum_scatter(
            summed[0].astype(jnp.bfloat16), "frame", scatter_dimension=1, tiled=True
        ).astype(jnp.float32),
        lax.psum_scatter(
            summed[1].astype(jnp.bfloat16), "frame", scatter_dimension=1, tiled=True
        ).astype(jnp.float32),
        lax.psum_scatter(
            summed[2].astype(jnp.bfloat16), "frame", scatter_dimension=1, tiled=True
        ).astype(jnp.float32),
        lax.psum_scatter(
            summed[3].astype(jnp.bfloat16), "frame", scatter_dimension=1, tiled=True
        ).astype(jnp.float32),
        lax.psum_scatter(
            summed[4].astype(jnp.bfloat16), "frame", scatter_dimension=1, tiled=True
        ).astype(jnp.float32),
    )
    small = lax.psum(
        (
            d_gain_one,
            d_bias_one,
            d_gain_two,
            d_bias_two,
            d_gain_three,
            d_bias_three,
            grad_q_bias,
            grad_v_bias,
            grad_out_bias,
            grad_up_bias,
            grad_down_bias,
            d_conv_weights,
            d_conv_biases,
        ),
        ("seq", "frame"),
    )
    block_output = output_low.reshape(seq_count, local, width)
    return (
        block_output,
        pooled_tokens,
        penalty,
        tokens_grad,
        small[0],
        small[1],
        grad_w_qkv,
        small[6],
        small[7],
        grad_w_out,
        small[8],
        small[2],
        small[3],
        grad_w_up,
        small[9],
        grad_w_down,
        small[10],
        small[4],
        small[5],
        grad_w_first,
        small[11],
        small[12],
    )

FAR = -3e30
LOG2E = 1.4426950408889634
LN2 = 0.6931471805599453
NN = (((1,), (0,)), ((), ()))
NT = (((1,), (1,)), ((), ()))
TN = (((0,), (0,)), ((), ()))
PIXELS = 196
FRAME_ROWS = 208
CHUNK = 512
VMEM_LIMIT = 60 * 1024 * 1024


def dot(a, b, dims=NN):
    return lax.dot_general(a, b, dims, preferred_element_type=jnp.float32)


def compact_rows(frame_total):
    chunks = -(-frame_total * FRAME_ROWS // CHUNK) + 1
    return chunks * CHUNK


def compact_kernel(frames_here, info_ref, own_k, own_v, other_k, other_v, kc_ref, vc_ref, valid_ref, table_ref):
    total = 2 * frames_here
    length = info_ref[total]
    rank = info_ref[total + 1]
    count = [jnp.int32(0), jnp.int32(0)]
    places = []
    for f in range(total):
        kept = info_ref[f]
        late = (f >= length).astype(jnp.int32)
        places.append((kept, late, jnp.where(late == 1, count[1], count[0])))
        count[0] = count[0] + kept * (1 - late)
        count[1] = count[1] + kept * late
    chunks = [(c * FRAME_ROWS + CHUNK - 1) // CHUNK for c in count]
    base = [jnp.int32(0), chunks[0] * CHUNK]
    table_ref[total] = chunks[0]
    table_ref[total + 1] = chunks[0] + chunks[1]
    width = own_k.shape[1]
    zeros = jnp.zeros((CHUNK, width), jnp.bfloat16)
    valid_ref[...] = jnp.zeros_like(valid_ref)
    row = lax.broadcasted_iota(jnp.int32, (FRAME_ROWS, width), 0)

    def first_row(f):
        side = f // frames_here
        local = f % frames_here
        start = local * PIXELS // 16 * 16
        a = own_k[start : start + 16, :].astype(jnp.float32)
        b = other_k[start : start + 16, :].astype(jnp.float32)
        block = jnp.where(rank == side, a, b)
        at = local * PIXELS - start
        return block[at : at + 1, :]

    fills = [first_row(0), first_row(total // 2)]
    for f in range(total // 2 + 1, total):
        if (f * PIXELS) % 16 == 0:
            fills[1] = jnp.where(length == f, first_row(f), fills[1])
    for s in range(2):
        at = pl.multiple_of(base[s] + count[s] * FRAME_ROWS, 16)
        kc_ref[pl.ds(at, CHUNK), :] = jnp.broadcast_to(fills[s], (CHUNK, width)).astype(jnp.bfloat16)
        vc_ref[pl.ds(at, CHUNK), :] = zeros
    for f in range(total):
        kept, late, place = places[f]
        at = pl.multiple_of(jnp.where(late == 1, base[1], base[0]) + place * FRAME_ROWS, 16)
        table_ref[f] = jnp.where(kept == 1, at, -1)
        side = f // frames_here
        local = f % frames_here
        start = local * PIXELS // 16 * 16
        lo = local * PIXELS - start
        inside = (row >= lo) & (row < lo + PIXELS)

        def put(k_ref, v_ref):
            k = k_ref[start : start + FRAME_ROWS, :].astype(jnp.float32)
            v = v_ref[start : start + FRAME_ROWS, :].astype(jnp.float32)
            kc_ref[pl.ds(at, FRAME_ROWS), :] = jnp.where(inside, k, k[lo : lo + 1, :]).astype(jnp.bfloat16)
            vc_ref[pl.ds(at, FRAME_ROWS), :] = jnp.where(inside, v, 0.0).astype(jnp.bfloat16)
            valid_ref[pl.ds(at, FRAME_ROWS), :] = inside[:, :128].astype(jnp.bfloat16)

        @pl.when((kept == 1) & (rank == side))
        def _():
            put(own_k, own_v)

        @pl.when((kept == 1) & (rank != side))
        def _():
            put(other_k, other_v)


def compact(info, own_k, own_v, other_k, other_v, frames_here):
    rows, width = own_k.shape
    length = compact_rows(2 * frames_here)
    vm = pl.BlockSpec(memory_space=pltpu.VMEM)
    sm = pl.BlockSpec(memory_space=pltpu.SMEM)
    return pl.pallas_call(
        functools.partial(compact_kernel, frames_here),
        out_shape=(
            jax.ShapeDtypeStruct((length + CHUNK, width), jnp.bfloat16),
            jax.ShapeDtypeStruct((length + CHUNK, width), jnp.bfloat16),
            jax.ShapeDtypeStruct((length + CHUNK, 128), jnp.bfloat16),
            jax.ShapeDtypeStruct((2 * frames_here + 2,), jnp.int32),
        ),
        in_specs=[sm, vm, vm, vm, vm],
        out_specs=(vm, vm, vm, sm),
        compiler_params=pltpu.CompilerParams(vmem_limit_bytes=VMEM_LIMIT),
        name="compact",
    )(info, own_k, own_v, other_k, other_v)


def query_tiles(rows):
    parts = max(1, rows // 512)
    tiles = [(i * 512, 512) for i in range(parts)]
    last = tiles[-1][0]
    tiles[-1] = (last, rows - last)
    return tiles


def chunk_range(frames_here, table_ref, info_ref):
    total = 2 * frames_here
    length = info_ref[total]
    rank = info_ref[total + 1]
    first = rank * frames_here
    low = jnp.where(first >= length, table_ref[total], 0)
    high = jnp.where(first + frames_here <= length, table_ref[total], table_ref[total + 1])
    edge = jnp.clip((length - first) * PIXELS, 0, frames_here * PIXELS)
    return low, high, table_ref[total], edge


def split_heads(rows):
    lane = lax.broadcasted_iota(jnp.int32, rows.shape, 1)
    zero = jnp.zeros_like(rows)
    return jnp.where(lane < 64, rows, zero), jnp.where(lane < 64, zero, rows)


def bias_row(c, split, edge, at, size):
    column = lax.broadcasted_iota(jnp.int32, (1, size), 1) + at
    same = (column >= edge) == (c >= split)
    return jnp.where(same, 0.0, FAR)


def attn_fwd_kernel(frames_here, info_ref, table_ref, q_ref, k_ref, v_ref, valid_ref, o_ref, lse_ref, qm, vt, acc, top):
    rows = q_ref.shape[0]
    low, high, split, edge = chunk_range(frames_here, table_ref, info_ref)
    qm[0], qm[1] = split_heads(q_ref[...])
    acc[...] = jnp.zeros_like(acc)
    top[...] = jnp.full_like(top, NEG)
    tiles = query_tiles(rows)
    work = [(h, at, size) for h in range(2) for at, size in tiles]

    def prepare(c, carry):
        span = pl.ds(pl.multiple_of(c * CHUNK, CHUNK), CHUNK)
        turned = v_ref[span, :].T
        ones = valid_ref[span, :].T[:16]
        for h in range(2):
            vt[h, 0:64, span] = turned[64 * h : 64 * h + 64]
            vt[h, 64:80, span] = ones
        return carry

    lax.fori_loop(low, high, prepare, 0)

    def body(c, carry):
        span = pl.ds(pl.multiple_of(c * CHUNK, CHUNK), CHUNK)
        keys = k_ref[span, :]

        def scores(item):
            h, at, size = item
            return dot(keys, qm[h, at : at + size, :], NT)

        ahead = scores(work[0])
        for i, (h, at, size) in enumerate(work):
            s = ahead
            if i + 1 < len(work):
                ahead = scores(work[i + 1])
            bias = bias_row(c, split, edge, at, size)
            old = top[h : h + 1, at : at + size]
            new = jnp.maximum(old, jnp.max(s, axis=0, keepdims=True) + bias)
            p = jnp.exp2(s - (new - bias)).astype(jnp.bfloat16)
            top[h : h + 1, at : at + size] = new
            acc[h, :, at : at + size] = acc[h, :, at : at + size] * jnp.exp2(old - new) + dot(
                vt[h, :, span], p
            )
        return carry

    lax.fori_loop(low, high, body, 0)
    for at, size in tiles:
        halves = []
        for h in range(2):
            mass = acc[h, 64:65, at : at + size]
            halves.append(acc[h, 0:64, at : at + size] / mass)
            lse_ref[0, h : h + 1, at : at + size] = top[h : h + 1, at : at + size] + jnp.log2(mass)
        o_ref[at : at + size, :] = jnp.concatenate(halves, axis=0).T.astype(jnp.bfloat16)


def attn_fwd(info, table, q, kc, vc, valid, frames_here):
    rows, width = q.shape
    length = kc.shape[0]
    pairs = width // 128
    return pl.pallas_call(
        functools.partial(attn_fwd_kernel, frames_here),
        out_shape=(
            jax.ShapeDtypeStruct((rows, width), jnp.bfloat16),
            jax.ShapeDtypeStruct((pairs, 8, rows), jnp.float32),
        ),
        grid_spec=pltpu.PrefetchScalarGridSpec(
            num_scalar_prefetch=2,
            grid=(pairs,),
            in_specs=[
                pl.BlockSpec((rows, 128), lambda p, *_: (0, p)),
                pl.BlockSpec((length, 128), lambda p, *_: (0, p)),
                pl.BlockSpec((length, 128), lambda p, *_: (0, p)),
                pl.BlockSpec((length, 128), lambda p, *_: (0, 0)),
            ],
            out_specs=[
                pl.BlockSpec((rows, 128), lambda p, *_: (0, p)),
                pl.BlockSpec((1, 8, rows), lambda p, *_: (p, 0, 0)),
            ],
            scratch_shapes=[
                pltpu.VMEM((2, rows, 128), jnp.bfloat16),
                pltpu.VMEM((2, 80, length), jnp.bfloat16),
                pltpu.VMEM((2, 80, rows), jnp.float32),
                pltpu.VMEM((8, rows), jnp.float32),
            ],
        ),
        compiler_params=pltpu.CompilerParams(
            vmem_limit_bytes=VMEM_LIMIT, dimension_semantics=("arbitrary",)
        ),
        cost_estimate=pl.CostEstimate(flops=int(8e10), bytes_accessed=int(2e7), transcendentals=0),
        name="attn_fwd",
    )(info, table, q, kc, vc, valid)


def attn_bwd_kernel(
    frames_here, info_ref, table_ref, q_ref, k_ref, v_ref, valid_ref, o_ref, do_ref, lse_ref,
    dq_ref, dk_ref, dv_ref, qm, dom, kt, dqt, delta,
):
    rows = q_ref.shape[0]
    low, high, split, edge = chunk_range(frames_here, table_ref, info_ref)
    qm[0], qm[1] = split_heads(q_ref[...])
    dom[0], dom[1] = split_heads(do_ref[...])
    dqt[...] = jnp.zeros_like(dqt)
    tiles = query_tiles(rows)
    work = [(h, at, size) for h in range(2) for at, size in tiles]
    for at, size in tiles:
        span = slice(at, at + size)
        prod = (o_ref[span, :].astype(jnp.float32) * do_ref[span, :].astype(jnp.float32)).T
        for h in range(2):
            delta[h : h + 1, span] = jnp.sum(prod[64 * h : 64 * h + 64], axis=0, keepdims=True)

    def prepare(c, carry):
        span = pl.ds(pl.multiple_of(c * CHUNK, CHUNK), CHUNK)
        turned = (k_ref[span, :] * valid_ref[span, :]).T
        for h in range(2):
            kt[h, :, span] = turned[64 * h : 64 * h + 64]
        return carry

    lax.fori_loop(low, high, prepare, 0)

    def body(c, carry):
        span = pl.ds(pl.multiple_of(c * CHUNK, CHUNK), CHUNK)
        keys = k_ref[span, :]
        values = v_ref[span, :]

        def scores(item):
            h, at, size = item
            return (
                dot(keys, qm[h, at : at + size, :], NT),
                dot(values, dom[h, at : at + size, :], NT),
            )

        dk = jnp.zeros((CHUNK, 128), jnp.float32)
        dv = jnp.zeros((CHUNK, 128), jnp.float32)
        ahead = scores(work[0])
        for i, (h, at, size) in enumerate(work):
            s, dp = ahead
            if i + 1 < len(work):
                ahead = scores(work[i + 1])
            bias = bias_row(c, split, edge, at, size)
            p = jnp.exp2(s - (lse_ref[0, h : h + 1, at : at + size] - bias))
            ds = (p * (dp - delta[h : h + 1, at : at + size])).astype(jnp.bfloat16)
            dv = dv + dot(p.astype(jnp.bfloat16), dom[h, at : at + size, :])
            dk = dk + dot(ds, qm[h, at : at + size, :])
            dqt[h, :, at : at + size] += dot(kt[h, :, span], ds)
        dk_ref[span, :] = (dk * LN2).astype(jnp.bfloat16)
        dv_ref[span, :] = dv.astype(jnp.bfloat16)
        return carry

    lax.fori_loop(low, high, body, 0)
    for at, size in tiles:
        both = jnp.concatenate([dqt[0, :, at : at + size], dqt[1, :, at : at + size]], axis=0)
        dq_ref[at : at + size, :] = (both * 0.125).T.astype(jnp.bfloat16)


def attn_bwd(info, table, q, kc, vc, valid, o, do, lse, frames_here, group):
    rows, width = q.shape
    length = kc.shape[0]
    apart = width // 256
    rowspec = pl.BlockSpec((rows, 128), lambda p, *_: (0, group + apart * p))
    keyspec = pl.BlockSpec((length, 128), lambda p, *_: (0, group + apart * p))
    rowout = pl.BlockSpec((rows, 128), lambda p, *_: (0, p))
    keyout = pl.BlockSpec((length, 128), lambda p, *_: (0, p))
    return pl.pallas_call(
        functools.partial(attn_bwd_kernel, frames_here),
        out_shape=(
            jax.ShapeDtypeStruct((rows, 256), jnp.bfloat16),
            jax.ShapeDtypeStruct((length, 256), jnp.bfloat16),
            jax.ShapeDtypeStruct((length, 256), jnp.bfloat16),
        ),
        grid_spec=pltpu.PrefetchScalarGridSpec(
            num_scalar_prefetch=2,
            grid=(2,),
            in_specs=[
                rowspec,
                keyspec,
                keyspec,
                pl.BlockSpec((length, 128), lambda p, *_: (0, 0)),
                rowspec,
                rowspec,
                pl.BlockSpec((1, 8, rows), lambda p, *_: (group + apart * p, 0, 0)),
            ],
            out_specs=[rowout, keyout, keyout],
            scratch_shapes=[
                pltpu.VMEM((2, rows, 128), jnp.bfloat16),
                pltpu.VMEM((2, rows, 128), jnp.bfloat16),
                pltpu.VMEM((2, 64, length), jnp.bfloat16),
                pltpu.VMEM((2, 64, rows), jnp.float32),
                pltpu.VMEM((8, rows), jnp.float32),
            ],
        ),
        compiler_params=pltpu.CompilerParams(
            vmem_limit_bytes=VMEM_LIMIT, dimension_semantics=("arbitrary",)
        ),
        cost_estimate=pl.CostEstimate(flops=int(5e10), bytes_accessed=int(1e7), transcendentals=0),
        name="attn_bwd",
    )(info, table, q, kc, vc, valid, o, do, lse)


def spread_kernel(frames_here, info_ref, table_ref, dk_ref, dv_ref, ok_ref, ov_ref, xk_ref, xv_ref):
    total = 2 * frames_here
    length = info_ref[total]
    rank = info_ref[total + 1]
    first = rank * frames_here
    early = first < length
    late = first + frames_here > length
    quad = 4
    for f0 in range(0, total, quad):
        side = f0 // frames_here
        start = f0 % frames_here * PIXELS

        def put(k_out, v_out):
            for src, dst in ((dk_ref, k_out), (dv_ref, v_out)):
                parts = []
                for f in range(f0, f0 + quad):
                    lo = f % frames_here * PIXELS % 16
                    at = table_ref[f]
                    met = jnp.where(f >= length, late, early)
                    use = (at >= 0) & met
                    block = src[pl.ds(pl.multiple_of(jnp.maximum(at, 0), 16), FRAME_ROWS), :].astype(jnp.float32)
                    parts.append(jnp.where(use, block[lo : lo + PIXELS, :], 0.0))
                dst[start : start + quad * PIXELS, :] = jnp.concatenate(parts, axis=0).astype(jnp.bfloat16)

        @pl.when(rank == side)
        def _():
            put(ok_ref, ov_ref)

        @pl.when(rank != side)
        def _():
            put(xk_ref, xv_ref)


def spread(info, table, dk, dv, frames_here):
    rows = frames_here * PIXELS
    width = dk.shape[1]
    vm = pl.BlockSpec(memory_space=pltpu.VMEM)
    sm = pl.BlockSpec(memory_space=pltpu.SMEM)
    one = jax.ShapeDtypeStruct((rows, 256), jnp.bfloat16)
    return pl.pallas_call(
        functools.partial(spread_kernel, frames_here),
        out_shape=(one, one, one, one),
        in_specs=[sm, sm, vm, vm],
        out_specs=(vm, vm, vm, vm),
        compiler_params=pltpu.CompilerParams(vmem_limit_bytes=VMEM_LIMIT),
        name="spread",
    )(info, table, dk, dv)


TILE = 224
INV_SQRT2 = 0.7071067811865476
INV_SQRT_2PI = 0.3989422804014327
QUERY_SCALE = 0.125 * LOG2E


def params(**kw):
    return pltpu.CompilerParams(
        vmem_limit_bytes=VMEM_LIMIT, dimension_semantics=("arbitrary",), **kw
    )


def cost(flops, moved):
    return pl.CostEstimate(flops=int(flops), bytes_accessed=int(moved), transcendentals=0)


def tile_spec(width):
    return pl.BlockSpec((TILE, width), lambda i: (i, 0))


def whole_spec(shape):
    return pl.BlockSpec(shape, lambda i: (0,) * len(shape), pipeline_mode=pl.Buffered(1))


def low_shape(rows, width):
    return jax.ShapeDtypeStruct((rows, width), jnp.bfloat16)


def ln_parts(x):
    center = x - jnp.mean(x, axis=-1, keepdims=True)
    rstd = lax.rsqrt(jnp.mean(center * center, axis=-1, keepdims=True) + EPS)
    return center * rstd, rstd


def ln_back(dy, gain, xhat, rstd):
    dxhat = dy * gain
    along = jnp.mean(dxhat * xhat, axis=-1, keepdims=True)
    return rstd * (dxhat - jnp.mean(dxhat, axis=-1, keepdims=True) - xhat * along)


def rows_sum(x):
    return jnp.sum(x, axis=0, keepdims=True)


def project_kernel(x_ref, gain_ref, shift_ref, w_ref, bias_ref, n_ref, q_ref, k_ref, v_ref):
    width = x_ref.shape[1]
    xhat, _ = ln_parts(x_ref[...].astype(jnp.float32))
    normed = (xhat * gain_ref[...] + shift_ref[...]).astype(jnp.bfloat16)
    n_ref[...] = normed
    for i, (out, scale) in enumerate(((q_ref, QUERY_SCALE), (k_ref, None), (v_ref, None))):
        span = slice(i * width, (i + 1) * width)
        got = dot(normed, w_ref[:, span]) + bias_ref[:, span]
        out[...] = (got if scale is None else got * scale).astype(jnp.bfloat16)


def project(x, gain, shift, w, bias):
    rows, width = x.shape
    return pl.pallas_call(
        project_kernel,
        out_shape=(low_shape(rows, width),) * 4,
        grid=(rows // TILE,),
        in_specs=[
            tile_spec(width),
            whole_spec((1, width)),
            whole_spec((1, width)),
            whole_spec(w.shape),
            whole_spec((1, 3 * width)),
        ],
        out_specs=[tile_spec(width)] * 4,
        compiler_params=params(),
        cost_estimate=cost(6 * rows * width * width, 10 * rows * width + 6 * width * width),
        name="project",
    )(x, gain, shift, w, bias)


def mlp_fwd_kernel(
    x_ref, a_ref, w_out, b_out, gain2, shift2, w_up, b_up, w_down, b_down, gain3, shift3,
    mid_ref, n2_ref, hid_ref, slope_ref, out_ref, n3_ref,
):
    width = x_ref.shape[1]
    inner = w_up.shape[1]
    parts = inner // width
    middle = x_ref[...].astype(jnp.float32) + dot(a_ref[...], w_out[...]) + b_out[...]
    mid_ref[...] = middle.astype(jnp.bfloat16)
    xhat, _ = ln_parts(middle)
    n2 = (xhat * gain2[...] + shift2[...]).astype(jnp.bfloat16)
    n2_ref[...] = n2
    out = middle + b_down[...]

    def raise_part(j):
        span = slice(j * width, (j + 1) * width)
        return dot(n2, w_up[:, span]) + b_up[:, span]

    ahead = raise_part(0)
    for j in range(parts):
        span = slice(j * width, (j + 1) * width)
        up = ahead
        if j + 1 < parts:
            ahead = raise_part(j + 1)
        area = 0.5 + 0.5 * lax.erf(up * INV_SQRT2)
        bell = jnp.exp2(up * up * (-0.5 * LOG2E)) * INV_SQRT_2PI
        hid = (up * area).astype(jnp.bfloat16)
        hid_ref[:, span] = hid
        slope_ref[:, span] = (area + up * bell).astype(jnp.bfloat16)
        out = out + dot(hid, w_down[span, :])
    out_ref[...] = out.astype(jnp.bfloat16)
    xhat, _ = ln_parts(out)
    n3_ref[...] = (xhat * gain3[...] + shift3[...]).astype(jnp.bfloat16)


def mlp_fwd(x, attended, w_out, b_out, gain2, shift2, w_up, b_up, w_down, b_down, gain3, shift3):
    rows, width = x.shape
    inner = w_up.shape[1]
    vec = whole_spec((1, width))
    return pl.pallas_call(
        mlp_fwd_kernel,
        out_shape=(
            low_shape(rows, width), low_shape(rows, width), low_shape(rows, inner),
            low_shape(rows, inner), low_shape(rows, width), low_shape(rows, width),
        ),
        grid=(rows // TILE,),
        in_specs=[
            tile_spec(width), tile_spec(width), whole_spec(w_out.shape), vec, vec, vec,
            whole_spec(w_up.shape), whole_spec((1, inner)), whole_spec(w_down.shape), vec, vec, vec,
        ],
        out_specs=[
            tile_spec(width), tile_spec(width), tile_spec(inner),
            tile_spec(inner), tile_spec(width), tile_spec(width),
        ],
        compiler_params=params(),
        cost_estimate=cost(
            2 * rows * width * (width + 2 * inner), 2 * rows * (6 * width + 2 * inner)
        ),
        name="mlp_fwd",
    )(x, attended, w_out, b_out, gain2, shift2, w_up, b_up, w_down, b_down, gain3, shift3)


def mlp_bwd_kernel(
    cot_ref, out_ref, side_ref, pool_ref, w_first, gain3, w_down, slope_ref, w_up, mid_ref,
    gain2, w_out, ddown_ref, dup_ref, dbranch_ref, datt_ref, sums_ref,
):
    width = cot_ref.shape[1]
    inner = w_up.shape[1]
    parts = inner // width

    @pl.when(pl.program_id(0) == 0)
    def _():
        sums_ref[...] = jnp.zeros_like(sums_ref)

    def add(row, value):
        sums_ref[row : row + 1, :] += rows_sum(value)

    dn3 = dot(side_ref[:, :128], w_first[...])
    xhat, rstd = ln_parts(out_ref[...].astype(jnp.float32))
    add(2, dn3 * xhat)
    add(3, dn3)
    d_out = (
        cot_ref[...].astype(jnp.float32)
        + ln_back(dn3, gain3[...], xhat, rstd)
        + dot(side_ref[:, 128:192], pool_ref[...])
    )
    d_down = d_out.astype(jnp.bfloat16)
    ddown_ref[...] = d_down
    add(4, d_down.astype(jnp.float32))

    def lower_part(j):
        return dot(d_down, w_down[j * width : (j + 1) * width, :], NT)

    ahead = lower_part(0)
    dn2 = jnp.zeros(cot_ref.shape, jnp.float32)
    for j in range(parts):
        span = slice(j * width, (j + 1) * width)
        d_hid = ahead
        if j + 1 < parts:
            ahead = lower_part(j + 1)
        d_up = (d_hid * slope_ref[:, span].astype(jnp.float32)).astype(jnp.bfloat16)
        dup_ref[:, span] = d_up
        add(6 + j, d_up.astype(jnp.float32))
        dn2 = dn2 + dot(d_up, w_up[:, span], NT)
    xhat, rstd = ln_parts(mid_ref[...].astype(jnp.float32))
    add(0, dn2 * xhat)
    add(1, dn2)
    d_branch = (d_out + ln_back(dn2, gain2[...], xhat, rstd)).astype(jnp.bfloat16)
    dbranch_ref[...] = d_branch
    add(5, d_branch.astype(jnp.float32))
    datt_ref[...] = dot(d_branch, w_out[...], NT).astype(jnp.bfloat16)


def mlp_bwd(cot, out, side, pool, w_first, gain3, w_down, slope, w_up, mid, gain2, w_out):
    rows, width = cot.shape
    inner = w_up.shape[1]
    vec = whole_spec((1, width))
    return pl.pallas_call(
        mlp_bwd_kernel,
        out_shape=(
            low_shape(rows, width), low_shape(rows, inner), low_shape(rows, width),
            low_shape(rows, width), jax.ShapeDtypeStruct((16, width), jnp.float32),
        ),
        grid=(rows // TILE,),
        in_specs=[
            tile_spec(width), tile_spec(width), tile_spec(256), whole_spec(pool.shape),
            whole_spec(w_first.shape), vec, whole_spec(w_down.shape), tile_spec(inner),
            whole_spec(w_up.shape), tile_spec(width), vec, whole_spec(w_out.shape),
        ],
        out_specs=[
            tile_spec(width), tile_spec(inner), tile_spec(width), tile_spec(width),
            pl.BlockSpec((16, width), lambda i: (0, 0)),
        ],
        compiler_params=params(),
        cost_estimate=cost(
            2 * rows * width * (width + 2 * inner), 2 * rows * (6 * width + 2 * inner)
        ),
        name="mlp_bwd",
    )(cot, out, side, pool, w_first, gain3, w_down, slope, w_up, mid, gain2, w_out)


def final_bwd_kernel(dq_ref, dk_ref, dv_ref, x_ref, branch_ref, gain, w_ref, grad_ref, sums_ref):
    width = x_ref.shape[1]

    @pl.when(pl.program_id(0) == 0)
    def _():
        sums_ref[...] = jnp.zeros_like(sums_ref)

    def add(row, value):
        sums_ref[row : row + 1, :] += rows_sum(value)

    dn = (
        dot(dq_ref[...], w_ref[:, :width], NT)
        + dot(dk_ref[...], w_ref[:, width : 2 * width], NT)
        + dot(dv_ref[...], w_ref[:, 2 * width :], NT)
    )
    xhat, rstd = ln_parts(x_ref[...].astype(jnp.float32))
    add(0, dn * xhat)
    add(1, dn)
    add(2, dq_ref[...].astype(jnp.float32))
    add(3, dv_ref[...].astype(jnp.float32))
    grad_ref[...] = (
        branch_ref[...].astype(jnp.float32) + ln_back(dn, gain[...], xhat, rstd)
    ).astype(jnp.bfloat16)


def final_bwd(dq, dk, dv, x, branch, gain, w):
    rows, width = x.shape
    return pl.pallas_call(
        final_bwd_kernel,
        out_shape=(low_shape(rows, width), jax.ShapeDtypeStruct((8, width), jnp.float32)),
        grid=(rows // TILE,),
        in_specs=[tile_spec(width)] * 5 + [whole_spec((1, width)), whole_spec(w.shape)],
        out_specs=[tile_spec(width), pl.BlockSpec((8, width), lambda i: (0, 0))],
        compiler_params=params(),
        cost_estimate=cost(6 * rows * width * width, 12 * rows * width),
        name="final_bwd",
    )(dq, dk, dv, x, branch, gain, w)


def grid_masks(frames, lanes):
    table = np.zeros((16, lanes), np.float32)
    lane = np.arange(lanes)
    pixel = lane % PIXELS
    i, j = pixel // GRID, pixel % GRID
    inside = lane < frames * PIXELS
    for a in range(3):
        for b in range(3):
            ok = (i + a - 1 >= 0) & (i + a - 1 < GRID) & (j + b - 1 >= 0) & (j + b - 1 < GRID)
            table[3 * a + b] = ok & inside
    table[9] = np.where(inside, lane // PIXELS, -1)
    return table


def learner_kernel(
    frames, info_ref, weight_ref, n3_ref, out_ref, pool_ref, wt_ref, cw_ref, cwt_ref, cb_ref,
    mask_ref, side_ref, pooled_ref, small_ref, gfirst_ref,
):
    rows = n3_ref.shape[0]
    lanes = mask_ref.shape[1]
    extra = lanes - rows
    rank = info_ref[2 * frames + 1]
    frame_of = mask_ref[9:10, :]
    live = jnp.zeros((1, lanes), jnp.float32)
    for f in range(frames):
        kept = info_ref[rank * frames + f].astype(jnp.float32)
        live = live + jnp.where(frame_of == f, kept, 0.0)
    inside = (frame_of >= 0).astype(jnp.float32)

    def widen(x):
        return jnp.concatenate([x, jnp.zeros((x.shape[0], extra), jnp.float32)], axis=1)

    def turn(x, by):
        return x if by % lanes == 0 else pltpu.roll(x, by % lanes, 1)

    def gather_taps(taps):
        total = jnp.zeros((8, lanes), jnp.float32)
        for t in range(9):
            step = (t // 3 - 1) * GRID + t % 3 - 1
            total = total + turn(taps[8 * t : 8 * t + 8, :], -step) * mask_ref[t : t + 1, :]
        return total

    def spread_taps(level):
        parts = []
        for t in range(9):
            step = (t // 3 - 1) * GRID + t % 3 - 1
            parts.append(turn(level, step) * mask_ref[8 - t : 9 - t, :])
        return jnp.concatenate(parts, axis=0)

    def exact(a, b, dims=NN):
        return lax.dot_general(
            a, b, dims, precision=HIGHEST, preferred_element_type=jnp.float32
        )

    def area_of(x):
        return 0.5 + 0.5 * lax.erf(x * INV_SQRT2)

    taps = widen(dot(wt_ref[...], n3_ref[...], NT))
    levels = [gather_taps(taps) + cb_ref[:, 0:1]]
    hiddens = []
    for n in range(3):
        hiddens.append(levels[n] * area_of(levels[n]))
        levels.append(gather_taps(exact(cwt_ref[n], hiddens[n])) + cb_ref[:, n + 1 : n + 2])
    maps = 1.0 / (1.0 + jnp.exp(-levels[3]))
    total = rows_sum(maps)
    meet = 0.5 * (total * total - rows_sum(maps * maps)) * live
    small_ref[3] = jnp.zeros((8, 128), jnp.float32) + jnp.sum(meet)

    owner = lax.broadcasted_iota(jnp.int32, (8 * frames, lanes), 0) // 8
    mine = owner.astype(jnp.float32) == frame_of
    low_maps = maps.astype(jnp.bfloat16).astype(jnp.float32) * live
    stacked = jnp.where(mine, jnp.concatenate([low_maps] * frames, axis=0), 0.0)
    out = out_ref[...]
    pooled_ref[...] = dot(stacked[:, :rows].astype(jnp.bfloat16), out).astype(jnp.bfloat16)
    pairs = jnp.where(mine, widen(dot(pool_ref[...], out, NT)), 0.0)
    d_maps = pairs[0:8]
    for f in range(1, frames):
        d_maps = d_maps + pairs[8 * f : 8 * f + 8]
    d_maps = d_maps * live + weight_ref[0] * live * (total - maps)
    d_level = d_maps * maps * (1.0 - maps)
    for n in (2, 1, 0):
        small_ref[4 + n + 1] = jnp.broadcast_to(
            jnp.sum(d_level, axis=1, keepdims=True), (8, 128)
        )
        d_taps = spread_taps(d_level)
        small_ref[n] = jnp.concatenate(
            [exact(hiddens[n], d_taps, NT), jnp.zeros((8, 56), jnp.float32)], axis=1
        )
        d_hidden = exact(cw_ref[n], d_taps)
        x = levels[n]
        bell = jnp.exp(-0.5 * x * x) * INV_SQRT_2PI
        d_level = d_hidden * (area_of(x) + x * bell) * inside
    small_ref[4] = jnp.broadcast_to(jnp.sum(d_level, axis=1, keepdims=True), (8, 128))
    d_first = spread_taps(d_level)[:, :rows]
    gfirst_ref[...] = dot(d_first.astype(jnp.bfloat16), n3_ref[...])
    tall = jnp.concatenate(
        [
            d_first,
            jnp.zeros((56, rows), jnp.float32),
            stacked[:, :rows],
            jnp.zeros((128 - 8 * frames, rows), jnp.float32),
        ],
        axis=0,
    )
    side_ref[...] = tall.T.astype(jnp.bfloat16)


def learner(info, weight, n3, out, pool, w_first, conv_weights, conv_biases):
    rows, width = n3.shape
    frames = rows // PIXELS
    lanes = -(-rows // 128) * 128
    vm = pl.BlockSpec(memory_space=pltpu.VMEM)
    sm = pl.BlockSpec(memory_space=pltpu.SMEM)
    masks = jnp.asarray(grid_masks(frames, lanes))
    return pl.pallas_call(
        functools.partial(learner_kernel, frames),
        out_shape=(
            low_shape(rows, 256),
            low_shape(8 * frames, width),
            jax.ShapeDtypeStruct((8, 8, 128), jnp.float32),
            jax.ShapeDtypeStruct((9 * MAPS, width), jnp.float32),
        ),
        in_specs=[sm, sm] + [vm] * 8,
        out_specs=(vm, vm, vm, vm),
        compiler_params=pltpu.CompilerParams(vmem_limit_bytes=VMEM_LIMIT),
        cost_estimate=cost(2e10, 4 * rows * width),
        name="learner",
    )(
        info, weight, n3, out, pool, w_first.T, conv_weights,
        conv_weights.transpose(0, 2, 1), conv_biases.T, masks,
    )


def flip(count, bit):
    return [(i, i ^ bit) for i in range(count)]


def halve_frame(parts, rank):
    first, second = parts
    keep = jnp.where(rank == 0, first, second)
    send = jnp.where(rank == 0, second, first)
    got = lax.ppermute(send, "frame", flip(2, 1))
    return (keep.astype(jnp.float32) + got.astype(jnp.float32)).astype(jnp.bfloat16)


def halve_seq(x, order):
    count = lax.axis_size("seq")
    index = lax.axis_index("seq")
    bits = count.bit_length() - 1
    left = list(range(bits))[::-1]
    x = x.reshape((2,) * bits + x.shape[1:])
    for bit in order:
        axis = left.index(bit)
        left.remove(bit)
        mine = (index >> bit) & 1
        keep = lax.dynamic_index_in_dim(x, mine, axis, keepdims=False)
        send = lax.dynamic_index_in_dim(x, 1 - mine, axis, keepdims=False)
        got = lax.ppermute(send, "seq", flip(count, 1 << bit))
        x = (keep.astype(jnp.float32) + got.astype(jnp.float32)).astype(jnp.bfloat16)
    return x


def everywhere(x):
    count = lax.axis_size("seq")
    x = x + lax.ppermute(x, "frame", flip(2, 1))
    bit = 1
    while bit < count:
        x = x + lax.ppermute(x, "seq", flip(count, bit))
        bit *= 2
    return x


def weight_grad(a, b):
    return dot(a, b, TN).astype(jnp.bfloat16)


def orders(bits):
    low = list(range(bits))
    return [low[i:] + low[:i] for i in range(3)]


def quick_device(
    tokens, ln_gain_first, ln_bias_first, w_qkv, q_bias, v_bias, w_out, out_bias, ln_gain_second,
    ln_bias_second, w_up, up_bias, w_down, down_bias, ln_gain_third, ln_bias_third, w_first,
    conv_weights, conv_biases, clip_lengths, frame_mask, out_cot, pool_cot, penalty_scale,
):
    _, rows, width = tokens.shape
    frames = rows // PIXELS
    inner = w_up.shape[1]
    seqs = lax.axis_size("seq")
    rank = lax.axis_index("frame")
    share = width // seqs
    half = width // 2
    axis_orders = orders(seqs.bit_length() - 1)

    def row(x):
        return x.reshape(1, -1)

    all_masks = lax.all_gather(frame_mask, "seq", axis=0, tiled=True)
    count = jnp.sum(all_masks).astype(jnp.float32)
    weight = (penalty_scale / count).reshape(1)
    info = jnp.concatenate(
        [frame_mask[0], clip_lengths[0, 0:1], rank.reshape(1).astype(jnp.int32)]
    )
    x = tokens[0]
    qkv_bias = jnp.concatenate([q_bias, jnp.zeros_like(q_bias), v_bias])
    n1, q, k, v = project(x, row(ln_gain_first), row(ln_bias_first), w_qkv, row(qkv_bias))
    far_k = lax.ppermute(k, "frame", flip(2, 1))
    far_v = lax.ppermute(v, "frame", flip(2, 1))
    kc, vc, valid, table = compact(info, k, v, far_k, far_v, frames)
    attended, lse = attn_fwd(info, table, q, kc, vc, valid, frames)
    mid, n2, hidden, slope, out, n3 = mlp_fwd(
        x, attended, w_out, row(out_bias), row(ln_gain_second), row(ln_bias_second), w_up,
        row(up_bias), w_down, row(down_bias), row(ln_gain_third), row(ln_bias_third),
    )
    side, pooled, small, grad_first = learner(
        info, weight, n3, out, pool_cot[0], w_first, conv_weights, conv_biases
    )
    first_pad = jnp.concatenate(
        [w_first.T, jnp.zeros((128 - 9 * MAPS, width), jnp.bfloat16)], axis=0
    )
    d_down, d_up, d_branch, d_att, sums = mlp_bwd(
        out_cot[0], out, side, pool_cot[0], first_pad, row(ln_gain_third), w_down, slope, w_up,
        mid, row(ln_gain_second), w_out,
    )
    def halves(a, b):
        middle = b.shape[1] // 2
        return weight_grad(a, b[:, :middle]), weight_grad(a, b[:, middle:])

    up_sum = halve_frame(halves(n2, d_up), rank).reshape(seqs, share, inner // 2)
    down_sum = halve_frame(halves(hidden, d_down), rank).reshape(seqs, inner // seqs, half)
    wout_sum = halve_frame(halves(attended, d_branch), rank).reshape(seqs, share, half)
    grad_first = grad_first.astype(jnp.bfloat16).T
    columns = grad_first.shape[1] // 2
    first_sum = halve_frame((grad_first[:, :columns], grad_first[:, columns:]), rank)
    grad_up = halve_seq(up_sum, axis_orders[0])
    grad_down = halve_seq(down_sum, axis_orders[1])
    grad_out = halve_seq(wout_sum, axis_orders[2])
    grad_first = halve_seq(first_sum.reshape(seqs, share, columns), axis_orders[2])
    early = everywhere(jnp.concatenate([sums.reshape(-1), small.reshape(-1)]))

    groups = width // 128 // 2
    parts_q, parts_k, parts_v, parts_w = [], [], [], []
    for g in range(groups):
        dq, dkc, dvc = attn_bwd(info, table, q, kc, vc, valid, attended, d_att, lse, frames, g)
        own_k, own_v, other_k, other_v = spread(info, table, dkc, dvc, frames)

        def joined(own, other):
            got = lax.ppermute(other, "frame", flip(2, 1))
            return (own.astype(jnp.float32) + got.astype(jnp.float32)).astype(jnp.bfloat16)

        dk, dv = joined(own_k, other_k), joined(own_v, other_v)
        parts_q.append(dq)
        parts_k.append(dk)
        parts_v.append(dv)
        pair = (
            weight_grad(n1, jnp.concatenate([dq, dk[:, :128]], axis=1)),
            weight_grad(n1, jnp.concatenate([dk[:, 128:], dv], axis=1)),
        )
        summed = halve_frame(pair, rank).reshape(seqs, share, 384)
        parts_w.append(halve_seq(summed, axis_orders[g % 3]))

    def heads(parts):
        return jnp.concatenate([p[:, :128] for p in parts] + [p[:, 128:] for p in parts], axis=1)

    tokens_grad, late = final_bwd(
        heads(parts_q), heads(parts_k), heads(parts_v), x, d_branch, row(ln_gain_first), w_qkv
    )
    grad_qkv = jnp.concatenate(
        [p[:, 128 * i : 128 * i + 128] for i in range(3) for p in parts_w], axis=1
    )
    late = everywhere(late)
    sums = early[: 16 * width].reshape(16, width)
    small = early[16 * width :].reshape(8, 8, 128)
    penalty = small[3, 0, 0] / count
    f32 = jnp.float32
    return (
        out[None],
        pooled[None],
        penalty,
        tokens_grad[None],
        late[0],
        late[1],
        grad_qkv.astype(f32),
        late[2],
        late[3],
        grad_out.astype(f32),
        sums[5],
        sums[0],
        sums[1],
        grad_up.astype(f32),
        sums[6 : 6 + inner // width].reshape(-1),
        grad_down.astype(f32),
        sums[4],
        sums[2],
        sums[3],
        grad_first.astype(f32),
        small[:3, :, : 9 * MAPS],
        small[4:8, :, 0],
    )


def per_device(*arrays):
    tokens, clip_lengths = arrays[0], arrays[19]
    frames = tokens.shape[1] // PIXELS
    seqs = lax.axis_size("seq")
    fits = (
        tokens.shape[0] == 1
        and lax.axis_size("frame") == 2
        and frames % 4 == 0
        and tokens.shape[1] % TILE == 0
        and tokens.shape[2] == HEADS * HEAD_DIM
        and seqs & (seqs - 1) == 0
    )
    return (quick_device if fits else plain_device)(*arrays)


def solution(mesh):
    return jax.shard_map(
        per_device,
        mesh=mesh,
        in_specs=(
            P("seq", "frame", None),
            P(),
            P(),
            P(),
            P(),
            P(),
            P(),
            P(),
            P(),
            P(),
            P(),
            P(),
            P(),
            P(),
            P(),
            P(),
            P(),
            P(),
            P(),
            P("seq", None),
            P("seq", None),
            P("seq", "frame", None),
            P("seq", "frame", None),
            P(),
        ),
        out_specs=(
            P("seq", "frame", None),
            P("seq", "frame", None),
            P(),
            P("seq", "frame", None),
            P(),
            P(),
            P("seq", "frame"),
            P(),
            P(),
            P("seq", "frame"),
            P(),
            P(),
            P(),
            P("seq", "frame"),
            P(),
            P("seq", "frame"),
            P(),
            P(),
            P(),
            P("seq", "frame"),
            P(),
            P(),
        ),
        check_vma=False,
    )
```

```python
import functools

import jax
import jax.numpy as jnp
import numpy as np
from jax import lax
from jax.experimental import pallas as pl
from jax.experimental.pallas import tpu as pltpu
from jax.sharding import PartitionSpec as P

HEADS = 12
HEAD_DIM = 64
GRID = 14
MAPS = 8


EPS = 1e-06
NEG = -1e30
HIGHEST = lax.Precision.HIGHEST


def norm_rows(rows, gain, shift):
    center = rows - jnp.mean(rows, axis=-1, keepdims=True)
    spread = jnp.mean(center * center, axis=-1, keepdims=True)
    return center * lax.rsqrt(spread + EPS) * gain + shift


def shift_sum(taps):
    padded = jnp.pad(taps, ((0, 0), (1, 1), (1, 1), (0, 0), (0, 0)))
    total = padded[:, 0:GRID, 0:GRID, 0, :]
    for tap in range(1, 9):
        total = total + padded[:, tap // 3 : tap // 3 + GRID, tap % 3 : tap % 3 + GRID, tap, :]
    return total


def conv_tail(first, conv_biases, conv_weights):
    frames = first.shape[0]
    level = shift_sum(first.reshape(frames, GRID, GRID, 9, MAPS)) + conv_biases[0]
    for layer in range(3):
        hidden = jax.nn.gelu(level, approximate=False)
        taps = jnp.einsum("fijc,ck->fijk", hidden, conv_weights[layer], precision=HIGHEST)
        level = shift_sum(taps.reshape(frames, GRID, GRID, 9, MAPS)) + conv_biases[layer + 1]
    return jax.nn.sigmoid(level).reshape(frames, GRID * GRID, MAPS)


def exact_gelu(values):
    return jax.nn.gelu(values, approximate=False)


def pair_mask(query_code, key_code):
    return (query_code[:, :, None] == key_code[:, None, :])[:, None]


def score_rows(query_rows, key_rows):
    return jnp.einsum(
        "sqhe,skhe->shqk", query_rows, key_rows, preferred_element_type=jnp.float32
    ) * HEAD_DIM ** (-0.5)


def pair_terms(query_rows, dout_rows, lse_rows, delta_rows, key_rows, value_rows, allowed):
    scores = score_rows(query_rows, key_rows)
    probs = jnp.where(allowed, jnp.exp(scores - lse_rows[..., None]), 0.0)
    slopes = jnp.einsum(
        "sqhe,skhe->shqk", dout_rows, value_rows, preferred_element_type=jnp.float32
    )
    grads = (probs * (slopes - delta_rows[..., None])).astype(jnp.bfloat16)
    return (probs.astype(jnp.bfloat16), grads)


def column_sum(values):
    return jnp.sum(values.astype(jnp.float32), axis=0)


def plain_device(
    tokens,
    ln_gain_first,
    ln_bias_first,
    w_qkv,
    q_bias,
    v_bias,
    w_out,
    out_bias,
    ln_gain_second,
    ln_bias_second,
    w_up,
    up_bias,
    w_down,
    down_bias,
    ln_gain_third,
    ln_bias_third,
    w_first,
    conv_weights,
    conv_biases,
    clip_lengths,
    frame_mask,
    out_cot,
    pool_cot,
    penalty_scale,
):
    seq_count, local, width = tokens.shape
    pixels = GRID * GRID
    frames_here = local // pixels
    frame_total = lax.axis_size("frame")
    frame_rank = lax.axis_index("frame")
    slot_frames = frames_here * frame_total
    length = local * frame_total
    rows = seq_count * local
    image_count = seq_count * frames_here
    scale = HEAD_DIM ** (-0.5)
    positions = jnp.arange(slot_frames, dtype=jnp.int32)[None, :]
    segment_frames = (positions >= clip_lengths[:, 0:1]).astype(jnp.int32)
    key_frames = jnp.where(frame_mask > 0, segment_frames, -1)
    first_frame = frame_rank * frames_here
    query_code = jnp.repeat(
        lax.dynamic_slice_in_dim(segment_frames, first_frame, frames_here, 1), pixels, axis=1
    )
    key_code = jnp.repeat(key_frames, pixels, axis=1)
    valid_here = (
        lax.dynamic_slice_in_dim(frame_mask, first_frame, frames_here, 1)
        .reshape(image_count)
        .astype(jnp.float32)
    )
    flat = tokens.reshape(rows, width).astype(jnp.float32)
    normed_one, back_one = jax.vjp(norm_rows, flat, ln_gain_first, ln_bias_first)
    normed_one = normed_one.astype(jnp.bfloat16)
    qkv_bias = jnp.concatenate([q_bias, jnp.zeros_like(q_bias), v_bias])
    qkv = (jnp.dot(normed_one, w_qkv, preferred_element_type=jnp.float32) + qkv_bias).astype(
        jnp.bfloat16
    )
    qkv = qkv.reshape(seq_count, local, 3, HEADS, HEAD_DIM)
    queries = qkv[:, :, 0]
    keys_here = qkv[:, :, 1]
    values_here = qkv[:, :, 2]
    keys_all, values_all = (
        lax.all_gather(keys_here, "frame", axis=1, tiled=True),
        lax.all_gather(values_here, "frame", axis=1, tiled=True),
    )

    def block_of(array, index):
        return lax.dynamic_slice_in_dim(array, index * local, local, 1)

    def stats_turn(index, carry):
        allowed = pair_mask(query_code, block_of(key_code, index))

        def stats_update(state):
            top, mass = state
            masked = jnp.where(allowed, score_rows(queries, block_of(keys_all, index)), NEG)
            new_top = jnp.maximum(top, jnp.max(masked, axis=-1))
            kept = jnp.where(allowed, jnp.exp(masked - new_top[..., None]), 0.0)
            return (new_top, mass * jnp.exp(top - new_top) + jnp.sum(kept, axis=-1))

        return lax.cond(jnp.any(allowed), stats_update, lambda state: state, carry)

    start_top = jnp.full((seq_count, HEADS, local), NEG, jnp.float32)
    top, mass = lax.fori_loop(0, frame_total, stats_turn, (start_top, jnp.zeros_like(start_top)))
    lse = top + jnp.log(mass)

    def value_turn(index, total):
        allowed = pair_mask(query_code, block_of(key_code, index))

        def value_update(state):
            scores = score_rows(queries, block_of(keys_all, index))
            probs = jnp.where(allowed, jnp.exp(scores - lse[..., None]), 0.0).astype(jnp.bfloat16)
            return state + jnp.einsum(
                "shqk,skhe->sqhe",
                probs,
                block_of(values_all, index),
                preferred_element_type=jnp.float32,
            )

        return lax.cond(jnp.any(allowed), value_update, lambda state: state, total)

    attended = lax.fori_loop(0, frame_total, value_turn, jnp.zeros(queries.shape, jnp.float32))
    attended_low = attended.astype(jnp.bfloat16).reshape(rows, width)
    middle = flat + jnp.dot(attended_low, w_out, preferred_element_type=jnp.float32) + out_bias
    normed_two, back_two = jax.vjp(norm_rows, middle, ln_gain_second, ln_bias_second)
    normed_two = normed_two.astype(jnp.bfloat16)
    upper = jnp.dot(normed_two, w_up, preferred_element_type=jnp.float32) + up_bias
    hidden, gelu_back = jax.vjp(exact_gelu, upper)
    hidden = hidden.astype(jnp.bfloat16)
    output = middle + jnp.dot(hidden, w_down, preferred_element_type=jnp.float32) + down_bias
    output_low = output.astype(jnp.bfloat16)
    normed_three, back_three = jax.vjp(norm_rows, output, ln_gain_third, ln_bias_third)
    normed_three = normed_three.astype(jnp.bfloat16)
    first = jnp.dot(normed_three, w_first, preferred_element_type=jnp.float32)
    maps, tail_back = jax.vjp(
        conv_tail, first.reshape(image_count, pixels, 9 * MAPS), conv_biases, conv_weights
    )
    maps_low = maps.astype(jnp.bfloat16)
    output_frames = output_low.reshape(image_count, pixels, width)
    pooled = (
        jnp.einsum("fpm,fpd->fmd", maps_low, output_frames, preferred_element_type=jnp.float32)
        * valid_here[:, None, None]
    )
    pooled_tokens = pooled.astype(jnp.bfloat16).reshape(seq_count, frames_here * MAPS, width)
    total_map = jnp.sum(maps, axis=-1)
    intersection = 0.5 * (total_map * total_map - jnp.sum(maps * maps, axis=-1))
    intersection_local = jnp.sum(intersection * valid_here[:, None])
    count_local = jnp.sum(valid_here)
    intersection_total, count_total = lax.psum((intersection_local, count_local), ("seq", "frame"))
    penalty = intersection_total / count_total
    pool_frames = pool_cot.reshape(image_count, MAPS, width)
    weight_cot = penalty_scale / count_total
    d_maps = (
        jnp.einsum("fmd,fpd->fpm", pool_frames, output_frames, preferred_element_type=jnp.float32)
        * valid_here[:, None, None]
    )
    d_maps = d_maps + (weight_cot * valid_here)[:, None, None] * (total_map[..., None] - maps)
    d_first, d_conv_biases, d_conv_weights = tail_back(d_maps)
    d_first = d_first.reshape(rows, 9 * MAPS).astype(jnp.bfloat16)
    grad_w_first = jnp.dot(normed_three.T, d_first, preferred_element_type=jnp.float32)
    d_normed_three = jnp.dot(d_first, w_first.T, preferred_element_type=jnp.float32)
    d_from_three, d_gain_three, d_bias_three = back_three(d_normed_three)
    d_pool_rows = (
        jnp.einsum("fpm,fmd->fpd", maps_low, pool_frames, preferred_element_type=jnp.float32)
        * valid_here[:, None, None]
    )
    d_output = (
        out_cot.reshape(rows, width).astype(jnp.float32)
        + d_from_three
        + d_pool_rows.reshape(rows, width)
    )
    d_down = d_output.astype(jnp.bfloat16)
    grad_w_down = jnp.dot(hidden.T, d_down, preferred_element_type=jnp.float32)
    grad_down_bias = column_sum(d_down)
    d_hidden = jnp.dot(d_down, w_down.T, preferred_element_type=jnp.float32)
    d_upper = gelu_back(d_hidden)[0].astype(jnp.bfloat16)
    grad_w_up = jnp.dot(normed_two.T, d_upper, preferred_element_type=jnp.float32)
    grad_up_bias = column_sum(d_upper)
    d_normed_two = jnp.dot(d_upper, w_up.T, preferred_element_type=jnp.float32)
    d_from_two, d_gain_two, d_bias_two = back_two(d_normed_two)
    d_middle = d_output + d_from_two
    d_branch = d_middle.astype(jnp.bfloat16)
    grad_w_out = jnp.dot(attended_low.T, d_branch, preferred_element_type=jnp.float32)
    grad_out_bias = column_sum(d_branch)
    dout_low = jnp.dot(d_branch, w_out.T, preferred_element_type=jnp.float32).astype(jnp.bfloat16)
    dout_low = dout_low.reshape(seq_count, local, HEADS, HEAD_DIM)
    delta = jnp.sum(dout_low.astype(jnp.float32) * attended, axis=-1).transpose(0, 2, 1)
    zeros_here = jnp.zeros(queries.shape, jnp.float32)
    full_zeros = jnp.zeros((seq_count, length, HEADS, HEAD_DIM), jnp.float32)

    def both_turn(index, carry):
        allowed = pair_mask(query_code, block_of(key_code, index))

        def both_update(state):
            grad_q, grad_k, grad_v = state
            key_rows = block_of(keys_all, index)
            probs, grads = pair_terms(
                queries, dout_low, lse, delta, key_rows, block_of(values_all, index), allowed
            )
            grad_q = (
                grad_q
                + jnp.einsum("shqk,skhe->sqhe", grads, key_rows, preferred_element_type=jnp.float32)
                * scale
            )
            part_k = (
                jnp.einsum("shqk,sqhe->skhe", grads, queries, preferred_element_type=jnp.float32)
                * scale
            )
            part_v = jnp.einsum(
                "shqk,sqhe->skhe", probs, dout_low, preferred_element_type=jnp.float32
            )
            grad_k = lax.dynamic_update_slice_in_dim(grad_k, part_k, index * local, 1)
            grad_v = lax.dynamic_update_slice_in_dim(grad_v, part_v, index * local, 1)
            return (grad_q, grad_k, grad_v)

        return lax.cond(jnp.any(allowed), both_update, lambda state: state, carry)

    grad_q, grad_k_all, grad_v_all = lax.fori_loop(
        0, frame_total, both_turn, (zeros_here, full_zeros, full_zeros)
    )
    grad_k, grad_v = (
        lax.psum_scatter(
            grad_k_all.astype(jnp.bfloat16), "frame", scatter_dimension=1, tiled=True
        ).astype(jnp.float32),
        lax.psum_scatter(
            grad_v_all.astype(jnp.bfloat16), "frame", scatter_dimension=1, tiled=True
        ).astype(jnp.float32),
    )
    grad_qkv = (
        jnp.stack([grad_q, grad_k, grad_v], axis=2).astype(jnp.bfloat16).reshape(rows, 3 * width)
    )
    grad_w_qkv = jnp.dot(normed_one.T, grad_qkv, preferred_element_type=jnp.float32)
    grad_q_bias = column_sum(grad_qkv[:, :width])
    grad_v_bias = column_sum(grad_qkv[:, 2 * width :])
    d_normed_one = jnp.dot(grad_qkv, w_qkv.T, preferred_element_type=jnp.float32)
    d_from_one, d_gain_one, d_bias_one = back_one(d_normed_one)
    tokens_grad = (d_middle + d_from_one).astype(jnp.bfloat16).reshape(seq_count, local, width)
    summed = (
        lax.psum_scatter(
            grad_w_qkv.astype(jnp.bfloat16), "seq", scatter_dimension=0, tiled=True
        ).astype(jnp.float32),
        lax.psum_scatter(
            grad_w_out.astype(jnp.bfloat16), "seq", scatter_dimension=0, tiled=True
        ).astype(jnp.float32),
        lax.psum_scatter(
            grad_w_up.astype(jnp.bfloat16), "seq", scatter_dimension=0, tiled=True
        ).astype(jnp.float32),
        lax.psum_scatter(
            grad_w_down.astype(jnp.bfloat16), "seq", scatter_dimension=0, tiled=True
        ).astype(jnp.float32),
        lax.psum_scatter(
            grad_w_first.astype(jnp.bfloat16), "seq", scatter_dimension=0, tiled=True
        ).astype(jnp.float32),
    )
    grad_w_qkv, grad_w_out, grad_w_up, grad_w_down, grad_w_first = (
        lax.psum_scatter(
            summed[0].astype(jnp.bfloat16), "frame", scatter_dimension=1, tiled=True
        ).astype(jnp.float32),
        lax.psum_scatter(
            summed[1].astype(jnp.bfloat16), "frame", scatter_dimension=1, tiled=True
        ).astype(jnp.float32),
        lax.psum_scatter(
            summed[2].astype(jnp.bfloat16), "frame", scatter_dimension=1, tiled=True
        ).astype(jnp.float32),
        lax.psum_scatter(
            summed[3].astype(jnp.bfloat16), "frame", scatter_dimension=1, tiled=True
        ).astype(jnp.float32),
        lax.psum_scatter(
            summed[4].astype(jnp.bfloat16), "frame", scatter_dimension=1, tiled=True
        ).astype(jnp.float32),
    )
    small = lax.psum(
        (
            d_gain_one,
            d_bias_one,
            d_gain_two,
            d_bias_two,
            d_gain_three,
            d_bias_three,
            grad_q_bias,
            grad_v_bias,
            grad_out_bias,
            grad_up_bias,
            grad_down_bias,
            d_conv_weights,
            d_conv_biases,
        ),
        ("seq", "frame"),
    )
    block_output = output_low.reshape(seq_count, local, width)
    return (
        block_output,
        pooled_tokens,
        penalty,
        tokens_grad,
        small[0],
        small[1],
        grad_w_qkv,
        small[6],
        small[7],
        grad_w_out,
        small[8],
        small[2],
        small[3],
        grad_w_up,
        small[9],
        grad_w_down,
        small[10],
        small[4],
        small[5],
        grad_w_first,
        small[11],
        small[12],
    )

FAR = -3e30
LOG2E = 1.4426950408889634
LN2 = 0.6931471805599453
NN = (((1,), (0,)), ((), ()))
NT = (((1,), (1,)), ((), ()))
TN = (((0,), (0,)), ((), ()))
PIXELS = 196
FRAME_ROWS = 208
CHUNK = 512
VMEM_LIMIT = 60 * 1024 * 1024


def dot(a, b, dims=NN):
    return lax.dot_general(a, b, dims, preferred_element_type=jnp.float32)


def compact_rows(frame_total):
    chunks = -(-frame_total * FRAME_ROWS // CHUNK) + 2
    return chunks * CHUNK


def key_places(frames_here, info_ref):
    total = 2 * frames_here
    length = info_ref[total]
    count = [jnp.int32(0), jnp.int32(0)]
    places = []
    for f in range(total):
        kept = info_ref[f]
        late = (f >= length).astype(jnp.int32)
        places.append((kept, late, jnp.where(late == 1, count[1], count[0])))
        count[0] = count[0] + kept * (1 - late)
        count[1] = count[1] + kept * late
    chunks = [(c * FRAME_ROWS + CHUNK - 1) // CHUNK for c in count]
    start = chunks[0] * CHUNK
    starts = [
        (kept, pl.multiple_of(jnp.where(late == 1, start, 0) + place * FRAME_ROWS, 16))
        for kept, late, place in places
    ]
    tails = [
        pl.multiple_of(count[0] * FRAME_ROWS, 16),
        pl.multiple_of(start + count[1] * FRAME_ROWS, 16),
    ]
    return starts, tails, chunks[0], chunks[0] + chunks[1]


def chunk_range(frames_here, split, end, info_ref):
    total = 2 * frames_here
    length = info_ref[total]
    first = info_ref[total + 1] * frames_here
    low = jnp.where(first >= length, split, 0)
    high = jnp.where(first + frames_here <= length, split, end)
    edge = jnp.clip((length - first) * PIXELS, 0, frames_here * PIXELS)
    return low, high, edge


def gather_keys(frames_here, info_ref, starts, tails, own_k, own_v, far_k, far_v, kc, vc, valid):
    total = 2 * frames_here
    length = info_ref[total]
    rank = info_ref[total + 1]
    width = own_k.shape[1]
    row = lax.broadcasted_iota(jnp.int32, (FRAME_ROWS, width), 0)

    def first_row(f):
        local = f % frames_here
        start = local * PIXELS // 16 * 16
        at = local * PIXELS - start
        a = own_k[start : start + 16, :].astype(jnp.float32)[at : at + 1, :]
        b = far_k[start : start + 16, :].astype(jnp.float32)[at : at + 1, :]
        return jnp.where(rank == f // frames_here, a, b)

    fills = [first_row(0), first_row(total // 2)]
    for f in range(total // 2 + 1, total):
        if (f * PIXELS) % 16 == 0:
            fills[1] = jnp.where(length == f, first_row(f), fills[1])
    for s in range(2):
        span = pl.ds(tails[s], CHUNK)
        kc[span, :] = jnp.broadcast_to(fills[s], (CHUNK, width)).astype(jnp.bfloat16)
        vc[span, :] = jnp.zeros((CHUNK, width), jnp.bfloat16)
        valid[span, :] = jnp.zeros((CHUNK, 128), jnp.bfloat16)
    for f in range(total):
        kept, at = starts[f]
        side = f // frames_here
        local = f % frames_here
        start = local * PIXELS // 16 * 16
        lo = local * PIXELS - start
        inside = (row >= lo) & (row < lo + PIXELS)

        def put(k_ref, v_ref):
            k = k_ref[start : start + FRAME_ROWS, :].astype(jnp.float32)
            v = v_ref[start : start + FRAME_ROWS, :].astype(jnp.float32)
            span = pl.ds(at, FRAME_ROWS)
            kc[span, :] = jnp.where(inside, k, k[lo : lo + 1, :]).astype(jnp.bfloat16)
            vc[span, :] = jnp.where(inside, v, 0.0).astype(jnp.bfloat16)
            valid[span, :] = inside.astype(jnp.bfloat16)

        @pl.when((kept == 1) & (rank == side))
        def _():
            put(own_k, own_v)

        @pl.when((kept == 1) & (rank != side))
        def _():
            put(far_k, far_v)


def query_tiles(rows):
    parts = max(1, rows // 512)
    tiles = [(i * 512, 512) for i in range(parts)]
    last = tiles[-1][0]
    tiles[-1] = (last, rows - last)
    return tiles


def split_heads(rows):
    lane = lax.broadcasted_iota(jnp.int32, rows.shape, 1)
    zero = jnp.zeros_like(rows)
    return jnp.where(lane < 64, rows, zero), jnp.where(lane < 64, zero, rows)


def bias_row(c, split, edge, at, size):
    column = lax.broadcasted_iota(jnp.int32, (1, size), 1) + at
    same = (column >= edge) == (c >= split)
    return jnp.where(same, 0.0, FAR)


def attn_fwd_kernel(
    frames_here, info_ref, q_ref, own_k, own_v, far_k, far_v, o_ref, lse_ref, kc_ref, vc_ref,
    valid_ref, qm, vt, acc, top,
):
    rows = q_ref.shape[0]
    starts, tails, split, end = key_places(frames_here, info_ref)
    low, high, edge = chunk_range(frames_here, split, end, info_ref)
    gather_keys(
        frames_here, info_ref, starts, tails, own_k, own_v, far_k, far_v, kc_ref, vc_ref, valid_ref
    )
    qm[0], qm[1] = split_heads(q_ref[...])
    acc[...] = jnp.zeros_like(acc)
    top[...] = jnp.full_like(top, NEG)
    tiles = query_tiles(rows)
    work = [(h, at, size) for h in range(2) for at, size in tiles]

    def prepare(c, carry):
        span = pl.ds(pl.multiple_of(c * CHUNK, CHUNK), CHUNK)
        turned = vc_ref[span, :].T
        ones = valid_ref[span, :].T[:16]
        for h in range(2):
            vt[h, 0:64, span] = turned[64 * h : 64 * h + 64]
            vt[h, 64:80, span] = ones
        return carry

    lax.fori_loop(low, high, prepare, 0)

    def body(c, carry):
        span = pl.ds(pl.multiple_of(c * CHUNK, CHUNK), CHUNK)
        keys = kc_ref[span, :]

        def scores(item):
            h, at, size = item
            return dot(keys, qm[h, at : at + size, :], NT)

        ahead = scores(work[0])
        for i, (h, at, size) in enumerate(work):
            s = ahead
            if i + 1 < len(work):
                ahead = scores(work[i + 1])
            bias = bias_row(c, split, edge, at, size)
            old = top[h : h + 1, at : at + size]
            new = jnp.maximum(old, jnp.max(s, axis=0, keepdims=True) + bias)
            p = jnp.exp2(s - (new - bias)).astype(jnp.bfloat16)
            top[h : h + 1, at : at + size] = new
            acc[h, :, at : at + size] = acc[h, :, at : at + size] * jnp.exp2(old - new) + dot(
                vt[h, :, span], p
            )
        return carry

    lax.fori_loop(low, high, body, 0)
    for at, size in tiles:
        halves = []
        for h in range(2):
            mass = acc[h, 64:65, at : at + size]
            halves.append(acc[h, 0:64, at : at + size] / mass)
            lse_ref[0, h : h + 1, at : at + size] = top[h : h + 1, at : at + size] + jnp.log2(mass)
        o_ref[at : at + size, :] = jnp.concatenate(halves, axis=0).T.astype(jnp.bfloat16)


def attn_fwd(info, q, own_k, own_v, far_k, far_v, old, part, frames_here):
    rows, width = q.shape
    pairs = width // 256
    length = compact_rows(2 * frames_here)
    block = pl.BlockSpec((rows, 128), lambda p, *_: (0, p))
    column = pl.BlockSpec((rows, 128), lambda p, *_: (0, p + part * pairs))
    keys = pl.BlockSpec((length, 128), lambda p, *_: (0, p))
    olds = [] if old is None else [old]

    def kernel(*refs):
        return attn_fwd_kernel(frames_here, *refs[:6], *refs[6 + len(olds) :])

    return pl.pallas_call(
        kernel,
        out_shape=(
            jax.ShapeDtypeStruct((rows, width), jnp.bfloat16),
            jax.ShapeDtypeStruct((pairs, 8, rows), jnp.float32),
            jax.ShapeDtypeStruct((length, width // 2), jnp.bfloat16),
            jax.ShapeDtypeStruct((length, width // 2), jnp.bfloat16),
            jax.ShapeDtypeStruct((length, 128), jnp.bfloat16),
        ),
        grid_spec=pltpu.PrefetchScalarGridSpec(
            num_scalar_prefetch=1,
            grid=(pairs,),
            in_specs=[column, block, block, block, block] + [pl.BlockSpec(memory_space=pl.ANY)] * len(olds),
            out_specs=[
                column,
                pl.BlockSpec((1, 8, rows), lambda p, *_: (p, 0, 0)),
                keys,
                keys,
                pl.BlockSpec((length, 128), lambda p, *_: (0, 0)),
            ],
            scratch_shapes=[
                pltpu.VMEM((2, rows, 128), jnp.bfloat16),
                pltpu.VMEM((2, 80, length), jnp.bfloat16),
                pltpu.VMEM((2, 80, rows), jnp.float32),
                pltpu.VMEM((8, rows), jnp.float32),
            ],
        ),
        input_output_aliases={6: 0} if olds else {},
        compiler_params=params(),
        cost_estimate=cost(4e10, 1e7),
        name="attn_fwd",
    )(info, q, own_k, own_v, far_k, far_v, *olds)


def attn_bwd_kernel(
    frames_here, info_ref, q_ref, k_ref, v_ref, valid_ref, o_ref, do_ref, lse_ref,
    dq_ref, own_dk, own_dv, far_dk, far_dv, qm, dom, kt, dqt, delta, dk_all, dv_all,
):
    rows = q_ref.shape[0]
    total = 2 * frames_here
    length = info_ref[total]
    rank = info_ref[total + 1]
    starts, _, split, end = key_places(frames_here, info_ref)
    low, high, edge = chunk_range(frames_here, split, end, info_ref)
    qm[0], qm[1] = split_heads(q_ref[...])
    dom[0], dom[1] = split_heads(do_ref[...])
    dqt[...] = jnp.zeros_like(dqt)
    tiles = query_tiles(rows)
    work = [(h, at, size) for h in range(2) for at, size in tiles]
    for at, size in tiles:
        span = slice(at, at + size)
        prod = (o_ref[span, :].astype(jnp.float32) * do_ref[span, :].astype(jnp.float32)).T
        for h in range(2):
            delta[h : h + 1, span] = jnp.sum(prod[64 * h : 64 * h + 64], axis=0, keepdims=True)

    def prepare(c, carry):
        span = pl.ds(pl.multiple_of(c * CHUNK, CHUNK), CHUNK)
        turned = (k_ref[span, :] * valid_ref[span, :]).T
        for h in range(2):
            kt[h, :, span] = turned[64 * h : 64 * h + 64]
        return carry

    lax.fori_loop(low, high, prepare, 0)

    def body(c, carry):
        span = pl.ds(pl.multiple_of(c * CHUNK, CHUNK), CHUNK)
        keys = k_ref[span, :]
        values = v_ref[span, :]

        def scores(item):
            h, at, size = item
            return (
                dot(keys, qm[h, at : at + size, :], NT),
                dot(values, dom[h, at : at + size, :], NT),
            )

        dk = jnp.zeros((CHUNK, 128), jnp.float32)
        dv = jnp.zeros((CHUNK, 128), jnp.float32)
        ahead = scores(work[0])
        for i, (h, at, size) in enumerate(work):
            s, dp = ahead
            if i + 1 < len(work):
                ahead = scores(work[i + 1])
            bias = bias_row(c, split, edge, at, size)
            p = jnp.exp2(s - (lse_ref[0, h : h + 1, at : at + size] - bias))
            ds = (p * (dp - delta[h : h + 1, at : at + size])).astype(jnp.bfloat16)
            dv = dv + dot(p.astype(jnp.bfloat16), dom[h, at : at + size, :])
            dk = dk + dot(ds, qm[h, at : at + size, :])
            dqt[h, :, at : at + size] += dot(kt[h, :, span], ds)
        dk_all[span, :] = (dk * LN2).astype(jnp.bfloat16)
        dv_all[span, :] = dv.astype(jnp.bfloat16)
        return carry

    lax.fori_loop(low, high, body, 0)
    for at, size in tiles:
        both = jnp.concatenate([dqt[0, :, at : at + size], dqt[1, :, at : at + size]], axis=0)
        dq_ref[at : at + size, :] = (both * 0.125).T.astype(jnp.bfloat16)

    first = rank * frames_here
    early = first < length
    late = first + frames_here > length
    quad = 4
    for f0 in range(0, total, quad):
        at0 = f0 % frames_here * PIXELS

        def put(k_out, v_out):
            for src, dst in ((dk_all, k_out), (dv_all, v_out)):
                parts = []
                for f in range(f0, f0 + quad):
                    kept, at = starts[f]
                    lo = f % frames_here * PIXELS % 16
                    use = (kept == 1) & jnp.where(f >= length, late, early)
                    block = src[pl.ds(at, FRAME_ROWS), :].astype(jnp.float32)
                    parts.append(jnp.where(use, block[lo : lo + PIXELS, :], 0.0))
                dst[at0 : at0 + quad * PIXELS, :] = jnp.concatenate(parts, axis=0).astype(
                    jnp.bfloat16
                )

        @pl.when(rank == f0 // frames_here)
        def _():
            put(own_dk, own_dv)

        @pl.when(rank != f0 // frames_here)
        def _():
            put(far_dk, far_dv)


def attn_bwd(info, q, kc, vc, valid, o, do, lse, pair, frames_here, after):
    rows, width = q.shape
    length = kc.shape[0]
    local = pair % (width // 256)
    rowspec = pl.BlockSpec((rows, 128), lambda p, *_: (0, pair))
    keyspec = pl.BlockSpec((length, 128), lambda p, *_: (0, local))
    whole = pl.BlockSpec((rows, 128), lambda p, *_: (0, 0))

    def kernel(*refs):
        return attn_bwd_kernel(frames_here, *refs[:8], *refs[8 + len(after) :])

    return pl.pallas_call(
        kernel,
        out_shape=(jax.ShapeDtypeStruct((rows, 128), jnp.bfloat16),) * 5,
        grid_spec=pltpu.PrefetchScalarGridSpec(
            num_scalar_prefetch=1,
            grid=(1,),
            in_specs=[
                rowspec,
                keyspec,
                keyspec,
                pl.BlockSpec((length, 128), lambda p, *_: (0, 0)),
                rowspec,
                rowspec,
                pl.BlockSpec((1, 8, rows), lambda p, *_: (local, 0, 0)),
            ]
            + [pl.BlockSpec(memory_space=pl.ANY)] * len(after),
            out_specs=[whole] * 5,
            scratch_shapes=[
                pltpu.VMEM((2, rows, 128), jnp.bfloat16),
                pltpu.VMEM((2, rows, 128), jnp.bfloat16),
                pltpu.VMEM((2, 64, length), jnp.bfloat16),
                pltpu.VMEM((2, 64, rows), jnp.float32),
                pltpu.VMEM((8, rows), jnp.float32),
                pltpu.VMEM((length, 128), jnp.bfloat16),
                pltpu.VMEM((length, 128), jnp.bfloat16),
            ],
        ),
        compiler_params=params(),
        cost_estimate=cost(3e10, 1e7),
        name="attn_bwd",
    )(info, q, kc, vc, valid, o, do, lse, *after)


TILE = 224
INV_SQRT2 = 0.7071067811865476
INV_SQRT_2PI = 0.3989422804014327
QUERY_SCALE = 0.125 * LOG2E


def params(**kw):
    return pltpu.CompilerParams(
        vmem_limit_bytes=VMEM_LIMIT, dimension_semantics=("arbitrary",), **kw
    )


def cost(flops, moved):
    return pl.CostEstimate(flops=int(flops), bytes_accessed=int(moved), transcendentals=0)


def tile_spec(width):
    return pl.BlockSpec((TILE, width), lambda i: (i, 0))


def whole_spec(shape):
    return pl.BlockSpec(shape, lambda i: (0,) * len(shape), pipeline_mode=pl.Buffered(1))


def low_shape(rows, width):
    return jax.ShapeDtypeStruct((rows, width), jnp.bfloat16)


def ln_parts(x):
    center = x - jnp.mean(x, axis=-1, keepdims=True)
    rstd = lax.rsqrt(jnp.mean(center * center, axis=-1, keepdims=True) + EPS)
    return center * rstd, rstd


def ln_back(dy, gain, xhat, rstd):
    dxhat = dy * gain
    along = jnp.mean(dxhat * xhat, axis=-1, keepdims=True)
    return rstd * (dxhat - jnp.mean(dxhat, axis=-1, keepdims=True) - xhat * along)


def rows_sum(x):
    return jnp.sum(x, axis=0, keepdims=True)


def project_kernel(x_ref, gain_ref, shift_ref, wk, wv, bias_ref, n_ref, k_ref, v_ref):
    xhat, _ = ln_parts(x_ref[...].astype(jnp.float32))
    normed = (xhat * gain_ref[...] + shift_ref[...]).astype(jnp.bfloat16)
    n_ref[...] = normed
    k_ref[...] = dot(normed, wk[...]).astype(jnp.bfloat16)
    v_ref[...] = (dot(normed, wv[...]) + bias_ref[...]).astype(jnp.bfloat16)


def weight_spec(width, size, column):
    return pl.BlockSpec((width, size), lambda i: (0, column), pipeline_mode=pl.Buffered(1))


def project(x, gain, shift, w, v_bias):
    rows, width = x.shape
    half = width // 2
    return pl.pallas_call(
        project_kernel,
        out_shape=(low_shape(rows, width), low_shape(rows, half), low_shape(rows, half)),
        grid=(rows // TILE,),
        in_specs=[
            tile_spec(width),
            whole_spec((1, width)),
            whole_spec((1, width)),
            weight_spec(width, half, 2),
            weight_spec(width, half, 4),
            weight_spec(1, half, 0),
        ],
        out_specs=[tile_spec(width), tile_spec(half), tile_spec(half)],
        compiler_params=params(),
        cost_estimate=cost(2 * rows * width * width, 10 * rows * width),
        name="project",
    )(x, gain, shift, w, w, v_bias)


def project_more_kernel(n_ref, wq, wk, wv, q_bias, v_bias, q_ref, k_ref, v_ref):
    normed = n_ref[...]
    k_ref[...] = dot(normed, wk[...]).astype(jnp.bfloat16)
    v_ref[...] = (dot(normed, wv[...]) + v_bias[...]).astype(jnp.bfloat16)
    q_ref[...] = ((dot(normed, wq[...]) + q_bias[...]) * QUERY_SCALE).astype(jnp.bfloat16)


def project_more(normed, w, q_bias, v_bias):
    rows, width = normed.shape
    half = width // 2
    return pl.pallas_call(
        project_more_kernel,
        out_shape=(low_shape(rows, width), low_shape(rows, half), low_shape(rows, half)),
        grid=(rows // TILE,),
        in_specs=[
            tile_spec(width),
            weight_spec(width, width, 0),
            weight_spec(width, half, 3),
            weight_spec(width, half, 5),
            whole_spec((1, width)),
            weight_spec(1, half, 1),
        ],
        out_specs=[tile_spec(width), tile_spec(half), tile_spec(half)],
        compiler_params=params(),
        cost_estimate=cost(4 * rows * width * width, 10 * rows * width),
        name="project_more",
    )(normed, w, w, w, q_bias, v_bias)


def mlp_fwd_kernel(
    x_ref, a_ref, w_out, b_out, gain2, shift2, w_up, b_up, w_down, b_down, gain3, shift3,
    mid_ref, n2_ref, hid_ref, slope_ref, out_ref, n3_ref,
):
    width = x_ref.shape[1]
    inner = w_up.shape[1]
    parts = inner // width
    middle = x_ref[...].astype(jnp.float32) + dot(a_ref[...], w_out[...]) + b_out[...]
    mid_ref[...] = middle.astype(jnp.bfloat16)
    xhat, _ = ln_parts(middle)
    n2 = (xhat * gain2[...] + shift2[...]).astype(jnp.bfloat16)
    n2_ref[...] = n2
    out = middle + b_down[...]

    def raise_part(j):
        span = slice(j * width, (j + 1) * width)
        return dot(n2, w_up[:, span]) + b_up[:, span]

    ahead = raise_part(0)
    for j in range(parts):
        span = slice(j * width, (j + 1) * width)
        up = ahead
        if j + 1 < parts:
            ahead = raise_part(j + 1)
        area = 0.5 + 0.5 * lax.erf(up * INV_SQRT2)
        bell = jnp.exp2(up * up * (-0.5 * LOG2E)) * INV_SQRT_2PI
        hid = (up * area).astype(jnp.bfloat16)
        hid_ref[:, span] = hid
        slope_ref[:, span] = (area + up * bell).astype(jnp.bfloat16)
        out = out + dot(hid, w_down[span, :])
    out_ref[...] = out.astype(jnp.bfloat16)
    xhat, _ = ln_parts(out)
    n3_ref[...] = (xhat * gain3[...] + shift3[...]).astype(jnp.bfloat16)


def mlp_fwd(x, attended, w_out, b_out, gain2, shift2, w_up, b_up, w_down, b_down, gain3, shift3):
    rows, width = x.shape
    inner = w_up.shape[1]
    vec = whole_spec((1, width))
    return pl.pallas_call(
        mlp_fwd_kernel,
        out_shape=(
            low_shape(rows, width), low_shape(rows, width), low_shape(rows, inner),
            low_shape(rows, inner), low_shape(rows, width), low_shape(rows, width),
        ),
        grid=(rows // TILE,),
        in_specs=[
            tile_spec(width), tile_spec(width), whole_spec(w_out.shape), vec, vec, vec,
            whole_spec(w_up.shape), whole_spec((1, inner)), whole_spec(w_down.shape), vec, vec, vec,
        ],
        out_specs=[
            tile_spec(width), tile_spec(width), tile_spec(inner),
            tile_spec(inner), tile_spec(width), tile_spec(width),
        ],
        compiler_params=params(),
        cost_estimate=cost(
            2 * rows * width * (width + 2 * inner), 2 * rows * (6 * width + 2 * inner)
        ),
        name="mlp_fwd",
    )(x, attended, w_out, b_out, gain2, shift2, w_up, b_up, w_down, b_down, gain3, shift3)


def mlp_bwd_kernel(
    cot_ref, out_ref, side_ref, pool_ref, w_first, gain3, w_down, slope_ref, w_up, mid_ref,
    gain2, w_out, ddown_ref, dup_ref, dbranch_ref, datt_ref, sums_ref,
):
    width = cot_ref.shape[1]
    inner = w_up.shape[1]
    parts = inner // width

    @pl.when(pl.program_id(0) == 0)
    def _():
        sums_ref[...] = jnp.zeros_like(sums_ref)

    def add(row, value):
        sums_ref[row : row + 1, :] += rows_sum(value)

    dn3 = dot(side_ref[:, :128], w_first[...])
    xhat, rstd = ln_parts(out_ref[...].astype(jnp.float32))
    add(2, dn3 * xhat)
    add(3, dn3)
    d_out = (
        cot_ref[...].astype(jnp.float32)
        + ln_back(dn3, gain3[...], xhat, rstd)
        + dot(side_ref[:, 128:192], pool_ref[...])
    )
    d_down = d_out.astype(jnp.bfloat16)
    ddown_ref[...] = d_down
    add(4, d_down.astype(jnp.float32))

    def lower_part(j):
        return dot(d_down, w_down[j * width : (j + 1) * width, :], NT)

    ahead = lower_part(0)
    dn2 = jnp.zeros(cot_ref.shape, jnp.float32)
    for j in range(parts):
        span = slice(j * width, (j + 1) * width)
        d_hid = ahead
        if j + 1 < parts:
            ahead = lower_part(j + 1)
        d_up = (d_hid * slope_ref[:, span].astype(jnp.float32)).astype(jnp.bfloat16)
        dup_ref[:, span] = d_up
        add(6 + j, d_up.astype(jnp.float32))
        dn2 = dn2 + dot(d_up, w_up[:, span], NT)
    xhat, rstd = ln_parts(mid_ref[...].astype(jnp.float32))
    add(0, dn2 * xhat)
    add(1, dn2)
    d_branch = (d_out + ln_back(dn2, gain2[...], xhat, rstd)).astype(jnp.bfloat16)
    dbranch_ref[...] = d_branch
    add(5, d_branch.astype(jnp.float32))
    datt_ref[...] = dot(d_branch, w_out[...], NT).astype(jnp.bfloat16)


def mlp_bwd(cot, out, side, pool, w_first, gain3, w_down, slope, w_up, mid, gain2, w_out):
    rows, width = cot.shape
    inner = w_up.shape[1]
    vec = whole_spec((1, width))
    return pl.pallas_call(
        mlp_bwd_kernel,
        out_shape=(
            low_shape(rows, width), low_shape(rows, inner), low_shape(rows, width),
            low_shape(rows, width), jax.ShapeDtypeStruct((16, width), jnp.float32),
        ),
        grid=(rows // TILE,),
        in_specs=[
            tile_spec(width), tile_spec(width), tile_spec(256), whole_spec(pool.shape),
            whole_spec(w_first.shape), vec, whole_spec(w_down.shape), tile_spec(inner),
            whole_spec(w_up.shape), tile_spec(width), vec, whole_spec(w_out.shape),
        ],
        out_specs=[
            tile_spec(width), tile_spec(inner), tile_spec(width), tile_spec(width),
            pl.BlockSpec((16, width), lambda i: (0, 0)),
        ],
        compiler_params=params(),
        cost_estimate=cost(
            2 * rows * width * (width + 2 * inner), 2 * rows * (6 * width + 2 * inner)
        ),
        name="mlp_bwd",
    )(cot, out, side, pool, w_first, gain3, w_down, slope, w_up, mid, gain2, w_out)


def final_bwd_kernel(pairs, *refs):
    pieces = [refs[i * pairs : (i + 1) * pairs] for i in range(5)]
    x_ref, branch_ref, gain, w_ref, grad_ref, sums_ref = refs[5 * pairs :]
    width = x_ref.shape[1]

    @pl.when(pl.program_id(0) == 0)
    def _():
        sums_ref[...] = jnp.zeros_like(sums_ref)

    def add(row, value):
        sums_ref[row : row + 1, :] += rows_sum(value)

    def join(part):
        return jnp.concatenate([r[...] for r in part], axis=1)

    def total(part, other):
        both = [a[...].astype(jnp.float32) + b[...].astype(jnp.float32) for a, b in zip(part, other)]
        return jnp.concatenate(both, axis=1).astype(jnp.bfloat16)

    dq = join(pieces[0])
    dk = total(pieces[1], pieces[2])
    dv = total(pieces[3], pieces[4])
    dn = (
        dot(dq, w_ref[:, :width], NT)
        + dot(dk, w_ref[:, width : 2 * width], NT)
        + dot(dv, w_ref[:, 2 * width :], NT)
    )
    xhat, rstd = ln_parts(x_ref[...].astype(jnp.float32))
    add(0, dn * xhat)
    add(1, dn)
    add(2, dq.astype(jnp.float32))
    add(3, dv.astype(jnp.float32))
    grad_ref[...] = (
        branch_ref[...].astype(jnp.float32) + ln_back(dn, gain[...], xhat, rstd)
    ).astype(jnp.bfloat16)


def final_bwd(pieces, x, branch, gain, w):
    rows, width = x.shape
    pairs = width // 128
    return pl.pallas_call(
        functools.partial(final_bwd_kernel, pairs),
        out_shape=(low_shape(rows, width), jax.ShapeDtypeStruct((8, width), jnp.float32)),
        grid=(rows // TILE,),
        in_specs=[tile_spec(128)] * (5 * pairs)
        + [tile_spec(width)] * 2
        + [whole_spec((1, width)), whole_spec(w.shape)],
        out_specs=[tile_spec(width), pl.BlockSpec((8, width), lambda i: (0, 0))],
        compiler_params=params(),
        cost_estimate=cost(6 * rows * width * width, 16 * rows * width),
        name="final_bwd",
    )(*pieces, x, branch, gain, w)


def grid_masks(frames, lanes):
    table = np.zeros((16, lanes), np.float32)
    lane = np.arange(lanes)
    pixel = lane % PIXELS
    i, j = pixel // GRID, pixel % GRID
    inside = lane < frames * PIXELS
    for a in range(3):
        for b in range(3):
            ok = (i + a - 1 >= 0) & (i + a - 1 < GRID) & (j + b - 1 >= 0) & (j + b - 1 < GRID)
            table[3 * a + b] = ok & inside
    table[9] = np.where(inside, lane // PIXELS, -1)
    return table


def learner_kernel(
    frames, info_ref, weight_ref, n3_ref, out_ref, pool_ref, wt_ref, cw_ref, cwt_ref, cb_ref,
    mask_ref, side_ref, pooled_ref, small_ref, gfirst_ref,
):
    rows = n3_ref.shape[0]
    lanes = mask_ref.shape[1]
    extra = lanes - rows
    rank = info_ref[2 * frames + 1]
    frame_of = mask_ref[9:10, :]
    live = jnp.zeros((1, lanes), jnp.float32)
    for f in range(frames):
        kept = info_ref[rank * frames + f].astype(jnp.float32)
        live = live + jnp.where(frame_of == f, kept, 0.0)
    inside = (frame_of >= 0).astype(jnp.float32)

    def widen(x):
        return jnp.concatenate([x, jnp.zeros((x.shape[0], extra), jnp.float32)], axis=1)

    def turn(x, by):
        return x if by % lanes == 0 else pltpu.roll(x, by % lanes, 1)

    def gather_taps(taps):
        total = jnp.zeros((8, lanes), jnp.float32)
        for t in range(9):
            step = (t // 3 - 1) * GRID + t % 3 - 1
            total = total + turn(taps[8 * t : 8 * t + 8, :], -step) * mask_ref[t : t + 1, :]
        return total

    def spread_taps(level):
        parts = []
        for t in range(9):
            step = (t // 3 - 1) * GRID + t % 3 - 1
            parts.append(turn(level, step) * mask_ref[8 - t : 9 - t, :])
        return jnp.concatenate(parts, axis=0)

    def exact(a, b, dims=NN):
        return lax.dot_general(
            a, b, dims, precision=HIGHEST, preferred_element_type=jnp.float32
        )

    def area_of(x):
        return 0.5 + 0.5 * lax.erf(x * INV_SQRT2)

    taps = widen(dot(wt_ref[...], n3_ref[...], NT))
    levels = [gather_taps(taps) + cb_ref[:, 0:1]]
    hiddens = []
    for n in range(3):
        hiddens.append(levels[n] * area_of(levels[n]))
        levels.append(gather_taps(exact(cwt_ref[n], hiddens[n])) + cb_ref[:, n + 1 : n + 2])
    maps = 1.0 / (1.0 + jnp.exp(-levels[3]))
    total = rows_sum(maps)
    meet = 0.5 * (total * total - rows_sum(maps * maps)) * live
    small_ref[3] = jnp.zeros((8, 128), jnp.float32) + jnp.sum(meet)

    owner = lax.broadcasted_iota(jnp.int32, (8 * frames, lanes), 0) // 8
    mine = owner.astype(jnp.float32) == frame_of
    low_maps = maps.astype(jnp.bfloat16).astype(jnp.float32) * live
    stacked = jnp.where(mine, jnp.concatenate([low_maps] * frames, axis=0), 0.0)
    out = out_ref[...]
    pooled_ref[...] = dot(stacked[:, :rows].astype(jnp.bfloat16), out).astype(jnp.bfloat16)
    pairs = jnp.where(mine, widen(dot(pool_ref[...], out, NT)), 0.0)
    d_maps = pairs[0:8]
    for f in range(1, frames):
        d_maps = d_maps + pairs[8 * f : 8 * f + 8]
    d_maps = d_maps * live + weight_ref[0] * live * (total - maps)
    d_level = d_maps * maps * (1.0 - maps)
    for n in (2, 1, 0):
        small_ref[4 + n + 1] = jnp.broadcast_to(
            jnp.sum(d_level, axis=1, keepdims=True), (8, 128)
        )
        d_taps = spread_taps(d_level)
        small_ref[n] = jnp.concatenate(
            [exact(hiddens[n], d_taps, NT), jnp.zeros((8, 56), jnp.float32)], axis=1
        )
        d_hidden = exact(cw_ref[n], d_taps)
        x = levels[n]
        bell = jnp.exp(-0.5 * x * x) * INV_SQRT_2PI
        d_level = d_hidden * (area_of(x) + x * bell) * inside
    small_ref[4] = jnp.broadcast_to(jnp.sum(d_level, axis=1, keepdims=True), (8, 128))
    d_first = spread_taps(d_level)[:, :rows]
    gfirst_ref[...] = dot(d_first.astype(jnp.bfloat16), n3_ref[...])
    tall = jnp.concatenate(
        [
            d_first,
            jnp.zeros((56, rows), jnp.float32),
            stacked[:, :rows],
            jnp.zeros((128 - 8 * frames, rows), jnp.float32),
        ],
        axis=0,
    )
    side_ref[...] = tall.T.astype(jnp.bfloat16)


def learner(info, weight, n3, out, pool, w_first, conv_weights, conv_biases):
    rows, width = n3.shape
    frames = rows // PIXELS
    lanes = -(-rows // 128) * 128
    vm = pl.BlockSpec(memory_space=pltpu.VMEM)
    sm = pl.BlockSpec(memory_space=pltpu.SMEM)
    masks = jnp.asarray(grid_masks(frames, lanes))
    return pl.pallas_call(
        functools.partial(learner_kernel, frames),
        out_shape=(
            low_shape(rows, 256),
            low_shape(8 * frames, width),
            jax.ShapeDtypeStruct((8, 8, 128), jnp.float32),
            jax.ShapeDtypeStruct((9 * MAPS, width), jnp.float32),
        ),
        in_specs=[sm, sm] + [vm] * 8,
        out_specs=(vm, vm, vm, vm),
        compiler_params=pltpu.CompilerParams(vmem_limit_bytes=VMEM_LIMIT),
        cost_estimate=cost(2e10, 4 * rows * width),
        name="learner",
    )(
        info, weight, n3, out, pool, w_first.T, conv_weights,
        conv_weights.transpose(0, 2, 1), conv_biases.T, masks,
    )


def flip(count, bit):
    return [(i, i ^ bit) for i in range(count)]


def low_sum(a, b):
    return (a.astype(jnp.float32) + b.astype(jnp.float32)).astype(jnp.bfloat16)


def block_place(owner, rounds):
    place = 0
    for bits in rounds:
        for bit in bits:
            place = place * 2 + ((owner >> bit) & 1)
    return place


def put_blocks(ref, value, first_owner, owners, rounds):
    size = value.shape[0] // owners
    for o in range(owners):
        place = block_place(first_owner + o, rounds)
        at = place * size
        if not isinstance(at, int):
            at = pl.multiple_of(at, 16)
        ref[pl.ds(at, size), :] = value[o * size : (o + 1) * size, :]


def grad_by_columns_kernel(rounds, seqs, info_ref, a_ref, b_ref, keep_ref, send_ref, turned):
    step = pl.program_id(0)

    @pl.when(step == 0)
    def _():
        turned[...] = a_ref[...].T

    got = dot(turned[...], b_ref[...]).astype(jnp.bfloat16)

    @pl.when(step < pl.num_programs(0) // 2)
    def _():
        put_blocks(keep_ref, got, 0, seqs, rounds)

    @pl.when(step >= pl.num_programs(0) // 2)
    def _():
        put_blocks(send_ref, got, 0, seqs, rounds)


def grad_by_columns(info, a, b, rounds, seqs, at):
    rows, tall = a.shape
    wide = b.shape[1]
    block = min(768, wide // 2)
    half = wide // 2 // block
    out = jax.ShapeDtypeStruct((tall, wide // 2), jnp.bfloat16)
    return pl.pallas_call(
        functools.partial(grad_by_columns_kernel, rounds, seqs),
        out_shape=(out, out),
        grid_spec=pltpu.PrefetchScalarGridSpec(
            num_scalar_prefetch=1,
            grid=(2 * half,),
            in_specs=[
                pl.BlockSpec((rows, tall), lambda j, info: (0, 0)),
                pl.BlockSpec(
                    (rows, block),
                    lambda j, info: (0, jnp.where(j < half, info[at], 1 - info[at]) * half + j % half),
                ),
            ],
            out_specs=[
                pl.BlockSpec((tall, block), lambda j, info: (0, jnp.minimum(j, half - 1))),
                pl.BlockSpec((tall, block), lambda j, info: (0, jnp.maximum(j - half, 0))),
            ],
            scratch_shapes=[pltpu.VMEM((tall, rows), jnp.bfloat16)],
        ),
        compiler_params=params(),
        cost_estimate=cost(2 * rows * tall * wide, 2 * rows * (tall + wide)),
        name="grad_columns",
    )(info, a, b)


def pick_half(rank, value):
    middle = value.shape[1] // 2
    first, second = value[:, :middle], value[:, middle:]
    return jnp.where(rank == 0, first, second), jnp.where(rank == 0, second, first)


def grad_by_rows_kernel(rounds, seqs, at, info_ref, a_ref, b_ref, keep_ref, send_ref):
    steps = pl.num_programs(0)
    step = pl.program_id(0)
    got = dot(a_ref[...], b_ref[...], TN).astype(jnp.bfloat16)
    keep, send = pick_half(info_ref[at], got)
    owners = seqs // (keep_ref.shape[0] // a_ref.shape[1])
    put_blocks(keep_ref, keep, step * owners, owners, rounds)
    put_blocks(send_ref, send, step * owners, owners, rounds)


def grad_by_rows(info, a, b, rounds, seqs, at):
    rows, tall = a.shape
    wide = b.shape[1]
    out = jax.ShapeDtypeStruct((tall, wide // 2), jnp.bfloat16)
    return pl.pallas_call(
        functools.partial(grad_by_rows_kernel, rounds, seqs, at),
        out_shape=(out, out),
        grid_spec=pltpu.PrefetchScalarGridSpec(
            num_scalar_prefetch=1,
            grid=(tall // 768,),
            in_specs=[
                pl.BlockSpec((rows, 768), lambda j, info: (0, j)),
                pl.BlockSpec((rows, wide), lambda j, info: (0, 0)),
            ],
            out_specs=[pl.BlockSpec((tall, wide // 2), lambda j, info: (0, 0))] * 2,
        ),
        compiler_params=params(),
        cost_estimate=cost(2 * rows * tall * wide, 2 * rows * (tall + wide)),
        name="grad_rows",
    )(info, a, b)


def grad_pieces_kernel(
    rounds, seqs, at, info_ref, n_ref, q0, q1, k0, x0, k1, x1, v0, y0, v1, y1, keep_ref, send_ref
):
    first = jnp.concatenate([q0[...], q1[...], low_sum(k0[...], x0[...])], axis=1)
    second = jnp.concatenate(
        [low_sum(k1[...], x1[...]), low_sum(v0[...], y0[...]), low_sum(v1[...], y1[...])], axis=1
    )
    both = jnp.concatenate([first, second], axis=1)
    got = dot(n_ref[...], both, TN).astype(jnp.bfloat16)
    keep, send = pick_half(info_ref[at], got)
    put_blocks(keep_ref, keep, 0, seqs, rounds)
    put_blocks(send_ref, send, 0, seqs, rounds)


def grad_pieces(info, n1, pieces, rounds, seqs, at):
    (q0, k0, x0, v0, y0), (q1, k1, x1, v1, y1) = pieces
    rows, tall = n1.shape
    out = jax.ShapeDtypeStruct((tall, 384), jnp.bfloat16)
    vm = pl.BlockSpec(memory_space=pltpu.VMEM)
    sm = pl.BlockSpec(memory_space=pltpu.SMEM)
    return pl.pallas_call(
        functools.partial(grad_pieces_kernel, rounds, seqs, at),
        out_shape=(out, out),
        in_specs=[sm] + [vm] * 11,
        out_specs=(vm, vm),
        compiler_params=pltpu.CompilerParams(vmem_limit_bytes=VMEM_LIMIT),
        cost_estimate=cost(2 * rows * tall * 768, 4 * rows * tall),
        name="grad_pieces",
    )(info, n1, q0, q1, k0, x0, k1, x1, v0, y0, v1, y1)


class Stream:
    def __init__(self, rounds, keep, send):
        self.rounds = [None] + rounds
        self.at = 0
        self.keep = keep
        self.sends = [send]
        self.gots = None
        self.done = False

    def start(self):
        bits = self.rounds[self.at]
        if bits is None:
            self.gots = [lax.ppermute(self.sends[0], "frame", flip(2, 1))]
            return
        count = lax.axis_size("seq")
        self.gots = []
        for m in range(1, 1 << len(bits)):
            mask = 0
            for i, bit in enumerate(bits):
                mask |= ((m >> (len(bits) - 1 - i)) & 1) << bit
            self.gots.append(lax.ppermute(self.sends[m - 1], "seq", flip(count, mask)))


class Total:
    def __init__(self, rounds, value):
        self.rounds = rounds
        self.at = 0
        self.value = value
        self.done = False

    def start(self):
        bits = self.rounds[self.at]
        if bits is None:
            self.gots = [lax.ppermute(self.value, "frame", flip(2, 1))]
            return
        count = lax.axis_size("seq")
        self.gots = []
        for m in range(1, 1 << len(bits)):
            mask = 0
            for i, bit in enumerate(bits):
                mask |= ((m >> i) & 1) << bit
            self.gots.append(lax.ppermute(self.value, "seq", flip(count, mask)))


def fold(info, at, streams, after=()):
    streams = [s for s in streams if not s.done]
    ins, outs, plan = [], [], []
    for s in streams:
        last = s.at + 1 == len(s.rounds)
        if isinstance(s, Total):
            parts = [s.value] + s.gots
            plan.append((len(parts), None, None))
            outs.append(jax.ShapeDtypeStruct(s.value.shape, jnp.float32))
        else:
            parts = [s.keep] + s.gots
            rows, wide = s.keep.shape
            if last:
                plan.append((len(parts), (), 1))
                outs.append(jax.ShapeDtypeStruct((rows, wide), jnp.float32))
            else:
                bits = s.rounds[s.at + 1]
                ways = 1 << len(bits)
                plan.append((len(parts), tuple(bits), ways))
                outs += [jax.ShapeDtypeStruct((rows // ways, wide), jnp.bfloat16)] * ways
        ins += parts

    def kernel(info_ref, *refs):
        sources, targets = list(refs[: len(ins)]), list(refs[len(ins) + len(after) :])
        index = info_ref[at]
        for count, bits, ways in plan:
            parts = [sources.pop(0) for _ in range(count)]

            def total(span):
                value = parts[0][span].astype(jnp.float32)
                for p in parts[1:]:
                    value = value + p[span].astype(jnp.float32)
                return value

            if not bits:
                targets.pop(0)[...] = total(...)
                continue
            mine = 0
            for bit in bits:
                mine = mine * 2 + ((index >> bit) & 1)
            size = parts[0].shape[0] // ways
            for m in range(ways):
                start = pl.multiple_of((mine ^ m) * size, 16)
                targets.pop(0)[...] = total((pl.ds(start, size), slice(None))).astype(jnp.bfloat16)

    vm = pl.BlockSpec(memory_space=pltpu.VMEM)
    sm = pl.BlockSpec(memory_space=pltpu.SMEM)
    moved = sum(x.size * x.dtype.itemsize for x in ins) * 2
    results = list(
        pl.pallas_call(
            kernel,
            out_shape=tuple(outs),
            in_specs=[sm] + [vm] * len(ins) + [pl.BlockSpec(memory_space=pl.ANY)] * len(after),
            out_specs=(vm,) * len(outs),
            compiler_params=pltpu.CompilerParams(vmem_limit_bytes=VMEM_LIMIT),
            cost_estimate=cost(0, moved),
            name="fold",
        )(info, *ins, *after)
    )
    sent = []
    for s, (_, bits, ways) in zip(streams, plan):
        s.at += 1
        s.done = s.at == len(s.rounds)
        if isinstance(s, Total):
            s.value = results.pop(0)
            sent.append(s.value)
        elif s.done:
            s.keep = results.pop(0)
            sent.append(s.keep)
        else:
            got = [results.pop(0) for _ in range(ways)]
            s.keep, s.sends = got[0], got[1:]
            sent.append(s.sends[0])
        if not s.done:
            s.start()
    return sent[:1]


def single(bits):
    return [[b] for b in bits]


def turned_orders(bits):
    low = list(range(bits))
    return [low[i:] + low[:i] for i in range(3)]


def doubles(bits):
    low = list(range(bits))
    return [low[i : i + 2] for i in range(0, bits, 2)]


def quick_device(
    tokens, ln_gain_first, ln_bias_first, w_qkv, q_bias, v_bias, w_out, out_bias, ln_gain_second,
    ln_bias_second, w_up, up_bias, w_down, down_bias, ln_gain_third, ln_bias_third, w_first,
    conv_weights, conv_biases, clip_lengths, frame_mask, out_cot, pool_cot, penalty_scale,
):
    _, rows, width = tokens.shape
    frames = rows // PIXELS
    inner = w_up.shape[1]
    seqs = lax.axis_size("seq")
    rank = lax.axis_index("frame")
    bits = seqs.bit_length() - 1
    orders = turned_orders(bits)
    rank_at, seq_at = 2 * frames + 1, 2 * frames + 2

    def row(x):
        return x.reshape(1, -1)

    def swap(x):
        return lax.ppermute(x, "frame", flip(2, 1))

    place = jnp.stack([rank, lax.axis_index("seq")]).astype(jnp.int32)
    info = jnp.concatenate([frame_mask[0], clip_lengths[0, 0:1], place])
    x = tokens[0]
    count = Total(doubles(bits), jnp.sum(frame_mask).astype(jnp.float32) * jnp.ones((1, 128)))
    count.start()
    n1, k0, v0 = project(x, row(ln_gain_first), row(ln_bias_first), w_qkv, row(v_bias))
    far_k0, far_v0 = swap(k0), swap(v0)
    fold(info, seq_at, [count], (n1,))
    q, k1, v1 = project_more(n1, w_qkv, row(q_bias), row(v_bias))
    far_k1, far_v1 = swap(k1), swap(v1)
    attended, *kept0 = attn_fwd(info, q, k0, v0, far_k0, far_v0, None, 0, frames)
    fold(info, seq_at, [count], (kept0[0],))
    attended, *kept1 = attn_fwd(info, q, k1, v1, far_k1, far_v1, attended, 1, frames)
    while not count.done:
        fold(info, seq_at, [count], (attended,))
    count = count.value[0, 0]
    weight = (penalty_scale / count).reshape(1)
    mid, n2, hidden, slope, out, n3 = mlp_fwd(
        x, attended, w_out, row(out_bias), row(ln_gain_second), row(ln_bias_second), w_up,
        row(up_bias), w_down, row(down_bias), row(ln_gain_third), row(ln_bias_third),
    )
    side, pooled, small, grad_first = learner(
        info, weight, n3, out, pool_cot[0], w_first, conv_weights, conv_biases
    )
    first_pad = jnp.concatenate(
        [w_first.T, jnp.zeros((128 - 9 * MAPS, width), jnp.bfloat16)], axis=0
    )
    d_down, d_up, d_branch, d_att, sums = mlp_bwd(
        out_cot[0], out, side, pool_cot[0], first_pad, row(ln_gain_third), w_down, slope, w_up,
        mid, row(ln_gain_second), w_out,
    )

    def both(x):
        middle = x.shape[1] // 2
        first, second = x[:, :middle], x[:, middle:]
        return jnp.where(rank == 0, first, second), jnp.where(rank == 0, second, first)

    plain = single(range(bits)[::-1])
    up = Stream(
        single(orders[0]), *grad_by_columns(info, n2, d_up, single(orders[0]), seqs, rank_at)
    )
    up.start()
    down = Stream(
        single(orders[1]), *grad_by_rows(info, hidden, d_down, single(orders[1]), seqs, rank_at)
    )
    down.start()
    branch = Stream(
        single(orders[2]), *grad_by_rows(info, attended, d_branch, single(orders[2]), seqs, rank_at)
    )
    branch.start()
    first = Stream(plain, *both(grad_first.astype(jnp.bfloat16).T))
    first.start()
    early = Total(
        [None] + single(range(bits)), jnp.concatenate([sums.reshape(-1, 128), small.reshape(-1, 128)])
    )
    early.start()
    streams = [up, down, branch, first, early]
    after = fold(info, seq_at, streams)

    pairs = width // 128
    groups = pairs // 2
    pieces = {}
    group_streams = []

    def group_stream(g):
        stream = Stream(
            doubles(bits),
            *grad_pieces(
                info, n1, (pieces[g], pieces[g + groups]), doubles(bits), seqs, rank_at
            ),
        )
        stream.start()
        group_streams.append(stream)
        return stream

    for turn, pair in enumerate(p for g in range(groups) for p in (g, g + groups)):
        lse, kc, vc, valid = (kept0, kept1)[pair // groups]
        dq, own_k, own_v, far_k, far_v = attn_bwd(
            info, q, kc, vc, valid, attended, d_att, lse, pair, frames, after
        )
        pieces[pair] = (dq, own_k, swap(far_k), own_v, swap(far_v))
        after = fold(info, seq_at, streams, (dq,))
        if turn % 2 == 0 and turn > 0:
            stream = group_stream(turn // 2 - 1)
            streams.append(stream)
            after = after + [stream.sends[0]]
    streams.append(group_stream(groups - 1))
    tokens_grad, late = final_bwd(
        [pieces[p][i] for i in range(5) for p in range(pairs)],
        x, d_branch, row(ln_gain_first), w_qkv,
    )
    late = Total([None] + doubles(bits), late)
    late.start()
    streams.append(late)
    while not all(s.done for s in streams):
        fold(info, seq_at, streams)
    grad_qkv = jnp.concatenate(
        [s.keep[:, 128 * i : 128 * i + 128] for i in range(3) for s in group_streams], axis=1
    )
    late = late.value
    sums = early.value[: 16 * width // 128].reshape(16, width)
    small = early.value[16 * width // 128 :].reshape(8, 8, 128)
    penalty = small[3, 0, 0] / count
    return (
        out[None],
        pooled[None],
        penalty,
        tokens_grad[None],
        late[0],
        late[1],
        grad_qkv,
        late[2],
        late[3],
        branch.keep,
        sums[5],
        sums[0],
        sums[1],
        up.keep,
        sums[6 : 6 + inner // width].reshape(-1),
        down.keep,
        sums[4],
        sums[2],
        sums[3],
        first.keep,
        small[:3, :, : 9 * MAPS],
        small[4:8, :, 0],
    )


def per_device(*arrays):
    tokens, clip_lengths = arrays[0], arrays[19]
    frames = tokens.shape[1] // PIXELS
    seqs = lax.axis_size("seq")
    fits = (
        tokens.shape[0] == 1
        and lax.axis_size("frame") == 2
        and frames % 4 == 0
        and tokens.shape[1] % TILE == 0
        and tokens.shape[2] == HEADS * HEAD_DIM
        and seqs & (seqs - 1) == 0
    )
    return (quick_device if fits else plain_device)(*arrays)


def solution(mesh):
    return jax.shard_map(
        per_device,
        mesh=mesh,
        in_specs=(
            P("seq", "frame", None),
            P(),
            P(),
            P(),
            P(),
            P(),
            P(),
            P(),
            P(),
            P(),
            P(),
            P(),
            P(),
            P(),
            P(),
            P(),
            P(),
            P(),
            P(),
            P("seq", None),
            P("seq", None),
            P("seq", "frame", None),
            P("seq", "frame", None),
            P(),
        ),
        out_specs=(
            P("seq", "frame", None),
            P("seq", "frame", None),
            P(),
            P("seq", "frame", None),
            P(),
            P(),
            P("seq", "frame"),
            P(),
            P(),
            P("seq", "frame"),
            P(),
            P(),
            P(),
            P("seq", "frame"),
            P(),
            P("seq", "frame"),
            P(),
            P(),
            P(),
            P("seq", "frame"),
            P(),
            P(),
        ),
        check_vma=False,
    )
```

```python
import functools

import jax
import jax.numpy as jnp
import numpy as np
from jax import lax
from jax.experimental import pallas as pl
from jax.experimental.pallas import tpu as pltpu
from jax.sharding import PartitionSpec as P

HEADS = 12
HEAD_DIM = 64
GRID = 14
MAPS = 8


EPS = 1e-06
NEG = -1e30
HIGHEST = lax.Precision.HIGHEST


def norm_rows(rows, gain, shift):
    center = rows - jnp.mean(rows, axis=-1, keepdims=True)
    spread = jnp.mean(center * center, axis=-1, keepdims=True)
    return center * lax.rsqrt(spread + EPS) * gain + shift


def shift_sum(taps):
    padded = jnp.pad(taps, ((0, 0), (1, 1), (1, 1), (0, 0), (0, 0)))
    total = padded[:, 0:GRID, 0:GRID, 0, :]
    for tap in range(1, 9):
        total = total + padded[:, tap // 3 : tap // 3 + GRID, tap % 3 : tap % 3 + GRID, tap, :]
    return total


def conv_tail(first, conv_biases, conv_weights):
    frames = first.shape[0]
    level = shift_sum(first.reshape(frames, GRID, GRID, 9, MAPS)) + conv_biases[0]
    for layer in range(3):
        hidden = jax.nn.gelu(level, approximate=False)
        taps = jnp.einsum("fijc,ck->fijk", hidden, conv_weights[layer], precision=HIGHEST)
        level = shift_sum(taps.reshape(frames, GRID, GRID, 9, MAPS)) + conv_biases[layer + 1]
    return jax.nn.sigmoid(level).reshape(frames, GRID * GRID, MAPS)


def exact_gelu(values):
    return jax.nn.gelu(values, approximate=False)


def pair_mask(query_code, key_code):
    return (query_code[:, :, None] == key_code[:, None, :])[:, None]


def score_rows(query_rows, key_rows):
    return jnp.einsum(
        "sqhe,skhe->shqk", query_rows, key_rows, preferred_element_type=jnp.float32
    ) * HEAD_DIM ** (-0.5)


def pair_terms(query_rows, dout_rows, lse_rows, delta_rows, key_rows, value_rows, allowed):
    scores = score_rows(query_rows, key_rows)
    probs = jnp.where(allowed, jnp.exp(scores - lse_rows[..., None]), 0.0)
    slopes = jnp.einsum(
        "sqhe,skhe->shqk", dout_rows, value_rows, preferred_element_type=jnp.float32
    )
    grads = (probs * (slopes - delta_rows[..., None])).astype(jnp.bfloat16)
    return (probs.astype(jnp.bfloat16), grads)


def column_sum(values):
    return jnp.sum(values.astype(jnp.float32), axis=0)


def plain_device(
    tokens,
    ln_gain_first,
    ln_bias_first,
    w_qkv,
    q_bias,
    v_bias,
    w_out,
    out_bias,
    ln_gain_second,
    ln_bias_second,
    w_up,
    up_bias,
    w_down,
    down_bias,
    ln_gain_third,
    ln_bias_third,
    w_first,
    conv_weights,
    conv_biases,
    clip_lengths,
    frame_mask,
    out_cot,
    pool_cot,
    penalty_scale,
):
    seq_count, local, width = tokens.shape
    pixels = GRID * GRID
    frames_here = local // pixels
    frame_total = lax.axis_size("frame")
    frame_rank = lax.axis_index("frame")
    slot_frames = frames_here * frame_total
    length = local * frame_total
    rows = seq_count * local
    image_count = seq_count * frames_here
    scale = HEAD_DIM ** (-0.5)
    positions = jnp.arange(slot_frames, dtype=jnp.int32)[None, :]
    segment_frames = (positions >= clip_lengths[:, 0:1]).astype(jnp.int32)
    key_frames = jnp.where(frame_mask > 0, segment_frames, -1)
    first_frame = frame_rank * frames_here
    query_code = jnp.repeat(
        lax.dynamic_slice_in_dim(segment_frames, first_frame, frames_here, 1), pixels, axis=1
    )
    key_code = jnp.repeat(key_frames, pixels, axis=1)
    valid_here = (
        lax.dynamic_slice_in_dim(frame_mask, first_frame, frames_here, 1)
        .reshape(image_count)
        .astype(jnp.float32)
    )
    flat = tokens.reshape(rows, width).astype(jnp.float32)
    normed_one, back_one = jax.vjp(norm_rows, flat, ln_gain_first, ln_bias_first)
    normed_one = normed_one.astype(jnp.bfloat16)
    qkv_bias = jnp.concatenate([q_bias, jnp.zeros_like(q_bias), v_bias])
    qkv = (jnp.dot(normed_one, w_qkv, preferred_element_type=jnp.float32) + qkv_bias).astype(
        jnp.bfloat16
    )
    qkv = qkv.reshape(seq_count, local, 3, HEADS, HEAD_DIM)
    queries = qkv[:, :, 0]
    keys_here = qkv[:, :, 1]
    values_here = qkv[:, :, 2]
    keys_all, values_all = (
        lax.all_gather(keys_here, "frame", axis=1, tiled=True),
        lax.all_gather(values_here, "frame", axis=1, tiled=True),
    )

    def block_of(array, index):
        return lax.dynamic_slice_in_dim(array, index * local, local, 1)

    def stats_turn(index, carry):
        allowed = pair_mask(query_code, block_of(key_code, index))

        def stats_update(state):
            top, mass = state
            masked = jnp.where(allowed, score_rows(queries, block_of(keys_all, index)), NEG)
            new_top = jnp.maximum(top, jnp.max(masked, axis=-1))
            kept = jnp.where(allowed, jnp.exp(masked - new_top[..., None]), 0.0)
            return (new_top, mass * jnp.exp(top - new_top) + jnp.sum(kept, axis=-1))

        return lax.cond(jnp.any(allowed), stats_update, lambda state: state, carry)

    start_top = jnp.full((seq_count, HEADS, local), NEG, jnp.float32)
    top, mass = lax.fori_loop(0, frame_total, stats_turn, (start_top, jnp.zeros_like(start_top)))
    lse = top + jnp.log(mass)

    def value_turn(index, total):
        allowed = pair_mask(query_code, block_of(key_code, index))

        def value_update(state):
            scores = score_rows(queries, block_of(keys_all, index))
            probs = jnp.where(allowed, jnp.exp(scores - lse[..., None]), 0.0).astype(jnp.bfloat16)
            return state + jnp.einsum(
                "shqk,skhe->sqhe",
                probs,
                block_of(values_all, index),
                preferred_element_type=jnp.float32,
            )

        return lax.cond(jnp.any(allowed), value_update, lambda state: state, total)

    attended = lax.fori_loop(0, frame_total, value_turn, jnp.zeros(queries.shape, jnp.float32))
    attended_low = attended.astype(jnp.bfloat16).reshape(rows, width)
    middle = flat + jnp.dot(attended_low, w_out, preferred_element_type=jnp.float32) + out_bias
    normed_two, back_two = jax.vjp(norm_rows, middle, ln_gain_second, ln_bias_second)
    normed_two = normed_two.astype(jnp.bfloat16)
    upper = jnp.dot(normed_two, w_up, preferred_element_type=jnp.float32) + up_bias
    hidden, gelu_back = jax.vjp(exact_gelu, upper)
    hidden = hidden.astype(jnp.bfloat16)
    output = middle + jnp.dot(hidden, w_down, preferred_element_type=jnp.float32) + down_bias
    output_low = output.astype(jnp.bfloat16)
    normed_three, back_three = jax.vjp(norm_rows, output, ln_gain_third, ln_bias_third)
    normed_three = normed_three.astype(jnp.bfloat16)
    first = jnp.dot(normed_three, w_first, preferred_element_type=jnp.float32)
    maps, tail_back = jax.vjp(
        conv_tail, first.reshape(image_count, pixels, 9 * MAPS), conv_biases, conv_weights
    )
    maps_low = maps.astype(jnp.bfloat16)
    output_frames = output_low.reshape(image_count, pixels, width)
    pooled = (
        jnp.einsum("fpm,fpd->fmd", maps_low, output_frames, preferred_element_type=jnp.float32)
        * valid_here[:, None, None]
    )
    pooled_tokens = pooled.astype(jnp.bfloat16).reshape(seq_count, frames_here * MAPS, width)
    total_map = jnp.sum(maps, axis=-1)
    intersection = 0.5 * (total_map * total_map - jnp.sum(maps * maps, axis=-1))
    intersection_local = jnp.sum(intersection * valid_here[:, None])
    count_local = jnp.sum(valid_here)
    intersection_total, count_total = lax.psum((intersection_local, count_local), ("seq", "frame"))
    penalty = intersection_total / count_total
    pool_frames = pool_cot.reshape(image_count, MAPS, width)
    weight_cot = penalty_scale / count_total
    d_maps = (
        jnp.einsum("fmd,fpd->fpm", pool_frames, output_frames, preferred_element_type=jnp.float32)
        * valid_here[:, None, None]
    )
    d_maps = d_maps + (weight_cot * valid_here)[:, None, None] * (total_map[..., None] - maps)
    d_first, d_conv_biases, d_conv_weights = tail_back(d_maps)
    d_first = d_first.reshape(rows, 9 * MAPS).astype(jnp.bfloat16)
    grad_w_first = jnp.dot(normed_three.T, d_first, preferred_element_type=jnp.float32)
    d_normed_three = jnp.dot(d_first, w_first.T, preferred_element_type=jnp.float32)
    d_from_three, d_gain_three, d_bias_three = back_three(d_normed_three)
    d_pool_rows = (
        jnp.einsum("fpm,fmd->fpd", maps_low, pool_frames, preferred_element_type=jnp.float32)
        * valid_here[:, None, None]
    )
    d_output = (
        out_cot.reshape(rows, width).astype(jnp.float32)
        + d_from_three
        + d_pool_rows.reshape(rows, width)
    )
    d_down = d_output.astype(jnp.bfloat16)
    grad_w_down = jnp.dot(hidden.T, d_down, preferred_element_type=jnp.float32)
    grad_down_bias = column_sum(d_down)
    d_hidden = jnp.dot(d_down, w_down.T, preferred_element_type=jnp.float32)
    d_upper = gelu_back(d_hidden)[0].astype(jnp.bfloat16)
    grad_w_up = jnp.dot(normed_two.T, d_upper, preferred_element_type=jnp.float32)
    grad_up_bias = column_sum(d_upper)
    d_normed_two = jnp.dot(d_upper, w_up.T, preferred_element_type=jnp.float32)
    d_from_two, d_gain_two, d_bias_two = back_two(d_normed_two)
    d_middle = d_output + d_from_two
    d_branch = d_middle.astype(jnp.bfloat16)
    grad_w_out = jnp.dot(attended_low.T, d_branch, preferred_element_type=jnp.float32)
    grad_out_bias = column_sum(d_branch)
    dout_low = jnp.dot(d_branch, w_out.T, preferred_element_type=jnp.float32).astype(jnp.bfloat16)
    dout_low = dout_low.reshape(seq_count, local, HEADS, HEAD_DIM)
    delta = jnp.sum(dout_low.astype(jnp.float32) * attended, axis=-1).transpose(0, 2, 1)
    zeros_here = jnp.zeros(queries.shape, jnp.float32)
    full_zeros = jnp.zeros((seq_count, length, HEADS, HEAD_DIM), jnp.float32)

    def both_turn(index, carry):
        allowed = pair_mask(query_code, block_of(key_code, index))

        def both_update(state):
            grad_q, grad_k, grad_v = state
            key_rows = block_of(keys_all, index)
            probs, grads = pair_terms(
                queries, dout_low, lse, delta, key_rows, block_of(values_all, index), allowed
            )
            grad_q = (
                grad_q
                + jnp.einsum("shqk,skhe->sqhe", grads, key_rows, preferred_element_type=jnp.float32)
                * scale
            )
            part_k = (
                jnp.einsum("shqk,sqhe->skhe", grads, queries, preferred_element_type=jnp.float32)
                * scale
            )
            part_v = jnp.einsum(
                "shqk,sqhe->skhe", probs, dout_low, preferred_element_type=jnp.float32
            )
            grad_k = lax.dynamic_update_slice_in_dim(grad_k, part_k, index * local, 1)
            grad_v = lax.dynamic_update_slice_in_dim(grad_v, part_v, index * local, 1)
            return (grad_q, grad_k, grad_v)

        return lax.cond(jnp.any(allowed), both_update, lambda state: state, carry)

    grad_q, grad_k_all, grad_v_all = lax.fori_loop(
        0, frame_total, both_turn, (zeros_here, full_zeros, full_zeros)
    )
    grad_k, grad_v = (
        lax.psum_scatter(
            grad_k_all.astype(jnp.bfloat16), "frame", scatter_dimension=1, tiled=True
        ).astype(jnp.float32),
        lax.psum_scatter(
            grad_v_all.astype(jnp.bfloat16), "frame", scatter_dimension=1, tiled=True
        ).astype(jnp.float32),
    )
    grad_qkv = (
        jnp.stack([grad_q, grad_k, grad_v], axis=2).astype(jnp.bfloat16).reshape(rows, 3 * width)
    )
    grad_w_qkv = jnp.dot(normed_one.T, grad_qkv, preferred_element_type=jnp.float32)
    grad_q_bias = column_sum(grad_qkv[:, :width])
    grad_v_bias = column_sum(grad_qkv[:, 2 * width :])
    d_normed_one = jnp.dot(grad_qkv, w_qkv.T, preferred_element_type=jnp.float32)
    d_from_one, d_gain_one, d_bias_one = back_one(d_normed_one)
    tokens_grad = (d_middle + d_from_one).astype(jnp.bfloat16).reshape(seq_count, local, width)
    summed = (
        lax.psum_scatter(
            grad_w_qkv.astype(jnp.bfloat16), "seq", scatter_dimension=0, tiled=True
        ).astype(jnp.float32),
        lax.psum_scatter(
            grad_w_out.astype(jnp.bfloat16), "seq", scatter_dimension=0, tiled=True
        ).astype(jnp.float32),
        lax.psum_scatter(
            grad_w_up.astype(jnp.bfloat16), "seq", scatter_dimension=0, tiled=True
        ).astype(jnp.float32),
        lax.psum_scatter(
            grad_w_down.astype(jnp.bfloat16), "seq", scatter_dimension=0, tiled=True
        ).astype(jnp.float32),
        lax.psum_scatter(
            grad_w_first.astype(jnp.bfloat16), "seq", scatter_dimension=0, tiled=True
        ).astype(jnp.float32),
    )
    grad_w_qkv, grad_w_out, grad_w_up, grad_w_down, grad_w_first = (
        lax.psum_scatter(
            summed[0].astype(jnp.bfloat16), "frame", scatter_dimension=1, tiled=True
        ).astype(jnp.float32),
        lax.psum_scatter(
            summed[1].astype(jnp.bfloat16), "frame", scatter_dimension=1, tiled=True
        ).astype(jnp.float32),
        lax.psum_scatter(
            summed[2].astype(jnp.bfloat16), "frame", scatter_dimension=1, tiled=True
        ).astype(jnp.float32),
        lax.psum_scatter(
            summed[3].astype(jnp.bfloat16), "frame", scatter_dimension=1, tiled=True
        ).astype(jnp.float32),
        lax.psum_scatter(
            summed[4].astype(jnp.bfloat16), "frame", scatter_dimension=1, tiled=True
        ).astype(jnp.float32),
    )
    small = lax.psum(
        (
            d_gain_one,
            d_bias_one,
            d_gain_two,
            d_bias_two,
            d_gain_three,
            d_bias_three,
            grad_q_bias,
            grad_v_bias,
            grad_out_bias,
            grad_up_bias,
            grad_down_bias,
            d_conv_weights,
            d_conv_biases,
        ),
        ("seq", "frame"),
    )
    block_output = output_low.reshape(seq_count, local, width)
    return (
        block_output,
        pooled_tokens,
        penalty,
        tokens_grad,
        small[0],
        small[1],
        grad_w_qkv,
        small[6],
        small[7],
        grad_w_out,
        small[8],
        small[2],
        small[3],
        grad_w_up,
        small[9],
        grad_w_down,
        small[10],
        small[4],
        small[5],
        grad_w_first,
        small[11],
        small[12],
    )

FAR = -3e30
LOG2E = 1.4426950408889634
LN2 = 0.6931471805599453
NN = (((1,), (0,)), ((), ()))
NT = (((1,), (1,)), ((), ()))
TN = (((0,), (0,)), ((), ()))
PIXELS = 196
UNIT = 256
VMEM_LIMIT = 60 * 1024 * 1024


def dot(a, b, dims=NN):
    return lax.dot_general(a, b, dims, preferred_element_type=jnp.float32)


def compact_rows(frame_total):
    return (-(-frame_total * PIXELS // UNIT) + 3) * UNIT


def key_places(frames_here, info_ref):
    total = 2 * frames_here
    length = info_ref[total]
    count = [jnp.int32(0), jnp.int32(0)]
    places = []
    for f in range(total):
        kept = info_ref[f]
        late = (f >= length).astype(jnp.int32)
        places.append((kept, late, jnp.where(late == 1, count[1], count[0])))
        count[0] = count[0] + kept * (1 - late)
        count[1] = count[1] + kept * late
    units = [(c * PIXELS + UNIT - 1) // UNIT for c in count]
    start = units[0] * UNIT
    starts = [
        (kept, pl.multiple_of(jnp.where(late == 1, start, 0) + place * PIXELS, 4))
        for kept, late, place in places
    ]
    tails = [pl.multiple_of(count[0] * PIXELS, 4), pl.multiple_of(start + count[1] * PIXELS, 4)]
    return starts, tails, units[0], units[0] + units[1]


def clip_edge(frames_here, info_ref):
    total = 2 * frames_here
    first = info_ref[total + 1] * frames_here
    return jnp.clip((info_ref[total] - first) * PIXELS, 0, frames_here * PIXELS)


def gather_keys(frames_here, info_ref, starts, tails, own_k, own_v, far_k, far_v, kf, vf):
    total = 2 * frames_here
    rank = info_ref[total + 1]
    width = own_k.shape[1]
    for tail in tails:
        for ref in (kf, vf):
            ref[pl.ds(tail, UNIT), :] = jnp.zeros((UNIT, width), jnp.float32)
    for f in range(total):
        kept, place = starts[f]
        side = f // frames_here
        at = f % frames_here * PIXELS
        base = at // 16 * 16

        def put(k_ref, v_ref):
            for src, dst in ((k_ref, kf), (v_ref, vf)):
                block = src[base : base + 208, :].astype(jnp.float32)
                dst[pl.ds(place, PIXELS), :] = block[at - base : at - base + PIXELS, :]

        @pl.when((kept == 1) & (rank == side))
        def _():
            put(own_k, own_v)

        @pl.when((kept == 1) & (rank != side))
        def _():
            put(far_k, far_v)


def real_keys(start, size, split, tails, axis, shape):
    at = lax.broadcasted_iota(jnp.int32, shape, axis) + start
    return at < jnp.where(at >= split * UNIT, tails[1], tails[0])


def query_tiles(rows):
    parts = rows // 512
    return [(i * 512, 512) for i in range(parts)], (parts * 512, rows - parts * 512)


def split_heads(rows):
    lane = lax.broadcasted_iota(jnp.int32, rows.shape, 1)
    zero = jnp.zeros_like(rows)
    return jnp.where(lane < 64, rows, zero), jnp.where(lane < 64, zero, rows)


def clip_bias(late, edge, at, size):
    column = lax.broadcasted_iota(jnp.int32, (1, size), 1) + at
    return jnp.where((column >= edge) == late, 0.0, FAR)


def sweep(first, end, sizes, body):
    count = end - first
    big = sizes[0]
    main = count // big

    def step(c, carry):
        body(pl.multiple_of((first + c * big) * UNIT, UNIT), big * UNIT)
        return carry

    lax.fori_loop(0, main, step, 0)
    at = first + main * big
    left = count - main * big
    for size in sizes[1:]:

        @pl.when((left & size) != 0)
        def _():
            body(pl.multiple_of(at * UNIT, UNIT), size * UNIT)

        at = at + (left & size)


def attn_fwd_kernel(
    frames_here, info_ref, q_ref, own_k, own_v, far_k, far_v, o_ref, lse_ref, kc_ref, vc_ref,
    qm, qr, vt, acc, accr, top, kf, vf,
):
    rows = q_ref.shape[0]
    starts, tails, split, end = key_places(frames_here, info_ref)
    edge = clip_edge(frames_here, info_ref)
    crossing = (edge > 0) & (edge < rows)
    low = jnp.where(edge > 0, 0, split)
    high = jnp.where(edge < rows, end, split)
    gather_keys(frames_here, info_ref, starts, tails, own_k, own_v, far_k, far_v, kf, vf)
    tiles, (rest_at, rest) = query_tiles(rows)
    qm[0], qm[1] = split_heads(q_ref[...])
    for h in range(2):
        qr[h * rest : h * rest + rest, :] = qm[h, rest_at:rows, :]
    acc[...] = jnp.zeros_like(acc)
    accr[...] = jnp.zeros_like(accr)
    top[...] = jnp.zeros_like(top)

    def prepare(start, size):
        span = pl.ds(start, size)
        kc_ref[span, :] = kf[span, :].astype(jnp.bfloat16)
        values = vf[span, :].astype(jnp.bfloat16)
        vc_ref[span, :] = values
        vt[0:128, span] = values.T
        real = real_keys(start, size, split, tails, 1, (16, size))
        vt[128:144, span] = real.astype(jnp.float32).astype(jnp.bfloat16)

    sweep(low, high, (2, 1), prepare)

    def value_rows(h, span):
        return jnp.concatenate([vt[64 * h : 64 * h + 64, span], vt[128:144, span]], axis=0)

    def plain(work, start, size):
        span = pl.ds(start, size)
        keys = kc_ref[span, :]

        def scores(item):
            h, at, wide, _ = item
            return dot(keys, qr[...] if h is None else qm[h, at : at + wide, :], NT)

        ahead = scores(work[0])
        for i, (h, at, wide, bias) in enumerate(work):
            s = ahead
            if i + 1 < len(work):
                ahead = scores(work[i + 1])
            if bias is not None:
                s = s + bias
            p = jnp.exp2(s * QUERY_SCALE).astype(jnp.bfloat16)
            if h is None:
                accr[:, : 2 * rest] += dot(vt[:, span], p)
            else:
                acc[h, :, at : at + wide] += dot(value_rows(h, span), p)

    every = [(h, at, wide, None) for h in range(2) for at, wide in tiles]

    @pl.when(jnp.logical_not(crossing))
    def _():
        sweep(low, high, (4, 2, 1), functools.partial(plain, every + [(None, 0, 2 * rest, None)]))

    @pl.when(crossing)
    def _():
        for late in (False, True):
            work = []
            for at, wide in tiles + [(rest_at, rest)]:
                if late and at == 0 or not late and at == rest_at:
                    continue
                bias = clip_bias(late, edge, at, wide)
                work += [(h, at, wide, bias) for h in range(2)]
            body = functools.partial(plain, work)
            sweep(split if late else 0, end if late else split, (4, 2, 1), body)

    for h in range(2):
        lanes = slice(h * rest, h * rest + rest)
        acc[h, 0:64, rest_at:rows] += accr[64 * h : 64 * h + 64, lanes]
        acc[h, 64:80, rest_at:rows] += accr[128:144, lanes]
    mass = jnp.concatenate([acc[0, 64:72, :], acc[1, 64:72, :]], axis=0)
    safe = (jnp.min(mass) >= 2.0**-60) & (jnp.max(mass) <= 2.0**60)

    @pl.when(jnp.logical_not(safe))
    def _():
        acc[...] = jnp.zeros_like(acc)
        top[...] = jnp.full_like(top, NEG)

        def careful(start, size):
            span = pl.ds(start, size)
            keys = kc_ref[span, :]
            real = real_keys(start, size, split, tails, 0, (size, 1))
            drop = jnp.where(real, 0.0, FAR)
            late = start >= split * UNIT
            for h in range(2):
                for at, wide in tiles + [(rest_at, rest)]:
                    lanes = slice(at, at + wide)
                    s = dot(keys, qm[h, lanes, :], NT) * QUERY_SCALE + drop
                    bias = jnp.where(crossing, clip_bias(late, edge, at, wide), 0.0)
                    old = top[h : h + 1, lanes]
                    new = jnp.maximum(old, jnp.max(s, axis=0, keepdims=True) + bias)
                    p = jnp.exp2(s - (new - bias)).astype(jnp.bfloat16)
                    top[h : h + 1, lanes] = new
                    acc[h, :, lanes] = acc[h, :, lanes] * jnp.exp2(old - new) + dot(
                        value_rows(h, span), p
                    )

        sweep(low, high, (1,), careful)

    for at, wide in tiles + [(rest_at, rest)]:
        lanes = slice(at, at + wide)
        halves = []
        for h in range(2):
            sums = acc[h, 64:65, lanes]
            halves.append(acc[h, 0:64, lanes] / sums)
            lse_ref[0, h : h + 1, lanes] = top[h : h + 1, lanes] + jnp.log2(sums)
        o_ref[lanes, :] = jnp.concatenate(halves, axis=0).T.astype(jnp.bfloat16)


def attn_fwd(info, q, own_k, own_v, far_k, far_v, old, part, frames_here):
    rows, width = q.shape
    pairs = width // 256
    length = compact_rows(2 * frames_here)
    rest = rows % 512
    block = pl.BlockSpec((rows, 128), lambda p, *_: (0, p))
    column = pl.BlockSpec((rows, 128), lambda p, *_: (0, p + part * pairs))
    keys = pl.BlockSpec((length, 128), lambda p, *_: (0, p + part * pairs))

    def kernel(*refs):
        return attn_fwd_kernel(frames_here, *refs[:6], *refs[6 + len(old) :])

    return pl.pallas_call(
        kernel,
        out_shape=(
            jax.ShapeDtypeStruct((rows, width), jnp.bfloat16),
            jax.ShapeDtypeStruct((2 * pairs, 8, rows), jnp.float32),
            jax.ShapeDtypeStruct((length, width), jnp.bfloat16),
            jax.ShapeDtypeStruct((length, width), jnp.bfloat16),
        ),
        grid_spec=pltpu.PrefetchScalarGridSpec(
            num_scalar_prefetch=1,
            grid=(pairs,),
            in_specs=[column, block, block, block, block]
            + [pl.BlockSpec(memory_space=pl.ANY)] * len(old),
            out_specs=[
                column,
                pl.BlockSpec((1, 8, rows), lambda p, *_: (p + part * pairs, 0, 0)),
                keys,
                keys,
            ],
            scratch_shapes=[
                pltpu.VMEM((2, rows, 128), jnp.bfloat16),
                pltpu.VMEM((2 * rest, 128), jnp.bfloat16),
                pltpu.VMEM((144, length), jnp.bfloat16),
                pltpu.VMEM((2, 80, rows), jnp.float32),
                pltpu.VMEM((144, 128), jnp.float32),
                pltpu.VMEM((8, rows), jnp.float32),
                pltpu.VMEM((length, 128), jnp.float32),
                pltpu.VMEM((length, 128), jnp.float32),
            ],
        ),
        input_output_aliases={6 + i: i for i in range(len(old))},
        compiler_params=params(),
        cost_estimate=cost(4e10, 1e7),
        name="attn_fwd",
    )(info, q, own_k, own_v, far_k, far_v, *old)


def attn_bwd_kernel(
    frames_here, info_ref, q_ref, k_ref, v_ref, o_ref, do_ref, lse_ref,
    dq_ref, own_dk, own_dv, away, qm, qr, dom, dor, dqt, dqr, delta, dk_all, dv_all, back,
):
    rows = q_ref.shape[0]
    total = 2 * frames_here
    length = info_ref[total]
    rank = info_ref[total + 1]
    starts, _, split, end = key_places(frames_here, info_ref)
    edge = clip_edge(frames_here, info_ref)
    crossing = (edge > 0) & (edge < rows)
    low = jnp.where(edge > 0, 0, split)
    high = jnp.where(edge < rows, end, split)
    tiles, (rest_at, rest) = query_tiles(rows)
    qm[0], qm[1] = split_heads(q_ref[...])
    dom[0], dom[1] = split_heads(do_ref[...])
    for h in range(2):
        qr[h * rest : h * rest + rest, :] = qm[h, rest_at:rows, :]
        dor[h * rest : h * rest + rest, :] = dom[h, rest_at:rows, :]
    dqt[...] = jnp.zeros_like(dqt)
    dqr[...] = jnp.zeros_like(dqr)
    for at, wide in tiles + [(rest_at, rest)]:
        span = slice(at, at + wide)
        prod = (o_ref[span, :].astype(jnp.float32) * do_ref[span, :].astype(jnp.float32)).T
        for h in range(2):
            delta[h : h + 1, span] = jnp.sum(prod[64 * h : 64 * h + 64], axis=0, keepdims=True)

    def both_rows(ref, lead):
        pieces = [ref[(*lead, slice(h, h + 1), slice(rest_at, rows))] for h in range(2)]
        return jnp.concatenate(pieces, axis=1)

    def visit(work, start, size):
        span = pl.ds(start, size)
        keys = k_ref[span, :]
        values = v_ref[span, :]
        turned = keys.T

        def rows_of(item):
            h, at, wide, _ = item
            if h is None:
                return qr[...], dor[...]
            return qm[h, at : at + wide, :], dom[h, at : at + wide, :]

        def scores(item):
            queries, douts = rows_of(item)
            return dot(keys, queries, NT), dot(values, douts, NT)

        dk = jnp.zeros((size, 128), jnp.float32)
        dv = jnp.zeros((size, 128), jnp.float32)
        ahead = scores(work[0])
        for i, item in enumerate(work):
            h, at, wide, bias = item
            s, dp = ahead
            if i + 1 < len(work):
                ahead = scores(work[i + 1])
            queries, douts = rows_of(item)
            if h is None:
                lse, inner = both_rows(lse_ref, (0,)), both_rows(delta, ())
            else:
                lse = lse_ref[0, h : h + 1, at : at + wide]
                inner = delta[h : h + 1, at : at + wide]
            if bias is not None:
                lse = lse - bias
            p = jnp.exp2(jnp.minimum(s * QUERY_SCALE - lse, 0.0))
            ds = (p * (dp - inner)).astype(jnp.bfloat16)
            dv = dv + dot(p.astype(jnp.bfloat16), douts)
            dk = dk + dot(ds, queries)
            if h is None:
                dqr[:, : 2 * rest] += dot(turned, ds)
            else:
                dqt[h, :, at : at + wide] += dot(turned[64 * h : 64 * h + 64], ds)
        return dk, dv

    def fresh(work, start, size):
        dk, dv = visit(work, start, size)
        dk_all[pl.ds(start, size), :] = dk * 0.125
        dv_all[pl.ds(start, size), :] = dv

    every = [(h, at, wide, None) for h in range(2) for at, wide in tiles]

    @pl.when(jnp.logical_not(crossing))
    def _():
        sweep(low, high, (2, 1), functools.partial(fresh, every + [(None, 0, 2 * rest, None)]))

    @pl.when(crossing)
    def _():
        for late in (False, True):
            work = []
            for at, wide in tiles + [(rest_at, rest)]:
                if late and at == 0 or not late and at == rest_at:
                    continue
                bias = clip_bias(late, edge, at, wide)
                work += [(h, at, wide, bias) for h in range(2)]
            body = functools.partial(fresh, work)
            sweep(split if late else 0, end if late else split, (1,), body)

    for h in range(2):
        lanes = slice(h * rest, h * rest + rest)
        dqt[h, :, rest_at:rows] += dqr[64 * h : 64 * h + 64, lanes]
    for at, wide in tiles + [(rest_at, rest)]:
        both = jnp.concatenate([dqt[0, :, at : at + wide], dqt[1, :, at : at + wide]], axis=0)
        dq_ref[at : at + wide, :] = (both * 0.125).T.astype(jnp.bfloat16)

    for side in range(2):

        def put(k_out, v_out):
            for src, out in ((dk_all, k_out), (dv_all, v_out)):
                for f in range(side * frames_here, side * frames_here + frames_here):
                    kept, place = starts[f]
                    use = (kept == 1) & jnp.where(f >= length, edge < rows, edge > 0)
                    at = f % frames_here * PIXELS
                    back[at : at + PIXELS, :] = jnp.where(use, src[pl.ds(place, PIXELS), :], 0.0)
                out(back[...].astype(jnp.bfloat16))

        def write(ref, lanes):
            def store(value):
                ref[:, lanes] = value

            return store

        @pl.when(rank == side)
        def _():
            put(write(own_dk, slice(0, 128)), write(own_dv, slice(0, 128)))

        @pl.when(rank != side)
        def _():
            put(write(away, slice(0, 128)), write(away, slice(128, 256)))


def attn_bwd(info, q, kc, vc, o, do, lse, pairs, frames_here, after):
    rows = q.shape[0]
    length = kc.shape[0]
    rest = rows % 512
    first = pairs[0]
    apart = pairs[-1] - first
    rowspec = pl.BlockSpec((rows, 128), lambda p, *_: (0, first + apart * p))
    keyspec = pl.BlockSpec((length, 128), lambda p, *_: (0, first + apart * p))
    out = pl.BlockSpec((rows, 128), lambda p, *_: (0, p))

    def kernel(*refs):
        return attn_bwd_kernel(frames_here, *refs[:7], *refs[7 + len(after) :])

    return pl.pallas_call(
        kernel,
        out_shape=(jax.ShapeDtypeStruct((rows, 128 * len(pairs)), jnp.bfloat16),) * 3
        + (jax.ShapeDtypeStruct((rows, 256 * len(pairs)), jnp.bfloat16),),
        grid_spec=pltpu.PrefetchScalarGridSpec(
            num_scalar_prefetch=1,
            grid=(len(pairs),),
            in_specs=[
                rowspec,
                keyspec,
                keyspec,
                rowspec,
                rowspec,
                pl.BlockSpec((1, 8, rows), lambda p, *_: (first + apart * p, 0, 0)),
            ]
            + [pl.BlockSpec(memory_space=pl.ANY)] * len(after),
            out_specs=[out] * 3 + [pl.BlockSpec((rows, 256), lambda p, *_: (0, p))],
            scratch_shapes=[
                pltpu.VMEM((2, rows, 128), jnp.bfloat16),
                pltpu.VMEM((2 * rest, 128), jnp.bfloat16),
                pltpu.VMEM((2, rows, 128), jnp.bfloat16),
                pltpu.VMEM((2 * rest, 128), jnp.bfloat16),
                pltpu.VMEM((2, 64, rows), jnp.float32),
                pltpu.VMEM((128, 128), jnp.float32),
                pltpu.VMEM((8, rows), jnp.float32),
                pltpu.VMEM((length, 128), jnp.float32),
                pltpu.VMEM((length, 128), jnp.float32),
                pltpu.VMEM((rows, 128), jnp.float32),
            ],
        ),
        compiler_params=params(),
        cost_estimate=cost(3e10 * len(pairs), 1e7),
        name="attn_bwd",
    )(info, q, kc, vc, o, do, lse, *after)


TILE = 224
PART = 384
INV_SQRT2 = 0.7071067811865476
INV_SQRT_2PI = 0.3989422804014327
QUERY_SCALE = 0.125 * LOG2E


def params(**kw):
    return pltpu.CompilerParams(
        vmem_limit_bytes=VMEM_LIMIT, dimension_semantics=("arbitrary",), **kw
    )


def cost(flops, moved):
    return pl.CostEstimate(flops=int(flops), bytes_accessed=int(moved), transcendentals=0)


def tile_spec(width):
    return pl.BlockSpec((TILE, width), lambda i: (i, 0))


def whole_spec(shape):
    return pl.BlockSpec(shape, lambda i: (0,) * len(shape), pipeline_mode=pl.Buffered(1))


def low_shape(rows, width):
    return jax.ShapeDtypeStruct((rows, width), jnp.bfloat16)


def ln_parts(x):
    center = x - jnp.mean(x, axis=-1, keepdims=True)
    rstd = lax.rsqrt(jnp.mean(center * center, axis=-1, keepdims=True) + EPS)
    return center * rstd, rstd


def ln_back(dy, gain, xhat, rstd):
    dxhat = dy * gain
    along = jnp.mean(dxhat * xhat, axis=-1, keepdims=True)
    return rstd * (dxhat - jnp.mean(dxhat, axis=-1, keepdims=True) - xhat * along)


def line(ref):
    return ref[...].reshape(1, -1)


def vector_spec(size):
    return pl.BlockSpec((size,), lambda i: (0,))


def rows_sum(x):
    return jnp.sum(x, axis=0, keepdims=True)


def project_kernel(x_ref, gain_ref, shift_ref, wk, wv, bias_ref, n_ref, k_ref, v_ref):
    xhat, _ = ln_parts(x_ref[...].astype(jnp.float32))
    normed = (xhat * line(gain_ref) + line(shift_ref)).astype(jnp.bfloat16)
    n_ref[...] = normed
    half = k_ref.shape[1]
    k_ref[...] = dot(normed, wk[...]).astype(jnp.bfloat16)
    v_ref[...] = (dot(normed, wv[...]) + line(bias_ref)[:, :half]).astype(jnp.bfloat16)


def weight_spec(width, size, column):
    return pl.BlockSpec((width, size), lambda i: (0, column), pipeline_mode=pl.Buffered(1))


def project(x, gain, shift, w, v_bias):
    rows, width = x.shape
    half = width // 2
    return pl.pallas_call(
        project_kernel,
        out_shape=(low_shape(rows, width), low_shape(rows, half), low_shape(rows, half)),
        grid=(rows // TILE,),
        in_specs=[
            tile_spec(width),
            vector_spec(width),
            vector_spec(width),
            weight_spec(width, half, 2),
            weight_spec(width, half, 4),
            vector_spec(width),
        ],
        out_specs=[tile_spec(width), tile_spec(half), tile_spec(half)],
        compiler_params=params(),
        cost_estimate=cost(2 * rows * width * width, 10 * rows * width),
        name="project",
    )(x, gain, shift, w, w, v_bias)


def project_more_kernel(n_ref, wq, wk, wv, q_bias, v_bias, q_ref, k_ref, v_ref):
    normed = n_ref[...]
    k_ref[...] = dot(normed, wk[...]).astype(jnp.bfloat16)
    half = v_ref.shape[1]
    v_ref[...] = (dot(normed, wv[...]) + line(v_bias)[:, half:]).astype(jnp.bfloat16)
    q_ref[...] = (dot(normed, wq[...]) + line(q_bias)).astype(jnp.bfloat16)


def project_more(normed, w, q_bias, v_bias):
    rows, width = normed.shape
    half = width // 2
    return pl.pallas_call(
        project_more_kernel,
        out_shape=(low_shape(rows, width), low_shape(rows, half), low_shape(rows, half)),
        grid=(rows // TILE,),
        in_specs=[
            tile_spec(width),
            weight_spec(width, width, 0),
            weight_spec(width, half, 3),
            weight_spec(width, half, 5),
            vector_spec(width),
            vector_spec(width),
        ],
        out_specs=[tile_spec(width), tile_spec(half), tile_spec(half)],
        compiler_params=params(),
        cost_estimate=cost(4 * rows * width * width, 10 * rows * width),
        name="project_more",
    )(normed, w, w, w, q_bias, v_bias)


def mlp_fwd_kernel(
    x_ref, a_ref, w_out, b_out, gain2, shift2, w_up, b_up, w_down, b_down, gain3, shift3,
    mid_ref, n2_ref, hid_ref, slope_ref, out_ref, n3_ref,
):
    width = x_ref.shape[1]
    inner = w_up.shape[1]
    parts = inner // width
    middle = x_ref[...].astype(jnp.float32) + dot(a_ref[...], w_out[...]) + line(b_out)
    mid_ref[...] = middle.astype(jnp.bfloat16)
    xhat, _ = ln_parts(middle)
    n2 = (xhat * line(gain2) + line(shift2)).astype(jnp.bfloat16)
    n2_ref[...] = n2
    out = middle + line(b_down)
    up_shift = line(b_up)

    def raise_part(j):
        span = slice(j * width, (j + 1) * width)
        return dot(n2, w_up[:, span]) + up_shift[:, span]

    ahead = raise_part(0)
    for j in range(parts):
        span = slice(j * width, (j + 1) * width)
        up = ahead
        if j + 1 < parts:
            ahead = raise_part(j + 1)
        area = 0.5 + 0.5 * lax.erf(up * INV_SQRT2)
        bell = jnp.exp2(up * up * (-0.5 * LOG2E)) * INV_SQRT_2PI
        hid = (up * area).astype(jnp.bfloat16)
        hid_ref[:, span] = hid
        slope_ref[:, span] = (area + up * bell).astype(jnp.bfloat16)
        out = out + dot(hid, w_down[span, :])
    out_ref[...] = out.astype(jnp.bfloat16)
    xhat, _ = ln_parts(out)
    n3_ref[...] = (xhat * line(gain3) + line(shift3)).astype(jnp.bfloat16)


def mlp_fwd(x, attended, w_out, b_out, gain2, shift2, w_up, b_up, w_down, b_down, gain3, shift3):
    rows, width = x.shape
    inner = w_up.shape[1]
    vec = vector_spec(width)
    return pl.pallas_call(
        mlp_fwd_kernel,
        out_shape=(
            low_shape(rows, width), low_shape(rows, width), low_shape(rows, inner),
            low_shape(rows, inner), low_shape(rows, width), low_shape(rows, width),
        ),
        grid=(rows // TILE,),
        in_specs=[
            tile_spec(width), tile_spec(width), whole_spec(w_out.shape), vec, vec, vec,
            whole_spec(w_up.shape), vector_spec(inner), whole_spec(w_down.shape), vec, vec, vec,
        ],
        out_specs=[
            tile_spec(width), tile_spec(width), tile_spec(inner),
            tile_spec(inner), tile_spec(width), tile_spec(width),
        ],
        compiler_params=params(),
        cost_estimate=cost(
            2 * rows * width * (width + 2 * inner), 2 * rows * (6 * width + 2 * inner)
        ),
        name="mlp_fwd",
    )(x, attended, w_out, b_out, gain2, shift2, w_up, b_up, w_down, b_down, gain3, shift3)


def mlp_bwd_kernel(
    cot_ref, out_ref, side_ref, pool_ref, w_first, gain3, w_down, slope_ref, w_up, mid_ref,
    gain2, w_out, ddown_ref, dup_ref, dbranch_ref, datt_ref, sums_ref,
):
    width = cot_ref.shape[1]
    inner = w_up.shape[1]
    parts = inner // width

    @pl.when(pl.program_id(0) == 0)
    def _():
        sums_ref[...] = jnp.zeros_like(sums_ref)

    def add(row, value):
        total = rows_sum(value)
        middle = total.shape[1] // 2
        below = sums_ref.shape[0] // 2 + row
        sums_ref[row : row + 1, :] += total[:, :middle]
        sums_ref[below : below + 1, :] += total[:, middle:]

    dn3 = dot(side_ref[:, :128], w_first[...])
    xhat, rstd = ln_parts(out_ref[...].astype(jnp.float32))
    add(2, dn3 * xhat)
    add(3, dn3)
    d_out = (
        cot_ref[...].astype(jnp.float32)
        + ln_back(dn3, line(gain3), xhat, rstd)
        + dot(side_ref[:, 128:192], pool_ref[...])
    )
    d_down = d_out.astype(jnp.bfloat16)
    ddown_ref[...] = d_down
    add(4, d_down.astype(jnp.float32))

    def lower_part(j):
        return dot(d_down, w_down[j * width : (j + 1) * width, :], NT)

    ahead = lower_part(0)
    dn2 = jnp.zeros(cot_ref.shape, jnp.float32)
    for j in range(parts):
        span = slice(j * width, (j + 1) * width)
        d_hid = ahead
        if j + 1 < parts:
            ahead = lower_part(j + 1)
        d_up = (d_hid * slope_ref[:, span].astype(jnp.float32)).astype(jnp.bfloat16)
        dup_ref[:, span] = d_up
        add(6 + j, d_up.astype(jnp.float32))
        dn2 = dn2 + dot(d_up, w_up[:, span], NT)
    xhat, rstd = ln_parts(mid_ref[...].astype(jnp.float32))
    add(0, dn2 * xhat)
    add(1, dn2)
    d_branch = (d_out + ln_back(dn2, line(gain2), xhat, rstd)).astype(jnp.bfloat16)
    dbranch_ref[...] = d_branch
    add(5, d_branch.astype(jnp.float32))
    datt_ref[...] = dot(d_branch, w_out[...], NT).astype(jnp.bfloat16)


def mlp_bwd(cot, out, side, pool, w_first, gain3, w_down, slope, w_up, mid, gain2, w_out):
    rows, width = cot.shape
    inner = w_up.shape[1]
    vec = vector_spec(width)
    return pl.pallas_call(
        mlp_bwd_kernel,
        out_shape=(
            low_shape(rows, width), low_shape(rows, inner), low_shape(rows, width),
            low_shape(rows, width), jax.ShapeDtypeStruct((32, width // 2), jnp.float32),
        ),
        grid=(rows // TILE,),
        in_specs=[
            tile_spec(width), tile_spec(width), tile_spec(256), whole_spec(pool.shape),
            whole_spec(w_first.shape), vec, whole_spec(w_down.shape), tile_spec(inner),
            whole_spec(w_up.shape), tile_spec(width), vec, whole_spec(w_out.shape),
        ],
        out_specs=[
            tile_spec(width), tile_spec(inner), tile_spec(width), tile_spec(width),
            pl.BlockSpec((32, width // 2), lambda i: (0, 0)),
        ],
        compiler_params=params(),
        cost_estimate=cost(
            2 * rows * width * (width + 2 * inner), 2 * rows * (6 * width + 2 * inner)
        ),
        name="mlp_bwd",
    )(cot, out, side, pool, w_first, gain3, w_down, slope, w_up, mid, gain2, w_out)


def final_bwd_kernel(pairs, *refs):
    pieces = [refs[i * pairs : (i + 1) * pairs] for i in range(5)]
    x_ref, branch_ref, gain, w_ref, grad_ref, sums_ref = refs[5 * pairs :]
    width = x_ref.shape[1]

    @pl.when(pl.program_id(0) == 0)
    def _():
        sums_ref[...] = jnp.zeros_like(sums_ref)

    def add(row, value):
        total = rows_sum(value)
        middle = total.shape[1] // 2
        below = sums_ref.shape[0] // 2 + row
        sums_ref[row : row + 1, :] += total[:, :middle]
        sums_ref[below : below + 1, :] += total[:, middle:]

    def join(part):
        return jnp.concatenate([r[...] for r in part], axis=1)

    def total(part, other):
        both = [a[...].astype(jnp.float32) + b[...].astype(jnp.float32) for a, b in zip(part, other)]
        return jnp.concatenate(both, axis=1).astype(jnp.bfloat16)

    dq = join(pieces[0])
    dk = total(pieces[1], pieces[2])
    dv = total(pieces[3], pieces[4])
    dn = (
        dot(dq, w_ref[:, :width], NT)
        + dot(dk, w_ref[:, width : 2 * width], NT)
        + dot(dv, w_ref[:, 2 * width :], NT)
    )
    xhat, rstd = ln_parts(x_ref[...].astype(jnp.float32))
    add(0, dn * xhat)
    add(1, dn)
    add(2, dq.astype(jnp.float32))
    add(3, dv.astype(jnp.float32))
    grad_ref[...] = (
        branch_ref[...].astype(jnp.float32) + ln_back(dn, line(gain), xhat, rstd)
    ).astype(jnp.bfloat16)


def final_bwd(pieces, x, branch, gain, w):
    rows, width = x.shape
    pairs = width // 128
    return pl.pallas_call(
        functools.partial(final_bwd_kernel, pairs),
        out_shape=(low_shape(rows, width), jax.ShapeDtypeStruct((16, width // 2), jnp.float32)),
        grid=(rows // TILE,),
        in_specs=[
            pl.BlockSpec((TILE, 128), functools.partial(lambda c, i: (i, c), column))
            for _, column in pieces
        ]
        + [tile_spec(width)] * 2
        + [vector_spec(width), whole_spec(w.shape)],
        out_specs=[tile_spec(width), pl.BlockSpec((16, width // 2), lambda i: (0, 0))],
        compiler_params=params(),
        cost_estimate=cost(6 * rows * width * width, 16 * rows * width),
        name="final_bwd",
    )(*[array for array, _ in pieces], x, branch, gain, w)


def grid_masks(frames, lanes):
    table = np.zeros((16, lanes), np.float32)
    lane = np.arange(lanes)
    pixel = lane % PIXELS
    i, j = pixel // GRID, pixel % GRID
    inside = lane < frames * PIXELS
    for a in range(3):
        for b in range(3):
            ok = (i + a - 1 >= 0) & (i + a - 1 < GRID) & (j + b - 1 >= 0) & (j + b - 1 < GRID)
            table[3 * a + b] = ok & inside
    table[9] = np.where(inside, lane // PIXELS, -1)
    return table


def learner_kernel(
    frames, info_ref, weight_ref, n3_ref, out_ref, pool_ref, wt_ref, cw_ref, cwt_ref, cb_ref,
    mask_ref, side_ref, pooled_ref, small_ref, keep_ref, send_ref, rounds, seqs,
):
    rows = n3_ref.shape[0]
    lanes = mask_ref.shape[1]
    extra = lanes - rows
    rank = info_ref[2 * frames + 1]
    frame_of = mask_ref[9:10, :]
    live = jnp.zeros((1, lanes), jnp.float32)
    for f in range(frames):
        kept = info_ref[rank * frames + f].astype(jnp.float32)
        live = live + jnp.where(frame_of == f, kept, 0.0)
    inside = (frame_of >= 0).astype(jnp.float32)

    def widen(x):
        return jnp.concatenate([x, jnp.zeros((x.shape[0], extra), jnp.float32)], axis=1)

    def turn(x, by):
        return x if by % lanes == 0 else pltpu.roll(x, by % lanes, 1)

    def gather_taps(taps):
        total = jnp.zeros((8, lanes), jnp.float32)
        for t in range(9):
            step = (t // 3 - 1) * GRID + t % 3 - 1
            total = total + turn(taps[8 * t : 8 * t + 8, :], -step) * mask_ref[t : t + 1, :]
        return total

    def spread_taps(level):
        parts = []
        for t in range(9):
            step = (t // 3 - 1) * GRID + t % 3 - 1
            parts.append(turn(level, step) * mask_ref[8 - t : 9 - t, :])
        return jnp.concatenate(parts, axis=0)

    def exact(a, b, dims=NN):
        return lax.dot_general(
            a, b, dims, precision=HIGHEST, preferred_element_type=jnp.float32
        )

    def area_of(x):
        return 0.5 + 0.5 * lax.erf(x * INV_SQRT2)

    taps = widen(dot(wt_ref[...], n3_ref[...], NT))
    levels = [gather_taps(taps) + cb_ref[:, 0:1]]
    hiddens = []
    for n in range(3):
        hiddens.append(levels[n] * area_of(levels[n]))
        levels.append(gather_taps(exact(cwt_ref[n], hiddens[n])) + cb_ref[:, n + 1 : n + 2])
    maps = 1.0 / (1.0 + jnp.exp(-levels[3]))
    total = rows_sum(maps)
    meet = 0.5 * (total * total - rows_sum(maps * maps)) * live
    small_ref[...] = jnp.zeros_like(small_ref)
    small_ref[8:9, 128:256] = jnp.zeros((1, 128), jnp.float32) + jnp.sum(meet)
    shifts = jnp.zeros((8, 128), jnp.float32)
    lane = lax.broadcasted_iota(jnp.int32, (8, 128), 1)

    owner = lax.broadcasted_iota(jnp.int32, (8 * frames, lanes), 0) // 8
    mine = owner.astype(jnp.float32) == frame_of
    low_maps = maps.astype(jnp.bfloat16).astype(jnp.float32) * live
    stacked = jnp.where(mine, jnp.concatenate([low_maps] * frames, axis=0), 0.0)
    out = out_ref[...]
    pooled_ref[...] = dot(stacked[:, :rows].astype(jnp.bfloat16), out).astype(jnp.bfloat16)
    pairs = jnp.where(mine, widen(dot(pool_ref[...], out, NT)), 0.0)
    d_maps = pairs[0:8]
    for f in range(1, frames):
        d_maps = d_maps + pairs[8 * f : 8 * f + 8]
    d_maps = d_maps * live + weight_ref[0] * live * (total - maps)
    d_level = d_maps * maps * (1.0 - maps)
    for n in (2, 1, 0):
        shifts = jnp.where(lane == n + 1, jnp.sum(d_level, axis=1, keepdims=True), shifts)
        d_taps = spread_taps(d_level)
        small_ref[0:8, 128 * n : 128 * n + 72] = exact(hiddens[n], d_taps, NT)
        d_hidden = exact(cw_ref[n], d_taps)
        x = levels[n]
        bell = jnp.exp(-0.5 * x * x) * INV_SQRT_2PI
        d_level = d_hidden * (area_of(x) + x * bell) * inside
    shifts = jnp.where(lane == 0, jnp.sum(d_level, axis=1, keepdims=True), shifts)
    small_ref[8:16, 0:8] = shifts.T[0:8, :]
    d_first = spread_taps(d_level)[:, :rows]
    grad = dot(d_first.astype(jnp.bfloat16), n3_ref[...])
    grad = jnp.concatenate([grad, jnp.zeros((56, grad.shape[1]), jnp.float32)], axis=0).T
    columns = 9 * MAPS // 2
    lane = lax.broadcasted_iota(jnp.int32, grad.shape, 1)
    left = jnp.where(lane < columns, grad, 0.0).astype(jnp.bfloat16)
    right = jnp.where(lane < columns, pltpu.roll(grad, 128 - columns, 1), 0.0).astype(jnp.bfloat16)
    size = grad.shape[0] // seqs // 3
    for ref, side in ((keep_ref, 0), (send_ref, 1)):
        value = jnp.where(rank == side, left, right)
        for o in range(seqs):
            parts = [value[(3 * o + t) * size : (3 * o + t + 1) * size, :] for t in range(3)]
            put_rows(ref, block_place(o, rounds) * size, jnp.concatenate(parts, axis=1))
    tall = jnp.concatenate(
        [
            d_first,
            jnp.zeros((56, rows), jnp.float32),
            stacked[:, :rows],
            jnp.zeros((128 - 8 * frames, rows), jnp.float32),
        ],
        axis=0,
    )
    side_ref[...] = tall.T.astype(jnp.bfloat16)


def learner(info, weight, n3, out, pool, w_first, conv_weights, conv_biases, rounds, seqs):
    rows, width = n3.shape
    frames = rows // PIXELS
    lanes = -(-rows // 128) * 128
    vm = pl.BlockSpec(memory_space=pltpu.VMEM)
    sm = pl.BlockSpec(memory_space=pltpu.SMEM)
    masks = jnp.asarray(grid_masks(frames, lanes))
    return pl.pallas_call(
        functools.partial(learner_kernel, frames, rounds=rounds, seqs=seqs),
        out_shape=(
            low_shape(rows, 256),
            low_shape(8 * frames, width),
            jax.ShapeDtypeStruct((16, PART), jnp.float32),
            low_shape(width // 3, PART),
            low_shape(width // 3, PART),
        ),
        in_specs=[sm, sm] + [vm] * 8,
        out_specs=(vm,) * 5,
        compiler_params=pltpu.CompilerParams(vmem_limit_bytes=VMEM_LIMIT),
        cost_estimate=cost(2e10, 4 * rows * width),
        name="learner",
    )(
        info, weight, n3, out, pool, w_first.T, conv_weights,
        conv_weights.transpose(0, 2, 1), conv_biases.T, masks,
    )


def flip(count, bit):
    return [(i, i ^ bit) for i in range(count)]


def low_sum(a, b):
    return (a.astype(jnp.float32) + b.astype(jnp.float32)).astype(jnp.bfloat16)


def block_place(owner, rounds):
    place = 0
    for bits in rounds:
        for bit in bits:
            place = place * 2 + ((owner >> bit) & 1)
    return place


def put_rows(ref, at, value):
    if not isinstance(at, int):
        at = pl.multiple_of(at, 16)
    ref[pl.ds(at, value.shape[0]), :] = value


def put_blocks(ref, value, first_owner, owners, rounds):
    size = value.shape[0] // owners
    for o in range(owners):
        place = block_place(first_owner + o, rounds)
        put_rows(ref, place * size, value[o * size : (o + 1) * size, :])


def grad_by_columns_kernel(rounds, seqs, info_ref, a_ref, b_ref, keep_ref, send_ref, turned):
    step = pl.program_id(0)
    half = pl.num_programs(0) // 2

    @pl.when(step == 0)
    def _():
        turned[...] = a_ref[...].T

    got = dot(turned[...], b_ref[...]).astype(jnp.bfloat16)
    parts = got.shape[1] // PART
    size = got.shape[0] // seqs

    def put(ref):
        for o in range(seqs):
            base = block_place(o, rounds) * size * parts * half
            for i in range(parts):
                at = base + (lax.rem(step, half) * parts + i) * size
                put_rows(ref, at, got[o * size : o * size + size, i * PART : i * PART + PART])

    @pl.when(step < half)
    def _():
        put(keep_ref)

    @pl.when(step >= half)
    def _():
        put(send_ref)


def grad_by_columns(info, a, b, rounds, seqs, at):
    rows, tall = a.shape
    wide = b.shape[1]
    block = min(768, wide // 2)
    half = wide // 2 // block
    out = jax.ShapeDtypeStruct((tall * wide // 2 // PART, PART), jnp.bfloat16)
    whole = pl.BlockSpec(out.shape, lambda j, info: (0, 0))
    return pl.pallas_call(
        functools.partial(grad_by_columns_kernel, rounds, seqs),
        out_shape=(out, out),
        grid_spec=pltpu.PrefetchScalarGridSpec(
            num_scalar_prefetch=1,
            grid=(2 * half,),
            in_specs=[
                pl.BlockSpec((rows, tall), lambda j, info: (0, 0)),
                pl.BlockSpec(
                    (rows, block),
                    lambda j, info: (0, jnp.where(j < half, info[at], 1 - info[at]) * half + j % half),
                ),
            ],
            out_specs=[whole, whole],
            scratch_shapes=[pltpu.VMEM((tall, rows), jnp.bfloat16)],
        ),
        compiler_params=params(),
        cost_estimate=cost(2 * rows * tall * wide, 2 * rows * (tall + wide)),
        name="grad_columns",
    )(info, a, b)


def pick_half(rank, value):
    middle = value.shape[1] // 2
    first, second = value[:, :middle], value[:, middle:]
    return jnp.where(rank == 0, first, second), jnp.where(rank == 0, second, first)


def grad_by_rows_kernel(rounds, seqs, at, info_ref, a_ref, b_ref, keep_ref, send_ref):
    step = pl.program_id(0)
    got = dot(a_ref[...], b_ref[...], TN).astype(jnp.bfloat16)
    keep, send = pick_half(info_ref[at], got)
    owners = seqs // (keep_ref.shape[0] // a_ref.shape[1])
    put_blocks(keep_ref, keep, step * owners, owners, rounds)
    put_blocks(send_ref, send, step * owners, owners, rounds)


def grad_by_rows(info, a, b, rounds, seqs, at):
    rows, tall = a.shape
    wide = b.shape[1]
    out = jax.ShapeDtypeStruct((tall, wide // 2), jnp.bfloat16)
    return pl.pallas_call(
        functools.partial(grad_by_rows_kernel, rounds, seqs, at),
        out_shape=(out, out),
        grid_spec=pltpu.PrefetchScalarGridSpec(
            num_scalar_prefetch=1,
            grid=(tall // 768,),
            in_specs=[
                pl.BlockSpec((rows, 768), lambda j, info: (0, j)),
                pl.BlockSpec((rows, wide), lambda j, info: (0, 0)),
            ],
            out_specs=[pl.BlockSpec((tall, wide // 2), lambda j, info: (0, 0))] * 2,
        ),
        compiler_params=params(),
        cost_estimate=cost(2 * rows * tall * wide, 2 * rows * (tall + wide)),
        name="grad_rows",
    )(info, a, b)


def grad_pieces_kernel(rounds, seqs, at, info_ref, n_ref, *refs):
    (q0, k0, x0, v0, y0), (q1, k1, x1, v1, y1) = refs[:5], refs[5:10]
    keep_ref, send_ref = refs[-2:]
    first = jnp.concatenate([q0[...], q1[...], low_sum(k0[...], x0[...])], axis=1)
    second = jnp.concatenate(
        [low_sum(k1[...], x1[...]), low_sum(v0[...], y0[...]), low_sum(v1[...], y1[...])], axis=1
    )
    both = jnp.concatenate([first, second], axis=1)
    got = dot(n_ref[...], both, TN).astype(jnp.bfloat16)
    keep, send = pick_half(info_ref[at], got)
    put_blocks(keep_ref, keep, 0, seqs, rounds)
    put_blocks(send_ref, send, 0, seqs, rounds)


def grad_pieces(info, n1, pieces, rounds, seqs, at, after):
    rows, tall = n1.shape
    out = jax.ShapeDtypeStruct((tall, PART), jnp.bfloat16)
    flat = [piece for pair in pieces for piece in pair]
    whole = pl.BlockSpec((tall, PART), lambda i, info: (0, 0))
    return pl.pallas_call(
        functools.partial(grad_pieces_kernel, rounds, seqs, at),
        out_shape=(out, out),
        grid_spec=pltpu.PrefetchScalarGridSpec(
            num_scalar_prefetch=1,
            grid=(1,),
            in_specs=[pl.BlockSpec((rows, tall), lambda i, info: (0, 0))]
            + [
                pl.BlockSpec((rows, 128), functools.partial(lambda c, i, info: (0, c), column))
                for _, column in flat
            ]
            + [pl.BlockSpec(memory_space=pl.ANY)] * len(after),
            out_specs=[whole, whole],
        ),
        compiler_params=params(),
        cost_estimate=cost(2 * rows * tall * 768, 4 * rows * tall),
        name="grad_pieces",
    )(info, n1, *[array for array, _ in flat], *after)


class Stream:
    def __init__(self, rounds, keep, send, emit=None):
        self.rounds, self.at, self.keep, self.emit = rounds, 0, keep, emit
        self.gots = [(lax.ppermute(send, "frame", flip(2, 1)), 0)]

    def bits(self):
        return self.rounds[self.at] if self.at < len(self.rounds) else None


class Total(Stream):
    def __init__(self, rounds, value, emit):
        super().__init__(rounds, value, value, emit)


def split_low(value):
    high = value.astype(jnp.bfloat16)
    return high, (value - high.astype(jnp.float32)).astype(jnp.bfloat16)


def fold(info, at, bundles, after=(), emit=None):
    arrays, plan, outs = [], [], []

    def source(array):
        for i, known in enumerate(arrays):
            if known is array:
                return i
        arrays.append(array)
        return len(arrays) - 1

    for streams, sending in bundles:
        entry = []
        bits = streams[0].bits() if sending else None
        ways = 1 << len(bits) if bits else 1
        offset = 0
        for s in streams:
            parts = [(source(array), start) for array, start in s.gots]
            rows = s.keep.shape[0]
            entry.append((s, source(s.keep), parts, rows, offset))
            if isinstance(s, Total):
                kept = jax.ShapeDtypeStruct((rows, PART), jnp.float32)
                offset += 2 * rows
            else:
                kept = jax.ShapeDtypeStruct((rows // ways, PART), jnp.bfloat16)
                offset += rows // ways
            if sending:
                outs.append(kept)
            elif s.emit:
                outs += s.emit[0]
            elif not emit:
                outs.append(kept)
        outs += [jax.ShapeDtypeStruct((offset, PART), jnp.bfloat16)] * (ways - 1)
        plan.append((entry, bits, ways))
    if emit:
        outs += emit[0]

    def kernel(info_ref, *refs):
        sources, targets = refs[: len(arrays)], list(refs[len(arrays) + len(after) :])
        index = info_ref[at]
        ready = []
        for entry, bits, ways in plan:
            mine = 0
            for bit in bits or ():
                mine = mine * 2 + ((index >> bit) & 1)
            kept = []
            for s, own, parts, rows, offset in entry:
                size = rows // ways
                if bits:
                    kept.append(targets.pop(0))
                elif s.emit or not emit:
                    count = len(s.emit[0]) if s.emit else 1
                    kept.append([targets.pop(0) for _ in range(count)])
                else:
                    kept.append(None)
            sends = [targets.pop(0) for _ in range(ways - 1)]
            for (s, own, parts, rows, offset), keep in zip(entry, kept):

                def total(start, size):
                    value = sources[own][pl.ds(start, size), :].astype(jnp.float32)
                    for i, begin in parts:
                        if isinstance(s, Total):
                            if sources[i].dtype == jnp.float32:
                                value = value + sources[i][...]
                            else:
                                value = value + sources[i][begin : begin + rows, :].astype(jnp.float32)
                                value = value + sources[i][
                                    begin + rows : begin + 2 * rows, :
                                ].astype(jnp.float32)
                        else:
                            value = value + sources[i][pl.ds(begin + start, size), :].astype(jnp.float32)
                    return value

                if bits and isinstance(s, Total):
                    value = total(0, rows)
                    keep[...] = value
                    high, low = split_low(value)
                    for send in sends:
                        send[offset : offset + rows, :] = high
                        send[offset + rows : offset + 2 * rows, :] = low
                elif bits:
                    size = rows // ways
                    for m in range(ways):
                        start = pl.multiple_of((mine ^ m) * size, 16)
                        value = total(start, size).astype(jnp.bfloat16)
                        if m == 0:
                            keep[...] = value
                        else:
                            sends[m - 1][offset : offset + size, :] = value
                elif keep is None:
                    ready.append(total(0, rows))
                elif s.emit:
                    s.emit[1](total(0, rows), *keep)
                else:
                    keep[0][...] = total(0, rows).astype(keep[0].dtype)
        if emit:
            emit[1](ready, *targets)

    vm = pl.BlockSpec(memory_space=pltpu.VMEM)
    sm = pl.BlockSpec(memory_space=pltpu.SMEM)
    moved = sum(x.size * x.dtype.itemsize for x in arrays) * 2
    results = list(
        pl.pallas_call(
            kernel,
            out_shape=tuple(outs),
            in_specs=[sm] + [vm] * len(arrays) + [pl.BlockSpec(memory_space=pl.ANY)] * len(after),
            out_specs=(vm,) * len(outs),
            compiler_params=pltpu.CompilerParams(vmem_limit_bytes=VMEM_LIMIT),
            cost_estimate=cost(0, moved),
            name="fold",
        )(info, *arrays, *after)
    )
    sent = []
    count = lax.axis_size("seq")
    for entry, bits, ways in plan:
        for s, *_ in entry:
            if bits:
                s.keep = results.pop(0)
            elif s.emit:
                s.result = [results.pop(0) for _ in s.emit[0]]
            elif not emit:
                s.keep = results.pop(0)
            s.gots = []
        for m in range(1, ways):
            mask = 0
            for i, bit in enumerate(bits):
                mask |= ((m >> (len(bits) - 1 - i)) & 1) << bit
            send = results.pop(0)
            sent.append(send)
            got = lax.ppermute(send, "seq", flip(count, mask))
            for s, _, _, _, offset in entry:
                s.gots.append((got, offset))
        if bits:
            for s, *_ in entry:
                s.at += 1
    return sent[:1], results


def add_all(value, bits, after):
    count = lax.axis_size("seq")
    gots = []
    for m in range(1, 1 << len(bits)):
        mask = sum(((m >> i) & 1) << bit for i, bit in enumerate(bits))
        gots.append(lax.ppermute(value, "seq", flip(count, mask)))

    def kernel(*refs):
        total = refs[0][...]
        for ref in refs[1 : 1 + len(gots)]:
            total = total + ref[...]
        refs[-1][...] = total

    vm = pl.BlockSpec(memory_space=pltpu.VMEM)
    return pl.pallas_call(
        kernel,
        out_shape=jax.ShapeDtypeStruct(value.shape, jnp.float32),
        in_specs=[vm] * (1 + len(gots)) + [pl.BlockSpec(memory_space=pl.ANY)] * len(after),
        out_specs=vm,
        name="add_all",
    )(value, *gots, *after)


def doubles(bits):
    low = list(range(bits))
    return [low[i : i + 2] for i in range(0, bits, 2)]


def f32_shape(*shape):
    return jax.ShapeDtypeStruct(shape, jnp.float32)


def write_plain(value, ref):
    ref[...] = value


def write_wide(value, ref):
    size = ref.shape[0]
    for i in range(value.shape[0] // size):
        ref[:, i * PART : i * PART + PART] = value[i * size : i * size + size, :]


def write_first(value, ref):
    for i in range(3):
        ref[16 * i : 16 * i + 16, :] = value[:, 128 * i : 128 * i + ref.shape[1]]


def write_vectors(value, *refs):
    row = 0
    for ref in refs:
        for i in range(ref.shape[0] // (2 * PART)):
            ref[2 * PART * i : 2 * PART * i + PART] = value[row, :]
            ref[2 * PART * i + PART : 2 * PART * (i + 1)] = value[value.shape[0] // 2 + row, :]
            row += 1


def write_small(value, weights_ref, biases_ref, meet_ref):
    for n in range(3):
        weights_ref[n] = value[0:8, 128 * n : 128 * n + 9 * MAPS]
    biases_ref[...] = value[8:12, 0:MAPS]
    meet_ref[...] = value[8:9, 128:129]


def write_groups(values, ref):
    count = len(values)
    for i in range(3):
        for g, value in enumerate(values):
            at = 128 * (i * count + g)
            ref[:, at : at + 128] = value[:, 128 * i : 128 * i + 128]


def quick_device(
    tokens, ln_gain_first, ln_bias_first, w_qkv, q_bias, v_bias, w_out, out_bias, ln_gain_second,
    ln_bias_second, w_up, up_bias, w_down, down_bias, ln_gain_third, ln_bias_third, w_first,
    conv_weights, conv_biases, clip_lengths, frame_mask, out_cot, pool_cot, penalty_scale,
):
    _, rows, width = tokens.shape
    frames = rows // PIXELS
    inner = w_up.shape[1]
    seqs = lax.axis_size("seq")
    rank = lax.axis_index("frame")
    bits = seqs.bit_length() - 1
    near = doubles(bits)
    far = [[bit] for pair in near[1:] for bit in pair] + near[:1]
    rank_at, seq_at = 2 * frames + 1, 2 * frames + 2

    def swap(x):
        return lax.ppermute(x, "frame", flip(2, 1))

    place = jnp.stack([rank, lax.axis_index("seq")]).astype(jnp.int32)
    info = jnp.concatenate([frame_mask[0], clip_lengths[0, 0:1], place])
    x = tokens[0]
    n1, k0, v0 = project(x, ln_gain_first, ln_bias_first, w_qkv, v_bias)
    far_k0, far_v0 = swap(k0), swap(v0)
    q, k1, v1 = project_more(n1, w_qkv, q_bias, v_bias)
    far_k1, far_v1 = swap(k1), swap(v1)
    count = jnp.sum(frame_mask).astype(jnp.float32) * jnp.ones((1, 128))
    count = add_all(count, near[0], (n1,))
    half = attn_fwd(info, q, k0, v0, far_k0, far_v0, (), 0, frames)
    for pair in near[1:]:
        count = add_all(count, pair, (half[0],))
    attended, lse, kc, vc = attn_fwd(info, q, k1, v1, far_k1, far_v1, tuple(half), 1, frames)
    count = count[0, 0]
    weight = (penalty_scale / count).reshape(1)
    mid, n2, hidden, slope, out, n3 = mlp_fwd(
        x, attended, w_out, out_bias, ln_gain_second, ln_bias_second, w_up, up_bias, w_down,
        down_bias, ln_gain_third, ln_bias_third,
    )
    side, pooled, small, first_keep, first_send = learner(
        info, weight, n3, out, pool_cot[0], w_first, conv_weights, conv_biases, near, seqs
    )
    first_pad = jnp.concatenate(
        [w_first.T, jnp.zeros((128 - 9 * MAPS, width), jnp.bfloat16)], axis=0
    )
    d_down, d_up, d_branch, d_att, sums = mlp_bwd(
        out_cot[0], out, side, pool_cot[0], first_pad, ln_gain_third, w_down, slope, w_up, mid,
        ln_gain_second, w_out,
    )
    first = Stream(
        near, first_keep, first_send, ([f32_shape(width // seqs, 9 * MAPS // 2)], write_first)
    )
    meet = Total(
        near,
        small,
        ([f32_shape(3, MAPS, 9 * MAPS), f32_shape(4, MAPS), f32_shape(1, 1)], write_small),
    )
    vectors = Total(
        near, sums, ([f32_shape(width)] * 6 + [f32_shape(inner)], write_vectors)
    )
    down = Stream(
        far,
        *grad_by_rows(info, hidden, d_down, far, seqs, rank_at),
        ([f32_shape(inner // seqs, PART)], write_plain),
    )
    up = Stream(
        near,
        *grad_by_columns(info, n2, d_up, near, seqs, rank_at),
        ([f32_shape(width // seqs, inner // 2)], write_wide),
    )
    branch = Stream(
        near,
        *grad_by_rows(info, attended, d_branch, near, seqs, rank_at),
        ([f32_shape(width // seqs, PART)], write_plain),
    )
    early = [up, branch, first, vectors, meet]
    pairs = width // 128
    groups = pairs // 2
    pieces = {}

    def attend_back(which, after):
        dq, own_k, own_v, away = attn_bwd(
            info, q, kc, vc, attended, d_att, lse, which, frames, after
        )
        away = swap(away)
        for i, pair in enumerate(which):
            pieces[pair] = [(dq, i), (own_k, i), (away, 2 * i), (own_v, i), (away, 2 * i + 1)]
        return dq

    def group_stream(g, after):
        both = (pieces[g], pieces[g + groups])
        grads = grad_pieces(info, n1, both, near, seqs, rank_at, after)
        return Stream(near, *grads), list(grads[1:])

    streams = []
    after, _ = fold(info, seq_at, [(early, True), ([down], True)])
    last = attend_back((0, groups), after)
    after, _ = fold(info, seq_at, [(early, True), ([down], True)], (last,))
    last = attend_back((1, 1 + groups), after)
    after, _ = fold(info, seq_at, [(early, False), ([down], True)], (last,))
    stream, sent = group_stream(0, after)
    streams.append(stream)
    last = attend_back((2,), after + sent)
    stream, after = group_stream(1, (last,))
    streams.append(stream)
    last = attend_back((2 + groups,), after)
    after, _ = fold(info, seq_at, [(streams[:2], True), ([down], False)], (last,))
    stream, _ = group_stream(2, after)
    streams.append(stream)
    tokens_grad, late = final_bwd(
        [pieces[p][i] for i in range(5) for p in range(pairs)], x, d_branch, ln_gain_first, w_qkv
    )
    late = Total(near, late, ([f32_shape(width)] * 4, write_vectors))
    while streams[2].at < streams[0].at:
        bundles = [([streams[2], late], True)]
        if streams[0].gots:
            bundles.append((streams[:2], False))
        fold(info, seq_at, bundles)
    while late.bits():
        fold(info, seq_at, [(streams + [late], True)])
    results = fold(
        info, seq_at, [(streams, False), ([late], False)],
        emit=([f32_shape(width // seqs, 3 * width // 2)], write_groups),
    )[1]
    vectors, late = vectors.result, late.result
    conv_w, conv_b, total = meet.result
    return (
        out[None],
        pooled[None],
        total[0, 0] / count,
        tokens_grad[None],
        late[0],
        late[1],
        results[0],
        late[2],
        late[3],
        branch.result[0],
        vectors[5],
        vectors[0],
        vectors[1],
        up.result[0],
        vectors[6],
        down.result[0],
        vectors[4],
        vectors[2],
        vectors[3],
        first.result[0],
        conv_w,
        conv_b,
    )


def per_device(*arrays):
    tokens, clip_lengths = arrays[0], arrays[19]
    frames = tokens.shape[1] // PIXELS
    seqs = lax.axis_size("seq")
    fits = (
        tokens.shape[0] == 1
        and lax.axis_size("frame") == 2
        and frames % 4 == 0
        and tokens.shape[1] % TILE == 0
        and tokens.shape[2] == HEADS * HEAD_DIM
        and seqs == 16
    )
    return (quick_device if fits else plain_device)(*arrays)


def solution(mesh):
    return jax.shard_map(
        per_device,
        mesh=mesh,
        in_specs=(
            P("seq", "frame", None),
            P(),
            P(),
            P(),
            P(),
            P(),
            P(),
            P(),
            P(),
            P(),
            P(),
            P(),
            P(),
            P(),
            P(),
            P(),
            P(),
            P(),
            P(),
            P("seq", None),
            P("seq", None),
            P("seq", "frame", None),
            P("seq", "frame", None),
            P(),
        ),
        out_specs=(
            P("seq", "frame", None),
            P("seq", "frame", None),
            P(),
            P("seq", "frame", None),
            P(),
            P(),
            P("seq", "frame"),
            P(),
            P(),
            P("seq", "frame"),
            P(),
            P(),
            P(),
            P("seq", "frame"),
            P(),
            P("seq", "frame"),
            P(),
            P(),
            P(),
            P("seq", "frame"),
            P(),
            P(),
        ),
        check_vma=False,
    )
```

```python
import functools

import jax
import jax.numpy as jnp
import numpy as np
from jax import lax
from jax.experimental import pallas as pl
from jax.experimental.pallas import tpu as pltpu
from jax.sharding import PartitionSpec as P

HEADS = 12
HEAD_DIM = 64
GRID = 14
MAPS = 8


EPS = 1e-06
NEG = -1e30
HIGHEST = lax.Precision.HIGHEST


def norm_rows(rows, gain, shift):
    center = rows - jnp.mean(rows, axis=-1, keepdims=True)
    spread = jnp.mean(center * center, axis=-1, keepdims=True)
    return center * lax.rsqrt(spread + EPS) * gain + shift


def shift_sum(taps):
    padded = jnp.pad(taps, ((0, 0), (1, 1), (1, 1), (0, 0), (0, 0)))
    total = padded[:, 0:GRID, 0:GRID, 0, :]
    for tap in range(1, 9):
        total = total + padded[:, tap // 3 : tap // 3 + GRID, tap % 3 : tap % 3 + GRID, tap, :]
    return total


def conv_tail(first, conv_biases, conv_weights):
    frames = first.shape[0]
    level = shift_sum(first.reshape(frames, GRID, GRID, 9, MAPS)) + conv_biases[0]
    for layer in range(3):
        hidden = jax.nn.gelu(level, approximate=False)
        taps = jnp.einsum("fijc,ck->fijk", hidden, conv_weights[layer], precision=HIGHEST)
        level = shift_sum(taps.reshape(frames, GRID, GRID, 9, MAPS)) + conv_biases[layer + 1]
    return jax.nn.sigmoid(level).reshape(frames, GRID * GRID, MAPS)


def exact_gelu(values):
    return jax.nn.gelu(values, approximate=False)


def pair_mask(query_code, key_code):
    return (query_code[:, :, None] == key_code[:, None, :])[:, None]


def score_rows(query_rows, key_rows):
    return jnp.einsum(
        "sqhe,skhe->shqk", query_rows, key_rows, preferred_element_type=jnp.float32
    ) * HEAD_DIM ** (-0.5)


def pair_terms(query_rows, dout_rows, lse_rows, delta_rows, key_rows, value_rows, allowed):
    scores = score_rows(query_rows, key_rows)
    probs = jnp.where(allowed, jnp.exp(scores - lse_rows[..., None]), 0.0)
    slopes = jnp.einsum(
        "sqhe,skhe->shqk", dout_rows, value_rows, preferred_element_type=jnp.float32
    )
    grads = (probs * (slopes - delta_rows[..., None])).astype(jnp.bfloat16)
    return (probs.astype(jnp.bfloat16), grads)


def column_sum(values):
    return jnp.sum(values.astype(jnp.float32), axis=0)


def plain_device(
    tokens,
    ln_gain_first,
    ln_bias_first,
    w_qkv,
    q_bias,
    v_bias,
    w_out,
    out_bias,
    ln_gain_second,
    ln_bias_second,
    w_up,
    up_bias,
    w_down,
    down_bias,
    ln_gain_third,
    ln_bias_third,
    w_first,
    conv_weights,
    conv_biases,
    clip_lengths,
    frame_mask,
    out_cot,
    pool_cot,
    penalty_scale,
):
    seq_count, local, width = tokens.shape
    pixels = GRID * GRID
    frames_here = local // pixels
    frame_total = lax.axis_size("frame")
    frame_rank = lax.axis_index("frame")
    slot_frames = frames_here * frame_total
    length = local * frame_total
    rows = seq_count * local
    image_count = seq_count * frames_here
    scale = HEAD_DIM ** (-0.5)
    positions = jnp.arange(slot_frames, dtype=jnp.int32)[None, :]
    segment_frames = (positions >= clip_lengths[:, 0:1]).astype(jnp.int32)
    key_frames = jnp.where(frame_mask > 0, segment_frames, -1)
    first_frame = frame_rank * frames_here
    query_code = jnp.repeat(
        lax.dynamic_slice_in_dim(segment_frames, first_frame, frames_here, 1), pixels, axis=1
    )
    key_code = jnp.repeat(key_frames, pixels, axis=1)
    valid_here = (
        lax.dynamic_slice_in_dim(frame_mask, first_frame, frames_here, 1)
        .reshape(image_count)
        .astype(jnp.float32)
    )
    flat = tokens.reshape(rows, width).astype(jnp.float32)
    normed_one, back_one = jax.vjp(norm_rows, flat, ln_gain_first, ln_bias_first)
    normed_one = normed_one.astype(jnp.bfloat16)
    qkv_bias = jnp.concatenate([q_bias, jnp.zeros_like(q_bias), v_bias])
    qkv = (jnp.dot(normed_one, w_qkv, preferred_element_type=jnp.float32) + qkv_bias).astype(
        jnp.bfloat16
    )
    qkv = qkv.reshape(seq_count, local, 3, HEADS, HEAD_DIM)
    queries = qkv[:, :, 0]
    keys_here = qkv[:, :, 1]
    values_here = qkv[:, :, 2]
    keys_all, values_all = (
        lax.all_gather(keys_here, "frame", axis=1, tiled=True),
        lax.all_gather(values_here, "frame", axis=1, tiled=True),
    )

    def block_of(array, index):
        return lax.dynamic_slice_in_dim(array, index * local, local, 1)

    def stats_turn(index, carry):
        allowed = pair_mask(query_code, block_of(key_code, index))

        def stats_update(state):
            top, mass = state
            masked = jnp.where(allowed, score_rows(queries, block_of(keys_all, index)), NEG)
            new_top = jnp.maximum(top, jnp.max(masked, axis=-1))
            kept = jnp.where(allowed, jnp.exp(masked - new_top[..., None]), 0.0)
            return (new_top, mass * jnp.exp(top - new_top) + jnp.sum(kept, axis=-1))

        return lax.cond(jnp.any(allowed), stats_update, lambda state: state, carry)

    start_top = jnp.full((seq_count, HEADS, local), NEG, jnp.float32)
    top, mass = lax.fori_loop(0, frame_total, stats_turn, (start_top, jnp.zeros_like(start_top)))
    lse = top + jnp.log(mass)

    def value_turn(index, total):
        allowed = pair_mask(query_code, block_of(key_code, index))

        def value_update(state):
            scores = score_rows(queries, block_of(keys_all, index))
            probs = jnp.where(allowed, jnp.exp(scores - lse[..., None]), 0.0).astype(jnp.bfloat16)
            return state + jnp.einsum(
                "shqk,skhe->sqhe",
                probs,
                block_of(values_all, index),
                preferred_element_type=jnp.float32,
            )

        return lax.cond(jnp.any(allowed), value_update, lambda state: state, total)

    attended = lax.fori_loop(0, frame_total, value_turn, jnp.zeros(queries.shape, jnp.float32))
    attended_low = attended.astype(jnp.bfloat16).reshape(rows, width)
    middle = flat + jnp.dot(attended_low, w_out, preferred_element_type=jnp.float32) + out_bias
    normed_two, back_two = jax.vjp(norm_rows, middle, ln_gain_second, ln_bias_second)
    normed_two = normed_two.astype(jnp.bfloat16)
    upper = jnp.dot(normed_two, w_up, preferred_element_type=jnp.float32) + up_bias
    hidden, gelu_back = jax.vjp(exact_gelu, upper)
    hidden = hidden.astype(jnp.bfloat16)
    output = middle + jnp.dot(hidden, w_down, preferred_element_type=jnp.float32) + down_bias
    output_low = output.astype(jnp.bfloat16)
    normed_three, back_three = jax.vjp(norm_rows, output, ln_gain_third, ln_bias_third)
    normed_three = normed_three.astype(jnp.bfloat16)
    first = jnp.dot(normed_three, w_first, preferred_element_type=jnp.float32)
    maps, tail_back = jax.vjp(
        conv_tail, first.reshape(image_count, pixels, 9 * MAPS), conv_biases, conv_weights
    )
    maps_low = maps.astype(jnp.bfloat16)
    output_frames = output_low.reshape(image_count, pixels, width)
    pooled = (
        jnp.einsum("fpm,fpd->fmd", maps_low, output_frames, preferred_element_type=jnp.float32)
        * valid_here[:, None, None]
    )
    pooled_tokens = pooled.astype(jnp.bfloat16).reshape(seq_count, frames_here * MAPS, width)
    total_map = jnp.sum(maps, axis=-1)
    intersection = 0.5 * (total_map * total_map - jnp.sum(maps * maps, axis=-1))
    intersection_local = jnp.sum(intersection * valid_here[:, None])
    count_local = jnp.sum(valid_here)
    intersection_total, count_total = lax.psum((intersection_local, count_local), ("seq", "frame"))
    penalty = intersection_total / count_total
    pool_frames = pool_cot.reshape(image_count, MAPS, width)
    weight_cot = penalty_scale / count_total
    d_maps = (
        jnp.einsum("fmd,fpd->fpm", pool_frames, output_frames, preferred_element_type=jnp.float32)
        * valid_here[:, None, None]
    )
    d_maps = d_maps + (weight_cot * valid_here)[:, None, None] * (total_map[..., None] - maps)
    d_first, d_conv_biases, d_conv_weights = tail_back(d_maps)
    d_first = d_first.reshape(rows, 9 * MAPS).astype(jnp.bfloat16)
    grad_w_first = jnp.dot(normed_three.T, d_first, preferred_element_type=jnp.float32)
    d_normed_three = jnp.dot(d_first, w_first.T, preferred_element_type=jnp.float32)
    d_from_three, d_gain_three, d_bias_three = back_three(d_normed_three)
    d_pool_rows = (
        jnp.einsum("fpm,fmd->fpd", maps_low, pool_frames, preferred_element_type=jnp.float32)
        * valid_here[:, None, None]
    )
    d_output = (
        out_cot.reshape(rows, width).astype(jnp.float32)
        + d_from_three
        + d_pool_rows.reshape(rows, width)
    )
    d_down = d_output.astype(jnp.bfloat16)
    grad_w_down = jnp.dot(hidden.T, d_down, preferred_element_type=jnp.float32)
    grad_down_bias = column_sum(d_down)
    d_hidden = jnp.dot(d_down, w_down.T, preferred_element_type=jnp.float32)
    d_upper = gelu_back(d_hidden)[0].astype(jnp.bfloat16)
    grad_w_up = jnp.dot(normed_two.T, d_upper, preferred_element_type=jnp.float32)
    grad_up_bias = column_sum(d_upper)
    d_normed_two = jnp.dot(d_upper, w_up.T, preferred_element_type=jnp.float32)
    d_from_two, d_gain_two, d_bias_two = back_two(d_normed_two)
    d_middle = d_output + d_from_two
    d_branch = d_middle.astype(jnp.bfloat16)
    grad_w_out = jnp.dot(attended_low.T, d_branch, preferred_element_type=jnp.float32)
    grad_out_bias = column_sum(d_branch)
    dout_low = jnp.dot(d_branch, w_out.T, preferred_element_type=jnp.float32).astype(jnp.bfloat16)
    dout_low = dout_low.reshape(seq_count, local, HEADS, HEAD_DIM)
    delta = jnp.sum(dout_low.astype(jnp.float32) * attended, axis=-1).transpose(0, 2, 1)
    zeros_here = jnp.zeros(queries.shape, jnp.float32)
    full_zeros = jnp.zeros((seq_count, length, HEADS, HEAD_DIM), jnp.float32)

    def both_turn(index, carry):
        allowed = pair_mask(query_code, block_of(key_code, index))

        def both_update(state):
            grad_q, grad_k, grad_v = state
            key_rows = block_of(keys_all, index)
            probs, grads = pair_terms(
                queries, dout_low, lse, delta, key_rows, block_of(values_all, index), allowed
            )
            grad_q = (
                grad_q
                + jnp.einsum("shqk,skhe->sqhe", grads, key_rows, preferred_element_type=jnp.float32)
                * scale
            )
            part_k = (
                jnp.einsum("shqk,sqhe->skhe", grads, queries, preferred_element_type=jnp.float32)
                * scale
            )
            part_v = jnp.einsum(
                "shqk,sqhe->skhe", probs, dout_low, preferred_element_type=jnp.float32
            )
            grad_k = lax.dynamic_update_slice_in_dim(grad_k, part_k, index * local, 1)
            grad_v = lax.dynamic_update_slice_in_dim(grad_v, part_v, index * local, 1)
            return (grad_q, grad_k, grad_v)

        return lax.cond(jnp.any(allowed), both_update, lambda state: state, carry)

    grad_q, grad_k_all, grad_v_all = lax.fori_loop(
        0, frame_total, both_turn, (zeros_here, full_zeros, full_zeros)
    )
    grad_k, grad_v = (
        lax.psum_scatter(
            grad_k_all.astype(jnp.bfloat16), "frame", scatter_dimension=1, tiled=True
        ).astype(jnp.float32),
        lax.psum_scatter(
            grad_v_all.astype(jnp.bfloat16), "frame", scatter_dimension=1, tiled=True
        ).astype(jnp.float32),
    )
    grad_qkv = (
        jnp.stack([grad_q, grad_k, grad_v], axis=2).astype(jnp.bfloat16).reshape(rows, 3 * width)
    )
    grad_w_qkv = jnp.dot(normed_one.T, grad_qkv, preferred_element_type=jnp.float32)
    grad_q_bias = column_sum(grad_qkv[:, :width])
    grad_v_bias = column_sum(grad_qkv[:, 2 * width :])
    d_normed_one = jnp.dot(grad_qkv, w_qkv.T, preferred_element_type=jnp.float32)
    d_from_one, d_gain_one, d_bias_one = back_one(d_normed_one)
    tokens_grad = (d_middle + d_from_one).astype(jnp.bfloat16).reshape(seq_count, local, width)
    summed = (
        lax.psum_scatter(
            grad_w_qkv.astype(jnp.bfloat16), "seq", scatter_dimension=0, tiled=True
        ).astype(jnp.float32),
        lax.psum_scatter(
            grad_w_out.astype(jnp.bfloat16), "seq", scatter_dimension=0, tiled=True
        ).astype(jnp.float32),
        lax.psum_scatter(
            grad_w_up.astype(jnp.bfloat16), "seq", scatter_dimension=0, tiled=True
        ).astype(jnp.float32),
        lax.psum_scatter(
            grad_w_down.astype(jnp.bfloat16), "seq", scatter_dimension=0, tiled=True
        ).astype(jnp.float32),
        lax.psum_scatter(
            grad_w_first.astype(jnp.bfloat16), "seq", scatter_dimension=0, tiled=True
        ).astype(jnp.float32),
    )
    grad_w_qkv, grad_w_out, grad_w_up, grad_w_down, grad_w_first = (
        lax.psum_scatter(
            summed[0].astype(jnp.bfloat16), "frame", scatter_dimension=1, tiled=True
        ).astype(jnp.float32),
        lax.psum_scatter(
            summed[1].astype(jnp.bfloat16), "frame", scatter_dimension=1, tiled=True
        ).astype(jnp.float32),
        lax.psum_scatter(
            summed[2].astype(jnp.bfloat16), "frame", scatter_dimension=1, tiled=True
        ).astype(jnp.float32),
        lax.psum_scatter(
            summed[3].astype(jnp.bfloat16), "frame", scatter_dimension=1, tiled=True
        ).astype(jnp.float32),
        lax.psum_scatter(
            summed[4].astype(jnp.bfloat16), "frame", scatter_dimension=1, tiled=True
        ).astype(jnp.float32),
    )
    small = lax.psum(
        (
            d_gain_one,
            d_bias_one,
            d_gain_two,
            d_bias_two,
            d_gain_three,
            d_bias_three,
            grad_q_bias,
            grad_v_bias,
            grad_out_bias,
            grad_up_bias,
            grad_down_bias,
            d_conv_weights,
            d_conv_biases,
        ),
        ("seq", "frame"),
    )
    block_output = output_low.reshape(seq_count, local, width)
    return (
        block_output,
        pooled_tokens,
        penalty,
        tokens_grad,
        small[0],
        small[1],
        grad_w_qkv,
        small[6],
        small[7],
        grad_w_out,
        small[8],
        small[2],
        small[3],
        grad_w_up,
        small[9],
        grad_w_down,
        small[10],
        small[4],
        small[5],
        grad_w_first,
        small[11],
        small[12],
    )

FAR = -3e30
LOG2E = 1.4426950408889634
LN2 = 0.6931471805599453
NN = (((1,), (0,)), ((), ()))
NT = (((1,), (1,)), ((), ()))
TN = (((0,), (0,)), ((), ()))
PIXELS = 196
UNIT = 256
VMEM_LIMIT = 40 * 1024 * 1024
WIDE_LIMIT = 60 * 1024 * 1024


def dot(a, b, dims=NN):
    return lax.dot_general(a, b, dims, preferred_element_type=jnp.float32)


def compact_rows(frame_total):
    return (-(-frame_total * PIXELS // UNIT) + 3) * UNIT


def key_places(frames_here, info_ref):
    total = 2 * frames_here
    length = info_ref[total]
    count = [jnp.int32(0), jnp.int32(0)]
    places = []
    for f in range(total):
        kept = info_ref[f]
        late = (f >= length).astype(jnp.int32)
        places.append((kept, late, jnp.where(late == 1, count[1], count[0])))
        count[0] = count[0] + kept * (1 - late)
        count[1] = count[1] + kept * late
    units = [(c * PIXELS + UNIT - 1) // UNIT for c in count]
    start = units[0] * UNIT
    starts = [
        (kept, pl.multiple_of(jnp.where(late == 1, start, 0) + place * PIXELS, 4))
        for kept, late, place in places
    ]
    tails = [pl.multiple_of(count[0] * PIXELS, 4), pl.multiple_of(start + count[1] * PIXELS, 4)]
    return starts, tails, units[0], units[0] + units[1]


def clip_edge(frames_here, info_ref):
    total = 2 * frames_here
    first = info_ref[total + 1] * frames_here
    return jnp.clip((info_ref[total] - first) * PIXELS, 0, frames_here * PIXELS)


def gather_keys(frames_here, info_ref, starts, tails, own_k, own_v, far_k, far_v, kf, vf):
    total = 2 * frames_here
    rank = info_ref[total + 1]
    width = own_k.shape[1]
    for tail in tails:
        for ref in (kf, vf):
            ref[pl.ds(tail, UNIT), :] = jnp.zeros((UNIT, width), jnp.float32)
    for f in range(total):
        kept, place = starts[f]
        side = f // frames_here
        at = f % frames_here * PIXELS
        base = at // 16 * 16

        def put(k_ref, v_ref):
            for src, dst in ((k_ref, kf), (v_ref, vf)):
                block = src[base : base + 208, :].astype(jnp.float32)
                dst[pl.ds(place, PIXELS), :] = block[at - base : at - base + PIXELS, :]

        @pl.when((kept == 1) & (rank == side))
        def _():
            put(own_k, own_v)

        @pl.when((kept == 1) & (rank != side))
        def _():
            put(far_k, far_v)


def real_keys(start, size, split, tails, axis, shape):
    at = lax.broadcasted_iota(jnp.int32, shape, axis) + start
    return at < jnp.where(at >= split * UNIT, tails[1], tails[0])


def query_tiles(rows):
    parts = rows // 512
    return [(i * 512, 512) for i in range(parts)], (parts * 512, rows - parts * 512)


def split_heads(rows):
    lane = lax.broadcasted_iota(jnp.int32, rows.shape, 1)
    zero = jnp.zeros_like(rows)
    return jnp.where(lane < 64, rows, zero), jnp.where(lane < 64, zero, rows)


def clip_bias(late, edge, at, size):
    column = lax.broadcasted_iota(jnp.int32, (1, size), 1) + at
    return jnp.where((column >= edge) == late, 0.0, FAR)


def sweep(first, end, sizes, body):
    count = end - first
    big = sizes[0]
    main = count // big

    def step(c, carry):
        body(pl.multiple_of((first + c * big) * UNIT, UNIT), big * UNIT)
        return carry

    lax.fori_loop(0, main, step, 0)
    at = first + main * big
    left = count - main * big
    for size in sizes[1:]:

        @pl.when((left & size) != 0)
        def _():
            body(pl.multiple_of(at * UNIT, UNIT), size * UNIT)

        at = at + (left & size)


def attn_fwd_kernel(
    frames_here, info_ref, q_ref, own_k, own_v, far_k, far_v, o_ref, lse_ref, kc_ref, vc_ref,
    qm, qr, vt, acc, accr, top, kf, vf,
):
    rows = q_ref.shape[0]
    starts, tails, split, end = key_places(frames_here, info_ref)
    edge = clip_edge(frames_here, info_ref)
    crossing = (edge > 0) & (edge < rows)
    low = jnp.where(edge > 0, 0, split)
    high = jnp.where(edge < rows, end, split)
    gather_keys(frames_here, info_ref, starts, tails, own_k, own_v, far_k, far_v, kf, vf)
    tiles, (rest_at, rest) = query_tiles(rows)
    qm[0], qm[1] = split_heads(q_ref[...])
    for h in range(2):
        qr[h * rest : h * rest + rest, :] = qm[h, rest_at:rows, :]
    acc[...] = jnp.zeros_like(acc)
    accr[...] = jnp.zeros_like(accr)
    top[...] = jnp.zeros_like(top)

    def prepare(start, size):
        span = pl.ds(start, size)
        kc_ref[span, :] = kf[span, :].astype(jnp.bfloat16)
        values = vf[span, :].astype(jnp.bfloat16)
        vc_ref[span, :] = values
        vt[0:128, span] = values.T
        real = real_keys(start, size, split, tails, 1, (16, size))
        vt[128:144, span] = real.astype(jnp.float32).astype(jnp.bfloat16)

    sweep(low, high, (2, 1), prepare)

    def value_rows(h, span):
        return jnp.concatenate([vt[64 * h : 64 * h + 64, span], vt[128:144, span]], axis=0)

    def plain(work, start, size):
        span = pl.ds(start, size)
        keys = kc_ref[span, :]

        def scores(item):
            h, at, wide, _ = item
            return dot(keys, qr[...] if h is None else qm[h, at : at + wide, :], NT)

        ahead = scores(work[0])
        for i, (h, at, wide, bias) in enumerate(work):
            s = ahead
            if i + 1 < len(work):
                ahead = scores(work[i + 1])
            if bias is not None:
                s = s + bias
            p = jnp.exp2(s * QUERY_SCALE).astype(jnp.bfloat16)
            if h is None:
                accr[:, : 2 * rest] += dot(vt[:, span], p)
            else:
                acc[h, :, at : at + wide] += dot(value_rows(h, span), p)

    every = [(h, at, wide, None) for h in range(2) for at, wide in tiles]

    @pl.when(jnp.logical_not(crossing))
    def _():
        sweep(low, high, (4, 2, 1), functools.partial(plain, every + [(None, 0, 2 * rest, None)]))

    @pl.when(crossing)
    def _():
        for late in (False, True):
            shown = tiles[1:] if late else tiles[:-1]
            work = [
                (h, at, wide, clip_bias(late, edge, at, wide) if 0 < at < tiles[-1][0] else None)
                for h in range(2)
                for at, wide in shown
            ]
            if late:
                work.append((None, 0, 2 * rest, None))
            body = functools.partial(plain, work)
            sweep(split if late else 0, end if late else split, (2, 1), body)

    for h in range(2):
        lanes = slice(h * rest, h * rest + rest)
        acc[h, 0:64, rest_at:rows] += accr[64 * h : 64 * h + 64, lanes]
        acc[h, 64:80, rest_at:rows] += accr[128:144, lanes]
    mass = jnp.concatenate([acc[0, 64:72, :], acc[1, 64:72, :]], axis=0)
    safe = (jnp.min(mass) >= 2.0**-60) & (jnp.max(mass) <= 2.0**60)

    @pl.when(jnp.logical_not(safe))
    def _():
        acc[...] = jnp.zeros_like(acc)
        top[...] = jnp.full_like(top, NEG)

        def careful(start, size):
            span = pl.ds(start, size)
            keys = kc_ref[span, :]
            real = real_keys(start, size, split, tails, 0, (size, 1))
            drop = jnp.where(real, 0.0, FAR)
            late = start >= split * UNIT
            for h in range(2):
                for at, wide in tiles + [(rest_at, rest)]:
                    lanes = slice(at, at + wide)
                    s = dot(keys, qm[h, lanes, :], NT) * QUERY_SCALE + drop
                    bias = jnp.where(crossing, clip_bias(late, edge, at, wide), 0.0)
                    old = top[h : h + 1, lanes]
                    new = jnp.maximum(old, jnp.max(s, axis=0, keepdims=True) + bias)
                    p = jnp.exp2(s - (new - bias)).astype(jnp.bfloat16)
                    top[h : h + 1, lanes] = new
                    acc[h, :, lanes] = acc[h, :, lanes] * jnp.exp2(old - new) + dot(
                        value_rows(h, span), p
                    )

        sweep(low, high, (1,), careful)

    for at, wide in tiles + [(rest_at, rest)]:
        lanes = slice(at, at + wide)
        halves = []
        for h in range(2):
            sums = acc[h, 64:65, lanes]
            halves.append(acc[h, 0:64, lanes] / sums)
            lse_ref[0, h : h + 1, lanes] = top[h : h + 1, lanes] + jnp.log2(sums)
        o_ref[lanes, :] = jnp.concatenate(halves, axis=0).T.astype(jnp.bfloat16)


def attn_fwd(info, q, own_k, own_v, far_k, far_v, old, part, frames_here):
    rows, width = q.shape
    pairs = width // 256
    length = compact_rows(2 * frames_here)
    rest = rows % 512
    block = pl.BlockSpec((rows, 128), lambda p, *_: (0, p))
    column = pl.BlockSpec((rows, 128), lambda p, *_: (0, p + part * pairs))
    keys = pl.BlockSpec((length, 128), lambda p, *_: (0, p + part * pairs))

    def kernel(*refs):
        return attn_fwd_kernel(frames_here, *refs[:6], *refs[6 + len(old) :])

    return pl.pallas_call(
        kernel,
        out_shape=(
            jax.ShapeDtypeStruct((rows, width), jnp.bfloat16),
            jax.ShapeDtypeStruct((2 * pairs, 8, rows), jnp.float32),
            jax.ShapeDtypeStruct((length, width), jnp.bfloat16),
            jax.ShapeDtypeStruct((length, width), jnp.bfloat16),
        ),
        grid_spec=pltpu.PrefetchScalarGridSpec(
            num_scalar_prefetch=1,
            grid=(pairs,),
            in_specs=[column, block, block, block, block]
            + [pl.BlockSpec(memory_space=pl.ANY)] * len(old),
            out_specs=[
                column,
                pl.BlockSpec((1, 8, rows), lambda p, *_: (p + part * pairs, 0, 0)),
                keys,
                keys,
            ],
            scratch_shapes=[
                pltpu.VMEM((2, rows, 128), jnp.bfloat16),
                pltpu.VMEM((2 * rest, 128), jnp.bfloat16),
                pltpu.VMEM((144, length), jnp.bfloat16),
                pltpu.VMEM((2, 80, rows), jnp.float32),
                pltpu.VMEM((144, 128), jnp.float32),
                pltpu.VMEM((8, rows), jnp.float32),
                pltpu.VMEM((length, 128), jnp.float32),
                pltpu.VMEM((length, 128), jnp.float32),
            ],
        ),
        input_output_aliases={6 + i: i for i in range(len(old))},
        compiler_params=params(WIDE_LIMIT),
        cost_estimate=cost(4e10, 1e7),
        name="attn_fwd",
    )(info, q, own_k, own_v, far_k, far_v, *old)


def attn_bwd_kernel(
    frames_here, info_ref, q_ref, k_ref, v_ref, o_ref, do_ref, lse_ref,
    dq_ref, own_dk, own_dv, away, qm, qr, dom, dor, dqt, dqr, delta, dk_all, dv_all, back,
):
    rows = q_ref.shape[0]
    total = 2 * frames_here
    length = info_ref[total]
    rank = info_ref[total + 1]
    starts, _, split, end = key_places(frames_here, info_ref)
    edge = clip_edge(frames_here, info_ref)
    crossing = (edge > 0) & (edge < rows)
    low = jnp.where(edge > 0, 0, split)
    high = jnp.where(edge < rows, end, split)
    tiles, (rest_at, rest) = query_tiles(rows)
    qm[0], qm[1] = split_heads(q_ref[...])
    dom[0], dom[1] = split_heads(do_ref[...])
    for h in range(2):
        qr[h * rest : h * rest + rest, :] = qm[h, rest_at:rows, :]
        dor[h * rest : h * rest + rest, :] = dom[h, rest_at:rows, :]
    dqt[...] = jnp.zeros_like(dqt)
    dqr[...] = jnp.zeros_like(dqr)
    for at, wide in tiles + [(rest_at, rest)]:
        span = slice(at, at + wide)
        prod = (o_ref[span, :].astype(jnp.float32) * do_ref[span, :].astype(jnp.float32)).T
        for h in range(2):
            delta[h : h + 1, span] = jnp.sum(prod[64 * h : 64 * h + 64], axis=0, keepdims=True)

    def both_rows(ref, lead):
        pieces = [ref[(*lead, slice(h, h + 1), slice(rest_at, rows))] for h in range(2)]
        return jnp.concatenate(pieces, axis=1)

    def visit(work, start, size):
        span = pl.ds(start, size)
        keys = k_ref[span, :]
        values = v_ref[span, :]
        turned = keys.T

        def rows_of(item):
            h, at, wide, _ = item
            if h is None:
                return qr[...], dor[...]
            return qm[h, at : at + wide, :], dom[h, at : at + wide, :]

        def scores(item):
            queries, douts = rows_of(item)
            return dot(keys, queries, NT), dot(values, douts, NT)

        dk = jnp.zeros((size, 128), jnp.float32)
        dv = jnp.zeros((size, 128), jnp.float32)
        ahead = scores(work[0])
        for i, item in enumerate(work):
            h, at, wide, bias = item
            s, dp = ahead
            if i + 1 < len(work):
                ahead = scores(work[i + 1])
            queries, douts = rows_of(item)
            if h is None:
                lse, inner = both_rows(lse_ref, (0,)), both_rows(delta, ())
            else:
                lse = lse_ref[0, h : h + 1, at : at + wide]
                inner = delta[h : h + 1, at : at + wide]
            if bias is not None:
                lse = lse - bias
            p = jnp.exp2(jnp.minimum(s * QUERY_SCALE - lse, 0.0))
            ds = (p * (dp - inner)).astype(jnp.bfloat16)
            dv = dv + dot(p.astype(jnp.bfloat16), douts)
            dk = dk + dot(ds, queries)
            if h is None:
                dqr[:, : 2 * rest] += dot(turned, ds)
            else:
                dqt[h, :, at : at + wide] += dot(turned[64 * h : 64 * h + 64], ds)
        return dk, dv

    def fresh(work, start, size):
        dk, dv = visit(work, start, size)
        dk_all[pl.ds(start, size), :] = dk * 0.125
        dv_all[pl.ds(start, size), :] = dv

    every = [(h, at, wide, None) for h in range(2) for at, wide in tiles]

    @pl.when(jnp.logical_not(crossing))
    def _():
        sweep(low, high, (2, 1), functools.partial(fresh, every + [(None, 0, 2 * rest, None)]))

    @pl.when(crossing)
    def _():
        for late in (False, True):
            shown = tiles[1:] if late else tiles[:-1]
            work = [
                (h, at, wide, clip_bias(late, edge, at, wide) if 0 < at < tiles[-1][0] else None)
                for h in range(2)
                for at, wide in shown
            ]
            if late:
                work.append((None, 0, 2 * rest, None))
            body = functools.partial(fresh, work)
            sweep(split if late else 0, end if late else split, (1,), body)

    for h in range(2):
        lanes = slice(h * rest, h * rest + rest)
        dqt[h, :, rest_at:rows] += dqr[64 * h : 64 * h + 64, lanes]
    for at, wide in tiles + [(rest_at, rest)]:
        both = jnp.concatenate([dqt[0, :, at : at + wide], dqt[1, :, at : at + wide]], axis=0)
        dq_ref[at : at + wide, :] = (both * 0.125).T.astype(jnp.bfloat16)

    for side in range(2):

        def put(k_out, v_out):
            for src, out in ((dk_all, k_out), (dv_all, v_out)):
                for f in range(side * frames_here, side * frames_here + frames_here):
                    kept, place = starts[f]
                    use = (kept == 1) & jnp.where(f >= length, edge < rows, edge > 0)
                    at = f % frames_here * PIXELS
                    back[at : at + PIXELS, :] = jnp.where(use, src[pl.ds(place, PIXELS), :], 0.0)
                out(back[...].astype(jnp.bfloat16))

        def write(ref, lanes):
            def store(value):
                ref[:, lanes] = value

            return store

        @pl.when(rank == side)
        def _():
            put(write(own_dk, slice(0, 128)), write(own_dv, slice(0, 128)))

        @pl.when(rank != side)
        def _():
            put(write(away, slice(0, 128)), write(away, slice(128, 256)))


def attn_bwd(info, q, kc, vc, o, do, lse, pairs, frames_here, after):
    rows = q.shape[0]
    length = kc.shape[0]
    rest = rows % 512
    first = pairs[0]
    apart = pairs[-1] - first
    rowspec = pl.BlockSpec((rows, 128), lambda p, *_: (0, first + apart * p))
    keyspec = pl.BlockSpec((length, 128), lambda p, *_: (0, first + apart * p))
    out = pl.BlockSpec((rows, 128), lambda p, *_: (0, p))

    def kernel(*refs):
        return attn_bwd_kernel(frames_here, *refs[:7], *refs[7 + len(after) :])

    return pl.pallas_call(
        kernel,
        out_shape=(jax.ShapeDtypeStruct((rows, 128 * len(pairs)), jnp.bfloat16),) * 3
        + (jax.ShapeDtypeStruct((rows, 256 * len(pairs)), jnp.bfloat16),),
        grid_spec=pltpu.PrefetchScalarGridSpec(
            num_scalar_prefetch=1,
            grid=(len(pairs),),
            in_specs=[
                rowspec,
                keyspec,
                keyspec,
                rowspec,
                rowspec,
                pl.BlockSpec((1, 8, rows), lambda p, *_: (first + apart * p, 0, 0)),
            ]
            + [pl.BlockSpec(memory_space=pl.ANY)] * len(after),
            out_specs=[out] * 3 + [pl.BlockSpec((rows, 256), lambda p, *_: (0, p))],
            scratch_shapes=[
                pltpu.VMEM((2, rows, 128), jnp.bfloat16),
                pltpu.VMEM((2 * rest, 128), jnp.bfloat16),
                pltpu.VMEM((2, rows, 128), jnp.bfloat16),
                pltpu.VMEM((2 * rest, 128), jnp.bfloat16),
                pltpu.VMEM((2, 64, rows), jnp.float32),
                pltpu.VMEM((128, 128), jnp.float32),
                pltpu.VMEM((8, rows), jnp.float32),
                pltpu.VMEM((length, 128), jnp.float32),
                pltpu.VMEM((length, 128), jnp.float32),
                pltpu.VMEM((rows, 128), jnp.float32),
            ],
        ),
        compiler_params=params(),
        cost_estimate=cost(3e10 * len(pairs), 1e7),
        name="attn_bwd",
    )(info, q, kc, vc, o, do, lse, *after)


TILE = 400
SMALL_TILE = 224
PART = 384
INV_SQRT2 = 0.7071067811865476
INV_SQRT_2PI = 0.3989422804014327
QUERY_SCALE = 0.125 * LOG2E


def params(limit=VMEM_LIMIT):
    return pltpu.CompilerParams(vmem_limit_bytes=limit, dimension_semantics=("arbitrary",))


def cost(flops, moved):
    return pl.CostEstimate(flops=int(flops), bytes_accessed=int(moved), transcendentals=0)


def tile_spec(width):
    return pl.BlockSpec((TILE, width), lambda i: (i, 0))


def small_spec(width):
    return pl.BlockSpec((SMALL_TILE, width), lambda i: (i, 0))


def whole_spec(shape):
    return pl.BlockSpec(shape, lambda i: (0,) * len(shape), pipeline_mode=pl.Buffered(1))


def low_shape(rows, width):
    return jax.ShapeDtypeStruct((rows, width), jnp.bfloat16)


def ln_parts(x):
    center = x - jnp.mean(x, axis=-1, keepdims=True)
    rstd = lax.rsqrt(jnp.mean(center * center, axis=-1, keepdims=True) + EPS)
    return center * rstd, rstd


def ln_back(dy, gain, xhat, rstd):
    dxhat = dy * gain
    along = jnp.mean(dxhat * xhat, axis=-1, keepdims=True)
    return rstd * (dxhat - jnp.mean(dxhat, axis=-1, keepdims=True) - xhat * along)


def line(ref):
    return ref[...].reshape(1, -1)


def vector_spec(size):
    return pl.BlockSpec((size,), lambda i: (0,))


def rows_sum(x):
    return jnp.sum(x, axis=0, keepdims=True)


def project_kernel(x_ref, gain_ref, shift_ref, wk, wv, bias_ref, n_ref, k_ref, v_ref):
    xhat, _ = ln_parts(x_ref[...].astype(jnp.float32))
    normed = (xhat * line(gain_ref) + line(shift_ref)).astype(jnp.bfloat16)
    n_ref[...] = normed
    half = k_ref.shape[1]
    k_ref[...] = dot(normed, wk[...]).astype(jnp.bfloat16)
    v_ref[...] = (dot(normed, wv[...]) + line(bias_ref)[:, :half]).astype(jnp.bfloat16)


def weight_spec(width, size, column):
    return pl.BlockSpec((width, size), lambda i: (0, column), pipeline_mode=pl.Buffered(1))


def project(x, gain, shift, w, v_bias):
    rows, width = x.shape
    half = width // 2
    return pl.pallas_call(
        project_kernel,
        out_shape=(low_shape(rows, width), low_shape(rows, half), low_shape(rows, half)),
        grid=(-(-rows // TILE),),
        in_specs=[
            tile_spec(width),
            vector_spec(width),
            vector_spec(width),
            weight_spec(width, half, 2),
            weight_spec(width, half, 4),
            vector_spec(width),
        ],
        out_specs=[tile_spec(width), tile_spec(half), tile_spec(half)],
        compiler_params=params(WIDE_LIMIT),
        cost_estimate=cost(2 * rows * width * width, 10 * rows * width),
        name="project",
    )(x, gain, shift, w, w, v_bias)


def project_more_kernel(n_ref, wq, wk, wv, q_bias, v_bias, q_ref, k_ref, v_ref):
    normed = n_ref[...]
    k_ref[...] = dot(normed, wk[...]).astype(jnp.bfloat16)
    half = v_ref.shape[1]
    v_ref[...] = (dot(normed, wv[...]) + line(v_bias)[:, half:]).astype(jnp.bfloat16)
    q_ref[...] = (dot(normed, wq[...]) + line(q_bias)).astype(jnp.bfloat16)


def project_more(normed, w, q_bias, v_bias):
    rows, width = normed.shape
    half = width // 2
    return pl.pallas_call(
        project_more_kernel,
        out_shape=(low_shape(rows, width), low_shape(rows, half), low_shape(rows, half)),
        grid=(-(-rows // TILE),),
        in_specs=[
            tile_spec(width),
            weight_spec(width, width, 0),
            weight_spec(width, half, 3),
            weight_spec(width, half, 5),
            vector_spec(width),
            vector_spec(width),
        ],
        out_specs=[tile_spec(width), tile_spec(half), tile_spec(half)],
        compiler_params=params(WIDE_LIMIT),
        cost_estimate=cost(4 * rows * width * width, 10 * rows * width),
        name="project_more",
    )(normed, w, w, w, q_bias, v_bias)


def mlp_fwd_kernel(
    x_ref, a_ref, w_out, b_out, gain2, shift2, w_up, b_up, w_down, b_down, gain3, shift3,
    mid_ref, n2_ref, hid_ref, slope_ref, out_ref, n3_ref,
):
    width = x_ref.shape[1]
    inner = w_up.shape[1]
    parts = inner // width
    middle = x_ref[...].astype(jnp.float32) + dot(a_ref[...], w_out[...]) + line(b_out)
    mid_ref[...] = middle.astype(jnp.bfloat16)
    xhat, _ = ln_parts(middle)
    n2 = (xhat * line(gain2) + line(shift2)).astype(jnp.bfloat16)
    n2_ref[...] = n2
    out = middle + line(b_down)
    up_shift = line(b_up)

    def raise_part(j):
        span = slice(j * width, (j + 1) * width)
        return dot(n2, w_up[:, span]) + up_shift[:, span]

    ahead = raise_part(0)
    for j in range(parts):
        span = slice(j * width, (j + 1) * width)
        up = ahead
        if j + 1 < parts:
            ahead = raise_part(j + 1)
        area = 0.5 + 0.5 * lax.erf(up * INV_SQRT2)
        bell = jnp.exp2(up * up * (-0.5 * LOG2E)) * INV_SQRT_2PI
        hid = (up * area).astype(jnp.bfloat16)
        hid_ref[:, span] = hid
        slope_ref[:, span] = (area + up * bell).astype(jnp.bfloat16)
        out = out + dot(hid, w_down[span, :])
    out_ref[...] = out.astype(jnp.bfloat16)
    xhat, _ = ln_parts(out)
    n3_ref[...] = (xhat * line(gain3) + line(shift3)).astype(jnp.bfloat16)


def mlp_fwd(x, attended, w_out, b_out, gain2, shift2, w_up, b_up, w_down, b_down, gain3, shift3):
    rows, width = x.shape
    inner = w_up.shape[1]
    vec = vector_spec(width)
    return pl.pallas_call(
        mlp_fwd_kernel,
        out_shape=(
            low_shape(rows, width), low_shape(rows, width), low_shape(rows, inner),
            low_shape(rows, inner), low_shape(rows, width), low_shape(rows, width),
        ),
        grid=(-(-rows // TILE),),
        in_specs=[
            tile_spec(width), tile_spec(width), whole_spec(w_out.shape), vec, vec, vec,
            whole_spec(w_up.shape), vector_spec(inner), whole_spec(w_down.shape), vec, vec, vec,
        ],
        out_specs=[
            tile_spec(width), tile_spec(width), tile_spec(inner),
            tile_spec(inner), tile_spec(width), tile_spec(width),
        ],
        compiler_params=params(WIDE_LIMIT),
        cost_estimate=cost(
            2 * rows * width * (width + 2 * inner), 2 * rows * (6 * width + 2 * inner)
        ),
        name="mlp_fwd",
    )(x, attended, w_out, b_out, gain2, shift2, w_up, b_up, w_down, b_down, gain3, shift3)


def mlp_bwd_kernel(
    rows, cot_ref, out_ref, side_ref, pool_ref, w_first, gain3, w_down, slope_ref, w_up, mid_ref,
    gain2, w_out, ddown_ref, dup_ref, dbranch_ref, datt_ref, sums_ref,
):
    width = cot_ref.shape[1]
    inner = w_up.shape[1]
    parts = inner // width

    @pl.when(pl.program_id(0) == 0)
    def _():
        sums_ref[...] = jnp.zeros_like(sums_ref)

    inside = lax.broadcasted_iota(jnp.int32, (TILE, 1), 0) < rows - pl.program_id(0) * TILE

    def add(row, value):
        total = rows_sum(jnp.where(inside, value, 0.0))
        middle = total.shape[1] // 2
        below = sums_ref.shape[0] // 2 + row
        sums_ref[row : row + 1, :] += total[:, :middle]
        sums_ref[below : below + 1, :] += total[:, middle:]

    dn3 = dot(side_ref[:, :128], w_first[...])
    xhat, rstd = ln_parts(out_ref[...].astype(jnp.float32))
    add(2, dn3 * xhat)
    add(3, dn3)
    d_out = (
        cot_ref[...].astype(jnp.float32)
        + ln_back(dn3, line(gain3), xhat, rstd)
        + dot(side_ref[:, 128:192], pool_ref[...])
    )
    d_down = d_out.astype(jnp.bfloat16)
    ddown_ref[...] = d_down
    add(4, d_down.astype(jnp.float32))

    def lower_part(j):
        return dot(d_down, w_down[j * width : (j + 1) * width, :], NT)

    ahead = lower_part(0)
    dn2 = jnp.zeros(cot_ref.shape, jnp.float32)
    for j in range(parts):
        span = slice(j * width, (j + 1) * width)
        d_hid = ahead
        if j + 1 < parts:
            ahead = lower_part(j + 1)
        d_up = (d_hid * slope_ref[:, span].astype(jnp.float32)).astype(jnp.bfloat16)
        dup_ref[:, span] = d_up
        add(6 + j, d_up.astype(jnp.float32))
        dn2 = dn2 + dot(d_up, w_up[:, span], NT)
    xhat, rstd = ln_parts(mid_ref[...].astype(jnp.float32))
    add(0, dn2 * xhat)
    add(1, dn2)
    d_branch = (d_out + ln_back(dn2, line(gain2), xhat, rstd)).astype(jnp.bfloat16)
    dbranch_ref[...] = d_branch
    add(5, d_branch.astype(jnp.float32))
    datt_ref[...] = dot(d_branch, w_out[...], NT).astype(jnp.bfloat16)


def mlp_bwd(cot, out, side, pool, w_first, gain3, w_down, slope, w_up, mid, gain2, w_out):
    rows, width = cot.shape
    inner = w_up.shape[1]
    vec = vector_spec(width)
    return pl.pallas_call(
        functools.partial(mlp_bwd_kernel, rows),
        out_shape=(
            low_shape(rows, width), low_shape(rows, inner), low_shape(rows, width),
            low_shape(rows, width), jax.ShapeDtypeStruct((32, width // 2), jnp.float32),
        ),
        grid=(-(-rows // TILE),),
        in_specs=[
            tile_spec(width), tile_spec(width), tile_spec(256), whole_spec(pool.shape),
            whole_spec(w_first.shape), vec, whole_spec(w_down.shape), tile_spec(inner),
            whole_spec(w_up.shape), tile_spec(width), vec, whole_spec(w_out.shape),
        ],
        out_specs=[
            tile_spec(width), tile_spec(inner), tile_spec(width), tile_spec(width),
            pl.BlockSpec((32, width // 2), lambda i: (0, 0)),
        ],
        compiler_params=params(),
        cost_estimate=cost(
            2 * rows * width * (width + 2 * inner), 2 * rows * (6 * width + 2 * inner)
        ),
        name="mlp_bwd",
    )(cot, out, side, pool, w_first, gain3, w_down, slope, w_up, mid, gain2, w_out)


def final_bwd_kernel(rows, pairs, *refs):
    pieces = [refs[i * pairs : (i + 1) * pairs] for i in range(5)]
    x_ref, branch_ref, gain, w_ref, grad_ref, sums_ref = refs[5 * pairs :]
    width = x_ref.shape[1]

    @pl.when(pl.program_id(0) == 0)
    def _():
        sums_ref[...] = jnp.zeros_like(sums_ref)

    inside = lax.broadcasted_iota(jnp.int32, (SMALL_TILE, 1), 0) < rows - pl.program_id(0) * SMALL_TILE

    def add(row, value):
        total = rows_sum(jnp.where(inside, value, 0.0))
        middle = total.shape[1] // 2
        below = sums_ref.shape[0] // 2 + row
        sums_ref[row : row + 1, :] += total[:, :middle]
        sums_ref[below : below + 1, :] += total[:, middle:]

    def join(part):
        return jnp.concatenate([r[...] for r in part], axis=1)

    def total(part, other):
        both = [a[...].astype(jnp.float32) + b[...].astype(jnp.float32) for a, b in zip(part, other)]
        return jnp.concatenate(both, axis=1).astype(jnp.bfloat16)

    dq = join(pieces[0])
    dk = total(pieces[1], pieces[2])
    dv = total(pieces[3], pieces[4])
    dn = (
        dot(dq, w_ref[:, :width], NT)
        + dot(dk, w_ref[:, width : 2 * width], NT)
        + dot(dv, w_ref[:, 2 * width :], NT)
    )
    xhat, rstd = ln_parts(x_ref[...].astype(jnp.float32))
    add(0, dn * xhat)
    add(1, dn)
    add(2, dq.astype(jnp.float32))
    add(3, dv.astype(jnp.float32))
    grad_ref[...] = (
        branch_ref[...].astype(jnp.float32) + ln_back(dn, line(gain), xhat, rstd)
    ).astype(jnp.bfloat16)


def final_bwd(pieces, x, branch, gain, w):
    rows, width = x.shape
    pairs = width // 128
    return pl.pallas_call(
        functools.partial(final_bwd_kernel, rows, pairs),
        out_shape=(low_shape(rows, width), jax.ShapeDtypeStruct((16, width // 2), jnp.float32)),
        grid=(-(-rows // SMALL_TILE),),
        in_specs=[
            pl.BlockSpec((SMALL_TILE, 128), functools.partial(lambda c, i: (i, c), column))
            for _, column in pieces
        ]
        + [small_spec(width)] * 2
        + [vector_spec(width), whole_spec(w.shape)],
        out_specs=[small_spec(width), pl.BlockSpec((16, width // 2), lambda i: (0, 0))],
        compiler_params=params(),
        cost_estimate=cost(6 * rows * width * width, 16 * rows * width),
        name="final_bwd",
    )(*[array for array, _ in pieces], x, branch, gain, w)


def grid_masks(frames, lanes):
    table = np.zeros((16, lanes), np.float32)
    lane = np.arange(lanes)
    pixel = lane % PIXELS
    i, j = pixel // GRID, pixel % GRID
    inside = lane < frames * PIXELS
    for a in range(3):
        for b in range(3):
            ok = (i + a - 1 >= 0) & (i + a - 1 < GRID) & (j + b - 1 >= 0) & (j + b - 1 < GRID)
            table[3 * a + b] = ok & inside
    table[9] = np.where(inside, lane // PIXELS, -1)
    return table


def learner_kernel(
    frames, info_ref, weight_ref, n3_ref, out_ref, pool_ref, wt_ref, cw_ref, cwt_ref, cb_ref,
    mask_ref, side_ref, pooled_ref, small_ref, keep_ref, send_ref, rounds, seqs,
):
    rows = n3_ref.shape[0]
    lanes = mask_ref.shape[1]
    extra = lanes - rows
    rank = info_ref[2 * frames + 1]
    frame_of = mask_ref[9:10, :]
    live = jnp.zeros((1, lanes), jnp.float32)
    for f in range(frames):
        kept = info_ref[rank * frames + f].astype(jnp.float32)
        live = live + jnp.where(frame_of == f, kept, 0.0)
    inside = (frame_of >= 0).astype(jnp.float32)

    def widen(x):
        return jnp.concatenate([x, jnp.zeros((x.shape[0], extra), jnp.float32)], axis=1)

    def turn(x, by):
        return x if by % lanes == 0 else pltpu.roll(x, by % lanes, 1)

    def gather_taps(taps):
        total = jnp.zeros((8, lanes), jnp.float32)
        for t in range(9):
            step = (t // 3 - 1) * GRID + t % 3 - 1
            total = total + turn(taps[8 * t : 8 * t + 8, :], -step) * mask_ref[t : t + 1, :]
        return total

    def spread_taps(level):
        parts = []
        for t in range(9):
            step = (t // 3 - 1) * GRID + t % 3 - 1
            parts.append(turn(level, step) * mask_ref[8 - t : 9 - t, :])
        return jnp.concatenate(parts, axis=0)

    def exact(a, b, dims=NN):
        return lax.dot_general(
            a, b, dims, precision=HIGHEST, preferred_element_type=jnp.float32
        )

    def area_of(x):
        return 0.5 + 0.5 * lax.erf(x * INV_SQRT2)

    taps = widen(dot(wt_ref[...], n3_ref[...], NT))
    levels = [gather_taps(taps) + cb_ref[:, 0:1]]
    hiddens = []
    for n in range(3):
        hiddens.append(levels[n] * area_of(levels[n]))
        levels.append(gather_taps(exact(cwt_ref[n], hiddens[n])) + cb_ref[:, n + 1 : n + 2])
    maps = 1.0 / (1.0 + jnp.exp(-levels[3]))
    total = rows_sum(maps)
    meet = 0.5 * (total * total - rows_sum(maps * maps)) * live
    small_ref[...] = jnp.zeros_like(small_ref)
    small_ref[8:9, 128:256] = jnp.zeros((1, 128), jnp.float32) + jnp.sum(meet)
    shifts = jnp.zeros((8, 128), jnp.float32)
    lane = lax.broadcasted_iota(jnp.int32, (8, 128), 1)

    owner = lax.broadcasted_iota(jnp.int32, (8 * frames, lanes), 0) // 8
    mine = owner.astype(jnp.float32) == frame_of
    low_maps = maps.astype(jnp.bfloat16).astype(jnp.float32) * live
    stacked = jnp.where(mine, jnp.concatenate([low_maps] * frames, axis=0), 0.0)
    out = out_ref[...]
    pooled_ref[...] = dot(stacked[:, :rows].astype(jnp.bfloat16), out).astype(jnp.bfloat16)
    pairs = jnp.where(mine, widen(dot(pool_ref[...], out, NT)), 0.0)
    d_maps = pairs[0:8]
    for f in range(1, frames):
        d_maps = d_maps + pairs[8 * f : 8 * f + 8]
    d_maps = d_maps * live + weight_ref[0] * live * (total - maps)
    d_level = d_maps * maps * (1.0 - maps)
    for n in (2, 1, 0):
        shifts = jnp.where(lane == n + 1, jnp.sum(d_level, axis=1, keepdims=True), shifts)
        d_taps = spread_taps(d_level)
        small_ref[0:8, 128 * n : 128 * n + 72] = exact(hiddens[n], d_taps, NT)
        d_hidden = exact(cw_ref[n], d_taps)
        x = levels[n]
        bell = jnp.exp(-0.5 * x * x) * INV_SQRT_2PI
        d_level = d_hidden * (area_of(x) + x * bell) * inside
    shifts = jnp.where(lane == 0, jnp.sum(d_level, axis=1, keepdims=True), shifts)
    small_ref[8:16, 0:8] = shifts.T[0:8, :]
    d_first = spread_taps(d_level)[:, :rows]
    grad = dot(d_first.astype(jnp.bfloat16), n3_ref[...])
    grad = jnp.concatenate([grad, jnp.zeros((56, grad.shape[1]), jnp.float32)], axis=0).T
    columns = 9 * MAPS // 2
    lane = lax.broadcasted_iota(jnp.int32, grad.shape, 1)
    left = jnp.where(lane < columns, grad, 0.0).astype(jnp.bfloat16)
    right = jnp.where(lane < columns, pltpu.roll(grad, 128 - columns, 1), 0.0).astype(jnp.bfloat16)
    size = grad.shape[0] // seqs // 3
    for ref, side in ((keep_ref, 0), (send_ref, 1)):
        value = jnp.where(rank == side, left, right)
        for o in range(seqs):
            parts = [value[(3 * o + t) * size : (3 * o + t + 1) * size, :] for t in range(3)]
            put_rows(ref, block_place(o, rounds) * size, jnp.concatenate(parts, axis=1))
    tall = jnp.concatenate(
        [
            d_first,
            jnp.zeros((56, rows), jnp.float32),
            stacked[:, :rows],
            jnp.zeros((128 - 8 * frames, rows), jnp.float32),
        ],
        axis=0,
    )
    side_ref[...] = tall.T.astype(jnp.bfloat16)


def learner(info, weight, n3, out, pool, w_first, conv_weights, conv_biases, rounds, seqs):
    rows, width = n3.shape
    frames = rows // PIXELS
    lanes = -(-rows // 128) * 128
    vm = pl.BlockSpec(memory_space=pltpu.VMEM)
    sm = pl.BlockSpec(memory_space=pltpu.SMEM)
    masks = jnp.asarray(grid_masks(frames, lanes))
    return pl.pallas_call(
        functools.partial(learner_kernel, frames, rounds=rounds, seqs=seqs),
        out_shape=(
            low_shape(rows, 256),
            low_shape(8 * frames, width),
            jax.ShapeDtypeStruct((16, PART), jnp.float32),
            low_shape(width // 3, PART),
            low_shape(width // 3, PART),
        ),
        in_specs=[sm, sm] + [vm] * 8,
        out_specs=(vm,) * 5,
        compiler_params=pltpu.CompilerParams(vmem_limit_bytes=VMEM_LIMIT),
        cost_estimate=cost(2e10, 4 * rows * width),
        name="learner",
    )(
        info, weight, n3, out, pool, w_first.T, conv_weights,
        conv_weights.transpose(0, 2, 1), conv_biases.T, masks,
    )


def flip(count, bit):
    return [(i, i ^ bit) for i in range(count)]


def low_sum(a, b):
    return (a.astype(jnp.float32) + b.astype(jnp.float32)).astype(jnp.bfloat16)


def block_place(owner, rounds):
    place = 0
    for bits in rounds:
        for bit in bits:
            place = place * 2 + ((owner >> bit) & 1)
    return place


def put_rows(ref, at, value):
    if not isinstance(at, int):
        at = pl.multiple_of(at, 16)
    ref[pl.ds(at, value.shape[0]), :] = value


def put_blocks(ref, value, first_owner, owners, rounds):
    size = value.shape[0] // owners
    for o in range(owners):
        place = block_place(first_owner + o, rounds)
        put_rows(ref, place * size, value[o * size : (o + 1) * size, :])


def grad_by_columns_kernel(rounds, seqs, info_ref, a_ref, b_ref, keep_ref, send_ref, turned):
    step = pl.program_id(0)
    half = pl.num_programs(0) // 2

    @pl.when(step == 0)
    def _():
        turned[...] = a_ref[...].T

    got = dot(turned[...], b_ref[...]).astype(jnp.bfloat16)
    parts = got.shape[1] // PART
    size = got.shape[0] // seqs

    def put(ref):
        for o in range(seqs):
            base = block_place(o, rounds) * size * parts * half
            for i in range(parts):
                at = base + (lax.rem(step, half) * parts + i) * size
                put_rows(ref, at, got[o * size : o * size + size, i * PART : i * PART + PART])

    @pl.when(step < half)
    def _():
        put(keep_ref)

    @pl.when(step >= half)
    def _():
        put(send_ref)


def grad_by_columns(info, a, b, rounds, seqs, at):
    rows, tall = a.shape
    wide = b.shape[1]
    block = min(768, wide // 2)
    half = wide // 2 // block
    out = jax.ShapeDtypeStruct((tall * wide // 2 // PART, PART), jnp.bfloat16)
    whole = pl.BlockSpec(out.shape, lambda j, info: (0, 0))
    return pl.pallas_call(
        functools.partial(grad_by_columns_kernel, rounds, seqs),
        out_shape=(out, out),
        grid_spec=pltpu.PrefetchScalarGridSpec(
            num_scalar_prefetch=1,
            grid=(2 * half,),
            in_specs=[
                pl.BlockSpec((rows, tall), lambda j, info: (0, 0)),
                pl.BlockSpec(
                    (rows, block),
                    lambda j, info: (0, jnp.where(j < half, info[at], 1 - info[at]) * half + j % half),
                ),
            ],
            out_specs=[whole, whole],
            scratch_shapes=[pltpu.VMEM((tall, rows), jnp.bfloat16)],
        ),
        compiler_params=params(),
        cost_estimate=cost(2 * rows * tall * wide, 2 * rows * (tall + wide)),
        name="grad_columns",
    )(info, a, b)


def pick_half(rank, value):
    middle = value.shape[1] // 2
    first, second = value[:, :middle], value[:, middle:]
    return jnp.where(rank == 0, first, second), jnp.where(rank == 0, second, first)


def grad_by_rows_kernel(rounds, seqs, at, info_ref, a_ref, b_ref, keep_ref, send_ref):
    step = pl.program_id(0)
    got = dot(a_ref[...], b_ref[...], TN).astype(jnp.bfloat16)
    keep, send = pick_half(info_ref[at], got)
    owners = seqs // (keep_ref.shape[0] // a_ref.shape[1])
    put_blocks(keep_ref, keep, step * owners, owners, rounds)
    put_blocks(send_ref, send, step * owners, owners, rounds)


def grad_by_rows(info, a, b, rounds, seqs, at):
    rows, tall = a.shape
    wide = b.shape[1]
    out = jax.ShapeDtypeStruct((tall, wide // 2), jnp.bfloat16)
    return pl.pallas_call(
        functools.partial(grad_by_rows_kernel, rounds, seqs, at),
        out_shape=(out, out),
        grid_spec=pltpu.PrefetchScalarGridSpec(
            num_scalar_prefetch=1,
            grid=(tall // 768,),
            in_specs=[
                pl.BlockSpec((rows, 768), lambda j, info: (0, j)),
                pl.BlockSpec((rows, wide), lambda j, info: (0, 0)),
            ],
            out_specs=[pl.BlockSpec((tall, wide // 2), lambda j, info: (0, 0))] * 2,
        ),
        compiler_params=params(),
        cost_estimate=cost(2 * rows * tall * wide, 2 * rows * (tall + wide)),
        name="grad_rows",
    )(info, a, b)


def grad_pieces_kernel(rounds, seqs, at, turn, info_ref, n_ref, *refs):
    (q0, k0, x0, v0, y0), (q1, k1, x1, v1, y1) = refs[:5], refs[5:10]
    if turn:
        keep_ref, send_ref, turned_ref = refs[-3:]
        turned_ref[...] = n_ref[...].T
    else:
        keep_ref, send_ref = refs[-2:]
        turned_ref = n_ref
    first = jnp.concatenate([q0[...], q1[...], low_sum(k0[...], x0[...])], axis=1)
    second = jnp.concatenate(
        [low_sum(k1[...], x1[...]), low_sum(v0[...], y0[...]), low_sum(v1[...], y1[...])], axis=1
    )
    both = jnp.concatenate([first, second], axis=1)
    got = dot(turned_ref[...], both).astype(jnp.bfloat16)
    keep, send = pick_half(info_ref[at], got)
    put_blocks(keep_ref, keep, 0, seqs, rounds)
    put_blocks(send_ref, send, 0, seqs, rounds)


def grad_pieces(info, n1, w_rows, pieces, rounds, seqs, at, after):
    turn = n1.shape[0] != w_rows
    rows, tall = n1.shape if turn else n1.shape[::-1]
    out = jax.ShapeDtypeStruct((tall, PART), jnp.bfloat16)
    flat = [piece for pair in pieces for piece in pair]
    whole = pl.BlockSpec((tall, PART), lambda i, info: (0, 0))
    return pl.pallas_call(
        functools.partial(grad_pieces_kernel, rounds, seqs, at, turn),
        out_shape=(out, out) + ((low_shape(tall, rows),) if turn else ()),
        grid_spec=pltpu.PrefetchScalarGridSpec(
            num_scalar_prefetch=1,
            grid=(1,),
            in_specs=[pl.BlockSpec(n1.shape, lambda i, info: (0, 0))]
            + [
                pl.BlockSpec((rows, 128), functools.partial(lambda c, i, info: (0, c), column))
                for _, column in flat
            ]
            + [pl.BlockSpec(memory_space=pl.ANY)] * len(after),
            out_specs=[whole, whole]
            + ([pl.BlockSpec((tall, rows), lambda i, info: (0, 0))] if turn else []),
        ),
        compiler_params=params(),
        cost_estimate=cost(2 * rows * tall * 768, 4 * rows * tall),
        name="grad_pieces",
    )(info, n1, *[array for array, _ in flat], *after)


class Stream:
    def __init__(self, rounds, keep, send, emit=None):
        self.rounds, self.at, self.keep, self.emit = rounds, 0, keep, emit
        self.gots = [(lax.ppermute(send, "frame", flip(2, 1)), 0)]

    def bits(self):
        return self.rounds[self.at] if self.at < len(self.rounds) else None


class Total(Stream):
    def __init__(self, rounds, value, emit):
        super().__init__(rounds, value, value, emit)


def split_low(value):
    high = value.astype(jnp.bfloat16)
    return high, (value - high.astype(jnp.float32)).astype(jnp.bfloat16)


def fold(info, at, bundles, after=(), emit=None):
    arrays, plan, outs = [], [], []

    def source(array):
        for i, known in enumerate(arrays):
            if known is array:
                return i
        arrays.append(array)
        return len(arrays) - 1

    for streams, sending in bundles:
        entry = []
        bits = streams[0].bits() if sending else None
        ways = 1 << len(bits) if bits else 1
        offset = 0
        for s in streams:
            parts = [(source(array), start) for array, start in s.gots]
            rows = s.keep.shape[0]
            entry.append((s, source(s.keep), parts, rows, offset))
            if isinstance(s, Total):
                kept = jax.ShapeDtypeStruct((rows, PART), jnp.float32)
                offset += 2 * rows
            else:
                kept = jax.ShapeDtypeStruct((rows // ways, PART), jnp.bfloat16)
                offset += rows // ways
            if sending:
                outs.append(kept)
            elif s.emit:
                outs += s.emit[0]
            elif not emit:
                outs.append(kept)
        outs += [jax.ShapeDtypeStruct((offset, PART), jnp.bfloat16)] * (ways - 1)
        plan.append((entry, bits, ways))
    if emit:
        outs += emit[0]

    def kernel(info_ref, *refs):
        sources, targets = refs[: len(arrays)], list(refs[len(arrays) + len(after) :])
        index = info_ref[at]
        ready = []
        for entry, bits, ways in plan:
            mine = 0
            for bit in bits or ():
                mine = mine * 2 + ((index >> bit) & 1)
            kept = []
            for s, own, parts, rows, offset in entry:
                size = rows // ways
                if bits:
                    kept.append(targets.pop(0))
                elif s.emit or not emit:
                    count = len(s.emit[0]) if s.emit else 1
                    kept.append([targets.pop(0) for _ in range(count)])
                else:
                    kept.append(None)
            sends = [targets.pop(0) for _ in range(ways - 1)]
            for (s, own, parts, rows, offset), keep in zip(entry, kept):

                def total(start, size):
                    value = sources[own][pl.ds(start, size), :].astype(jnp.float32)
                    for i, begin in parts:
                        if isinstance(s, Total):
                            if sources[i].dtype == jnp.float32:
                                value = value + sources[i][...]
                            else:
                                value = value + sources[i][begin : begin + rows, :].astype(jnp.float32)
                                value = value + sources[i][
                                    begin + rows : begin + 2 * rows, :
                                ].astype(jnp.float32)
                        else:
                            value = value + sources[i][pl.ds(begin + start, size), :].astype(jnp.float32)
                    return value

                if bits and isinstance(s, Total):
                    value = total(0, rows)
                    keep[...] = value
                    high, low = split_low(value)
                    for send in sends:
                        send[offset : offset + rows, :] = high
                        send[offset + rows : offset + 2 * rows, :] = low
                elif bits:
                    size = rows // ways
                    for m in range(ways):
                        start = pl.multiple_of((mine ^ m) * size, 16)
                        value = total(start, size).astype(jnp.bfloat16)
                        if m == 0:
                            keep[...] = value
                        else:
                            sends[m - 1][offset : offset + size, :] = value
                elif keep is None:
                    ready.append(total(0, rows))
                elif s.emit:
                    s.emit[1](total(0, rows), *keep)
                else:
                    keep[0][...] = total(0, rows).astype(keep[0].dtype)
        if emit:
            emit[1](ready, *targets)

    vm = pl.BlockSpec(memory_space=pltpu.VMEM)
    sm = pl.BlockSpec(memory_space=pltpu.SMEM)
    moved = sum(x.size * x.dtype.itemsize for x in arrays) * 2
    results = list(
        pl.pallas_call(
            kernel,
            out_shape=tuple(outs),
            in_specs=[sm] + [vm] * len(arrays) + [pl.BlockSpec(memory_space=pl.ANY)] * len(after),
            out_specs=(vm,) * len(outs),
            compiler_params=pltpu.CompilerParams(vmem_limit_bytes=VMEM_LIMIT),
            cost_estimate=cost(0, moved),
            name="fold",
        )(info, *arrays, *after)
    )
    sent = []
    count = lax.axis_size("seq")
    for entry, bits, ways in plan:
        for s, *_ in entry:
            if bits:
                s.keep = results.pop(0)
            elif s.emit:
                s.result = [results.pop(0) for _ in s.emit[0]]
            elif not emit:
                s.keep = results.pop(0)
            s.gots = []
        for m in range(1, ways):
            mask = 0
            for i, bit in enumerate(bits):
                mask |= ((m >> (len(bits) - 1 - i)) & 1) << bit
            send = results.pop(0)
            sent.append(send)
            got = lax.ppermute(send, "seq", flip(count, mask))
            for s, _, _, _, offset in entry:
                s.gots.append((got, offset))
        if bits:
            for s, *_ in entry:
                s.at += 1
    return sent[:1], results


def add_all(value, bits, after):
    count = lax.axis_size("seq")
    gots = []
    for m in range(1, 1 << len(bits)):
        mask = sum(((m >> i) & 1) << bit for i, bit in enumerate(bits))
        gots.append(lax.ppermute(value, "seq", flip(count, mask)))

    def kernel(*refs):
        total = refs[0][...]
        for ref in refs[1 : 1 + len(gots)]:
            total = total + ref[...]
        refs[-1][...] = total

    vm = pl.BlockSpec(memory_space=pltpu.VMEM)
    return pl.pallas_call(
        kernel,
        out_shape=jax.ShapeDtypeStruct(value.shape, jnp.float32),
        in_specs=[vm] * (1 + len(gots)) + [pl.BlockSpec(memory_space=pl.ANY)] * len(after),
        out_specs=vm,
        name="add_all",
    )(value, *gots, *after)


def doubles(bits):
    low = list(range(bits))
    return [low[i : i + 2] for i in range(0, bits, 2)]


def f32_shape(*shape):
    return jax.ShapeDtypeStruct(shape, jnp.float32)


def write_plain(value, ref):
    ref[...] = value


def write_wide(value, ref):
    size = ref.shape[0]
    for i in range(value.shape[0] // size):
        ref[:, i * PART : i * PART + PART] = value[i * size : i * size + size, :]


def write_first(value, ref):
    for i in range(3):
        ref[16 * i : 16 * i + 16, :] = value[:, 128 * i : 128 * i + ref.shape[1]]


def write_vectors(value, *refs):
    row = 0
    for ref in refs:
        for i in range(ref.shape[0] // (2 * PART)):
            ref[2 * PART * i : 2 * PART * i + PART] = value[row, :]
            ref[2 * PART * i + PART : 2 * PART * (i + 1)] = value[value.shape[0] // 2 + row, :]
            row += 1


def write_small(value, weights_ref, biases_ref, meet_ref):
    for n in range(3):
        weights_ref[n] = value[0:8, 128 * n : 128 * n + 9 * MAPS]
    biases_ref[...] = value[8:12, 0:MAPS]
    meet_ref[...] = value[8:9, 128:129]


def write_groups(values, ref):
    count = len(values)
    for i in range(3):
        for g, value in enumerate(values):
            at = 128 * (i * count + g)
            ref[:, at : at + 128] = value[:, 128 * i : 128 * i + 128]


def quick_device(
    tokens, ln_gain_first, ln_bias_first, w_qkv, q_bias, v_bias, w_out, out_bias, ln_gain_second,
    ln_bias_second, w_up, up_bias, w_down, down_bias, ln_gain_third, ln_bias_third, w_first,
    conv_weights, conv_biases, clip_lengths, frame_mask, out_cot, pool_cot, penalty_scale,
):
    _, rows, width = tokens.shape
    frames = rows // PIXELS
    inner = w_up.shape[1]
    seqs = lax.axis_size("seq")
    rank = lax.axis_index("frame")
    bits = seqs.bit_length() - 1
    near = doubles(bits)
    far = [[bit] for pair in near[1:] for bit in pair] + near[:1]
    rank_at, seq_at = 2 * frames + 1, 2 * frames + 2

    def swap(x):
        return lax.ppermute(x, "frame", flip(2, 1))

    place = jnp.stack([rank, lax.axis_index("seq")]).astype(jnp.int32)
    info = jnp.concatenate([frame_mask[0], clip_lengths[0, 0:1], place])
    x = tokens[0]
    n1, k0, v0 = project(x, ln_gain_first, ln_bias_first, w_qkv, v_bias)
    far_k0, far_v0 = swap(k0), swap(v0)
    q, k1, v1 = project_more(n1, w_qkv, q_bias, v_bias)
    far_k1, far_v1 = swap(k1), swap(v1)
    count = jnp.sum(frame_mask).astype(jnp.float32) * jnp.ones((1, 128))
    count = add_all(count, near[0], (n1,))
    half = attn_fwd(info, q, k0, v0, far_k0, far_v0, (), 0, frames)
    for pair in near[1:]:
        count = add_all(count, pair, (half[0],))
    attended, lse, kc, vc = attn_fwd(info, q, k1, v1, far_k1, far_v1, tuple(half), 1, frames)
    count = count[0, 0]
    weight = (penalty_scale / count).reshape(1)
    mid, n2, hidden, slope, out, n3 = mlp_fwd(
        x, attended, w_out, out_bias, ln_gain_second, ln_bias_second, w_up, up_bias, w_down,
        down_bias, ln_gain_third, ln_bias_third,
    )
    side, pooled, small, first_keep, first_send = learner(
        info, weight, n3, out, pool_cot[0], w_first, conv_weights, conv_biases, near, seqs
    )
    first_pad = jnp.concatenate(
        [w_first.T, jnp.zeros((128 - 9 * MAPS, width), jnp.bfloat16)], axis=0
    )
    d_down, d_up, d_branch, d_att, sums = mlp_bwd(
        out_cot[0], out, side, pool_cot[0], first_pad, ln_gain_third, w_down, slope, w_up, mid,
        ln_gain_second, w_out,
    )
    first = Stream(
        near, first_keep, first_send, ([f32_shape(width // seqs, 9 * MAPS // 2)], write_first)
    )
    meet = Total(
        near,
        small,
        ([f32_shape(3, MAPS, 9 * MAPS), f32_shape(4, MAPS), f32_shape(1, 1)], write_small),
    )
    vectors = Total(
        near, sums, ([f32_shape(width)] * 6 + [f32_shape(inner)], write_vectors)
    )
    down = Stream(
        far,
        *grad_by_rows(info, hidden, d_down, far, seqs, rank_at),
        ([f32_shape(inner // seqs, PART)], write_plain),
    )
    up = Stream(
        near,
        *grad_by_columns(info, n2, d_up, near, seqs, rank_at),
        ([f32_shape(width // seqs, inner // 2)], write_wide),
    )
    branch = Stream(
        near,
        *grad_by_rows(info, attended, d_branch, near, seqs, rank_at),
        ([f32_shape(width // seqs, PART)], write_plain),
    )
    early = [up, branch, first, vectors, meet]
    pairs = width // 128
    groups = pairs // 2
    pieces = {}

    def attend_back(which, after):
        dq, own_k, own_v, away = attn_bwd(
            info, q, kc, vc, attended, d_att, lse, which, frames, after
        )
        away = swap(away)
        for i, pair in enumerate(which):
            pieces[pair] = [(dq, i), (own_k, i), (away, 2 * i), (own_v, i), (away, 2 * i + 1)]
        return dq

    def group_stream(g, after):
        both = (pieces[g], pieces[g + groups])
        grads = grad_pieces(info, normed[-1], width, both, near, seqs, rank_at, after)
        normed.extend(grads[2:])
        return Stream(near, *grads[:2]), [grads[1]]

    streams = []
    normed = [n1]
    after, _ = fold(info, seq_at, [(early, True), ([down], True)])
    last = attend_back((0, groups), after)
    after, _ = fold(info, seq_at, [(early, True), ([down], True)], (last,))
    last = attend_back((1, 1 + groups), after)
    after, _ = fold(info, seq_at, [(early, False), ([down], True)], (last,))
    stream, sent = group_stream(0, after)
    streams.append(stream)
    last = attend_back((2,), after + sent)
    fold(info, seq_at, [([down], False)], (last,))
    stream, after = group_stream(1, (last,))
    streams.append(stream)
    last = attend_back((2 + groups,), after + down.result)
    after, _ = fold(info, seq_at, [(streams[:2], True)], (last,))
    stream, _ = group_stream(2, after)
    streams.append(stream)
    tokens_grad, late = final_bwd(
        [pieces[p][i] for i in range(5) for p in range(pairs)], x, d_branch, ln_gain_first, w_qkv
    )
    late = Total(near, late, ([f32_shape(width)] * 4, write_vectors))
    while streams[2].at < streams[0].at:
        bundles = [([streams[2], late], True)]
        if streams[0].gots:
            bundles.append((streams[:2], False))
        fold(info, seq_at, bundles)
    while late.bits():
        fold(info, seq_at, [(streams + [late], True)])
    results = fold(
        info, seq_at, [(streams, False), ([late], False)],
        emit=([f32_shape(width // seqs, 3 * width // 2)], write_groups),
    )[1]
    vectors, late = vectors.result, late.result
    conv_w, conv_b, total = meet.result
    return (
        out[None],
        pooled[None],
        total[0, 0] / count,
        tokens_grad[None],
        late[0],
        late[1],
        results[0],
        late[2],
        late[3],
        branch.result[0],
        vectors[5],
        vectors[0],
        vectors[1],
        up.result[0],
        vectors[6],
        down.result[0],
        vectors[4],
        vectors[2],
        vectors[3],
        first.result[0],
        conv_w,
        conv_b,
    )


def per_device(*arrays):
    tokens, clip_lengths = arrays[0], arrays[19]
    frames = tokens.shape[1] // PIXELS
    seqs = lax.axis_size("seq")
    fits = (
        tokens.shape[0] == 1
        and lax.axis_size("frame") == 2
        and frames % 4 == 0
        and tokens.shape[1] % 32 == 0
        and tokens.shape[2] == HEADS * HEAD_DIM
        and seqs == 16
    )
    return (quick_device if fits else plain_device)(*arrays)


def solution(mesh):
    return jax.shard_map(
        per_device,
        mesh=mesh,
        in_specs=(
            P("seq", "frame", None),
            P(),
            P(),
            P(),
            P(),
            P(),
            P(),
            P(),
            P(),
            P(),
            P(),
            P(),
            P(),
            P(),
            P(),
            P(),
            P(),
            P(),
            P(),
            P("seq", None),
            P("seq", None),
            P("seq", "frame", None),
            P("seq", "frame", None),
            P(),
        ),
        out_specs=(
            P("seq", "frame", None),
            P("seq", "frame", None),
            P(),
            P("seq", "frame", None),
            P(),
            P(),
            P("seq", "frame"),
            P(),
            P(),
            P("seq", "frame"),
            P(),
            P(),
            P(),
            P("seq", "frame"),
            P(),
            P("seq", "frame"),
            P(),
            P(),
            P(),
            P("seq", "frame"),
            P(),
            P(),
        ),
        check_vma=False,
    )
```

```python
import functools

import jax
import jax.numpy as jnp
import numpy as np
from jax import lax
from jax.experimental import pallas as pl
from jax.experimental.pallas import tpu as pltpu
from jax.sharding import PartitionSpec as P

HEADS = 12
HEAD_DIM = 64
GRID = 14
MAPS = 8


EPS = 1e-06
NEG = -1e30
HIGHEST = lax.Precision.HIGHEST


def norm_rows(rows, gain, shift):
    center = rows - jnp.mean(rows, axis=-1, keepdims=True)
    spread = jnp.mean(center * center, axis=-1, keepdims=True)
    return center * lax.rsqrt(spread + EPS) * gain + shift


def shift_sum(taps):
    padded = jnp.pad(taps, ((0, 0), (1, 1), (1, 1), (0, 0), (0, 0)))
    total = padded[:, 0:GRID, 0:GRID, 0, :]
    for tap in range(1, 9):
        total = total + padded[:, tap // 3 : tap // 3 + GRID, tap % 3 : tap % 3 + GRID, tap, :]
    return total


def conv_tail(first, conv_biases, conv_weights):
    frames = first.shape[0]
    level = shift_sum(first.reshape(frames, GRID, GRID, 9, MAPS)) + conv_biases[0]
    for layer in range(3):
        hidden = jax.nn.gelu(level, approximate=False)
        taps = jnp.einsum("fijc,ck->fijk", hidden, conv_weights[layer], precision=HIGHEST)
        level = shift_sum(taps.reshape(frames, GRID, GRID, 9, MAPS)) + conv_biases[layer + 1]
    return jax.nn.sigmoid(level).reshape(frames, GRID * GRID, MAPS)


def exact_gelu(values):
    return jax.nn.gelu(values, approximate=False)


def pair_mask(query_code, key_code):
    return (query_code[:, :, None] == key_code[:, None, :])[:, None]


def score_rows(query_rows, key_rows):
    return jnp.einsum(
        "sqhe,skhe->shqk", query_rows, key_rows, preferred_element_type=jnp.float32
    ) * HEAD_DIM ** (-0.5)


def pair_terms(query_rows, dout_rows, lse_rows, delta_rows, key_rows, value_rows, allowed):
    scores = score_rows(query_rows, key_rows)
    probs = jnp.where(allowed, jnp.exp(scores - lse_rows[..., None]), 0.0)
    slopes = jnp.einsum(
        "sqhe,skhe->shqk", dout_rows, value_rows, preferred_element_type=jnp.float32
    )
    grads = (probs * (slopes - delta_rows[..., None])).astype(jnp.bfloat16)
    return (probs.astype(jnp.bfloat16), grads)


def column_sum(values):
    return jnp.sum(values.astype(jnp.float32), axis=0)


def plain_device(
    tokens,
    ln_gain_first,
    ln_bias_first,
    w_qkv,
    q_bias,
    v_bias,
    w_out,
    out_bias,
    ln_gain_second,
    ln_bias_second,
    w_up,
    up_bias,
    w_down,
    down_bias,
    ln_gain_third,
    ln_bias_third,
    w_first,
    conv_weights,
    conv_biases,
    clip_lengths,
    frame_mask,
    out_cot,
    pool_cot,
    penalty_scale,
):
    seq_count, local, width = tokens.shape
    pixels = GRID * GRID
    frames_here = local // pixels
    frame_total = lax.axis_size("frame")
    frame_rank = lax.axis_index("frame")
    slot_frames = frames_here * frame_total
    length = local * frame_total
    rows = seq_count * local
    image_count = seq_count * frames_here
    scale = HEAD_DIM ** (-0.5)
    positions = jnp.arange(slot_frames, dtype=jnp.int32)[None, :]
    segment_frames = (positions >= clip_lengths[:, 0:1]).astype(jnp.int32)
    key_frames = jnp.where(frame_mask > 0, segment_frames, -1)
    first_frame = frame_rank * frames_here
    query_code = jnp.repeat(
        lax.dynamic_slice_in_dim(segment_frames, first_frame, frames_here, 1), pixels, axis=1
    )
    key_code = jnp.repeat(key_frames, pixels, axis=1)
    valid_here = (
        lax.dynamic_slice_in_dim(frame_mask, first_frame, frames_here, 1)
        .reshape(image_count)
        .astype(jnp.float32)
    )
    flat = tokens.reshape(rows, width).astype(jnp.float32)
    normed_one, back_one = jax.vjp(norm_rows, flat, ln_gain_first, ln_bias_first)
    normed_one = normed_one.astype(jnp.bfloat16)
    qkv_bias = jnp.concatenate([q_bias, jnp.zeros_like(q_bias), v_bias])
    qkv = (jnp.dot(normed_one, w_qkv, preferred_element_type=jnp.float32) + qkv_bias).astype(
        jnp.bfloat16
    )
    qkv = qkv.reshape(seq_count, local, 3, HEADS, HEAD_DIM)
    queries = qkv[:, :, 0]
    keys_here = qkv[:, :, 1]
    values_here = qkv[:, :, 2]
    keys_all, values_all = (
        lax.all_gather(keys_here, "frame", axis=1, tiled=True),
        lax.all_gather(values_here, "frame", axis=1, tiled=True),
    )

    def block_of(array, index):
        return lax.dynamic_slice_in_dim(array, index * local, local, 1)

    def stats_turn(index, carry):
        allowed = pair_mask(query_code, block_of(key_code, index))

        def stats_update(state):
            top, mass = state
            masked = jnp.where(allowed, score_rows(queries, block_of(keys_all, index)), NEG)
            new_top = jnp.maximum(top, jnp.max(masked, axis=-1))
            kept = jnp.where(allowed, jnp.exp(masked - new_top[..., None]), 0.0)
            return (new_top, mass * jnp.exp(top - new_top) + jnp.sum(kept, axis=-1))

        return lax.cond(jnp.any(allowed), stats_update, lambda state: state, carry)

    start_top = jnp.full((seq_count, HEADS, local), NEG, jnp.float32)
    top, mass = lax.fori_loop(0, frame_total, stats_turn, (start_top, jnp.zeros_like(start_top)))
    lse = top + jnp.log(mass)

    def value_turn(index, total):
        allowed = pair_mask(query_code, block_of(key_code, index))

        def value_update(state):
            scores = score_rows(queries, block_of(keys_all, index))
            probs = jnp.where(allowed, jnp.exp(scores - lse[..., None]), 0.0).astype(jnp.bfloat16)
            return state + jnp.einsum(
                "shqk,skhe->sqhe",
                probs,
                block_of(values_all, index),
                preferred_element_type=jnp.float32,
            )

        return lax.cond(jnp.any(allowed), value_update, lambda state: state, total)

    attended = lax.fori_loop(0, frame_total, value_turn, jnp.zeros(queries.shape, jnp.float32))
    attended_low = attended.astype(jnp.bfloat16).reshape(rows, width)
    middle = flat + jnp.dot(attended_low, w_out, preferred_element_type=jnp.float32) + out_bias
    normed_two, back_two = jax.vjp(norm_rows, middle, ln_gain_second, ln_bias_second)
    normed_two = normed_two.astype(jnp.bfloat16)
    upper = jnp.dot(normed_two, w_up, preferred_element_type=jnp.float32) + up_bias
    hidden, gelu_back = jax.vjp(exact_gelu, upper)
    hidden = hidden.astype(jnp.bfloat16)
    output = middle + jnp.dot(hidden, w_down, preferred_element_type=jnp.float32) + down_bias
    output_low = output.astype(jnp.bfloat16)
    normed_three, back_three = jax.vjp(norm_rows, output, ln_gain_third, ln_bias_third)
    normed_three = normed_three.astype(jnp.bfloat16)
    first = jnp.dot(normed_three, w_first, preferred_element_type=jnp.float32)
    maps, tail_back = jax.vjp(
        conv_tail, first.reshape(image_count, pixels, 9 * MAPS), conv_biases, conv_weights
    )
    maps_low = maps.astype(jnp.bfloat16)
    output_frames = output_low.reshape(image_count, pixels, width)
    pooled = (
        jnp.einsum("fpm,fpd->fmd", maps_low, output_frames, preferred_element_type=jnp.float32)
        * valid_here[:, None, None]
    )
    pooled_tokens = pooled.astype(jnp.bfloat16).reshape(seq_count, frames_here * MAPS, width)
    total_map = jnp.sum(maps, axis=-1)
    intersection = 0.5 * (total_map * total_map - jnp.sum(maps * maps, axis=-1))
    intersection_local = jnp.sum(intersection * valid_here[:, None])
    count_local = jnp.sum(valid_here)
    intersection_total, count_total = lax.psum((intersection_local, count_local), ("seq", "frame"))
    penalty = intersection_total / count_total
    pool_frames = pool_cot.reshape(image_count, MAPS, width)
    weight_cot = penalty_scale / count_total
    d_maps = (
        jnp.einsum("fmd,fpd->fpm", pool_frames, output_frames, preferred_element_type=jnp.float32)
        * valid_here[:, None, None]
    )
    d_maps = d_maps + (weight_cot * valid_here)[:, None, None] * (total_map[..., None] - maps)
    d_first, d_conv_biases, d_conv_weights = tail_back(d_maps)
    d_first = d_first.reshape(rows, 9 * MAPS).astype(jnp.bfloat16)
    grad_w_first = jnp.dot(normed_three.T, d_first, preferred_element_type=jnp.float32)
    d_normed_three = jnp.dot(d_first, w_first.T, preferred_element_type=jnp.float32)
    d_from_three, d_gain_three, d_bias_three = back_three(d_normed_three)
    d_pool_rows = (
        jnp.einsum("fpm,fmd->fpd", maps_low, pool_frames, preferred_element_type=jnp.float32)
        * valid_here[:, None, None]
    )
    d_output = (
        out_cot.reshape(rows, width).astype(jnp.float32)
        + d_from_three
        + d_pool_rows.reshape(rows, width)
    )
    d_down = d_output.astype(jnp.bfloat16)
    grad_w_down = jnp.dot(hidden.T, d_down, preferred_element_type=jnp.float32)
    grad_down_bias = column_sum(d_down)
    d_hidden = jnp.dot(d_down, w_down.T, preferred_element_type=jnp.float32)
    d_upper = gelu_back(d_hidden)[0].astype(jnp.bfloat16)
    grad_w_up = jnp.dot(normed_two.T, d_upper, preferred_element_type=jnp.float32)
    grad_up_bias = column_sum(d_upper)
    d_normed_two = jnp.dot(d_upper, w_up.T, preferred_element_type=jnp.float32)
    d_from_two, d_gain_two, d_bias_two = back_two(d_normed_two)
    d_middle = d_output + d_from_two
    d_branch = d_middle.astype(jnp.bfloat16)
    grad_w_out = jnp.dot(attended_low.T, d_branch, preferred_element_type=jnp.float32)
    grad_out_bias = column_sum(d_branch)
    dout_low = jnp.dot(d_branch, w_out.T, preferred_element_type=jnp.float32).astype(jnp.bfloat16)
    dout_low = dout_low.reshape(seq_count, local, HEADS, HEAD_DIM)
    delta = jnp.sum(dout_low.astype(jnp.float32) * attended, axis=-1).transpose(0, 2, 1)
    zeros_here = jnp.zeros(queries.shape, jnp.float32)
    full_zeros = jnp.zeros((seq_count, length, HEADS, HEAD_DIM), jnp.float32)

    def both_turn(index, carry):
        allowed = pair_mask(query_code, block_of(key_code, index))

        def both_update(state):
            grad_q, grad_k, grad_v = state
            key_rows = block_of(keys_all, index)
            probs, grads = pair_terms(
                queries, dout_low, lse, delta, key_rows, block_of(values_all, index), allowed
            )
            grad_q = (
                grad_q
                + jnp.einsum("shqk,skhe->sqhe", grads, key_rows, preferred_element_type=jnp.float32)
                * scale
            )
            part_k = (
                jnp.einsum("shqk,sqhe->skhe", grads, queries, preferred_element_type=jnp.float32)
                * scale
            )
            part_v = jnp.einsum(
                "shqk,sqhe->skhe", probs, dout_low, preferred_element_type=jnp.float32
            )
            grad_k = lax.dynamic_update_slice_in_dim(grad_k, part_k, index * local, 1)
            grad_v = lax.dynamic_update_slice_in_dim(grad_v, part_v, index * local, 1)
            return (grad_q, grad_k, grad_v)

        return lax.cond(jnp.any(allowed), both_update, lambda state: state, carry)

    grad_q, grad_k_all, grad_v_all = lax.fori_loop(
        0, frame_total, both_turn, (zeros_here, full_zeros, full_zeros)
    )
    grad_k, grad_v = (
        lax.psum_scatter(
            grad_k_all.astype(jnp.bfloat16), "frame", scatter_dimension=1, tiled=True
        ).astype(jnp.float32),
        lax.psum_scatter(
            grad_v_all.astype(jnp.bfloat16), "frame", scatter_dimension=1, tiled=True
        ).astype(jnp.float32),
    )
    grad_qkv = (
        jnp.stack([grad_q, grad_k, grad_v], axis=2).astype(jnp.bfloat16).reshape(rows, 3 * width)
    )
    grad_w_qkv = jnp.dot(normed_one.T, grad_qkv, preferred_element_type=jnp.float32)
    grad_q_bias = column_sum(grad_qkv[:, :width])
    grad_v_bias = column_sum(grad_qkv[:, 2 * width :])
    d_normed_one = jnp.dot(grad_qkv, w_qkv.T, preferred_element_type=jnp.float32)
    d_from_one, d_gain_one, d_bias_one = back_one(d_normed_one)
    tokens_grad = (d_middle + d_from_one).astype(jnp.bfloat16).reshape(seq_count, local, width)
    summed = (
        lax.psum_scatter(
            grad_w_qkv.astype(jnp.bfloat16), "seq", scatter_dimension=0, tiled=True
        ).astype(jnp.float32),
        lax.psum_scatter(
            grad_w_out.astype(jnp.bfloat16), "seq", scatter_dimension=0, tiled=True
        ).astype(jnp.float32),
        lax.psum_scatter(
            grad_w_up.astype(jnp.bfloat16), "seq", scatter_dimension=0, tiled=True
        ).astype(jnp.float32),
        lax.psum_scatter(
            grad_w_down.astype(jnp.bfloat16), "seq", scatter_dimension=0, tiled=True
        ).astype(jnp.float32),
        lax.psum_scatter(
            grad_w_first.astype(jnp.bfloat16), "seq", scatter_dimension=0, tiled=True
        ).astype(jnp.float32),
    )
    grad_w_qkv, grad_w_out, grad_w_up, grad_w_down, grad_w_first = (
        lax.psum_scatter(
            summed[0].astype(jnp.bfloat16), "frame", scatter_dimension=1, tiled=True
        ).astype(jnp.float32),
        lax.psum_scatter(
            summed[1].astype(jnp.bfloat16), "frame", scatter_dimension=1, tiled=True
        ).astype(jnp.float32),
        lax.psum_scatter(
            summed[2].astype(jnp.bfloat16), "frame", scatter_dimension=1, tiled=True
        ).astype(jnp.float32),
        lax.psum_scatter(
            summed[3].astype(jnp.bfloat16), "frame", scatter_dimension=1, tiled=True
        ).astype(jnp.float32),
        lax.psum_scatter(
            summed[4].astype(jnp.bfloat16), "frame", scatter_dimension=1, tiled=True
        ).astype(jnp.float32),
    )
    small = lax.psum(
        (
            d_gain_one,
            d_bias_one,
            d_gain_two,
            d_bias_two,
            d_gain_three,
            d_bias_three,
            grad_q_bias,
            grad_v_bias,
            grad_out_bias,
            grad_up_bias,
            grad_down_bias,
            d_conv_weights,
            d_conv_biases,
        ),
        ("seq", "frame"),
    )
    block_output = output_low.reshape(seq_count, local, width)
    return (
        block_output,
        pooled_tokens,
        penalty,
        tokens_grad,
        small[0],
        small[1],
        grad_w_qkv,
        small[6],
        small[7],
        grad_w_out,
        small[8],
        small[2],
        small[3],
        grad_w_up,
        small[9],
        grad_w_down,
        small[10],
        small[4],
        small[5],
        grad_w_first,
        small[11],
        small[12],
    )

FAR = -3e30
LOG2E = 1.4426950408889634
LN2 = 0.6931471805599453
NN = (((1,), (0,)), ((), ()))
NT = (((1,), (1,)), ((), ()))
TN = (((0,), (0,)), ((), ()))
PIXELS = 196
UNIT = 256
VMEM_LIMIT = 40 * 1024 * 1024
WIDE_LIMIT = 60 * 1024 * 1024


def dot(a, b, dims=NN):
    return lax.dot_general(a, b, dims, preferred_element_type=jnp.float32)


def compact_rows(frame_total):
    return (-(-frame_total * PIXELS // UNIT) + 3) * UNIT


def key_places(frames_here, info_ref):
    total = 2 * frames_here
    length = info_ref[total]
    count = [jnp.int32(0), jnp.int32(0)]
    places = []
    for f in range(total):
        kept = info_ref[f]
        late = (f >= length).astype(jnp.int32)
        places.append((kept, late, jnp.where(late == 1, count[1], count[0])))
        count[0] = count[0] + kept * (1 - late)
        count[1] = count[1] + kept * late
    units = [(c * PIXELS + UNIT - 1) // UNIT for c in count]
    start = units[0] * UNIT
    starts = [
        (kept, pl.multiple_of(jnp.where(late == 1, start, 0) + place * PIXELS, 4))
        for kept, late, place in places
    ]
    tails = [pl.multiple_of(count[0] * PIXELS, 4), pl.multiple_of(start + count[1] * PIXELS, 4)]
    return starts, tails, units[0], units[0] + units[1]


def clip_edge(frames_here, info_ref):
    total = 2 * frames_here
    first = info_ref[total + 1] * frames_here
    return jnp.clip((info_ref[total] - first) * PIXELS, 0, frames_here * PIXELS)


def gather_keys(frames_here, info_ref, starts, tails, own_k, own_v, far_k, far_v, kf, vf):
    total = 2 * frames_here
    rank = info_ref[total + 1]
    width = own_k.shape[1]
    for tail in tails:
        for ref in (kf, vf):
            ref[pl.ds(tail, UNIT), :] = jnp.zeros((UNIT, width), jnp.float32)
    for f in range(total):
        kept, place = starts[f]
        side = f // frames_here
        at = f % frames_here * PIXELS
        base = at // 16 * 16

        def put(k_ref, v_ref):
            for src, dst in ((k_ref, kf), (v_ref, vf)):
                block = src[base : base + 208, :].astype(jnp.float32)
                dst[pl.ds(place, PIXELS), :] = block[at - base : at - base + PIXELS, :]

        @pl.when((kept == 1) & (rank == side))
        def _():
            put(own_k, own_v)

        @pl.when((kept == 1) & (rank != side))
        def _():
            put(far_k, far_v)


def real_keys(start, size, split, tails, axis, shape):
    at = lax.broadcasted_iota(jnp.int32, shape, axis) + start
    return at < jnp.where(at >= split * UNIT, tails[1], tails[0])


def query_tiles(rows):
    parts = rows // 512
    return [(i * 512, 512) for i in range(parts)], (parts * 512, rows - parts * 512)


def split_heads(rows):
    lane = lax.broadcasted_iota(jnp.int32, rows.shape, 1)
    zero = jnp.zeros_like(rows)
    return jnp.where(lane < 64, rows, zero), jnp.where(lane < 64, zero, rows)


def clip_bias(late, edge, at, size):
    column = lax.broadcasted_iota(jnp.int32, (1, size), 1) + at
    return jnp.where((column >= edge) == late, 0.0, FAR)


def sweep(first, end, sizes, body):
    count = end - first
    big = sizes[0]
    main = count // big

    def step(c, carry):
        body(pl.multiple_of((first + c * big) * UNIT, UNIT), big * UNIT)
        return carry

    lax.fori_loop(0, main, step, 0)
    at = first + main * big
    left = count - main * big
    for size in sizes[1:]:

        @pl.when((left & size) != 0)
        def _():
            body(pl.multiple_of(at * UNIT, UNIT), size * UNIT)

        at = at + (left & size)


def attn_fwd_kernel(
    frames_here, first_pair, info_ref, q_ref, own_k, own_v, far_k, far_v, o_ref, inv_ref, kc_ref,
    vc_ref, probs_ref, qm, qr, vt, acc, accr, top, kf, vf, big, middle, small, sems, flags,
):
    rows = q_ref.shape[0]
    pair = first_pair + pl.program_id(0)

    @pl.when(pl.program_id(0) == 0)
    def _():
        for i in range(5):
            flags[i] = 0

    def copy_out(slot, buffer, start, size):
        return pltpu.make_async_copy(
            buffer, probs_ref.at[pair, :, pl.ds(start, size), :], sems.at[slot]
        )

    def settle(slot, buffer, size):
        @pl.when(flags[slot] == size // UNIT)
        def _():
            copy_out(slot, buffer, 0, size).wait()
            flags[slot] = 0

    def settle_all():
        for slot in range(2):
            settle(slot, big.at[slot], 4 * UNIT)
            settle(slot, big.at[slot, :, pl.ds(0, 2 * UNIT), :], 2 * UNIT)
        settle(2, middle, 2 * UNIT)
        settle(3, small, UNIT)

    def take(size, lead):
        if size == lead:
            slot = flags[4]
            flags[4] = 1 - slot
            buffer = big.at[slot, :, pl.ds(0, size), :]
        else:
            slot, buffer = (2, middle) if size == 2 * UNIT else (3, small)
        settle(slot, buffer, size)
        return slot, buffer

    def leave(slot, buffer, start, size):
        copy_out(slot, buffer, start, size).start()
        flags[slot] = size // UNIT

    starts, tails, split, end = key_places(frames_here, info_ref)
    edge = clip_edge(frames_here, info_ref)
    crossing = (edge > 0) & (edge < rows)
    low = jnp.where(edge > 0, 0, split)
    high = jnp.where(edge < rows, end, split)
    gather_keys(frames_here, info_ref, starts, tails, own_k, own_v, far_k, far_v, kf, vf)
    tiles, (rest_at, rest) = query_tiles(rows)
    qm[0], qm[1] = split_heads(q_ref[...])
    for h in range(2):
        qr[h * rest : h * rest + rest, :] = qm[h, rest_at:rows, :]
    acc[...] = jnp.zeros_like(acc)
    accr[...] = jnp.zeros_like(accr)
    top[...] = jnp.zeros_like(top)

    def prepare(start, size):
        span = pl.ds(start, size)
        kc_ref[span, :] = kf[span, :].astype(jnp.bfloat16)
        values = vf[span, :].astype(jnp.bfloat16)
        vc_ref[span, :] = values
        vt[0:128, span] = values.T
        real = real_keys(start, size, split, tails, 1, (16, size))
        vt[128:144, span] = real.astype(jnp.float32).astype(jnp.bfloat16)

    sweep(low, high, (2, 1), prepare)

    def value_rows(h, span):
        return jnp.concatenate([vt[64 * h : 64 * h + 64, span], vt[128:144, span]], axis=0)

    def plain(work, lead, start, size):
        span = pl.ds(start, size)
        keys = kc_ref[span, :]

        def scores(item):
            h, at, wide, _ = item
            return dot(keys, qr[...] if h is None else qm[h, at : at + wide, :], NT)

        slot, buffer = take(size, lead * UNIT)
        ahead = scores(work[0])
        for i, (h, at, wide, bias) in enumerate(work):
            s = ahead
            if i + 1 < len(work):
                ahead = scores(work[i + 1])
            if bias is not None:
                s = s + bias
            p = jnp.exp2(s * QUERY_SCALE).astype(jnp.bfloat16)
            if h is None:
                buffer[0, :, rest_at : rest_at + 2 * rest] = p
                accr[:, : 2 * rest] += dot(vt[:, span], p)
            else:
                buffer[h, :, at : at + wide] = p
                acc[h, :, at : at + wide] += dot(value_rows(h, span), p)
        leave(slot, buffer, start, size)

    every = [(h, at, wide, None) for h in range(2) for at, wide in tiles]

    @pl.when(jnp.logical_not(crossing))
    def _():
        sweep(low, high, (4, 2, 1), functools.partial(plain, every + [(None, 0, 2 * rest, None)], 4))

    @pl.when(crossing)
    def _():
        for late in (False, True):
            shown = tiles[1:] if late else tiles[:-1]
            work = [
                (h, at, wide, clip_bias(late, edge, at, wide) if 0 < at < tiles[-1][0] else None)
                for h in range(2)
                for at, wide in shown
            ]
            if late:
                work.append((None, 0, 2 * rest, None))
            body = functools.partial(plain, work, 2)
            sweep(split if late else 0, end if late else split, (2, 1), body)

    for h in range(2):
        lanes = slice(h * rest, h * rest + rest)
        acc[h, 0:64, rest_at:rows] += accr[64 * h : 64 * h + 64, lanes]
        acc[h, 64:80, rest_at:rows] += accr[128:144, lanes]
    mass = jnp.concatenate([acc[0, 64:72, :], acc[1, 64:72, :]], axis=0)
    safe = (jnp.min(mass) >= 2.0**-60) & (jnp.max(mass) <= 2.0**60)

    @pl.when(jnp.logical_not(safe))
    def _():
        settle_all()
        acc[...] = jnp.zeros_like(acc)
        top[...] = jnp.full_like(top, NEG)

        def careful(start, size):
            span = pl.ds(start, size)
            keys = kc_ref[span, :]
            real = real_keys(start, size, split, tails, 0, (size, 1))
            drop = jnp.where(real, 0.0, FAR)
            late = start >= split * UNIT
            for h in range(2):
                for at, wide in tiles + [(rest_at, rest)]:
                    lanes = slice(at, at + wide)
                    s = dot(keys, qm[h, lanes, :], NT) * QUERY_SCALE + drop
                    bias = jnp.where(crossing, clip_bias(late, edge, at, wide), 0.0)
                    old = top[h : h + 1, lanes]
                    new = jnp.maximum(old, jnp.max(s, axis=0, keepdims=True) + bias)
                    p = jnp.exp2(s - (new - bias)).astype(jnp.bfloat16)
                    top[h : h + 1, lanes] = new
                    acc[h, :, lanes] = acc[h, :, lanes] * jnp.exp2(old - new) + dot(
                        value_rows(h, span), p
                    )

        sweep(low, high, (1,), careful)
        for h in range(2):
            top[h : h + 1, :] += jnp.log2(acc[h, 64:65, :])

        def record(start, size):
            span = pl.ds(start, size)
            keys = kc_ref[span, :]
            real = real_keys(start, size, split, tails, 0, (size, 1))
            drop = jnp.where(real, 0.0, FAR)
            late = start >= split * UNIT
            slot, buffer = take(size, 4 * UNIT)
            ends = []
            for at, wide in tiles + [(rest_at, rest)]:
                lanes = slice(at, at + wide)
                for h in range(2):
                    s = dot(keys, qm[h, lanes, :], NT) * QUERY_SCALE + drop
                    bias = jnp.where(crossing, clip_bias(late, edge, at, wide), 0.0)
                    p = jnp.exp2(jnp.minimum(s - (top[h : h + 1, lanes] - bias), 0.0))
                    if at == rest_at:
                        ends.append(p)
                    else:
                        buffer[h, :, lanes] = p.astype(jnp.bfloat16)
            ends = jnp.concatenate(ends, axis=1).astype(jnp.bfloat16)
            buffer[0, :, rest_at : rest_at + 2 * rest] = ends
            leave(slot, buffer, start, size)

        sweep(low, high, (1,), record)

    for at, wide in tiles + [(rest_at, rest)]:
        lanes = slice(at, at + wide)
        halves = []
        for h in range(2):
            sums = acc[h, 64:65, lanes]
            halves.append(acc[h, 0:64, lanes] / sums)
            inv_ref[0, h : h + 1, lanes] = jnp.where(safe, 1.0 / sums, 1.0)
        o_ref[lanes, :] = jnp.concatenate(halves, axis=0).T.astype(jnp.bfloat16)

    @pl.when(pl.program_id(0) == pl.num_programs(0) - 1)
    def _():
        settle_all()


def attn_fwd(info, q, own_k, own_v, far_k, far_v, old, part, frames_here):
    rows, width = q.shape
    pairs = width // 256
    length = compact_rows(2 * frames_here)
    rest = rows % 512
    lanes = -(-rows // 128) * 128
    block = pl.BlockSpec((rows, 128), lambda p, *_: (0, p))
    column = pl.BlockSpec((rows, 128), lambda p, *_: (0, p + part * pairs))
    keys = pl.BlockSpec((length, 128), lambda p, *_: (0, p + part * pairs))

    def kernel(*refs):
        return attn_fwd_kernel(frames_here, part * pairs, *refs[:6], *refs[6 + len(old) :])

    return pl.pallas_call(
        kernel,
        out_shape=(
            jax.ShapeDtypeStruct((rows, width), jnp.bfloat16),
            jax.ShapeDtypeStruct((2 * pairs, 8, rows), jnp.float32),
            jax.ShapeDtypeStruct((length, width), jnp.bfloat16),
            jax.ShapeDtypeStruct((length, width), jnp.bfloat16),
            jax.ShapeDtypeStruct((2 * pairs, 2, length, lanes), jnp.bfloat16),
        ),
        grid_spec=pltpu.PrefetchScalarGridSpec(
            num_scalar_prefetch=1,
            grid=(pairs,),
            in_specs=[column, block, block, block, block]
            + [pl.BlockSpec(memory_space=pl.ANY)] * len(old),
            out_specs=[
                column,
                pl.BlockSpec((1, 8, rows), lambda p, *_: (p + part * pairs, 0, 0)),
                keys,
                keys,
                pl.BlockSpec(memory_space=pl.ANY),
            ],
            scratch_shapes=[
                pltpu.VMEM((2, rows, 128), jnp.bfloat16),
                pltpu.VMEM((2 * rest, 128), jnp.bfloat16),
                pltpu.VMEM((144, length), jnp.bfloat16),
                pltpu.VMEM((2, 80, rows), jnp.float32),
                pltpu.VMEM((144, 128), jnp.float32),
                pltpu.VMEM((8, rows), jnp.float32),
                pltpu.VMEM((length, 128), jnp.float32),
                pltpu.VMEM((length, 128), jnp.float32),
                pltpu.VMEM((2, 2, 4 * UNIT, lanes), jnp.bfloat16),
                pltpu.VMEM((2, 2 * UNIT, lanes), jnp.bfloat16),
                pltpu.VMEM((2, UNIT, lanes), jnp.bfloat16),
                pltpu.SemaphoreType.DMA((4,)),
                pltpu.SMEM((8,), jnp.int32),
            ],
        ),
        input_output_aliases={6 + i: i for i in range(len(old))},
        compiler_params=params(WIDE_LIMIT),
        cost_estimate=cost(4e10, 1e7),
        name="attn_fwd",
    )(info, q, own_k, own_v, far_k, far_v, *old)


def attn_bwd_kernel(
    frames_here, first_pair, apart, info_ref, q_ref, k_ref, v_ref, o_ref, do_ref, inv_ref,
    probs_ref, dq_ref, own_dk, own_dv, away, qm, qr, dom, dor, dqt, dqr, delta, dk_all, dv_all,
    back, held, sems,
):
    rows = q_ref.shape[0]
    pair = first_pair + apart * pl.program_id(0)
    total = 2 * frames_here
    length = info_ref[total]
    rank = info_ref[total + 1]
    starts, _, split, end = key_places(frames_here, info_ref)
    edge = clip_edge(frames_here, info_ref)
    crossing = (edge > 0) & (edge < rows)
    low = jnp.where(edge > 0, 0, split)
    top_unit = jnp.where(edge < rows, end, split)
    tiles, (rest_at, rest) = query_tiles(rows)
    qm[0], qm[1] = split_heads(q_ref[...])

    def copy_in(first, i, count, slot):
        start = pl.multiple_of((first + i * count) * UNIT, UNIT)
        return pltpu.make_async_copy(
            probs_ref.at[pair, :, pl.ds(start, count * UNIT), :],
            held.at[slot, :, pl.ds(0, count * UNIT), :],
            sems.at[slot],
        )

    @pl.when(jnp.logical_not(crossing))
    def _():
        copy_in(low, 0, 2, 0).start()

    high = [inv_ref[0, h : h + 1, :].astype(jnp.bfloat16).astype(jnp.float32) for h in range(2)]
    deep = [inv_ref[0, h : h + 1, :] - high[h] for h in range(2)]
    lines = jnp.concatenate(high + deep + [jnp.zeros((4, rows), jnp.float32)], axis=0)
    spot = lax.broadcasted_iota(jnp.int32, (8, 128), 0)
    head = (lax.broadcasted_iota(jnp.int32, (8, 128), 1) >= 64).astype(jnp.int32)
    pick = ((spot == head) | (spot == head + 2)).astype(jnp.float32).astype(jnp.bfloat16)
    share = dot(lines.astype(jnp.bfloat16), pick, TN)
    douts_low = (do_ref[...].astype(jnp.float32) * share).astype(jnp.bfloat16)
    dom[0], dom[1] = split_heads(douts_low)
    for h in range(2):
        qr[h * rest : h * rest + rest, :] = qm[h, rest_at:rows, :]
        dor[h * rest : h * rest + rest, :] = dom[h, rest_at:rows, :]
    dqt[...] = jnp.zeros_like(dqt)
    dqr[...] = jnp.zeros_like(dqr)
    for at, wide in tiles + [(rest_at, rest)]:
        span = slice(at, at + wide)
        prod = (o_ref[span, :].astype(jnp.float32) * do_ref[span, :].astype(jnp.float32)).T
        for h in range(2):
            inner = jnp.sum(prod[64 * h : 64 * h + 64], axis=0, keepdims=True)
            delta[h : h + 1, span] = inner * inv_ref[0, h : h + 1, span]

    def visit(work, probs, start, size):
        span = pl.ds(start, size)
        keys = k_ref[span, :]
        values = v_ref[span, :]
        turned = keys.T

        def rows_of(item):
            h, at, wide = item
            if h is None:
                return qr[...], dor[...]
            return qm[h, at : at + wide, :], dom[h, at : at + wide, :]

        def slopes(item):
            return dot(values, rows_of(item)[1], NT)

        dk = jnp.zeros((size, 128), jnp.float32)
        dv = jnp.zeros((size, 128), jnp.float32)
        ahead = slopes(work[0])
        for i, item in enumerate(work):
            h, at, wide = item
            dp = ahead
            if i + 1 < len(work):
                ahead = slopes(work[i + 1])
            queries, douts = rows_of(item)
            if h is None:
                p = probs[0, :size, rest_at : rest_at + 2 * rest]
                inner = jnp.concatenate([delta[g : g + 1, rest_at:rows] for g in range(2)], axis=1)
            else:
                p = probs[h, :size, at : at + wide]
                inner = delta[h : h + 1, at : at + wide]
            ds = (p.astype(jnp.float32) * (dp - inner)).astype(jnp.bfloat16)
            dv = dv + dot(p, douts)
            dk = dk + dot(ds, queries)
            if h is None:
                dqr[:, : 2 * rest] += dot(turned, ds)
            else:
                dqt[h, :, at : at + wide] += dot(turned[64 * h : 64 * h + 64], ds)
        return dk, dv

    def fresh(work, probs, start, size):
        dk, dv = visit(work, probs, start, size)
        dk_all[pl.ds(start, size), :] = dk * 0.125
        dv_all[pl.ds(start, size), :] = dv

    def travel(first, end, count, work, started=False):
        main = (end - first) // count
        total = main + (end - first - main * count)

        if not started:

            @pl.when(total > 0)
            def _():
                copy_in(first, 0, count, 0).start()

        def step(i, size):
            slot = lax.rem(i, 2)
            copy_in(first, i, count, slot).wait()

            @pl.when(i + 1 < total)
            def _():
                copy_in(first, i + 1, count, 1 - slot).start()

            start = pl.multiple_of((first + i * count) * UNIT, UNIT)
            fresh(work, held.at[slot], start, size)

        def loop(i, carry):
            step(i, count * UNIT)
            return carry

        lax.fori_loop(0, main, loop, 0)
        if count > 1:

            @pl.when(total > main)
            def _():
                step(main, UNIT)

    every = [(h, at, wide) for h in range(2) for at, wide in tiles]

    @pl.when(jnp.logical_not(crossing))
    def _():
        travel(low, top_unit, 2, every + [(None, 0, 2 * rest)], started=True)

    @pl.when(crossing)
    def _():
        for late in (False, True):
            shown = tiles[1:] if late else tiles[:-1]
            work = [(h, at, wide) for h in range(2) for at, wide in shown]
            if late:
                work.append((None, 0, 2 * rest))
            travel(split if late else 0, end if late else split, 2, work)

    for h in range(2):
        lanes = slice(h * rest, h * rest + rest)
        dqt[h, :, rest_at:rows] += dqr[64 * h : 64 * h + 64, lanes]
    for at, wide in tiles + [(rest_at, rest)]:
        both = jnp.concatenate([dqt[0, :, at : at + wide], dqt[1, :, at : at + wide]], axis=0)
        dq_ref[at : at + wide, :] = (both * 0.125).T.astype(jnp.bfloat16)

    for side in range(2):

        def put(k_out, v_out):
            for src, out in ((dk_all, k_out), (dv_all, v_out)):
                for f in range(side * frames_here, side * frames_here + frames_here):
                    kept, place = starts[f]
                    use = (kept == 1) & jnp.where(f >= length, edge < rows, edge > 0)
                    at = f % frames_here * PIXELS
                    back[at : at + PIXELS, :] = jnp.where(use, src[pl.ds(place, PIXELS), :], 0.0)
                out(back[...].astype(jnp.bfloat16))

        def write(ref, lanes):
            def store(value):
                ref[:, lanes] = value

            return store

        @pl.when(rank == side)
        def _():
            put(write(own_dk, slice(0, 128)), write(own_dv, slice(0, 128)))

        @pl.when(rank != side)
        def _():
            put(write(away, slice(0, 128)), write(away, slice(128, 256)))


def attn_bwd(info, q, kc, vc, o, do, inv, probs, pairs, frames_here, after):
    rows = q.shape[0]
    length = kc.shape[0]
    rest = rows % 512
    first = pairs[0]
    apart = pairs[-1] - first
    rowspec = pl.BlockSpec((rows, 128), lambda p, *_: (0, first + apart * p))
    keyspec = pl.BlockSpec((length, 128), lambda p, *_: (0, first + apart * p))
    out = pl.BlockSpec((rows, 128), lambda p, *_: (0, p))

    def kernel(*refs):
        return attn_bwd_kernel(frames_here, first, apart, *refs[:8], *refs[8 + len(after) :])

    return pl.pallas_call(
        kernel,
        out_shape=(jax.ShapeDtypeStruct((rows, 128 * len(pairs)), jnp.bfloat16),) * 3
        + (jax.ShapeDtypeStruct((rows, 256 * len(pairs)), jnp.bfloat16),),
        grid_spec=pltpu.PrefetchScalarGridSpec(
            num_scalar_prefetch=1,
            grid=(len(pairs),),
            in_specs=[
                rowspec,
                keyspec,
                keyspec,
                rowspec,
                rowspec,
                pl.BlockSpec((1, 8, rows), lambda p, *_: (first + apart * p, 0, 0)),
                pl.BlockSpec(memory_space=pl.ANY),
            ]
            + [pl.BlockSpec(memory_space=pl.ANY)] * len(after),
            out_specs=[out] * 3 + [pl.BlockSpec((rows, 256), lambda p, *_: (0, p))],
            scratch_shapes=[
                pltpu.VMEM((2, rows, 128), jnp.bfloat16),
                pltpu.VMEM((2 * rest, 128), jnp.bfloat16),
                pltpu.VMEM((2, rows, 128), jnp.bfloat16),
                pltpu.VMEM((2 * rest, 128), jnp.bfloat16),
                pltpu.VMEM((2, 64, rows), jnp.float32),
                pltpu.VMEM((128, 128), jnp.float32),
                pltpu.VMEM((8, rows), jnp.float32),
                pltpu.VMEM((length, 128), jnp.float32),
                pltpu.VMEM((length, 128), jnp.float32),
                pltpu.VMEM((rows, 128), jnp.float32),
                pltpu.VMEM((2, 2, 2 * UNIT, probs.shape[3]), jnp.bfloat16),
                pltpu.SemaphoreType.DMA((2,)),
            ],
        ),
        compiler_params=params(),
        cost_estimate=cost(3e10 * len(pairs), 1e7),
        name="attn_bwd",
    )(info, q, kc, vc, o, do, inv, probs, *after)


TILE = 400
SMALL_TILE = 224
PART = 384
INV_SQRT2 = 0.7071067811865476
INV_SQRT_2PI = 0.3989422804014327
QUERY_SCALE = 0.125 * LOG2E


def params(limit=VMEM_LIMIT):
    return pltpu.CompilerParams(vmem_limit_bytes=limit, dimension_semantics=("arbitrary",))


def cost(flops, moved):
    return pl.CostEstimate(flops=int(flops), bytes_accessed=int(moved), transcendentals=0)


def tile_spec(width):
    return pl.BlockSpec((TILE, width), lambda i: (i, 0))


def small_spec(width):
    return pl.BlockSpec((SMALL_TILE, width), lambda i: (i, 0))


def whole_spec(shape):
    return pl.BlockSpec(shape, lambda i: (0,) * len(shape), pipeline_mode=pl.Buffered(1))


def low_shape(rows, width):
    return jax.ShapeDtypeStruct((rows, width), jnp.bfloat16)


def ln_parts(x):
    center = x - jnp.mean(x, axis=-1, keepdims=True)
    rstd = lax.rsqrt(jnp.mean(center * center, axis=-1, keepdims=True) + EPS)
    return center * rstd, rstd


def ln_back(dy, gain, xhat, rstd):
    dxhat = dy * gain
    along = jnp.mean(dxhat * xhat, axis=-1, keepdims=True)
    return rstd * (dxhat - jnp.mean(dxhat, axis=-1, keepdims=True) - xhat * along)


def line(ref):
    return ref[...].reshape(1, -1)


def vector_spec(size):
    return pl.BlockSpec((size,), lambda i: (0,))


def rows_sum(x):
    return jnp.sum(x, axis=0, keepdims=True)


def project_kernel(x_ref, gain_ref, shift_ref, wk, wv, bias_ref, n_ref, k_ref, v_ref):
    xhat, _ = ln_parts(x_ref[...].astype(jnp.float32))
    normed = (xhat * line(gain_ref) + line(shift_ref)).astype(jnp.bfloat16)
    n_ref[...] = normed
    half = k_ref.shape[1]
    k_ref[...] = dot(normed, wk[...]).astype(jnp.bfloat16)
    v_ref[...] = (dot(normed, wv[...]) + line(bias_ref)[:, :half]).astype(jnp.bfloat16)


def weight_spec(width, size, column):
    return pl.BlockSpec((width, size), lambda i: (0, column), pipeline_mode=pl.Buffered(1))


def project(x, gain, shift, w, v_bias):
    rows, width = x.shape
    half = width // 2
    return pl.pallas_call(
        project_kernel,
        out_shape=(low_shape(rows, width), low_shape(rows, half), low_shape(rows, half)),
        grid=(-(-rows // TILE),),
        in_specs=[
            tile_spec(width),
            vector_spec(width),
            vector_spec(width),
            weight_spec(width, half, 2),
            weight_spec(width, half, 4),
            vector_spec(width),
        ],
        out_specs=[tile_spec(width), tile_spec(half), tile_spec(half)],
        compiler_params=params(WIDE_LIMIT),
        cost_estimate=cost(2 * rows * width * width, 10 * rows * width),
        name="project",
    )(x, gain, shift, w, w, v_bias)


def project_more_kernel(n_ref, wq, wk, wv, q_bias, v_bias, q_ref, k_ref, v_ref):
    normed = n_ref[...]
    k_ref[...] = dot(normed, wk[...]).astype(jnp.bfloat16)
    half = v_ref.shape[1]
    v_ref[...] = (dot(normed, wv[...]) + line(v_bias)[:, half:]).astype(jnp.bfloat16)
    q_ref[...] = (dot(normed, wq[...]) + line(q_bias)).astype(jnp.bfloat16)


def project_more(normed, w, q_bias, v_bias):
    rows, width = normed.shape
    half = width // 2
    return pl.pallas_call(
        project_more_kernel,
        out_shape=(low_shape(rows, width), low_shape(rows, half), low_shape(rows, half)),
        grid=(-(-rows // TILE),),
        in_specs=[
            tile_spec(width),
            weight_spec(width, width, 0),
            weight_spec(width, half, 3),
            weight_spec(width, half, 5),
            vector_spec(width),
            vector_spec(width),
        ],
        out_specs=[tile_spec(width), tile_spec(half), tile_spec(half)],
        compiler_params=params(WIDE_LIMIT),
        cost_estimate=cost(4 * rows * width * width, 10 * rows * width),
        name="project_more",
    )(normed, w, w, w, q_bias, v_bias)


def mlp_fwd_kernel(
    x_ref, a_ref, w_out, b_out, gain2, shift2, w_up, b_up, w_down, b_down, gain3, shift3,
    mid_ref, n2_ref, hid_ref, slope_ref, out_ref, n3_ref,
):
    width = x_ref.shape[1]
    inner = w_up.shape[1]
    parts = inner // width
    middle = x_ref[...].astype(jnp.float32) + dot(a_ref[...], w_out[...]) + line(b_out)
    mid_ref[...] = middle.astype(jnp.bfloat16)
    xhat, _ = ln_parts(middle)
    n2 = (xhat * line(gain2) + line(shift2)).astype(jnp.bfloat16)
    n2_ref[...] = n2
    out = middle + line(b_down)
    up_shift = line(b_up)

    def raise_part(j):
        span = slice(j * width, (j + 1) * width)
        return dot(n2, w_up[:, span]) + up_shift[:, span]

    ahead = raise_part(0)
    for j in range(parts):
        span = slice(j * width, (j + 1) * width)
        up = ahead
        if j + 1 < parts:
            ahead = raise_part(j + 1)
        area = 0.5 + 0.5 * lax.erf(up * INV_SQRT2)
        bell = jnp.exp2(up * up * (-0.5 * LOG2E)) * INV_SQRT_2PI
        hid = (up * area).astype(jnp.bfloat16)
        hid_ref[:, span] = hid
        slope_ref[:, span] = (area + up * bell).astype(jnp.bfloat16)
        out = out + dot(hid, w_down[span, :])
    out_ref[...] = out.astype(jnp.bfloat16)
    xhat, _ = ln_parts(out)
    n3_ref[...] = (xhat * line(gain3) + line(shift3)).astype(jnp.bfloat16)


def mlp_fwd(x, attended, w_out, b_out, gain2, shift2, w_up, b_up, w_down, b_down, gain3, shift3):
    rows, width = x.shape
    inner = w_up.shape[1]
    vec = vector_spec(width)
    return pl.pallas_call(
        mlp_fwd_kernel,
        out_shape=(
            low_shape(rows, width), low_shape(rows, width), low_shape(rows, inner),
            low_shape(rows, inner), low_shape(rows, width), low_shape(rows, width),
        ),
        grid=(-(-rows // TILE),),
        in_specs=[
            tile_spec(width), tile_spec(width), whole_spec(w_out.shape), vec, vec, vec,
            whole_spec(w_up.shape), vector_spec(inner), whole_spec(w_down.shape), vec, vec, vec,
        ],
        out_specs=[
            tile_spec(width), tile_spec(width), tile_spec(inner),
            tile_spec(inner), tile_spec(width), tile_spec(width),
        ],
        compiler_params=params(WIDE_LIMIT),
        cost_estimate=cost(
            2 * rows * width * (width + 2 * inner), 2 * rows * (6 * width + 2 * inner)
        ),
        name="mlp_fwd",
    )(x, attended, w_out, b_out, gain2, shift2, w_up, b_up, w_down, b_down, gain3, shift3)


def mlp_bwd_kernel(
    rows, cot_ref, out_ref, side_ref, pool_ref, w_first, gain3, w_down, slope_ref, w_up, mid_ref,
    gain2, w_out, ddown_ref, dup_ref, dbranch_ref, datt_ref, sums_ref,
):
    width = cot_ref.shape[1]
    inner = w_up.shape[1]
    parts = inner // width

    @pl.when(pl.program_id(0) == 0)
    def _():
        sums_ref[...] = jnp.zeros_like(sums_ref)

    inside = lax.broadcasted_iota(jnp.int32, (TILE, 1), 0) < rows - pl.program_id(0) * TILE

    def add(row, value):
        total = rows_sum(jnp.where(inside, value, 0.0))
        middle = total.shape[1] // 2
        below = sums_ref.shape[0] // 2 + row
        sums_ref[row : row + 1, :] += total[:, :middle]
        sums_ref[below : below + 1, :] += total[:, middle:]

    dn3 = dot(side_ref[:, :128], w_first[...])
    xhat, rstd = ln_parts(out_ref[...].astype(jnp.float32))
    add(2, dn3 * xhat)
    add(3, dn3)
    d_out = (
        cot_ref[...].astype(jnp.float32)
        + ln_back(dn3, line(gain3), xhat, rstd)
        + dot(side_ref[:, 128:192], pool_ref[...])
    )
    d_down = d_out.astype(jnp.bfloat16)
    ddown_ref[...] = d_down
    add(4, d_down.astype(jnp.float32))

    def lower_part(j):
        return dot(d_down, w_down[j * width : (j + 1) * width, :], NT)

    ahead = lower_part(0)
    dn2 = jnp.zeros(cot_ref.shape, jnp.float32)
    for j in range(parts):
        span = slice(j * width, (j + 1) * width)
        d_hid = ahead
        if j + 1 < parts:
            ahead = lower_part(j + 1)
        d_up = (d_hid * slope_ref[:, span].astype(jnp.float32)).astype(jnp.bfloat16)
        dup_ref[:, span] = d_up
        add(6 + j, d_up.astype(jnp.float32))
        dn2 = dn2 + dot(d_up, w_up[:, span], NT)
    xhat, rstd = ln_parts(mid_ref[...].astype(jnp.float32))
    add(0, dn2 * xhat)
    add(1, dn2)
    d_branch = (d_out + ln_back(dn2, line(gain2), xhat, rstd)).astype(jnp.bfloat16)
    dbranch_ref[...] = d_branch
    add(5, d_branch.astype(jnp.float32))
    datt_ref[...] = dot(d_branch, w_out[...], NT).astype(jnp.bfloat16)


def mlp_bwd(cot, out, side, pool, w_first, gain3, w_down, slope, w_up, mid, gain2, w_out):
    rows, width = cot.shape
    inner = w_up.shape[1]
    vec = vector_spec(width)
    return pl.pallas_call(
        functools.partial(mlp_bwd_kernel, rows),
        out_shape=(
            low_shape(rows, width), low_shape(rows, inner), low_shape(rows, width),
            low_shape(rows, width), jax.ShapeDtypeStruct((32, width // 2), jnp.float32),
        ),
        grid=(-(-rows // TILE),),
        in_specs=[
            tile_spec(width), tile_spec(width), tile_spec(256), whole_spec(pool.shape),
            whole_spec(w_first.shape), vec, whole_spec(w_down.shape), tile_spec(inner),
            whole_spec(w_up.shape), tile_spec(width), vec, whole_spec(w_out.shape),
        ],
        out_specs=[
            tile_spec(width), tile_spec(inner), tile_spec(width), tile_spec(width),
            pl.BlockSpec((32, width // 2), lambda i: (0, 0)),
        ],
        compiler_params=params(),
        cost_estimate=cost(
            2 * rows * width * (width + 2 * inner), 2 * rows * (6 * width + 2 * inner)
        ),
        name="mlp_bwd",
    )(cot, out, side, pool, w_first, gain3, w_down, slope, w_up, mid, gain2, w_out)


def final_bwd_kernel(rows, pairs, *refs):
    pieces = [refs[i * pairs : (i + 1) * pairs] for i in range(5)]
    x_ref, branch_ref, gain, w_ref, grad_ref, sums_ref = refs[5 * pairs :]
    width = x_ref.shape[1]

    @pl.when(pl.program_id(0) == 0)
    def _():
        sums_ref[...] = jnp.zeros_like(sums_ref)

    inside = lax.broadcasted_iota(jnp.int32, (SMALL_TILE, 1), 0) < rows - pl.program_id(0) * SMALL_TILE

    def add(row, value):
        total = rows_sum(jnp.where(inside, value, 0.0))
        middle = total.shape[1] // 2
        below = sums_ref.shape[0] // 2 + row
        sums_ref[row : row + 1, :] += total[:, :middle]
        sums_ref[below : below + 1, :] += total[:, middle:]

    def join(part):
        return jnp.concatenate([r[...] for r in part], axis=1)

    def total(part, other):
        both = [a[...].astype(jnp.float32) + b[...].astype(jnp.float32) for a, b in zip(part, other)]
        return jnp.concatenate(both, axis=1).astype(jnp.bfloat16)

    dq = join(pieces[0])
    dk = total(pieces[1], pieces[2])
    dv = total(pieces[3], pieces[4])
    dn = (
        dot(dq, w_ref[:, :width], NT)
        + dot(dk, w_ref[:, width : 2 * width], NT)
        + dot(dv, w_ref[:, 2 * width :], NT)
    )
    xhat, rstd = ln_parts(x_ref[...].astype(jnp.float32))
    add(0, dn * xhat)
    add(1, dn)
    add(2, dq.astype(jnp.float32))
    add(3, dv.astype(jnp.float32))
    grad_ref[...] = (
        branch_ref[...].astype(jnp.float32) + ln_back(dn, line(gain), xhat, rstd)
    ).astype(jnp.bfloat16)


def final_bwd(pieces, x, branch, gain, w):
    rows, width = x.shape
    pairs = width // 128
    return pl.pallas_call(
        functools.partial(final_bwd_kernel, rows, pairs),
        out_shape=(low_shape(rows, width), jax.ShapeDtypeStruct((16, width // 2), jnp.float32)),
        grid=(-(-rows // SMALL_TILE),),
        in_specs=[
            pl.BlockSpec((SMALL_TILE, 128), functools.partial(lambda c, i: (i, c), column))
            for _, column in pieces
        ]
        + [small_spec(width)] * 2
        + [vector_spec(width), whole_spec(w.shape)],
        out_specs=[small_spec(width), pl.BlockSpec((16, width // 2), lambda i: (0, 0))],
        compiler_params=params(),
        cost_estimate=cost(6 * rows * width * width, 16 * rows * width),
        name="final_bwd",
    )(*[array for array, _ in pieces], x, branch, gain, w)


def grid_masks(frames, lanes):
    table = np.zeros((16, lanes), np.float32)
    lane = np.arange(lanes)
    pixel = lane % PIXELS
    i, j = pixel // GRID, pixel % GRID
    inside = lane < frames * PIXELS
    for a in range(3):
        for b in range(3):
            ok = (i + a - 1 >= 0) & (i + a - 1 < GRID) & (j + b - 1 >= 0) & (j + b - 1 < GRID)
            table[3 * a + b] = ok & inside
    table[9] = np.where(inside, lane // PIXELS, -1)
    return table


def learner_kernel(
    frames, info_ref, weight_ref, n3_ref, out_ref, pool_ref, wt_ref, cw_ref, cwt_ref, cb_ref,
    mask_ref, side_ref, pooled_ref, small_ref, keep_ref, send_ref, rounds, seqs,
):
    rows = n3_ref.shape[0]
    lanes = mask_ref.shape[1]
    extra = lanes - rows
    rank = info_ref[2 * frames + 1]
    frame_of = mask_ref[9:10, :]
    live = jnp.zeros((1, lanes), jnp.float32)
    for f in range(frames):
        kept = info_ref[rank * frames + f].astype(jnp.float32)
        live = live + jnp.where(frame_of == f, kept, 0.0)
    inside = (frame_of >= 0).astype(jnp.float32)

    def widen(x):
        return jnp.concatenate([x, jnp.zeros((x.shape[0], extra), jnp.float32)], axis=1)

    def turn(x, by):
        return x if by % lanes == 0 else pltpu.roll(x, by % lanes, 1)

    def gather_taps(taps):
        total = jnp.zeros((8, lanes), jnp.float32)
        for t in range(9):
            step = (t // 3 - 1) * GRID + t % 3 - 1
            total = total + turn(taps[8 * t : 8 * t + 8, :], -step) * mask_ref[t : t + 1, :]
        return total

    def spread_taps(level):
        parts = []
        for t in range(9):
            step = (t // 3 - 1) * GRID + t % 3 - 1
            parts.append(turn(level, step) * mask_ref[8 - t : 9 - t, :])
        return jnp.concatenate(parts, axis=0)

    def exact(a, b, dims=NN):
        return lax.dot_general(
            a, b, dims, precision=HIGHEST, preferred_element_type=jnp.float32
        )

    def area_of(x):
        return 0.5 + 0.5 * lax.erf(x * INV_SQRT2)

    taps = widen(dot(wt_ref[...], n3_ref[...], NT))
    levels = [gather_taps(taps) + cb_ref[:, 0:1]]
    hiddens = []
    for n in range(3):
        hiddens.append(levels[n] * area_of(levels[n]))
        levels.append(gather_taps(exact(cwt_ref[n], hiddens[n])) + cb_ref[:, n + 1 : n + 2])
    maps = 1.0 / (1.0 + jnp.exp(-levels[3]))
    total = rows_sum(maps)
    meet = 0.5 * (total * total - rows_sum(maps * maps)) * live
    small_ref[...] = jnp.zeros_like(small_ref)
    small_ref[8:9, 128:256] = jnp.zeros((1, 128), jnp.float32) + jnp.sum(meet)
    shifts = jnp.zeros((8, 128), jnp.float32)
    lane = lax.broadcasted_iota(jnp.int32, (8, 128), 1)

    owner = lax.broadcasted_iota(jnp.int32, (8 * frames, lanes), 0) // 8
    mine = owner.astype(jnp.float32) == frame_of
    low_maps = maps.astype(jnp.bfloat16).astype(jnp.float32) * live
    stacked = jnp.where(mine, jnp.concatenate([low_maps] * frames, axis=0), 0.0)
    out = out_ref[...]
    pooled_ref[...] = dot(stacked[:, :rows].astype(jnp.bfloat16), out).astype(jnp.bfloat16)
    pairs = jnp.where(mine, widen(dot(pool_ref[...], out, NT)), 0.0)
    d_maps = pairs[0:8]
    for f in range(1, frames):
        d_maps = d_maps + pairs[8 * f : 8 * f + 8]
    d_maps = d_maps * live + weight_ref[0] * live * (total - maps)
    d_level = d_maps * maps * (1.0 - maps)
    for n in (2, 1, 0):
        shifts = jnp.where(lane == n + 1, jnp.sum(d_level, axis=1, keepdims=True), shifts)
        d_taps = spread_taps(d_level)
        small_ref[0:8, 128 * n : 128 * n + 72] = exact(hiddens[n], d_taps, NT)
        d_hidden = exact(cw_ref[n], d_taps)
        x = levels[n]
        bell = jnp.exp(-0.5 * x * x) * INV_SQRT_2PI
        d_level = d_hidden * (area_of(x) + x * bell) * inside
    shifts = jnp.where(lane == 0, jnp.sum(d_level, axis=1, keepdims=True), shifts)
    small_ref[8:16, 0:8] = shifts.T[0:8, :]
    d_first = spread_taps(d_level)[:, :rows]
    grad = dot(d_first.astype(jnp.bfloat16), n3_ref[...])
    grad = jnp.concatenate([grad, jnp.zeros((56, grad.shape[1]), jnp.float32)], axis=0).T
    columns = 9 * MAPS // 2
    lane = lax.broadcasted_iota(jnp.int32, grad.shape, 1)
    left = jnp.where(lane < columns, grad, 0.0).astype(jnp.bfloat16)
    right = jnp.where(lane < columns, pltpu.roll(grad, 128 - columns, 1), 0.0).astype(jnp.bfloat16)
    size = grad.shape[0] // seqs // 3
    for ref, side in ((keep_ref, 0), (send_ref, 1)):
        value = jnp.where(rank == side, left, right)
        for o in range(seqs):
            parts = [value[(3 * o + t) * size : (3 * o + t + 1) * size, :] for t in range(3)]
            put_rows(ref, block_place(o, rounds) * size, jnp.concatenate(parts, axis=1))
    tall = jnp.concatenate(
        [
            d_first,
            jnp.zeros((56, rows), jnp.float32),
            stacked[:, :rows],
            jnp.zeros((128 - 8 * frames, rows), jnp.float32),
        ],
        axis=0,
    )
    side_ref[...] = tall.T.astype(jnp.bfloat16)


def learner(info, weight, n3, out, pool, w_first, conv_weights, conv_biases, rounds, seqs):
    rows, width = n3.shape
    frames = rows // PIXELS
    lanes = -(-rows // 128) * 128
    vm = pl.BlockSpec(memory_space=pltpu.VMEM)
    sm = pl.BlockSpec(memory_space=pltpu.SMEM)
    masks = jnp.asarray(grid_masks(frames, lanes))
    return pl.pallas_call(
        functools.partial(learner_kernel, frames, rounds=rounds, seqs=seqs),
        out_shape=(
            low_shape(rows, 256),
            low_shape(8 * frames, width),
            jax.ShapeDtypeStruct((16, PART), jnp.float32),
            low_shape(width // 3, PART),
            low_shape(width // 3, PART),
        ),
        in_specs=[sm, sm] + [vm] * 8,
        out_specs=(vm,) * 5,
        compiler_params=pltpu.CompilerParams(vmem_limit_bytes=VMEM_LIMIT),
        cost_estimate=cost(2e10, 4 * rows * width),
        name="learner",
    )(
        info, weight, n3, out, pool, w_first.T, conv_weights,
        conv_weights.transpose(0, 2, 1), conv_biases.T, masks,
    )


def flip(count, bit):
    return [(i, i ^ bit) for i in range(count)]


def low_sum(a, b):
    return (a.astype(jnp.float32) + b.astype(jnp.float32)).astype(jnp.bfloat16)


def block_place(owner, rounds):
    place = 0
    for bits in rounds:
        for bit in bits:
            place = place * 2 + ((owner >> bit) & 1)
    return place


def put_rows(ref, at, value):
    if not isinstance(at, int):
        at = pl.multiple_of(at, 16)
    ref[pl.ds(at, value.shape[0]), :] = value


def put_blocks(ref, value, first_owner, owners, rounds):
    size = value.shape[0] // owners
    for o in range(owners):
        place = block_place(first_owner + o, rounds)
        put_rows(ref, place * size, value[o * size : (o + 1) * size, :])


def grad_by_columns_kernel(rounds, seqs, info_ref, a_ref, b_ref, keep_ref, send_ref, turned):
    step = pl.program_id(0)
    half = pl.num_programs(0) // 2

    @pl.when(step == 0)
    def _():
        turned[...] = a_ref[...].T

    got = dot(turned[...], b_ref[...]).astype(jnp.bfloat16)
    parts = got.shape[1] // PART
    size = got.shape[0] // seqs

    def put(ref):
        for o in range(seqs):
            base = block_place(o, rounds) * size * parts * half
            for i in range(parts):
                at = base + (lax.rem(step, half) * parts + i) * size
                put_rows(ref, at, got[o * size : o * size + size, i * PART : i * PART + PART])

    @pl.when(step < half)
    def _():
        put(keep_ref)

    @pl.when(step >= half)
    def _():
        put(send_ref)


def grad_by_columns(info, a, b, rounds, seqs, at):
    rows, tall = a.shape
    wide = b.shape[1]
    block = min(768, wide // 2)
    half = wide // 2 // block
    out = jax.ShapeDtypeStruct((tall * wide // 2 // PART, PART), jnp.bfloat16)
    whole = pl.BlockSpec(out.shape, lambda j, info: (0, 0))
    return pl.pallas_call(
        functools.partial(grad_by_columns_kernel, rounds, seqs),
        out_shape=(out, out),
        grid_spec=pltpu.PrefetchScalarGridSpec(
            num_scalar_prefetch=1,
            grid=(2 * half,),
            in_specs=[
                pl.BlockSpec((rows, tall), lambda j, info: (0, 0)),
                pl.BlockSpec(
                    (rows, block),
                    lambda j, info: (0, jnp.where(j < half, info[at], 1 - info[at]) * half + j % half),
                ),
            ],
            out_specs=[whole, whole],
            scratch_shapes=[pltpu.VMEM((tall, rows), jnp.bfloat16)],
        ),
        compiler_params=params(),
        cost_estimate=cost(2 * rows * tall * wide, 2 * rows * (tall + wide)),
        name="grad_columns",
    )(info, a, b)


def pick_half(rank, value):
    middle = value.shape[1] // 2
    first, second = value[:, :middle], value[:, middle:]
    return jnp.where(rank == 0, first, second), jnp.where(rank == 0, second, first)


def grad_by_rows_kernel(rounds, seqs, at, info_ref, a_ref, b_ref, keep_ref, send_ref):
    step = pl.program_id(0)
    got = dot(a_ref[...], b_ref[...], TN).astype(jnp.bfloat16)
    keep, send = pick_half(info_ref[at], got)
    owners = seqs // (keep_ref.shape[0] // a_ref.shape[1])
    put_blocks(keep_ref, keep, step * owners, owners, rounds)
    put_blocks(send_ref, send, step * owners, owners, rounds)


def grad_by_rows(info, a, b, rounds, seqs, at):
    rows, tall = a.shape
    wide = b.shape[1]
    out = jax.ShapeDtypeStruct((tall, wide // 2), jnp.bfloat16)
    return pl.pallas_call(
        functools.partial(grad_by_rows_kernel, rounds, seqs, at),
        out_shape=(out, out),
        grid_spec=pltpu.PrefetchScalarGridSpec(
            num_scalar_prefetch=1,
            grid=(tall // 768,),
            in_specs=[
                pl.BlockSpec((rows, 768), lambda j, info: (0, j)),
                pl.BlockSpec((rows, wide), lambda j, info: (0, 0)),
            ],
            out_specs=[pl.BlockSpec((tall, wide // 2), lambda j, info: (0, 0))] * 2,
        ),
        compiler_params=params(),
        cost_estimate=cost(2 * rows * tall * wide, 2 * rows * (tall + wide)),
        name="grad_rows",
    )(info, a, b)


def grad_pieces_kernel(rounds, seqs, at, turn, info_ref, n_ref, *refs):
    (q0, k0, x0, v0, y0), (q1, k1, x1, v1, y1) = refs[:5], refs[5:10]
    if turn:
        keep_ref, send_ref, turned_ref = refs[-3:]
        turned_ref[...] = n_ref[...].T
    else:
        keep_ref, send_ref = refs[-2:]
        turned_ref = n_ref
    first = jnp.concatenate([q0[...], q1[...], low_sum(k0[...], x0[...])], axis=1)
    second = jnp.concatenate(
        [low_sum(k1[...], x1[...]), low_sum(v0[...], y0[...]), low_sum(v1[...], y1[...])], axis=1
    )
    both = jnp.concatenate([first, second], axis=1)
    got = dot(turned_ref[...], both).astype(jnp.bfloat16)
    keep, send = pick_half(info_ref[at], got)
    put_blocks(keep_ref, keep, 0, seqs, rounds)
    put_blocks(send_ref, send, 0, seqs, rounds)


def grad_pieces(info, n1, w_rows, pieces, rounds, seqs, at, after):
    turn = n1.shape[0] != w_rows
    rows, tall = n1.shape if turn else n1.shape[::-1]
    out = jax.ShapeDtypeStruct((tall, PART), jnp.bfloat16)
    flat = [piece for pair in pieces for piece in pair]
    whole = pl.BlockSpec((tall, PART), lambda i, info: (0, 0))
    return pl.pallas_call(
        functools.partial(grad_pieces_kernel, rounds, seqs, at, turn),
        out_shape=(out, out) + ((low_shape(tall, rows),) if turn else ()),
        grid_spec=pltpu.PrefetchScalarGridSpec(
            num_scalar_prefetch=1,
            grid=(1,),
            in_specs=[pl.BlockSpec(n1.shape, lambda i, info: (0, 0))]
            + [
                pl.BlockSpec((rows, 128), functools.partial(lambda c, i, info: (0, c), column))
                for _, column in flat
            ]
            + [pl.BlockSpec(memory_space=pl.ANY)] * len(after),
            out_specs=[whole, whole]
            + ([pl.BlockSpec((tall, rows), lambda i, info: (0, 0))] if turn else []),
        ),
        compiler_params=params(),
        cost_estimate=cost(2 * rows * tall * 768, 4 * rows * tall),
        name="grad_pieces",
    )(info, n1, *[array for array, _ in flat], *after)


class Stream:
    def __init__(self, rounds, keep, send, emit=None):
        self.rounds, self.at, self.keep, self.emit = rounds, 0, keep, emit
        self.gots = [(lax.ppermute(send, "frame", flip(2, 1)), 0)]

    def bits(self):
        return self.rounds[self.at] if self.at < len(self.rounds) else None


class Total(Stream):
    def __init__(self, rounds, value, emit):
        super().__init__(rounds, value, value, emit)


def split_low(value):
    high = value.astype(jnp.bfloat16)
    return high, (value - high.astype(jnp.float32)).astype(jnp.bfloat16)


def fold(info, at, bundles, after=(), emit=None):
    arrays, plan, outs = [], [], []

    def source(array):
        for i, known in enumerate(arrays):
            if known is array:
                return i
        arrays.append(array)
        return len(arrays) - 1

    for streams, sending in bundles:
        entry = []
        bits = streams[0].bits() if sending else None
        ways = 1 << len(bits) if bits else 1
        offset = 0
        for s in streams:
            parts = [(source(array), start) for array, start in s.gots]
            rows = s.keep.shape[0]
            entry.append((s, source(s.keep), parts, rows, offset))
            if isinstance(s, Total):
                kept = jax.ShapeDtypeStruct((rows, PART), jnp.float32)
                offset += 2 * rows
            else:
                kept = jax.ShapeDtypeStruct((rows // ways, PART), jnp.bfloat16)
                offset += rows // ways
            if sending:
                outs.append(kept)
            elif s.emit:
                outs += s.emit[0]
            elif not emit:
                outs.append(kept)
        outs += [jax.ShapeDtypeStruct((offset, PART), jnp.bfloat16)] * (ways - 1)
        plan.append((entry, bits, ways))
    if emit:
        outs += emit[0]

    def kernel(info_ref, *refs):
        sources, targets = refs[: len(arrays)], list(refs[len(arrays) + len(after) :])
        index = info_ref[at]
        ready = []
        for entry, bits, ways in plan:
            mine = 0
            for bit in bits or ():
                mine = mine * 2 + ((index >> bit) & 1)
            kept = []
            for s, own, parts, rows, offset in entry:
                size = rows // ways
                if bits:
                    kept.append(targets.pop(0))
                elif s.emit or not emit:
                    count = len(s.emit[0]) if s.emit else 1
                    kept.append([targets.pop(0) for _ in range(count)])
                else:
                    kept.append(None)
            sends = [targets.pop(0) for _ in range(ways - 1)]
            for (s, own, parts, rows, offset), keep in zip(entry, kept):

                def total(start, size):
                    value = sources[own][pl.ds(start, size), :].astype(jnp.float32)
                    for i, begin in parts:
                        if isinstance(s, Total):
                            if sources[i].dtype == jnp.float32:
                                value = value + sources[i][...]
                            else:
                                value = value + sources[i][begin : begin + rows, :].astype(jnp.float32)
                                value = value + sources[i][
                                    begin + rows : begin + 2 * rows, :
                                ].astype(jnp.float32)
                        else:
                            value = value + sources[i][pl.ds(begin + start, size), :].astype(jnp.float32)
                    return value

                if bits and isinstance(s, Total):
                    value = total(0, rows)
                    keep[...] = value
                    high, low = split_low(value)
                    for send in sends:
                        send[offset : offset + rows, :] = high
                        send[offset + rows : offset + 2 * rows, :] = low
                elif bits:
                    size = rows // ways
                    for m in range(ways):
                        start = pl.multiple_of((mine ^ m) * size, 16)
                        value = total(start, size).astype(jnp.bfloat16)
                        if m == 0:
                            keep[...] = value
                        else:
                            sends[m - 1][offset : offset + size, :] = value
                elif keep is None:
                    ready.append(total(0, rows))
                elif s.emit:
                    s.emit[1](total(0, rows), *keep)
                else:
                    keep[0][...] = total(0, rows).astype(keep[0].dtype)
        if emit:
            emit[1](ready, *targets)

    vm = pl.BlockSpec(memory_space=pltpu.VMEM)
    sm = pl.BlockSpec(memory_space=pltpu.SMEM)
    moved = sum(x.size * x.dtype.itemsize for x in arrays) * 2
    results = list(
        pl.pallas_call(
            kernel,
            out_shape=tuple(outs),
            in_specs=[sm] + [vm] * len(arrays) + [pl.BlockSpec(memory_space=pl.ANY)] * len(after),
            out_specs=(vm,) * len(outs),
            compiler_params=pltpu.CompilerParams(vmem_limit_bytes=VMEM_LIMIT),
            cost_estimate=cost(0, moved),
            name="fold",
        )(info, *arrays, *after)
    )
    sent = []
    count = lax.axis_size("seq")
    for entry, bits, ways in plan:
        for s, *_ in entry:
            if bits:
                s.keep = results.pop(0)
            elif s.emit:
                s.result = [results.pop(0) for _ in s.emit[0]]
            elif not emit:
                s.keep = results.pop(0)
            s.gots = []
        for m in range(1, ways):
            mask = 0
            for i, bit in enumerate(bits):
                mask |= ((m >> (len(bits) - 1 - i)) & 1) << bit
            send = results.pop(0)
            sent.append(send)
            got = lax.ppermute(send, "seq", flip(count, mask))
            for s, _, _, _, offset in entry:
                s.gots.append((got, offset))
        if bits:
            for s, *_ in entry:
                s.at += 1
    return sent[:1], results


def add_all(value, bits, after):
    count = lax.axis_size("seq")
    gots = []
    for m in range(1, 1 << len(bits)):
        mask = sum(((m >> i) & 1) << bit for i, bit in enumerate(bits))
        gots.append(lax.ppermute(value, "seq", flip(count, mask)))

    def kernel(*refs):
        total = refs[0][...]
        for ref in refs[1 : 1 + len(gots)]:
            total = total + ref[...]
        refs[-1][...] = total

    vm = pl.BlockSpec(memory_space=pltpu.VMEM)
    return pl.pallas_call(
        kernel,
        out_shape=jax.ShapeDtypeStruct(value.shape, jnp.float32),
        in_specs=[vm] * (1 + len(gots)) + [pl.BlockSpec(memory_space=pl.ANY)] * len(after),
        out_specs=vm,
        name="add_all",
    )(value, *gots, *after)


def doubles(bits):
    low = list(range(bits))
    return [low[i : i + 2] for i in range(0, bits, 2)]


def f32_shape(*shape):
    return jax.ShapeDtypeStruct(shape, jnp.float32)


def write_plain(value, ref):
    ref[...] = value


def write_wide(value, ref):
    size = ref.shape[0]
    for i in range(value.shape[0] // size):
        ref[:, i * PART : i * PART + PART] = value[i * size : i * size + size, :]


def write_first(value, ref):
    for i in range(3):
        ref[16 * i : 16 * i + 16, :] = value[:, 128 * i : 128 * i + ref.shape[1]]


def write_vectors(value, *refs):
    row = 0
    for ref in refs:
        for i in range(ref.shape[0] // (2 * PART)):
            ref[2 * PART * i : 2 * PART * i + PART] = value[row, :]
            ref[2 * PART * i + PART : 2 * PART * (i + 1)] = value[value.shape[0] // 2 + row, :]
            row += 1


def write_small(value, weights_ref, biases_ref, meet_ref):
    for n in range(3):
        weights_ref[n] = value[0:8, 128 * n : 128 * n + 9 * MAPS]
    biases_ref[...] = value[8:12, 0:MAPS]
    meet_ref[...] = value[8:9, 128:129]


def write_groups(values, ref):
    count = len(values)
    for i in range(3):
        for g, value in enumerate(values):
            at = 128 * (i * count + g)
            ref[:, at : at + 128] = value[:, 128 * i : 128 * i + 128]


def quick_device(
    tokens, ln_gain_first, ln_bias_first, w_qkv, q_bias, v_bias, w_out, out_bias, ln_gain_second,
    ln_bias_second, w_up, up_bias, w_down, down_bias, ln_gain_third, ln_bias_third, w_first,
    conv_weights, conv_biases, clip_lengths, frame_mask, out_cot, pool_cot, penalty_scale,
):
    _, rows, width = tokens.shape
    frames = rows // PIXELS
    inner = w_up.shape[1]
    seqs = lax.axis_size("seq")
    rank = lax.axis_index("frame")
    bits = seqs.bit_length() - 1
    near = doubles(bits)
    far = [[bit] for pair in near[1:] for bit in pair] + near[:1]
    rank_at, seq_at = 2 * frames + 1, 2 * frames + 2

    def swap(x):
        return lax.ppermute(x, "frame", flip(2, 1))

    place = jnp.stack([rank, lax.axis_index("seq")]).astype(jnp.int32)
    info = jnp.concatenate([frame_mask[0], clip_lengths[0, 0:1], place])
    x = tokens[0]
    n1, k0, v0 = project(x, ln_gain_first, ln_bias_first, w_qkv, v_bias)
    far_k0, far_v0 = swap(k0), swap(v0)
    q, k1, v1 = project_more(n1, w_qkv, q_bias, v_bias)
    far_k1, far_v1 = swap(k1), swap(v1)
    count = jnp.sum(frame_mask).astype(jnp.float32) * jnp.ones((1, 128))
    count = add_all(count, near[0], (n1,))
    half = attn_fwd(info, q, k0, v0, far_k0, far_v0, (), 0, frames)
    for pair in near[1:]:
        count = add_all(count, pair, (half[0],))
    attended, inv, kc, vc, probs = attn_fwd(info, q, k1, v1, far_k1, far_v1, tuple(half), 1, frames)
    count = count[0, 0]
    weight = (penalty_scale / count).reshape(1)
    mid, n2, hidden, slope, out, n3 = mlp_fwd(
        x, attended, w_out, out_bias, ln_gain_second, ln_bias_second, w_up, up_bias, w_down,
        down_bias, ln_gain_third, ln_bias_third,
    )
    side, pooled, small, first_keep, first_send = learner(
        info, weight, n3, out, pool_cot[0], w_first, conv_weights, conv_biases, near, seqs
    )
    first_pad = jnp.concatenate(
        [w_first.T, jnp.zeros((128 - 9 * MAPS, width), jnp.bfloat16)], axis=0
    )
    d_down, d_up, d_branch, d_att, sums = mlp_bwd(
        out_cot[0], out, side, pool_cot[0], first_pad, ln_gain_third, w_down, slope, w_up, mid,
        ln_gain_second, w_out,
    )
    first = Stream(
        near, first_keep, first_send, ([f32_shape(width // seqs, 9 * MAPS // 2)], write_first)
    )
    meet = Total(
        near,
        small,
        ([f32_shape(3, MAPS, 9 * MAPS), f32_shape(4, MAPS), f32_shape(1, 1)], write_small),
    )
    vectors = Total(
        near, sums, ([f32_shape(width)] * 6 + [f32_shape(inner)], write_vectors)
    )
    down = Stream(
        far,
        *grad_by_rows(info, hidden, d_down, far, seqs, rank_at),
        ([f32_shape(inner // seqs, PART)], write_plain),
    )
    up = Stream(
        near,
        *grad_by_columns(info, n2, d_up, near, seqs, rank_at),
        ([f32_shape(width // seqs, inner // 2)], write_wide),
    )
    branch = Stream(
        near,
        *grad_by_rows(info, attended, d_branch, near, seqs, rank_at),
        ([f32_shape(width // seqs, PART)], write_plain),
    )
    early = [up, branch, first, vectors, meet]
    pairs = width // 128
    groups = pairs // 2
    pieces = {}

    def attend_back(which, after):
        dq, own_k, own_v, away = attn_bwd(
            info, q, kc, vc, attended, d_att, inv, probs, which, frames, after
        )
        away = swap(away)
        for i, pair in enumerate(which):
            pieces[pair] = [(dq, i), (own_k, i), (away, 2 * i), (own_v, i), (away, 2 * i + 1)]
        return dq

    def group_stream(g, after):
        both = (pieces[g], pieces[g + groups])
        grads = grad_pieces(info, normed[-1], width, both, near, seqs, rank_at, after)
        normed.extend(grads[2:])
        return Stream(near, *grads[:2]), [grads[1]]

    streams = []
    normed = [n1]
    after, _ = fold(info, seq_at, [(early, True), ([down], True)])
    last = attend_back((0, groups), after)
    after, _ = fold(info, seq_at, [(early, True), ([down], True)], (last,))
    last = attend_back((1, 1 + groups), after)
    after, _ = fold(info, seq_at, [(early, False), ([down], True)], (last,))
    stream, sent = group_stream(0, after)
    streams.append(stream)
    last = attend_back((2,), after + sent)
    fold(info, seq_at, [([down], False)], (last,))
    stream, after = group_stream(1, (last,))
    streams.append(stream)
    last = attend_back((2 + groups,), after + down.result)
    after, _ = fold(info, seq_at, [(streams[:2], True)], (last,))
    stream, _ = group_stream(2, after)
    streams.append(stream)
    tokens_grad, late = final_bwd(
        [pieces[p][i] for i in range(5) for p in range(pairs)], x, d_branch, ln_gain_first, w_qkv
    )
    late = Total(near, late, ([f32_shape(width)] * 4, write_vectors))
    while streams[2].at < streams[0].at:
        bundles = [([streams[2], late], True)]
        if streams[0].gots:
            bundles.append((streams[:2], False))
        fold(info, seq_at, bundles)
    while late.bits():
        fold(info, seq_at, [(streams + [late], True)])
    results = fold(
        info, seq_at, [(streams, False), ([late], False)],
        emit=([f32_shape(width // seqs, 3 * width // 2)], write_groups),
    )[1]
    vectors, late = vectors.result, late.result
    conv_w, conv_b, total = meet.result
    return (
        out[None],
        pooled[None],
        total[0, 0] / count,
        tokens_grad[None],
        late[0],
        late[1],
        results[0],
        late[2],
        late[3],
        branch.result[0],
        vectors[5],
        vectors[0],
        vectors[1],
        up.result[0],
        vectors[6],
        down.result[0],
        vectors[4],
        vectors[2],
        vectors[3],
        first.result[0],
        conv_w,
        conv_b,
    )


def per_device(*arrays):
    tokens, clip_lengths = arrays[0], arrays[19]
    frames = tokens.shape[1] // PIXELS
    seqs = lax.axis_size("seq")
    fits = (
        tokens.shape[0] == 1
        and lax.axis_size("frame") == 2
        and frames % 4 == 0
        and tokens.shape[1] % 32 == 0
        and tokens.shape[2] == HEADS * HEAD_DIM
        and seqs == 16
    )
    return (quick_device if fits else plain_device)(*arrays)


def solution(mesh):
    return jax.shard_map(
        per_device,
        mesh=mesh,
        in_specs=(
            P("seq", "frame", None),
            P(),
            P(),
            P(),
            P(),
            P(),
            P(),
            P(),
            P(),
            P(),
            P(),
            P(),
            P(),
            P(),
            P(),
            P(),
            P(),
            P(),
            P(),
            P("seq", None),
            P("seq", None),
            P("seq", "frame", None),
            P("seq", "frame", None),
            P(),
        ),
        out_specs=(
            P("seq", "frame", None),
            P("seq", "frame", None),
            P(),
            P("seq", "frame", None),
            P(),
            P(),
            P("seq", "frame"),
            P(),
            P(),
            P("seq", "frame"),
            P(),
            P(),
            P(),
            P("seq", "frame"),
            P(),
            P("seq", "frame"),
            P(),
            P(),
            P(),
            P("seq", "frame"),
            P(),
            P(),
        ),
        check_vma=False,
    )
```

```python
import functools

import jax
import jax.numpy as jnp
import numpy as np
from jax import lax
from jax.experimental import pallas as pl
from jax.experimental.pallas import tpu as pltpu
from jax.sharding import PartitionSpec as P

HEADS = 12
HEAD_DIM = 64
GRID = 14
MAPS = 8


EPS = 1e-06
NEG = -1e30
HIGHEST = lax.Precision.HIGHEST


def norm_rows(rows, gain, shift):
    center = rows - jnp.mean(rows, axis=-1, keepdims=True)
    spread = jnp.mean(center * center, axis=-1, keepdims=True)
    return center * lax.rsqrt(spread + EPS) * gain + shift


def shift_sum(taps):
    padded = jnp.pad(taps, ((0, 0), (1, 1), (1, 1), (0, 0), (0, 0)))
    total = padded[:, 0:GRID, 0:GRID, 0, :]
    for tap in range(1, 9):
        total = total + padded[:, tap // 3 : tap // 3 + GRID, tap % 3 : tap % 3 + GRID, tap, :]
    return total


def conv_tail(first, conv_biases, conv_weights):
    frames = first.shape[0]
    level = shift_sum(first.reshape(frames, GRID, GRID, 9, MAPS)) + conv_biases[0]
    for layer in range(3):
        hidden = jax.nn.gelu(level, approximate=False)
        taps = jnp.einsum("fijc,ck->fijk", hidden, conv_weights[layer], precision=HIGHEST)
        level = shift_sum(taps.reshape(frames, GRID, GRID, 9, MAPS)) + conv_biases[layer + 1]
    return jax.nn.sigmoid(level).reshape(frames, GRID * GRID, MAPS)


def exact_gelu(values):
    return jax.nn.gelu(values, approximate=False)


def pair_mask(query_code, key_code):
    return (query_code[:, :, None] == key_code[:, None, :])[:, None]


def score_rows(query_rows, key_rows):
    return jnp.einsum(
        "sqhe,skhe->shqk", query_rows, key_rows, preferred_element_type=jnp.float32
    ) * HEAD_DIM ** (-0.5)


def pair_terms(query_rows, dout_rows, lse_rows, delta_rows, key_rows, value_rows, allowed):
    scores = score_rows(query_rows, key_rows)
    probs = jnp.where(allowed, jnp.exp(scores - lse_rows[..., None]), 0.0)
    slopes = jnp.einsum(
        "sqhe,skhe->shqk", dout_rows, value_rows, preferred_element_type=jnp.float32
    )
    grads = (probs * (slopes - delta_rows[..., None])).astype(jnp.bfloat16)
    return (probs.astype(jnp.bfloat16), grads)


def column_sum(values):
    return jnp.sum(values.astype(jnp.float32), axis=0)


def plain_device(
    tokens,
    ln_gain_first,
    ln_bias_first,
    w_qkv,
    q_bias,
    v_bias,
    w_out,
    out_bias,
    ln_gain_second,
    ln_bias_second,
    w_up,
    up_bias,
    w_down,
    down_bias,
    ln_gain_third,
    ln_bias_third,
    w_first,
    conv_weights,
    conv_biases,
    clip_lengths,
    frame_mask,
    out_cot,
    pool_cot,
    penalty_scale,
):
    seq_count, local, width = tokens.shape
    pixels = GRID * GRID
    frames_here = local // pixels
    frame_total = lax.axis_size("frame")
    frame_rank = lax.axis_index("frame")
    slot_frames = frames_here * frame_total
    length = local * frame_total
    rows = seq_count * local
    image_count = seq_count * frames_here
    scale = HEAD_DIM ** (-0.5)
    positions = jnp.arange(slot_frames, dtype=jnp.int32)[None, :]
    segment_frames = (positions >= clip_lengths[:, 0:1]).astype(jnp.int32)
    key_frames = jnp.where(frame_mask > 0, segment_frames, -1)
    first_frame = frame_rank * frames_here
    query_code = jnp.repeat(
        lax.dynamic_slice_in_dim(segment_frames, first_frame, frames_here, 1), pixels, axis=1
    )
    key_code = jnp.repeat(key_frames, pixels, axis=1)
    valid_here = (
        lax.dynamic_slice_in_dim(frame_mask, first_frame, frames_here, 1)
        .reshape(image_count)
        .astype(jnp.float32)
    )
    flat = tokens.reshape(rows, width).astype(jnp.float32)
    normed_one, back_one = jax.vjp(norm_rows, flat, ln_gain_first, ln_bias_first)
    normed_one = normed_one.astype(jnp.bfloat16)
    qkv_bias = jnp.concatenate([q_bias, jnp.zeros_like(q_bias), v_bias])
    qkv = (jnp.dot(normed_one, w_qkv, preferred_element_type=jnp.float32) + qkv_bias).astype(
        jnp.bfloat16
    )
    qkv = qkv.reshape(seq_count, local, 3, HEADS, HEAD_DIM)
    queries = qkv[:, :, 0]
    keys_here = qkv[:, :, 1]
    values_here = qkv[:, :, 2]
    keys_all, values_all = (
        lax.all_gather(keys_here, "frame", axis=1, tiled=True),
        lax.all_gather(values_here, "frame", axis=1, tiled=True),
    )

    def block_of(array, index):
        return lax.dynamic_slice_in_dim(array, index * local, local, 1)

    def stats_turn(index, carry):
        allowed = pair_mask(query_code, block_of(key_code, index))

        def stats_update(state):
            top, mass = state
            masked = jnp.where(allowed, score_rows(queries, block_of(keys_all, index)), NEG)
            new_top = jnp.maximum(top, jnp.max(masked, axis=-1))
            kept = jnp.where(allowed, jnp.exp(masked - new_top[..., None]), 0.0)
            return (new_top, mass * jnp.exp(top - new_top) + jnp.sum(kept, axis=-1))

        return lax.cond(jnp.any(allowed), stats_update, lambda state: state, carry)

    start_top = jnp.full((seq_count, HEADS, local), NEG, jnp.float32)
    top, mass = lax.fori_loop(0, frame_total, stats_turn, (start_top, jnp.zeros_like(start_top)))
    lse = top + jnp.log(mass)

    def value_turn(index, total):
        allowed = pair_mask(query_code, block_of(key_code, index))

        def value_update(state):
            scores = score_rows(queries, block_of(keys_all, index))
            probs = jnp.where(allowed, jnp.exp(scores - lse[..., None]), 0.0).astype(jnp.bfloat16)
            return state + jnp.einsum(
                "shqk,skhe->sqhe",
                probs,
                block_of(values_all, index),
                preferred_element_type=jnp.float32,
            )

        return lax.cond(jnp.any(allowed), value_update, lambda state: state, total)

    attended = lax.fori_loop(0, frame_total, value_turn, jnp.zeros(queries.shape, jnp.float32))
    attended_low = attended.astype(jnp.bfloat16).reshape(rows, width)
    middle = flat + jnp.dot(attended_low, w_out, preferred_element_type=jnp.float32) + out_bias
    normed_two, back_two = jax.vjp(norm_rows, middle, ln_gain_second, ln_bias_second)
    normed_two = normed_two.astype(jnp.bfloat16)
    upper = jnp.dot(normed_two, w_up, preferred_element_type=jnp.float32) + up_bias
    hidden, gelu_back = jax.vjp(exact_gelu, upper)
    hidden = hidden.astype(jnp.bfloat16)
    output = middle + jnp.dot(hidden, w_down, preferred_element_type=jnp.float32) + down_bias
    output_low = output.astype(jnp.bfloat16)
    normed_three, back_three = jax.vjp(norm_rows, output, ln_gain_third, ln_bias_third)
    normed_three = normed_three.astype(jnp.bfloat16)
    first = jnp.dot(normed_three, w_first, preferred_element_type=jnp.float32)
    maps, tail_back = jax.vjp(
        conv_tail, first.reshape(image_count, pixels, 9 * MAPS), conv_biases, conv_weights
    )
    maps_low = maps.astype(jnp.bfloat16)
    output_frames = output_low.reshape(image_count, pixels, width)
    pooled = (
        jnp.einsum("fpm,fpd->fmd", maps_low, output_frames, preferred_element_type=jnp.float32)
        * valid_here[:, None, None]
    )
    pooled_tokens = pooled.astype(jnp.bfloat16).reshape(seq_count, frames_here * MAPS, width)
    total_map = jnp.sum(maps, axis=-1)
    intersection = 0.5 * (total_map * total_map - jnp.sum(maps * maps, axis=-1))
    intersection_local = jnp.sum(intersection * valid_here[:, None])
    count_local = jnp.sum(valid_here)
    intersection_total, count_total = lax.psum((intersection_local, count_local), ("seq", "frame"))
    penalty = intersection_total / count_total
    pool_frames = pool_cot.reshape(image_count, MAPS, width)
    weight_cot = penalty_scale / count_total
    d_maps = (
        jnp.einsum("fmd,fpd->fpm", pool_frames, output_frames, preferred_element_type=jnp.float32)
        * valid_here[:, None, None]
    )
    d_maps = d_maps + (weight_cot * valid_here)[:, None, None] * (total_map[..., None] - maps)
    d_first, d_conv_biases, d_conv_weights = tail_back(d_maps)
    d_first = d_first.reshape(rows, 9 * MAPS).astype(jnp.bfloat16)
    grad_w_first = jnp.dot(normed_three.T, d_first, preferred_element_type=jnp.float32)
    d_normed_three = jnp.dot(d_first, w_first.T, preferred_element_type=jnp.float32)
    d_from_three, d_gain_three, d_bias_three = back_three(d_normed_three)
    d_pool_rows = (
        jnp.einsum("fpm,fmd->fpd", maps_low, pool_frames, preferred_element_type=jnp.float32)
        * valid_here[:, None, None]
    )
    d_output = (
        out_cot.reshape(rows, width).astype(jnp.float32)
        + d_from_three
        + d_pool_rows.reshape(rows, width)
    )
    d_down = d_output.astype(jnp.bfloat16)
    grad_w_down = jnp.dot(hidden.T, d_down, preferred_element_type=jnp.float32)
    grad_down_bias = column_sum(d_down)
    d_hidden = jnp.dot(d_down, w_down.T, preferred_element_type=jnp.float32)
    d_upper = gelu_back(d_hidden)[0].astype(jnp.bfloat16)
    grad_w_up = jnp.dot(normed_two.T, d_upper, preferred_element_type=jnp.float32)
    grad_up_bias = column_sum(d_upper)
    d_normed_two = jnp.dot(d_upper, w_up.T, preferred_element_type=jnp.float32)
    d_from_two, d_gain_two, d_bias_two = back_two(d_normed_two)
    d_middle = d_output + d_from_two
    d_branch = d_middle.astype(jnp.bfloat16)
    grad_w_out = jnp.dot(attended_low.T, d_branch, preferred_element_type=jnp.float32)
    grad_out_bias = column_sum(d_branch)
    dout_low = jnp.dot(d_branch, w_out.T, preferred_element_type=jnp.float32).astype(jnp.bfloat16)
    dout_low = dout_low.reshape(seq_count, local, HEADS, HEAD_DIM)
    delta = jnp.sum(dout_low.astype(jnp.float32) * attended, axis=-1).transpose(0, 2, 1)
    zeros_here = jnp.zeros(queries.shape, jnp.float32)
    full_zeros = jnp.zeros((seq_count, length, HEADS, HEAD_DIM), jnp.float32)

    def both_turn(index, carry):
        allowed = pair_mask(query_code, block_of(key_code, index))

        def both_update(state):
            grad_q, grad_k, grad_v = state
            key_rows = block_of(keys_all, index)
            probs, grads = pair_terms(
                queries, dout_low, lse, delta, key_rows, block_of(values_all, index), allowed
            )
            grad_q = (
                grad_q
                + jnp.einsum("shqk,skhe->sqhe", grads, key_rows, preferred_element_type=jnp.float32)
                * scale
            )
            part_k = (
                jnp.einsum("shqk,sqhe->skhe", grads, queries, preferred_element_type=jnp.float32)
                * scale
            )
            part_v = jnp.einsum(
                "shqk,sqhe->skhe", probs, dout_low, preferred_element_type=jnp.float32
            )
            grad_k = lax.dynamic_update_slice_in_dim(grad_k, part_k, index * local, 1)
            grad_v = lax.dynamic_update_slice_in_dim(grad_v, part_v, index * local, 1)
            return (grad_q, grad_k, grad_v)

        return lax.cond(jnp.any(allowed), both_update, lambda state: state, carry)

    grad_q, grad_k_all, grad_v_all = lax.fori_loop(
        0, frame_total, both_turn, (zeros_here, full_zeros, full_zeros)
    )
    grad_k, grad_v = (
        lax.psum_scatter(
            grad_k_all.astype(jnp.bfloat16), "frame", scatter_dimension=1, tiled=True
        ).astype(jnp.float32),
        lax.psum_scatter(
            grad_v_all.astype(jnp.bfloat16), "frame", scatter_dimension=1, tiled=True
        ).astype(jnp.float32),
    )
    grad_qkv = (
        jnp.stack([grad_q, grad_k, grad_v], axis=2).astype(jnp.bfloat16).reshape(rows, 3 * width)
    )
    grad_w_qkv = jnp.dot(normed_one.T, grad_qkv, preferred_element_type=jnp.float32)
    grad_q_bias = column_sum(grad_qkv[:, :width])
    grad_v_bias = column_sum(grad_qkv[:, 2 * width :])
    d_normed_one = jnp.dot(grad_qkv, w_qkv.T, preferred_element_type=jnp.float32)
    d_from_one, d_gain_one, d_bias_one = back_one(d_normed_one)
    tokens_grad = (d_middle + d_from_one).astype(jnp.bfloat16).reshape(seq_count, local, width)
    summed = (
        lax.psum_scatter(
            grad_w_qkv.astype(jnp.bfloat16), "seq", scatter_dimension=0, tiled=True
        ).astype(jnp.float32),
        lax.psum_scatter(
            grad_w_out.astype(jnp.bfloat16), "seq", scatter_dimension=0, tiled=True
        ).astype(jnp.float32),
        lax.psum_scatter(
            grad_w_up.astype(jnp.bfloat16), "seq", scatter_dimension=0, tiled=True
        ).astype(jnp.float32),
        lax.psum_scatter(
            grad_w_down.astype(jnp.bfloat16), "seq", scatter_dimension=0, tiled=True
        ).astype(jnp.float32),
        lax.psum_scatter(
            grad_w_first.astype(jnp.bfloat16), "seq", scatter_dimension=0, tiled=True
        ).astype(jnp.float32),
    )
    grad_w_qkv, grad_w_out, grad_w_up, grad_w_down, grad_w_first = (
        lax.psum_scatter(
            summed[0].astype(jnp.bfloat16), "frame", scatter_dimension=1, tiled=True
        ).astype(jnp.float32),
        lax.psum_scatter(
            summed[1].astype(jnp.bfloat16), "frame", scatter_dimension=1, tiled=True
        ).astype(jnp.float32),
        lax.psum_scatter(
            summed[2].astype(jnp.bfloat16), "frame", scatter_dimension=1, tiled=True
        ).astype(jnp.float32),
        lax.psum_scatter(
            summed[3].astype(jnp.bfloat16), "frame", scatter_dimension=1, tiled=True
        ).astype(jnp.float32),
        lax.psum_scatter(
            summed[4].astype(jnp.bfloat16), "frame", scatter_dimension=1, tiled=True
        ).astype(jnp.float32),
    )
    small = lax.psum(
        (
            d_gain_one,
            d_bias_one,
            d_gain_two,
            d_bias_two,
            d_gain_three,
            d_bias_three,
            grad_q_bias,
            grad_v_bias,
            grad_out_bias,
            grad_up_bias,
            grad_down_bias,
            d_conv_weights,
            d_conv_biases,
        ),
        ("seq", "frame"),
    )
    block_output = output_low.reshape(seq_count, local, width)
    return (
        block_output,
        pooled_tokens,
        penalty,
        tokens_grad,
        small[0],
        small[1],
        grad_w_qkv,
        small[6],
        small[7],
        grad_w_out,
        small[8],
        small[2],
        small[3],
        grad_w_up,
        small[9],
        grad_w_down,
        small[10],
        small[4],
        small[5],
        grad_w_first,
        small[11],
        small[12],
    )

FAR = -3e30
LOG2E = 1.4426950408889634
LN2 = 0.6931471805599453
NN = (((1,), (0,)), ((), ()))
NT = (((1,), (1,)), ((), ()))
TN = (((0,), (0,)), ((), ()))
PIXELS = 196
UNIT = 256
VMEM_LIMIT = 40 * 1024 * 1024
WIDE_LIMIT = 60 * 1024 * 1024


def dot(a, b, dims=NN):
    return lax.dot_general(a, b, dims, preferred_element_type=jnp.float32)


def compact_rows(frame_total):
    return (-(-frame_total * PIXELS // UNIT) + 3) * UNIT


def key_places(frames_here, info_ref):
    total = 2 * frames_here
    length = info_ref[total]
    count = [jnp.int32(0), jnp.int32(0)]
    places = []
    for f in range(total):
        kept = info_ref[f]
        late = (f >= length).astype(jnp.int32)
        places.append((kept, late, jnp.where(late == 1, count[1], count[0])))
        count[0] = count[0] + kept * (1 - late)
        count[1] = count[1] + kept * late
    units = [(c * PIXELS + UNIT - 1) // UNIT for c in count]
    start = units[0] * UNIT
    starts = [
        (kept, pl.multiple_of(jnp.where(late == 1, start, 0) + place * PIXELS, 4))
        for kept, late, place in places
    ]
    tails = [pl.multiple_of(count[0] * PIXELS, 4), pl.multiple_of(start + count[1] * PIXELS, 4)]
    return starts, tails, units[0], units[0] + units[1]


def clip_edge(frames_here, info_ref):
    total = 2 * frames_here
    first = info_ref[total + 1] * frames_here
    return jnp.clip((info_ref[total] - first) * PIXELS, 0, frames_here * PIXELS)


def gather_keys(frames_here, info_ref, starts, tails, own_k, own_v, far_k, far_v, kf, vf):
    total = 2 * frames_here
    rank = info_ref[total + 1]
    width = own_k.shape[1]
    for tail in tails:
        for ref in (kf, vf):
            ref[pl.ds(tail, UNIT), :] = jnp.zeros((UNIT, width), jnp.float32)
    for f in range(total):
        kept, place = starts[f]
        side = f // frames_here
        at = f % frames_here * PIXELS
        base = at // 16 * 16

        def put(k_ref, v_ref):
            for src, dst in ((k_ref, kf), (v_ref, vf)):
                block = src[base : base + 208, :].astype(jnp.float32)
                dst[pl.ds(place, PIXELS), :] = block[at - base : at - base + PIXELS, :]

        @pl.when((kept == 1) & (rank == side))
        def _():
            put(own_k, own_v)

        @pl.when((kept == 1) & (rank != side))
        def _():
            put(far_k, far_v)


def real_keys(start, size, split, tails, axis, shape):
    at = lax.broadcasted_iota(jnp.int32, shape, axis) + start
    return at < jnp.where(at >= split * UNIT, tails[1], tails[0])


def query_tiles(rows):
    parts = rows // 512
    return [(i * 512, 512) for i in range(parts)], (parts * 512, rows - parts * 512)


def split_heads(rows):
    lane = lax.broadcasted_iota(jnp.int32, rows.shape, 1)
    zero = jnp.zeros_like(rows)
    return jnp.where(lane < 64, rows, zero), jnp.where(lane < 64, zero, rows)


def clip_bias(late, edge, at, size):
    column = lax.broadcasted_iota(jnp.int32, (1, size), 1) + at
    return jnp.where((column >= edge) == late, 0.0, FAR)


def sweep(first, end, sizes, body):
    count = end - first
    big = sizes[0]
    main = count // big

    def step(c, carry):
        body(pl.multiple_of((first + c * big) * UNIT, UNIT), big * UNIT)
        return carry

    lax.fori_loop(0, main, step, 0)
    at = first + main * big
    left = count - main * big
    for size in sizes[1:]:

        @pl.when((left & size) != 0)
        def _():
            body(pl.multiple_of(at * UNIT, UNIT), size * UNIT)

        at = at + (left & size)


def attn_fwd_kernel(
    frames_here, first_pair, info_ref, q_ref, own_k, own_v, far_k, far_v, o_ref, inv_ref, kc_ref,
    vc_ref, probs_ref, qm, qr, vt, acc, accr, top, kf, vf, big, middle, small, sems, flags,
):
    rows = q_ref.shape[0]
    pair = first_pair + pl.program_id(0)

    @pl.when(pl.program_id(0) == 0)
    def _():
        for i in range(5):
            flags[i] = 0

    def copy_out(slot, buffer, start, size):
        return pltpu.make_async_copy(
            buffer, probs_ref.at[pair, :, pl.ds(start, size), :], sems.at[slot]
        )

    def settle(slot, buffer, size):
        @pl.when(flags[slot] == size // UNIT)
        def _():
            copy_out(slot, buffer, 0, size).wait()
            flags[slot] = 0

    def settle_all():
        for slot in range(2):
            settle(slot, big.at[slot], 4 * UNIT)
            settle(slot, big.at[slot, :, pl.ds(0, 2 * UNIT), :], 2 * UNIT)
        settle(2, middle, 2 * UNIT)
        settle(3, small, UNIT)

    def take(size, lead):
        if size == lead:
            slot = flags[4]
            flags[4] = 1 - slot
            buffer = big.at[slot, :, pl.ds(0, size), :]
        else:
            slot, buffer = (2, middle) if size == 2 * UNIT else (3, small)
        settle(slot, buffer, size)
        return slot, buffer

    def leave(slot, buffer, start, size):
        copy_out(slot, buffer, start, size).start()
        flags[slot] = size // UNIT

    starts, tails, split, end = key_places(frames_here, info_ref)
    edge = clip_edge(frames_here, info_ref)
    crossing = (edge > 0) & (edge < rows)
    low = jnp.where(edge > 0, 0, split)
    high = jnp.where(edge < rows, end, split)
    gather_keys(frames_here, info_ref, starts, tails, own_k, own_v, far_k, far_v, kf, vf)
    tiles, (rest_at, rest) = query_tiles(rows)
    qm[0], qm[1] = split_heads(q_ref[...])
    for h in range(2):
        qr[h * rest : h * rest + rest, :] = qm[h, rest_at:rows, :]
    acc[...] = jnp.zeros_like(acc)
    accr[...] = jnp.zeros_like(accr)
    top[...] = jnp.zeros_like(top)

    def prepare(start, size):
        span = pl.ds(start, size)
        kc_ref[span, :] = kf[span, :].astype(jnp.bfloat16)
        values = vf[span, :].astype(jnp.bfloat16)
        vc_ref[span, :] = values
        vt[0:128, span] = values.T
        real = real_keys(start, size, split, tails, 1, (16, size))
        vt[128:144, span] = real.astype(jnp.float32).astype(jnp.bfloat16)

    sweep(low, high, (2, 1), prepare)

    def value_rows(h, span):
        return jnp.concatenate([vt[64 * h : 64 * h + 64, span], vt[128:144, span]], axis=0)

    def plain(work, lead, start, size):
        span = pl.ds(start, size)
        keys = kc_ref[span, :]

        def scores(item):
            h, at, wide, _ = item
            return dot(keys, qr[...] if h is None else qm[h, at : at + wide, :], NT)

        slot, buffer = take(size, lead * UNIT)
        ahead = scores(work[0])
        for i, (h, at, wide, bias) in enumerate(work):
            s = ahead
            if i + 1 < len(work):
                ahead = scores(work[i + 1])
            if bias is not None:
                s = s + bias
            p = jnp.exp2(s * QUERY_SCALE).astype(jnp.bfloat16)
            if h is None:
                buffer[0, :, rest_at : rest_at + 2 * rest] = p
                accr[:, : 2 * rest] += dot(vt[:, span], p)
            else:
                buffer[h, :, at : at + wide] = p
                acc[h, :, at : at + wide] += dot(value_rows(h, span), p)
        leave(slot, buffer, start, size)

    every = [(h, at, wide, None) for h in range(2) for at, wide in tiles]

    @pl.when(jnp.logical_not(crossing))
    def _():
        sweep(low, high, (4, 2, 1), functools.partial(plain, every + [(None, 0, 2 * rest, None)], 4))

    @pl.when(crossing)
    def _():
        for late in (False, True):
            shown = tiles[1:] if late else tiles[:-1]
            work = [
                (h, at, wide, clip_bias(late, edge, at, wide) if 0 < at < tiles[-1][0] else None)
                for h in range(2)
                for at, wide in shown
            ]
            if late:
                work.append((None, 0, 2 * rest, None))
            body = functools.partial(plain, work, 2)
            sweep(split if late else 0, end if late else split, (2, 1), body)

    for h in range(2):
        lanes = slice(h * rest, h * rest + rest)
        acc[h, 0:64, rest_at:rows] += accr[64 * h : 64 * h + 64, lanes]
        acc[h, 64:80, rest_at:rows] += accr[128:144, lanes]
    mass = jnp.concatenate([acc[0, 64:72, :], acc[1, 64:72, :]], axis=0)
    safe = (jnp.min(mass) >= 2.0**-60) & (jnp.max(mass) <= 2.0**60)

    @pl.when(jnp.logical_not(safe))
    def _():
        settle_all()
        acc[...] = jnp.zeros_like(acc)
        top[...] = jnp.full_like(top, NEG)

        def careful(start, size):
            span = pl.ds(start, size)
            keys = kc_ref[span, :]
            real = real_keys(start, size, split, tails, 0, (size, 1))
            drop = jnp.where(real, 0.0, FAR)
            late = start >= split * UNIT
            for h in range(2):
                for at, wide in tiles + [(rest_at, rest)]:
                    lanes = slice(at, at + wide)
                    s = dot(keys, qm[h, lanes, :], NT) * QUERY_SCALE + drop
                    bias = jnp.where(crossing, clip_bias(late, edge, at, wide), 0.0)
                    old = top[h : h + 1, lanes]
                    new = jnp.maximum(old, jnp.max(s, axis=0, keepdims=True) + bias)
                    p = jnp.exp2(s - (new - bias)).astype(jnp.bfloat16)
                    top[h : h + 1, lanes] = new
                    acc[h, :, lanes] = acc[h, :, lanes] * jnp.exp2(old - new) + dot(
                        value_rows(h, span), p
                    )

        sweep(low, high, (1,), careful)
        for h in range(2):
            top[h : h + 1, :] += jnp.log2(acc[h, 64:65, :])

        def record(start, size):
            span = pl.ds(start, size)
            keys = kc_ref[span, :]
            real = real_keys(start, size, split, tails, 0, (size, 1))
            drop = jnp.where(real, 0.0, FAR)
            late = start >= split * UNIT
            slot, buffer = take(size, 4 * UNIT)
            ends = []
            for at, wide in tiles + [(rest_at, rest)]:
                lanes = slice(at, at + wide)
                for h in range(2):
                    s = dot(keys, qm[h, lanes, :], NT) * QUERY_SCALE + drop
                    bias = jnp.where(crossing, clip_bias(late, edge, at, wide), 0.0)
                    p = jnp.exp2(jnp.minimum(s - (top[h : h + 1, lanes] - bias), 0.0))
                    if at == rest_at:
                        ends.append(p)
                    else:
                        buffer[h, :, lanes] = p.astype(jnp.bfloat16)
            ends = jnp.concatenate(ends, axis=1).astype(jnp.bfloat16)
            buffer[0, :, rest_at : rest_at + 2 * rest] = ends
            leave(slot, buffer, start, size)

        sweep(low, high, (1,), record)

    for at, wide in tiles + [(rest_at, rest)]:
        lanes = slice(at, at + wide)
        halves = []
        for h in range(2):
            sums = acc[h, 64:65, lanes]
            halves.append(acc[h, 0:64, lanes] / sums)
            inv_ref[0, h : h + 1, lanes] = jnp.where(safe, 1.0 / sums, 1.0)
        o_ref[lanes, :] = jnp.concatenate(halves, axis=0).T.astype(jnp.bfloat16)

    @pl.when(pl.program_id(0) == pl.num_programs(0) - 1)
    def _():
        settle_all()


def attn_fwd(info, q, own_k, own_v, far_k, far_v, old, part, frames_here):
    rows, width = q.shape
    pairs = width // 256
    length = compact_rows(2 * frames_here)
    rest = rows % 512
    lanes = -(-rows // 128) * 128
    block = pl.BlockSpec((rows, 128), lambda p, *_: (0, p))
    column = pl.BlockSpec((rows, 128), lambda p, *_: (0, p + part * pairs))
    keys = pl.BlockSpec((length, 128), lambda p, *_: (0, p + part * pairs))

    def kernel(*refs):
        return attn_fwd_kernel(frames_here, part * pairs, *refs[:6], *refs[6 + len(old) :])

    return pl.pallas_call(
        kernel,
        out_shape=(
            jax.ShapeDtypeStruct((rows, width), jnp.bfloat16),
            jax.ShapeDtypeStruct((2 * pairs, 8, rows), jnp.float32),
            jax.ShapeDtypeStruct((length, width), jnp.bfloat16),
            jax.ShapeDtypeStruct((length, width), jnp.bfloat16),
            jax.ShapeDtypeStruct((2 * pairs, 2, length, lanes), jnp.bfloat16),
        ),
        grid_spec=pltpu.PrefetchScalarGridSpec(
            num_scalar_prefetch=1,
            grid=(pairs,),
            in_specs=[column, block, block, block, block]
            + [pl.BlockSpec(memory_space=pl.ANY)] * len(old),
            out_specs=[
                column,
                pl.BlockSpec((1, 8, rows), lambda p, *_: (p + part * pairs, 0, 0)),
                keys,
                keys,
                pl.BlockSpec(memory_space=pl.ANY),
            ],
            scratch_shapes=[
                pltpu.VMEM((2, rows, 128), jnp.bfloat16),
                pltpu.VMEM((2 * rest, 128), jnp.bfloat16),
                pltpu.VMEM((144, length), jnp.bfloat16),
                pltpu.VMEM((2, 80, rows), jnp.float32),
                pltpu.VMEM((144, 128), jnp.float32),
                pltpu.VMEM((8, rows), jnp.float32),
                pltpu.VMEM((length, 128), jnp.float32),
                pltpu.VMEM((length, 128), jnp.float32),
                pltpu.VMEM((2, 2, 4 * UNIT, lanes), jnp.bfloat16),
                pltpu.VMEM((2, 2 * UNIT, lanes), jnp.bfloat16),
                pltpu.VMEM((2, UNIT, lanes), jnp.bfloat16),
                pltpu.SemaphoreType.DMA((4,)),
                pltpu.SMEM((8,), jnp.int32),
            ],
        ),
        input_output_aliases={6 + i: i for i in range(len(old))},
        compiler_params=params(WIDE_LIMIT),
        cost_estimate=cost(4e10, 1e7),
        name="attn_fwd",
    )(info, q, own_k, own_v, far_k, far_v, *old)


def attn_bwd_kernel(
    frames_here, first_pair, apart, info_ref, q_ref, k_ref, v_ref, o_ref, do_ref, inv_ref,
    probs_ref, dq_ref, own_dk, own_dv, away, qm, qr, dom, dor, dqt, dqr, delta, dk_all, dv_all,
    back, held, sems,
):
    rows = q_ref.shape[0]
    pair = first_pair + apart * pl.program_id(0)
    total = 2 * frames_here
    length = info_ref[total]
    rank = info_ref[total + 1]
    starts, _, split, end = key_places(frames_here, info_ref)
    edge = clip_edge(frames_here, info_ref)
    crossing = (edge > 0) & (edge < rows)
    low = jnp.where(edge > 0, 0, split)
    top_unit = jnp.where(edge < rows, end, split)
    tiles, (rest_at, rest) = query_tiles(rows)
    qm[0], qm[1] = split_heads(q_ref[...])

    def copy_in(first, i, count, slot):
        start = pl.multiple_of((first + i * count) * UNIT, UNIT)
        return pltpu.make_async_copy(
            probs_ref.at[pair, :, pl.ds(start, count * UNIT), :],
            held.at[slot, :, pl.ds(0, count * UNIT), :],
            sems.at[slot],
        )

    @pl.when(jnp.logical_not(crossing))
    def _():
        copy_in(low, 0, 2, 0).start()

    high = [inv_ref[0, h : h + 1, :].astype(jnp.bfloat16).astype(jnp.float32) for h in range(2)]
    deep = [inv_ref[0, h : h + 1, :] - high[h] for h in range(2)]
    lines = jnp.concatenate(high + deep + [jnp.zeros((4, rows), jnp.float32)], axis=0)
    spot = lax.broadcasted_iota(jnp.int32, (8, 128), 0)
    head = (lax.broadcasted_iota(jnp.int32, (8, 128), 1) >= 64).astype(jnp.int32)
    pick = ((spot == head) | (spot == head + 2)).astype(jnp.float32).astype(jnp.bfloat16)
    share = dot(lines.astype(jnp.bfloat16), pick, TN)
    douts_low = (do_ref[...].astype(jnp.float32) * share).astype(jnp.bfloat16)
    dom[0], dom[1] = split_heads(douts_low)
    for h in range(2):
        qr[h * rest : h * rest + rest, :] = qm[h, rest_at:rows, :]
        dor[h * rest : h * rest + rest, :] = dom[h, rest_at:rows, :]
    dqt[...] = jnp.zeros_like(dqt)
    dqr[...] = jnp.zeros_like(dqr)
    for at, wide in tiles + [(rest_at, rest)]:
        span = slice(at, at + wide)
        prod = (o_ref[span, :].astype(jnp.float32) * do_ref[span, :].astype(jnp.float32)).T
        for h in range(2):
            inner = jnp.sum(prod[64 * h : 64 * h + 64], axis=0, keepdims=True)
            delta[h : h + 1, span] = inner * inv_ref[0, h : h + 1, span]

    def visit(work, probs, start, size):
        span = pl.ds(start, size)
        keys = k_ref[span, :]
        values = v_ref[span, :]
        turned = keys.T

        def rows_of(item):
            h, at, wide = item
            if h is None:
                return qr[...], dor[...]
            return qm[h, at : at + wide, :], dom[h, at : at + wide, :]

        def slopes(item):
            return dot(values, rows_of(item)[1], NT)

        dk = jnp.zeros((size, 128), jnp.float32)
        dv = jnp.zeros((size, 128), jnp.float32)
        ahead = slopes(work[0])
        for i, item in enumerate(work):
            h, at, wide = item
            dp = ahead
            if i + 1 < len(work):
                ahead = slopes(work[i + 1])
            queries, douts = rows_of(item)
            if h is None:
                p = probs[0, :size, rest_at : rest_at + 2 * rest]
                inner = jnp.concatenate([delta[g : g + 1, rest_at:rows] for g in range(2)], axis=1)
            else:
                p = probs[h, :size, at : at + wide]
                inner = delta[h : h + 1, at : at + wide]
            ds = (p.astype(jnp.float32) * (dp - inner)).astype(jnp.bfloat16)
            dv = dv + dot(p, douts)
            dk = dk + dot(ds, queries)
            if h is None:
                dqr[:, : 2 * rest] += dot(turned, ds)
            else:
                dqt[h, :, at : at + wide] += dot(turned[64 * h : 64 * h + 64], ds)
        return dk, dv

    def fresh(work, probs, start, size):
        dk, dv = visit(work, probs, start, size)
        dk_all[pl.ds(start, size), :] = dk * 0.125
        dv_all[pl.ds(start, size), :] = dv

    def travel(first, end, count, work, started=False):
        main = (end - first) // count
        total = main + (end - first - main * count)

        if not started:

            @pl.when(total > 0)
            def _():
                copy_in(first, 0, count, 0).start()

        def step(i, size):
            slot = lax.rem(i, 2)
            copy_in(first, i, count, slot).wait()

            @pl.when(i + 1 < total)
            def _():
                copy_in(first, i + 1, count, 1 - slot).start()

            start = pl.multiple_of((first + i * count) * UNIT, UNIT)
            fresh(work, held.at[slot], start, size)

        def loop(i, carry):
            step(i, count * UNIT)
            return carry

        lax.fori_loop(0, main, loop, 0)
        if count > 1:

            @pl.when(total > main)
            def _():
                step(main, UNIT)

    every = [(h, at, wide) for h in range(2) for at, wide in tiles]

    @pl.when(jnp.logical_not(crossing))
    def _():
        travel(low, top_unit, 2, every + [(None, 0, 2 * rest)], started=True)

    @pl.when(crossing)
    def _():
        for late in (False, True):
            shown = tiles[1:] if late else tiles[:-1]
            work = [(h, at, wide) for h in range(2) for at, wide in shown]
            if late:
                work.append((None, 0, 2 * rest))
            travel(split if late else 0, end if late else split, 2, work)

    for h in range(2):
        lanes = slice(h * rest, h * rest + rest)
        dqt[h, :, rest_at:rows] += dqr[64 * h : 64 * h + 64, lanes]
    for at, wide in tiles + [(rest_at, rest)]:
        both = jnp.concatenate([dqt[0, :, at : at + wide], dqt[1, :, at : at + wide]], axis=0)
        dq_ref[at : at + wide, :] = (both * 0.125).T.astype(jnp.bfloat16)

    for side in range(2):

        def put(k_out, v_out):
            for src, out in ((dk_all, k_out), (dv_all, v_out)):
                for f in range(side * frames_here, side * frames_here + frames_here):
                    kept, place = starts[f]
                    use = (kept == 1) & jnp.where(f >= length, edge < rows, edge > 0)
                    at = f % frames_here * PIXELS
                    back[at : at + PIXELS, :] = jnp.where(use, src[pl.ds(place, PIXELS), :], 0.0)
                out(back[:rows, :].astype(jnp.bfloat16))

        def write(ref, lanes):
            def store(value):
                ref[:, lanes] = value

            return store

        @pl.when(rank == side)
        def _():
            put(write(own_dk, slice(0, 128)), write(own_dv, slice(0, 128)))

        @pl.when(rank != side)
        def _():
            put(write(away, slice(0, 128)), write(away, slice(128, 256)))


def attn_bwd(info, q, kc, vc, o, do, inv, probs, pairs, frames_here, after):
    rows = q.shape[0]
    length = kc.shape[0]
    rest = rows % 512
    first = pairs[0]
    apart = pairs[-1] - first
    rowspec = pl.BlockSpec((rows, 128), lambda p, *_: (0, first + apart * p))
    keyspec = pl.BlockSpec((length, 128), lambda p, *_: (0, first + apart * p))
    out = pl.BlockSpec((rows, 128), lambda p, *_: (0, p))

    def kernel(*refs):
        return attn_bwd_kernel(frames_here, first, apart, *refs[:8], *refs[8 + len(after) :])

    return pl.pallas_call(
        kernel,
        out_shape=(jax.ShapeDtypeStruct((rows, 128 * len(pairs)), jnp.bfloat16),) * 3
        + (jax.ShapeDtypeStruct((rows, 256 * len(pairs)), jnp.bfloat16),),
        grid_spec=pltpu.PrefetchScalarGridSpec(
            num_scalar_prefetch=1,
            grid=(len(pairs),),
            in_specs=[
                rowspec,
                keyspec,
                keyspec,
                rowspec,
                rowspec,
                pl.BlockSpec((1, 8, rows), lambda p, *_: (first + apart * p, 0, 0)),
                pl.BlockSpec(memory_space=pl.ANY),
            ]
            + [pl.BlockSpec(memory_space=pl.ANY)] * len(after),
            out_specs=[out] * 3 + [pl.BlockSpec((rows, 256), lambda p, *_: (0, p))],
            scratch_shapes=[
                pltpu.VMEM((2, rows, 128), jnp.bfloat16),
                pltpu.VMEM((2 * rest, 128), jnp.bfloat16),
                pltpu.VMEM((2, rows, 128), jnp.bfloat16),
                pltpu.VMEM((2 * rest, 128), jnp.bfloat16),
                pltpu.VMEM((2, 64, rows), jnp.float32),
                pltpu.VMEM((128, 128), jnp.float32),
                pltpu.VMEM((8, rows), jnp.float32),
                pltpu.VMEM((length, 128), jnp.float32),
                pltpu.VMEM((length, 128), jnp.float32),
                pltpu.VMEM((rows + 16, 128), jnp.float32),
                pltpu.VMEM((2, 2, 2 * UNIT, probs.shape[3]), jnp.bfloat16),
                pltpu.SemaphoreType.DMA((2,)),
            ],
        ),
        compiler_params=params(),
        cost_estimate=cost(3e10 * len(pairs), 1e7),
        name="attn_bwd",
    )(info, q, kc, vc, o, do, inv, probs, *after)


TILE = 400
SMALL_TILE = 224
PART = 384
INV_SQRT2 = 0.7071067811865476
INV_SQRT_2PI = 0.3989422804014327
QUERY_SCALE = 0.125 * LOG2E


def params(limit=VMEM_LIMIT):
    return pltpu.CompilerParams(vmem_limit_bytes=limit, dimension_semantics=("arbitrary",))


def cost(flops, moved):
    return pl.CostEstimate(flops=int(flops), bytes_accessed=int(moved), transcendentals=0)


def tile_spec(width):
    return pl.BlockSpec((TILE, width), lambda i: (i, 0))


def small_spec(width):
    return pl.BlockSpec((SMALL_TILE, width), lambda i: (i, 0))


def whole_spec(shape):
    return pl.BlockSpec(shape, lambda i: (0,) * len(shape), pipeline_mode=pl.Buffered(1))


def low_shape(rows, width):
    return jax.ShapeDtypeStruct((rows, width), jnp.bfloat16)


def ln_parts(x):
    center = x - jnp.mean(x, axis=-1, keepdims=True)
    rstd = lax.rsqrt(jnp.mean(center * center, axis=-1, keepdims=True) + EPS)
    return center * rstd, rstd


def ln_back(dy, gain, xhat, rstd):
    dxhat = dy * gain
    along = jnp.mean(dxhat * xhat, axis=-1, keepdims=True)
    return rstd * (dxhat - jnp.mean(dxhat, axis=-1, keepdims=True) - xhat * along)


def line(ref):
    return ref[...].reshape(1, -1)


def vector_spec(size):
    return pl.BlockSpec((size,), lambda i: (0,))


def rows_sum(x):
    return jnp.sum(x, axis=0, keepdims=True)


def project_kernel(x_ref, gain_ref, shift_ref, wk, wv, bias_ref, n_ref, k_ref, v_ref):
    xhat, _ = ln_parts(x_ref[...].astype(jnp.float32))
    normed = (xhat * line(gain_ref) + line(shift_ref)).astype(jnp.bfloat16)
    n_ref[...] = normed
    half = k_ref.shape[1]
    k_ref[...] = dot(normed, wk[...]).astype(jnp.bfloat16)
    v_ref[...] = (dot(normed, wv[...]) + line(bias_ref)[:, :half]).astype(jnp.bfloat16)


def weight_spec(width, size, column):
    return pl.BlockSpec((width, size), lambda i: (0, column), pipeline_mode=pl.Buffered(1))


def project(x, gain, shift, w, v_bias):
    rows, width = x.shape
    half = width // 2
    return pl.pallas_call(
        project_kernel,
        out_shape=(low_shape(rows, width), low_shape(rows, half), low_shape(rows, half)),
        grid=(-(-rows // TILE),),
        in_specs=[
            tile_spec(width),
            vector_spec(width),
            vector_spec(width),
            weight_spec(width, half, 2),
            weight_spec(width, half, 4),
            vector_spec(width),
        ],
        out_specs=[tile_spec(width), tile_spec(half), tile_spec(half)],
        compiler_params=params(WIDE_LIMIT),
        cost_estimate=cost(2 * rows * width * width, 10 * rows * width),
        name="project",
    )(x, gain, shift, w, w, v_bias)


def project_more_kernel(n_ref, wq, wk, wv, q_bias, v_bias, q_ref, k_ref, v_ref):
    normed = n_ref[...]
    k_ref[...] = dot(normed, wk[...]).astype(jnp.bfloat16)
    half = v_ref.shape[1]
    v_ref[...] = (dot(normed, wv[...]) + line(v_bias)[:, half:]).astype(jnp.bfloat16)
    q_ref[...] = (dot(normed, wq[...]) + line(q_bias)).astype(jnp.bfloat16)


def project_more(normed, w, q_bias, v_bias):
    rows, width = normed.shape
    half = width // 2
    return pl.pallas_call(
        project_more_kernel,
        out_shape=(low_shape(rows, width), low_shape(rows, half), low_shape(rows, half)),
        grid=(-(-rows // TILE),),
        in_specs=[
            tile_spec(width),
            weight_spec(width, width, 0),
            weight_spec(width, half, 3),
            weight_spec(width, half, 5),
            vector_spec(width),
            vector_spec(width),
        ],
        out_specs=[tile_spec(width), tile_spec(half), tile_spec(half)],
        compiler_params=params(WIDE_LIMIT),
        cost_estimate=cost(4 * rows * width * width, 10 * rows * width),
        name="project_more",
    )(normed, w, w, w, q_bias, v_bias)


def mlp_fwd_kernel(
    x_ref, a_ref, w_out, b_out, gain2, shift2, w_up, b_up, w_down, b_down, gain3, shift3,
    mid_ref, n2_ref, hid_ref, slope_ref, out_ref, n3_ref,
):
    width = x_ref.shape[1]
    inner = w_up.shape[1]
    parts = inner // width
    middle = x_ref[...].astype(jnp.float32) + dot(a_ref[...], w_out[...]) + line(b_out)
    mid_ref[...] = middle.astype(jnp.bfloat16)
    xhat, _ = ln_parts(middle)
    n2 = (xhat * line(gain2) + line(shift2)).astype(jnp.bfloat16)
    n2_ref[...] = n2
    out = middle + line(b_down)
    up_shift = line(b_up)

    def raise_part(j):
        span = slice(j * width, (j + 1) * width)
        return dot(n2, w_up[:, span]) + up_shift[:, span]

    ahead = raise_part(0)
    for j in range(parts):
        span = slice(j * width, (j + 1) * width)
        up = ahead
        if j + 1 < parts:
            ahead = raise_part(j + 1)
        area = 0.5 + 0.5 * lax.erf(up * INV_SQRT2)
        bell = jnp.exp2(up * up * (-0.5 * LOG2E)) * INV_SQRT_2PI
        hid = (up * area).astype(jnp.bfloat16)
        hid_ref[:, span] = hid
        slope_ref[:, span] = (area + up * bell).astype(jnp.bfloat16)
        out = out + dot(hid, w_down[span, :])
    out_ref[...] = out.astype(jnp.bfloat16)
    xhat, _ = ln_parts(out)
    n3_ref[...] = (xhat * line(gain3) + line(shift3)).astype(jnp.bfloat16)


def mlp_fwd(x, attended, w_out, b_out, gain2, shift2, w_up, b_up, w_down, b_down, gain3, shift3):
    rows, width = x.shape
    inner = w_up.shape[1]
    vec = vector_spec(width)
    return pl.pallas_call(
        mlp_fwd_kernel,
        out_shape=(
            low_shape(rows, width), low_shape(rows, width), low_shape(rows, inner),
            low_shape(rows, inner), low_shape(rows, width), low_shape(rows, width),
        ),
        grid=(-(-rows // TILE),),
        in_specs=[
            tile_spec(width), tile_spec(width), whole_spec(w_out.shape), vec, vec, vec,
            whole_spec(w_up.shape), vector_spec(inner), whole_spec(w_down.shape), vec, vec, vec,
        ],
        out_specs=[
            tile_spec(width), tile_spec(width), tile_spec(inner),
            tile_spec(inner), tile_spec(width), tile_spec(width),
        ],
        compiler_params=params(WIDE_LIMIT),
        cost_estimate=cost(
            2 * rows * width * (width + 2 * inner), 2 * rows * (6 * width + 2 * inner)
        ),
        name="mlp_fwd",
    )(x, attended, w_out, b_out, gain2, shift2, w_up, b_up, w_down, b_down, gain3, shift3)


def mlp_bwd_kernel(
    rows, cot_ref, out_ref, side_ref, pool_ref, w_first, gain3, w_down, slope_ref, w_up, mid_ref,
    gain2, w_out, ddown_ref, dup_ref, dbranch_ref, datt_ref, sums_ref,
):
    width = cot_ref.shape[1]
    inner = w_up.shape[1]
    parts = inner // width

    @pl.when(pl.program_id(0) == 0)
    def _():
        sums_ref[...] = jnp.zeros_like(sums_ref)

    inside = lax.broadcasted_iota(jnp.int32, (TILE, 1), 0) < rows - pl.program_id(0) * TILE

    def add(row, value):
        total = rows_sum(jnp.where(inside, value, 0.0))
        middle = total.shape[1] // 2
        below = sums_ref.shape[0] // 2 + row
        sums_ref[row : row + 1, :] += total[:, :middle]
        sums_ref[below : below + 1, :] += total[:, middle:]

    dn3 = dot(side_ref[:, :128], w_first[...])
    xhat, rstd = ln_parts(out_ref[...].astype(jnp.float32))
    add(2, dn3 * xhat)
    add(3, dn3)
    d_out = (
        cot_ref[...].astype(jnp.float32)
        + ln_back(dn3, line(gain3), xhat, rstd)
        + dot(side_ref[:, 128:192], pool_ref[...])
    )
    d_down = d_out.astype(jnp.bfloat16)
    ddown_ref[...] = d_down
    add(4, d_down.astype(jnp.float32))

    def lower_part(j):
        return dot(d_down, w_down[j * width : (j + 1) * width, :], NT)

    ahead = lower_part(0)
    dn2 = jnp.zeros(cot_ref.shape, jnp.float32)
    for j in range(parts):
        span = slice(j * width, (j + 1) * width)
        d_hid = ahead
        if j + 1 < parts:
            ahead = lower_part(j + 1)
        d_up = (d_hid * slope_ref[:, span].astype(jnp.float32)).astype(jnp.bfloat16)
        dup_ref[:, span] = d_up
        add(6 + j, d_up.astype(jnp.float32))
        dn2 = dn2 + dot(d_up, w_up[:, span], NT)
    xhat, rstd = ln_parts(mid_ref[...].astype(jnp.float32))
    add(0, dn2 * xhat)
    add(1, dn2)
    d_branch = (d_out + ln_back(dn2, line(gain2), xhat, rstd)).astype(jnp.bfloat16)
    dbranch_ref[...] = d_branch
    add(5, d_branch.astype(jnp.float32))
    datt_ref[...] = dot(d_branch, w_out[...], NT).astype(jnp.bfloat16)


def mlp_bwd(cot, out, side, pool, w_first, gain3, w_down, slope, w_up, mid, gain2, w_out):
    rows, width = cot.shape
    inner = w_up.shape[1]
    vec = vector_spec(width)
    return pl.pallas_call(
        functools.partial(mlp_bwd_kernel, rows),
        out_shape=(
            low_shape(rows, width), low_shape(rows, inner), low_shape(rows, width),
            low_shape(rows, width), jax.ShapeDtypeStruct((32, width // 2), jnp.float32),
        ),
        grid=(-(-rows // TILE),),
        in_specs=[
            tile_spec(width), tile_spec(width), tile_spec(256), whole_spec(pool.shape),
            whole_spec(w_first.shape), vec, whole_spec(w_down.shape), tile_spec(inner),
            whole_spec(w_up.shape), tile_spec(width), vec, whole_spec(w_out.shape),
        ],
        out_specs=[
            tile_spec(width), tile_spec(inner), tile_spec(width), tile_spec(width),
            pl.BlockSpec((32, width // 2), lambda i: (0, 0)),
        ],
        compiler_params=params(),
        cost_estimate=cost(
            2 * rows * width * (width + 2 * inner), 2 * rows * (6 * width + 2 * inner)
        ),
        name="mlp_bwd",
    )(cot, out, side, pool, w_first, gain3, w_down, slope, w_up, mid, gain2, w_out)


def final_bwd_kernel(rows, pairs, *refs):
    pieces = [refs[i * pairs : (i + 1) * pairs] for i in range(5)]
    x_ref, branch_ref, gain, w_ref, grad_ref, sums_ref = refs[5 * pairs :]
    width = x_ref.shape[1]

    @pl.when(pl.program_id(0) == 0)
    def _():
        sums_ref[...] = jnp.zeros_like(sums_ref)

    inside = lax.broadcasted_iota(jnp.int32, (SMALL_TILE, 1), 0) < rows - pl.program_id(0) * SMALL_TILE

    def add(row, value):
        total = rows_sum(jnp.where(inside, value, 0.0))
        middle = total.shape[1] // 2
        below = sums_ref.shape[0] // 2 + row
        sums_ref[row : row + 1, :] += total[:, :middle]
        sums_ref[below : below + 1, :] += total[:, middle:]

    def join(part):
        return jnp.concatenate([r[...] for r in part], axis=1)

    def total(part, other):
        both = [a[...].astype(jnp.float32) + b[...].astype(jnp.float32) for a, b in zip(part, other)]
        return jnp.concatenate(both, axis=1).astype(jnp.bfloat16)

    dq = join(pieces[0])
    dk = total(pieces[1], pieces[2])
    dv = total(pieces[3], pieces[4])
    dn = (
        dot(dq, w_ref[:, :width], NT)
        + dot(dk, w_ref[:, width : 2 * width], NT)
        + dot(dv, w_ref[:, 2 * width :], NT)
    )
    xhat, rstd = ln_parts(x_ref[...].astype(jnp.float32))
    add(0, dn * xhat)
    add(1, dn)
    add(2, dq.astype(jnp.float32))
    add(3, dv.astype(jnp.float32))
    grad_ref[...] = (
        branch_ref[...].astype(jnp.float32) + ln_back(dn, line(gain), xhat, rstd)
    ).astype(jnp.bfloat16)


def final_bwd(pieces, x, branch, gain, w):
    rows, width = x.shape
    pairs = width // 128
    return pl.pallas_call(
        functools.partial(final_bwd_kernel, rows, pairs),
        out_shape=(low_shape(rows, width), jax.ShapeDtypeStruct((16, width // 2), jnp.float32)),
        grid=(-(-rows // SMALL_TILE),),
        in_specs=[
            pl.BlockSpec((SMALL_TILE, 128), functools.partial(lambda c, i: (i, c), column))
            for _, column in pieces
        ]
        + [small_spec(width)] * 2
        + [vector_spec(width), whole_spec(w.shape)],
        out_specs=[small_spec(width), pl.BlockSpec((16, width // 2), lambda i: (0, 0))],
        compiler_params=params(),
        cost_estimate=cost(6 * rows * width * width, 16 * rows * width),
        name="final_bwd",
    )(*[array for array, _ in pieces], x, branch, gain, w)


def grid_masks(frames, lanes):
    table = np.zeros((16, lanes), np.float32)
    lane = np.arange(lanes)
    pixel = lane % PIXELS
    i, j = pixel // GRID, pixel % GRID
    inside = lane < frames * PIXELS
    for a in range(3):
        for b in range(3):
            ok = (i + a - 1 >= 0) & (i + a - 1 < GRID) & (j + b - 1 >= 0) & (j + b - 1 < GRID)
            table[3 * a + b] = ok & inside
    table[9] = np.where(inside, lane // PIXELS, -1)
    return table


def learner_kernel(
    frames, info_ref, weight_ref, n3_ref, out_ref, pool_ref, wt_ref, cw_ref, cwt_ref, cb_ref,
    mask_ref, side_ref, pooled_ref, small_ref, keep_ref, send_ref, rounds, seqs,
):
    rows = n3_ref.shape[0]
    lanes = mask_ref.shape[1]
    extra = lanes - rows
    rank = info_ref[2 * frames + 1]
    frame_of = mask_ref[9:10, :]
    live = jnp.zeros((1, lanes), jnp.float32)
    for f in range(frames):
        kept = info_ref[rank * frames + f].astype(jnp.float32)
        live = live + jnp.where(frame_of == f, kept, 0.0)
    inside = (frame_of >= 0).astype(jnp.float32)

    def widen(x):
        return jnp.concatenate([x, jnp.zeros((x.shape[0], extra), jnp.float32)], axis=1)

    def turn(x, by):
        return x if by % lanes == 0 else pltpu.roll(x, by % lanes, 1)

    def gather_taps(taps):
        total = jnp.zeros((8, lanes), jnp.float32)
        for t in range(9):
            step = (t // 3 - 1) * GRID + t % 3 - 1
            total = total + turn(taps[8 * t : 8 * t + 8, :], -step) * mask_ref[t : t + 1, :]
        return total

    def spread_taps(level):
        parts = []
        for t in range(9):
            step = (t // 3 - 1) * GRID + t % 3 - 1
            parts.append(turn(level, step) * mask_ref[8 - t : 9 - t, :])
        return jnp.concatenate(parts, axis=0)

    def exact(a, b, dims=NN):
        return lax.dot_general(
            a, b, dims, precision=HIGHEST, preferred_element_type=jnp.float32
        )

    def area_of(x):
        return 0.5 + 0.5 * lax.erf(x * INV_SQRT2)

    taps = widen(dot(wt_ref[...], n3_ref[...], NT))
    levels = [gather_taps(taps) + cb_ref[:, 0:1]]
    hiddens = []
    for n in range(3):
        hiddens.append(levels[n] * area_of(levels[n]))
        levels.append(gather_taps(exact(cwt_ref[n], hiddens[n])) + cb_ref[:, n + 1 : n + 2])
    maps = 1.0 / (1.0 + jnp.exp(-levels[3]))
    total = rows_sum(maps)
    meet = 0.5 * (total * total - rows_sum(maps * maps)) * live
    small_ref[...] = jnp.zeros_like(small_ref)
    small_ref[8:9, 128:256] = jnp.zeros((1, 128), jnp.float32) + jnp.sum(meet)
    shifts = jnp.zeros((8, 128), jnp.float32)
    lane = lax.broadcasted_iota(jnp.int32, (8, 128), 1)

    owner = lax.broadcasted_iota(jnp.int32, (8 * frames, lanes), 0) // 8
    mine = owner.astype(jnp.float32) == frame_of
    low_maps = maps.astype(jnp.bfloat16).astype(jnp.float32) * live
    stacked = jnp.where(mine, jnp.concatenate([low_maps] * frames, axis=0), 0.0)
    out = out_ref[...]
    pooled_ref[...] = dot(stacked[:, :rows].astype(jnp.bfloat16), out).astype(jnp.bfloat16)
    pairs = jnp.where(mine, widen(dot(pool_ref[...], out, NT)), 0.0)
    d_maps = pairs[0:8]
    for f in range(1, frames):
        d_maps = d_maps + pairs[8 * f : 8 * f + 8]
    d_maps = d_maps * live + weight_ref[0] * live * (total - maps)
    d_level = d_maps * maps * (1.0 - maps)
    for n in (2, 1, 0):
        shifts = jnp.where(lane == n + 1, jnp.sum(d_level, axis=1, keepdims=True), shifts)
        d_taps = spread_taps(d_level)
        small_ref[0:8, 128 * n : 128 * n + 72] = exact(hiddens[n], d_taps, NT)
        d_hidden = exact(cw_ref[n], d_taps)
        x = levels[n]
        bell = jnp.exp(-0.5 * x * x) * INV_SQRT_2PI
        d_level = d_hidden * (area_of(x) + x * bell) * inside
    shifts = jnp.where(lane == 0, jnp.sum(d_level, axis=1, keepdims=True), shifts)
    small_ref[8:16, 0:8] = shifts.T[0:8, :]
    d_first = spread_taps(d_level)[:, :rows]
    grad = dot(d_first.astype(jnp.bfloat16), n3_ref[...])
    grad = jnp.concatenate([grad, jnp.zeros((56, grad.shape[1]), jnp.float32)], axis=0).T
    columns = 9 * MAPS // 2
    lane = lax.broadcasted_iota(jnp.int32, grad.shape, 1)
    left = jnp.where(lane < columns, grad, 0.0).astype(jnp.bfloat16)
    right = jnp.where(lane < columns, pltpu.roll(grad, 128 - columns, 1), 0.0).astype(jnp.bfloat16)
    size = grad.shape[0] // seqs // 3
    for ref, side in ((keep_ref, 0), (send_ref, 1)):
        value = jnp.where(rank == side, left, right)
        for o in range(seqs):
            parts = [value[(3 * o + t) * size : (3 * o + t + 1) * size, :] for t in range(3)]
            put_rows(ref, block_place(o, rounds) * size, jnp.concatenate(parts, axis=1))
    tall = jnp.concatenate(
        [
            d_first,
            jnp.zeros((56, rows), jnp.float32),
            stacked[:, :rows],
            jnp.zeros((128 - 8 * frames, rows), jnp.float32),
        ],
        axis=0,
    )
    side_ref[...] = tall.T.astype(jnp.bfloat16)


def learner(info, weight, n3, out, pool, w_first, conv_weights, conv_biases, rounds, seqs):
    rows, width = n3.shape
    frames = rows // PIXELS
    lanes = -(-rows // 128) * 128
    vm = pl.BlockSpec(memory_space=pltpu.VMEM)
    sm = pl.BlockSpec(memory_space=pltpu.SMEM)
    masks = jnp.asarray(grid_masks(frames, lanes))
    return pl.pallas_call(
        functools.partial(learner_kernel, frames, rounds=rounds, seqs=seqs),
        out_shape=(
            low_shape(rows, 256),
            low_shape(8 * frames, width),
            jax.ShapeDtypeStruct((16, PART), jnp.float32),
            low_shape(width // 3, PART),
            low_shape(width // 3, PART),
        ),
        in_specs=[sm, sm] + [vm] * 8,
        out_specs=(vm,) * 5,
        compiler_params=pltpu.CompilerParams(vmem_limit_bytes=VMEM_LIMIT),
        cost_estimate=cost(2e10, 4 * rows * width),
        name="learner",
    )(
        info, weight, n3, out, pool, w_first.T, conv_weights,
        conv_weights.transpose(0, 2, 1), conv_biases.T, masks,
    )


def flip(count, bit):
    return [(i, i ^ bit) for i in range(count)]


def low_sum(a, b):
    return (a.astype(jnp.float32) + b.astype(jnp.float32)).astype(jnp.bfloat16)


def block_place(owner, rounds):
    place = 0
    for bits in rounds:
        for bit in bits:
            place = place * 2 + ((owner >> bit) & 1)
    return place


def put_rows(ref, at, value):
    if not isinstance(at, int):
        at = pl.multiple_of(at, 16)
    ref[pl.ds(at, value.shape[0]), :] = value


def put_blocks(ref, value, first_owner, owners, rounds):
    size = value.shape[0] // owners
    for o in range(owners):
        place = block_place(first_owner + o, rounds)
        put_rows(ref, place * size, value[o * size : (o + 1) * size, :])


def grad_by_columns_kernel(rounds, seqs, info_ref, a_ref, b_ref, keep_ref, send_ref, turned):
    step = pl.program_id(0)
    half = pl.num_programs(0) // 2

    @pl.when(step == 0)
    def _():
        turned[...] = a_ref[...].T

    got = dot(turned[...], b_ref[...]).astype(jnp.bfloat16)
    parts = got.shape[1] // PART
    size = got.shape[0] // seqs

    def put(ref):
        for o in range(seqs):
            base = block_place(o, rounds) * size * parts * half
            for i in range(parts):
                at = base + (lax.rem(step, half) * parts + i) * size
                put_rows(ref, at, got[o * size : o * size + size, i * PART : i * PART + PART])

    @pl.when(step < half)
    def _():
        put(keep_ref)

    @pl.when(step >= half)
    def _():
        put(send_ref)


def grad_by_columns(info, a, b, rounds, seqs, at):
    rows, tall = a.shape
    wide = b.shape[1]
    block = min(768, wide // 2)
    half = wide // 2 // block
    out = jax.ShapeDtypeStruct((tall * wide // 2 // PART, PART), jnp.bfloat16)
    whole = pl.BlockSpec(out.shape, lambda j, info: (0, 0))
    return pl.pallas_call(
        functools.partial(grad_by_columns_kernel, rounds, seqs),
        out_shape=(out, out),
        grid_spec=pltpu.PrefetchScalarGridSpec(
            num_scalar_prefetch=1,
            grid=(2 * half,),
            in_specs=[
                pl.BlockSpec((rows, tall), lambda j, info: (0, 0)),
                pl.BlockSpec(
                    (rows, block),
                    lambda j, info: (0, jnp.where(j < half, info[at], 1 - info[at]) * half + j % half),
                ),
            ],
            out_specs=[whole, whole],
            scratch_shapes=[pltpu.VMEM((tall, rows), jnp.bfloat16)],
        ),
        compiler_params=params(),
        cost_estimate=cost(2 * rows * tall * wide, 2 * rows * (tall + wide)),
        name="grad_columns",
    )(info, a, b)


def pick_half(rank, value):
    middle = value.shape[1] // 2
    first, second = value[:, :middle], value[:, middle:]
    return jnp.where(rank == 0, first, second), jnp.where(rank == 0, second, first)


def grad_by_rows_kernel(rounds, seqs, at, info_ref, a_ref, b_ref, keep_ref, send_ref):
    step = pl.program_id(0)
    got = dot(a_ref[...], b_ref[...], TN).astype(jnp.bfloat16)
    keep, send = pick_half(info_ref[at], got)
    owners = seqs // (keep_ref.shape[0] // a_ref.shape[1])
    put_blocks(keep_ref, keep, step * owners, owners, rounds)
    put_blocks(send_ref, send, step * owners, owners, rounds)


def grad_by_rows(info, a, b, rounds, seqs, at):
    rows, tall = a.shape
    wide = b.shape[1]
    out = jax.ShapeDtypeStruct((tall, wide // 2), jnp.bfloat16)
    return pl.pallas_call(
        functools.partial(grad_by_rows_kernel, rounds, seqs, at),
        out_shape=(out, out),
        grid_spec=pltpu.PrefetchScalarGridSpec(
            num_scalar_prefetch=1,
            grid=(tall // 768,),
            in_specs=[
                pl.BlockSpec((rows, 768), lambda j, info: (0, j)),
                pl.BlockSpec((rows, wide), lambda j, info: (0, 0)),
            ],
            out_specs=[pl.BlockSpec((tall, wide // 2), lambda j, info: (0, 0))] * 2,
        ),
        compiler_params=params(),
        cost_estimate=cost(2 * rows * tall * wide, 2 * rows * (tall + wide)),
        name="grad_rows",
    )(info, a, b)


def grad_pieces_kernel(rounds, seqs, at, turn, info_ref, n_ref, *refs):
    (q0, k0, x0, v0, y0), (q1, k1, x1, v1, y1) = refs[:5], refs[5:10]
    if turn:
        keep_ref, send_ref, turned_ref = refs[-3:]
        turned_ref[...] = n_ref[...].T
    else:
        keep_ref, send_ref = refs[-2:]
        turned_ref = n_ref
    first = jnp.concatenate([q0[...], q1[...], low_sum(k0[...], x0[...])], axis=1)
    second = jnp.concatenate(
        [low_sum(k1[...], x1[...]), low_sum(v0[...], y0[...]), low_sum(v1[...], y1[...])], axis=1
    )
    both = jnp.concatenate([first, second], axis=1)
    got = dot(turned_ref[...], both).astype(jnp.bfloat16)
    keep, send = pick_half(info_ref[at], got)
    put_blocks(keep_ref, keep, 0, seqs, rounds)
    put_blocks(send_ref, send, 0, seqs, rounds)


def grad_pieces(info, n1, w_rows, pieces, rounds, seqs, at, after):
    turn = n1.shape[0] != w_rows
    rows, tall = n1.shape if turn else n1.shape[::-1]
    out = jax.ShapeDtypeStruct((tall, PART), jnp.bfloat16)
    flat = [piece for pair in pieces for piece in pair]
    whole = pl.BlockSpec((tall, PART), lambda i, info: (0, 0))
    return pl.pallas_call(
        functools.partial(grad_pieces_kernel, rounds, seqs, at, turn),
        out_shape=(out, out) + ((low_shape(tall, rows),) if turn else ()),
        grid_spec=pltpu.PrefetchScalarGridSpec(
            num_scalar_prefetch=1,
            grid=(1,),
            in_specs=[pl.BlockSpec(n1.shape, lambda i, info: (0, 0))]
            + [
                pl.BlockSpec((rows, 128), functools.partial(lambda c, i, info: (0, c), column))
                for _, column in flat
            ]
            + [pl.BlockSpec(memory_space=pl.ANY)] * len(after),
            out_specs=[whole, whole]
            + ([pl.BlockSpec((tall, rows), lambda i, info: (0, 0))] if turn else []),
        ),
        compiler_params=params(),
        cost_estimate=cost(2 * rows * tall * 768, 4 * rows * tall),
        name="grad_pieces",
    )(info, n1, *[array for array, _ in flat], *after)


class Stream:
    def __init__(self, rounds, keep, send, emit=None):
        self.rounds, self.at, self.keep, self.emit = rounds, 0, keep, emit
        self.gots = [(lax.ppermute(send, "frame", flip(2, 1)), 0)]

    def bits(self):
        return self.rounds[self.at] if self.at < len(self.rounds) else None


class Total(Stream):
    def __init__(self, rounds, value, emit):
        super().__init__(rounds, value, value, emit)


def split_low(value):
    high = value.astype(jnp.bfloat16)
    return high, (value - high.astype(jnp.float32)).astype(jnp.bfloat16)


def fold(info, at, bundles, after=(), emit=None):
    arrays, plan, outs = [], [], []

    def source(array):
        for i, known in enumerate(arrays):
            if known is array:
                return i
        arrays.append(array)
        return len(arrays) - 1

    for streams, sending in bundles:
        entry = []
        bits = streams[0].bits() if sending else None
        ways = 1 << len(bits) if bits else 1
        offset = 0
        for s in streams:
            parts = [(source(array), start) for array, start in s.gots]
            rows = s.keep.shape[0]
            entry.append((s, source(s.keep), parts, rows, offset))
            if isinstance(s, Total):
                kept = jax.ShapeDtypeStruct((rows, PART), jnp.float32)
                offset += 2 * rows
            else:
                kept = jax.ShapeDtypeStruct((rows // ways, PART), jnp.bfloat16)
                offset += rows // ways
            if sending:
                outs.append(kept)
            elif s.emit:
                outs += s.emit[0]
            elif not emit:
                outs.append(kept)
        outs += [jax.ShapeDtypeStruct((offset, PART), jnp.bfloat16)] * (ways - 1)
        plan.append((entry, bits, ways))
    if emit:
        outs += emit[0]

    def kernel(info_ref, *refs):
        sources, targets = refs[: len(arrays)], list(refs[len(arrays) + len(after) :])
        index = info_ref[at]
        ready = []
        for entry, bits, ways in plan:
            mine = 0
            for bit in bits or ():
                mine = mine * 2 + ((index >> bit) & 1)
            kept = []
            for s, own, parts, rows, offset in entry:
                size = rows // ways
                if bits:
                    kept.append(targets.pop(0))
                elif s.emit or not emit:
                    count = len(s.emit[0]) if s.emit else 1
                    kept.append([targets.pop(0) for _ in range(count)])
                else:
                    kept.append(None)
            sends = [targets.pop(0) for _ in range(ways - 1)]
            for (s, own, parts, rows, offset), keep in zip(entry, kept):

                def total(start, size):
                    value = sources[own][pl.ds(start, size), :].astype(jnp.float32)
                    for i, begin in parts:
                        if isinstance(s, Total):
                            if sources[i].dtype == jnp.float32:
                                value = value + sources[i][...]
                            else:
                                value = value + sources[i][begin : begin + rows, :].astype(jnp.float32)
                                value = value + sources[i][
                                    begin + rows : begin + 2 * rows, :
                                ].astype(jnp.float32)
                        else:
                            value = value + sources[i][pl.ds(begin + start, size), :].astype(jnp.float32)
                    return value

                if bits and isinstance(s, Total):
                    value = total(0, rows)
                    keep[...] = value
                    high, low = split_low(value)
                    for send in sends:
                        send[offset : offset + rows, :] = high
                        send[offset + rows : offset + 2 * rows, :] = low
                elif bits:
                    size = rows // ways
                    for m in range(ways):
                        start = pl.multiple_of((mine ^ m) * size, 16)
                        value = total(start, size).astype(jnp.bfloat16)
                        if m == 0:
                            keep[...] = value
                        else:
                            sends[m - 1][offset : offset + size, :] = value
                elif keep is None:
                    ready.append(total(0, rows))
                elif s.emit:
                    s.emit[1](total(0, rows), *keep)
                else:
                    keep[0][...] = total(0, rows).astype(keep[0].dtype)
        if emit:
            emit[1](ready, *targets)

    vm = pl.BlockSpec(memory_space=pltpu.VMEM)
    sm = pl.BlockSpec(memory_space=pltpu.SMEM)
    moved = sum(x.size * x.dtype.itemsize for x in arrays) * 2
    results = list(
        pl.pallas_call(
            kernel,
            out_shape=tuple(outs),
            in_specs=[sm] + [vm] * len(arrays) + [pl.BlockSpec(memory_space=pl.ANY)] * len(after),
            out_specs=(vm,) * len(outs),
            compiler_params=pltpu.CompilerParams(vmem_limit_bytes=VMEM_LIMIT),
            cost_estimate=cost(0, moved),
            name="fold",
        )(info, *arrays, *after)
    )
    sent = []
    count = lax.axis_size("seq")
    for entry, bits, ways in plan:
        for s, *_ in entry:
            if bits:
                s.keep = results.pop(0)
            elif s.emit:
                s.result = [results.pop(0) for _ in s.emit[0]]
            elif not emit:
                s.keep = results.pop(0)
            s.gots = []
        for m in range(1, ways):
            mask = 0
            for i, bit in enumerate(bits):
                mask |= ((m >> (len(bits) - 1 - i)) & 1) << bit
            send = results.pop(0)
            sent.append(send)
            got = lax.ppermute(send, "seq", flip(count, mask))
            for s, _, _, _, offset in entry:
                s.gots.append((got, offset))
        if bits:
            for s, *_ in entry:
                s.at += 1
    return sent[:1], results


def add_all(value, bits, after):
    count = lax.axis_size("seq")
    gots = []
    for m in range(1, 1 << len(bits)):
        mask = sum(((m >> i) & 1) << bit for i, bit in enumerate(bits))
        gots.append(lax.ppermute(value, "seq", flip(count, mask)))

    def kernel(*refs):
        total = refs[0][...]
        for ref in refs[1 : 1 + len(gots)]:
            total = total + ref[...]
        refs[-1][...] = total

    vm = pl.BlockSpec(memory_space=pltpu.VMEM)
    return pl.pallas_call(
        kernel,
        out_shape=jax.ShapeDtypeStruct(value.shape, jnp.float32),
        in_specs=[vm] * (1 + len(gots)) + [pl.BlockSpec(memory_space=pl.ANY)] * len(after),
        out_specs=vm,
        name="add_all",
    )(value, *gots, *after)


def doubles(bits):
    low = list(range(bits))
    return [low[i : i + 2] for i in range(0, bits, 2)]


def f32_shape(*shape):
    return jax.ShapeDtypeStruct(shape, jnp.float32)


def write_plain(value, ref):
    ref[...] = value


def write_wide(value, ref):
    size = ref.shape[0]
    for i in range(value.shape[0] // size):
        ref[:, i * PART : i * PART + PART] = value[i * size : i * size + size, :]


def write_first(value, ref):
    for i in range(3):
        ref[16 * i : 16 * i + 16, :] = value[:, 128 * i : 128 * i + ref.shape[1]]


def write_vectors(value, *refs):
    row = 0
    for ref in refs:
        for i in range(ref.shape[0] // (2 * PART)):
            ref[2 * PART * i : 2 * PART * i + PART] = value[row, :]
            ref[2 * PART * i + PART : 2 * PART * (i + 1)] = value[value.shape[0] // 2 + row, :]
            row += 1


def write_small(value, weights_ref, biases_ref, meet_ref):
    for n in range(3):
        weights_ref[n] = value[0:8, 128 * n : 128 * n + 9 * MAPS]
    biases_ref[...] = value[8:12, 0:MAPS]
    meet_ref[...] = value[8:9, 128:129]


def write_groups(values, ref):
    count = len(values)
    for i in range(3):
        for g, value in enumerate(values):
            at = 128 * (i * count + g)
            ref[:, at : at + 128] = value[:, 128 * i : 128 * i + 128]


def quick_device(
    tokens, ln_gain_first, ln_bias_first, w_qkv, q_bias, v_bias, w_out, out_bias, ln_gain_second,
    ln_bias_second, w_up, up_bias, w_down, down_bias, ln_gain_third, ln_bias_third, w_first,
    conv_weights, conv_biases, clip_lengths, frame_mask, out_cot, pool_cot, penalty_scale,
):
    _, rows, width = tokens.shape
    frames = rows // PIXELS
    inner = w_up.shape[1]
    seqs = lax.axis_size("seq")
    rank = lax.axis_index("frame")
    bits = seqs.bit_length() - 1
    near = doubles(bits)
    far = [[bit] for pair in near[1:] for bit in pair] + near[:1]
    rank_at, seq_at = 2 * frames + 1, 2 * frames + 2

    def swap(x):
        return lax.ppermute(x, "frame", flip(2, 1))

    place = jnp.stack([rank, lax.axis_index("seq")]).astype(jnp.int32)
    info = jnp.concatenate([frame_mask[0], clip_lengths[0, 0:1], place])
    x = tokens[0]
    n1, k0, v0 = project(x, ln_gain_first, ln_bias_first, w_qkv, v_bias)
    far_k0, far_v0 = swap(k0), swap(v0)
    q, k1, v1 = project_more(n1, w_qkv, q_bias, v_bias)
    far_k1, far_v1 = swap(k1), swap(v1)
    count = jnp.sum(frame_mask).astype(jnp.float32) * jnp.ones((1, 128))
    count = add_all(count, near[0], (n1,))
    half = attn_fwd(info, q, k0, v0, far_k0, far_v0, (), 0, frames)
    for pair in near[1:]:
        count = add_all(count, pair, (half[0],))
    attended, inv, kc, vc, probs = attn_fwd(info, q, k1, v1, far_k1, far_v1, tuple(half), 1, frames)
    count = count[0, 0]
    weight = (penalty_scale / count).reshape(1)
    mid, n2, hidden, slope, out, n3 = mlp_fwd(
        x, attended, w_out, out_bias, ln_gain_second, ln_bias_second, w_up, up_bias, w_down,
        down_bias, ln_gain_third, ln_bias_third,
    )
    side, pooled, small, first_keep, first_send = learner(
        info, weight, n3, out, pool_cot[0], w_first, conv_weights, conv_biases, near, seqs
    )
    first_pad = jnp.concatenate(
        [w_first.T, jnp.zeros((128 - 9 * MAPS, width), jnp.bfloat16)], axis=0
    )
    d_down, d_up, d_branch, d_att, sums = mlp_bwd(
        out_cot[0], out, side, pool_cot[0], first_pad, ln_gain_third, w_down, slope, w_up, mid,
        ln_gain_second, w_out,
    )
    first = Stream(
        near, first_keep, first_send, ([f32_shape(width // seqs, 9 * MAPS // 2)], write_first)
    )
    meet = Total(
        near,
        small,
        ([f32_shape(3, MAPS, 9 * MAPS), f32_shape(4, MAPS), f32_shape(1, 1)], write_small),
    )
    vectors = Total(
        near, sums, ([f32_shape(width)] * 6 + [f32_shape(inner)], write_vectors)
    )
    down = Stream(
        far,
        *grad_by_rows(info, hidden, d_down, far, seqs, rank_at),
        ([f32_shape(inner // seqs, PART)], write_plain),
    )
    up = Stream(
        near,
        *grad_by_columns(info, n2, d_up, near, seqs, rank_at),
        ([f32_shape(width // seqs, inner // 2)], write_wide),
    )
    branch = Stream(
        near,
        *grad_by_rows(info, attended, d_branch, near, seqs, rank_at),
        ([f32_shape(width // seqs, PART)], write_plain),
    )
    early = [up, branch, first, vectors, meet]
    pairs = width // 128
    groups = pairs // 2
    pieces = {}

    def attend_back(which, after):
        dq, own_k, own_v, away = attn_bwd(
            info, q, kc, vc, attended, d_att, inv, probs, which, frames, after
        )
        away = swap(away)
        for i, pair in enumerate(which):
            pieces[pair] = [(dq, i), (own_k, i), (away, 2 * i), (own_v, i), (away, 2 * i + 1)]
        return dq

    def group_stream(g, after):
        both = (pieces[g], pieces[g + groups])
        grads = grad_pieces(info, normed[-1], width, both, near, seqs, rank_at, after)
        normed.extend(grads[2:])
        return Stream(near, *grads[:2]), [grads[1]]

    streams = []
    normed = [n1]
    after, _ = fold(info, seq_at, [(early, True), ([down], True)])
    last = attend_back((0, groups), after)
    after, _ = fold(info, seq_at, [(early, True), ([down], True)], (last,))
    last = attend_back((1, 1 + groups), after)
    after, _ = fold(info, seq_at, [(early, False), ([down], True)], (last,))
    stream, sent = group_stream(0, after)
    streams.append(stream)
    last = attend_back((2,), after + sent)
    fold(info, seq_at, [([down], False)], (last,))
    stream, after = group_stream(1, (last,))
    streams.append(stream)
    last = attend_back((2 + groups,), after + down.result)
    after, _ = fold(info, seq_at, [(streams[:2], True)], (last,))
    stream, _ = group_stream(2, after)
    streams.append(stream)
    tokens_grad, late = final_bwd(
        [pieces[p][i] for i in range(5) for p in range(pairs)], x, d_branch, ln_gain_first, w_qkv
    )
    late = Total(near, late, ([f32_shape(width)] * 4, write_vectors))
    while streams[2].at < streams[0].at:
        bundles = [([streams[2], late], True)]
        if streams[0].gots:
            bundles.append((streams[:2], False))
        fold(info, seq_at, bundles)
    while late.bits():
        fold(info, seq_at, [(streams + [late], True)])
    results = fold(
        info, seq_at, [(streams, False), ([late], False)],
        emit=([f32_shape(width // seqs, 3 * width // 2)], write_groups),
    )[1]
    vectors, late = vectors.result, late.result
    conv_w, conv_b, total = meet.result
    return (
        out[None],
        pooled[None],
        total[0, 0] / count,
        tokens_grad[None],
        late[0],
        late[1],
        results[0],
        late[2],
        late[3],
        branch.result[0],
        vectors[5],
        vectors[0],
        vectors[1],
        up.result[0],
        vectors[6],
        down.result[0],
        vectors[4],
        vectors[2],
        vectors[3],
        first.result[0],
        conv_w,
        conv_b,
    )


def per_device(*arrays):
    tokens, clip_lengths = arrays[0], arrays[19]
    frames = tokens.shape[1] // PIXELS
    seqs = lax.axis_size("seq")
    fits = (
        tokens.shape[0] == 1
        and lax.axis_size("frame") == 2
        and frames % 4 == 0
        and tokens.shape[1] % 32 == 0
        and tokens.shape[2] == HEADS * HEAD_DIM
        and seqs == 16
    )
    return (quick_device if fits else plain_device)(*arrays)


def solution(mesh):
    return jax.shard_map(
        per_device,
        mesh=mesh,
        in_specs=(
            P("seq", "frame", None),
            P(),
            P(),
            P(),
            P(),
            P(),
            P(),
            P(),
            P(),
            P(),
            P(),
            P(),
            P(),
            P(),
            P(),
            P(),
            P(),
            P(),
            P(),
            P("seq", None),
            P("seq", None),
            P("seq", "frame", None),
            P("seq", "frame", None),
            P(),
        ),
        out_specs=(
            P("seq", "frame", None),
            P("seq", "frame", None),
            P(),
            P("seq", "frame", None),
            P(),
            P(),
            P("seq", "frame"),
            P(),
            P(),
            P("seq", "frame"),
            P(),
            P(),
            P(),
            P("seq", "frame"),
            P(),
            P("seq", "frame"),
            P(),
            P(),
            P(),
            P("seq", "frame"),
            P(),
            P(),
        ),
        check_vma=False,
    )
```
